32 devices in a mesh: section: 2 (over x), row: 8 (over z, core), col: 2 (over y).
Axes of the slice: x: 2, y: 2, z: 4, core: 2. Of those that a mesh axis runs over, the one named last changes fastest.
Arguments:
- inputs: bfloat16 [2, 4096, 768], P(None, ('row', 'col')), may hold values from -6 to 6
- cotangent: bfloat16 [2, 4096, 768], P(None, ('row', 'col')), may hold values from -6 to 6
- segments: int32 [2, 4096], P(None, ('row', 'col')), may hold values from 0 to 63, never falling along the last dimension, each value on 1 to 256 neighbouring positions
- routes: int32 [2, 2, 4096, 2], P('section', None, ('row', 'col')), may hold values from 0 to 31, all different within a row
- order: int32 [2, 2, 16, 256], P('section', None, ('row', 'col')), may hold values from 0 to 255, each once within a row
- attn_gain: bfloat16 [2, 768], P('section', ('row', 'col')), may hold values from 0.25 to 1.75
- qkv_weight: bfloat16 [2, 768, 2304], P('section', ('row', 'col')), may hold values from -0.21875 to 0.21875
- position_bias: bfloat16 [2, 384], P('section', ('row', 'col')), may hold values from -4 to 4
- out_weight: bfloat16 [2, 768, 768], P('section', ('row', 'col')), may hold values from -0.875 to 0.875
- moe_gain: bfloat16 [2, 768], P('section', ('row', 'col')), may hold values from 0.25 to 1.75
- router_weight: bfloat16 [2, 768, 32], P('section', ('row', 'col')), may hold values from -0.15625 to 0.15625
- expert_in: bfloat16 [2, 32, 768, 3072], P('section', 'row', None, 'col'), may hold values from -0.21875 to 0.21875
- expert_out: bfloat16 [2, 32, 3072, 768], P('section', 'row', 'col'), may hold values from -0.109375 to 0.109375
Outputs:
- layer_out: bfloat16 [2, 2, 4096, 768], P('section', None, ('row', 'col'))
- layer_in_grad: float32 [2, 2, 4096, 768], P('section', None, ('row', 'col'))
- attn_gain_grad: float32 [2, 768], P('section', ('row', 'col'))
- qkv_grad: float32 [2, 768, 2304], P('section', ('row', 'col'))
- bias_grad: float32 [2, 384], P('section', ('row', 'col'))
- out_grad: float32 [2, 768, 768], P('section', ('row', 'col'))
- moe_gain_grad: float32 [2, 768], P('section', ('row', 'col'))
- router_grad: float32 [2, 768, 32], P('section', ('row', 'col'))
- expert_in_grad: float32 [2, 32, 768, 3072], P('section', 'row', None, 'col')
- expert_out_grad: float32 [2, 32, 3072, 768], P('section', 'row', 'col')
The draws below stay inside these ranges and needn't reach their ends.
Inputs may be any that keep to these rules, and one draw needn't show every extreme that they name: `segments`: numbers never fall along a micro-batch; a document has at most 256 tokens. `routes`: A token names 2 different experts. `order`: each aligned block of 256 entries holds every value once.
All inputs are finite; a program needn't handle non-finite values.
Results may differ from the reference program's by a relative error of at most 0.024.
Values may be sent and summed in bfloat16 or wider, within the bound.
A program may use at most 320 MiB of HBM per device.

```python
import math
import jax
import jax.numpy as jnp
import numpy as np
from jax import lax

D = 768
ATTENTION_HEADS = 12
HEAD_DIM = 64
FF = 3072
TOP = 2
DISTANCE_BUCKETS = 32
MAX_DIST = 128
MICRO = 2
TOK_DEV = 256
EXPERTS = 32
GROUPS = 16
TOKENS = 4096
CAP = 20
N_ROW = 8
N_COL = 2


def spiked(values, key, source, target, shards_of, factor):
    owner, partner = [(jnp.arange(values.shape[dim]) // (values.shape[dim] // shards_of)).reshape([-1 if axis == dim else 1 for axis in range(values.ndim)]) for dim in (source, target)]
    chosen = jax.random.permutation(key, shards_of)[partner]
    strong = (owner == chosen) | (owner == (partner + shards_of // 2) % shards_of)
    return jnp.where(strong, factor * values, values)


def level_of(own_key, extent, shards, least, largest):
    def one(axis_at, shards_of):
        heights = jax.random.uniform(jax.random.fold_in(jax.random.fold_in(own_key, 6), axis_at), (shards_of,), jnp.float32, least / len(shards), largest / len(shards))
        return jnp.repeat(jnp.exp(heights), extent[axis_at] // shards_of).reshape((-1,) + (1,) * (len(extent) - axis_at - 1))

    loudness = one(*shards[0])
    for cut in shards[1:]:
        loudness = loudness * one(*cut)
    return loudness


def distinct(rng, rows, amount, top, lift):
    order = jax.random.permutation(jax.random.fold_in(rng, 1), amount)
    favour = order
    for power in range(3):
        favour = favour * favour // amount
    favour = favour * lift // amount
    lots = jax.random.randint(jax.random.fold_in(rng, 2), (rows, amount), 0, 4096) + favour
    fixed_rows = jax.random.permutation(jax.random.fold_in(rng, 3), rows)[jnp.arange(amount) % rows]
    lots = jnp.where(jnp.arange(rows)[:, None] == fixed_rows[None, :], 1 << 14, lots)
    merit = lots * amount + jnp.arange(amount)
    return lax.top_k(merit.astype(jnp.int32), top)[1].astype(jnp.int32)


def split_up(count, total, most, slope):
    weights = [(1 << 20) // math.isqrt(rank ** slope) + 1 for rank in range(2, count + 1)]
    rest, counts = total - most - (count - 1), [1] * (count - 1)
    while rest > 0:
        candidates = [i for i in range(count - 1) if counts[i] < most]
        mass, left = sum([weights[i] for i in candidates]), rest
        for i in candidates:
            addition = min(most - counts[i], max(1, left * weights[i] // mass), rest)
            counts[i] = counts[i] + addition
            rest = rest - addition
    return np.array([most] + counts)


def ragged(stream_key, count, total, most, lean):
    if count == 2:
        one = jax.random.randint(stream_key, (), max(1, total - most), min(most, total - 1) + 1)
        return jnp.stack([one, total - one])
    lengths = jnp.asarray(split_up(count, total, most, lean), jnp.int32)
    pairs = (count - 1) // 2
    source_of, taker = lengths[1:1 + 2 * pairs:2], lengths[2:2 + 2 * pairs:2]
    room = jnp.minimum(source_of - 1, most - taker)
    shifted = jax.random.randint(jax.random.fold_in(stream_key, 1), (pairs,), 0, 1 << 20) % (room + 1)
    lengths = lengths.at[1:1 + 2 * pairs:2].set(source_of - shifted).at[2:2 + 2 * pairs:2].set(taker + shifted)
    return lengths[jax.random.permutation(jax.random.fold_in(stream_key, 2), count)]


def scatter_about(own_key, shape, deviation, reach, split=(), kind=jnp.bfloat16):
    drawn = jax.random.normal(own_key, shape, jnp.float32) * deviation
    if len(split) > 0:
        drawn = level_of(own_key, shape, split, -0.22, 0.18) * drawn
    return jnp.clip(drawn, min=-reach, max=reach).astype(kind)


def noise_with(stream_key, extent, scale, limit, split, heavy, kind=jnp.bfloat16):
    entries = scale * jax.random.normal(stream_key, extent, jnp.float32)
    if split:
        entries = entries * level_of(stream_key, extent, split, -0.22, 0.18)
    return jnp.clip(spiked(entries, jax.random.fold_in(stream_key, 3), *heavy), -limit, limit).astype(kind)


def setup_inputs(seed: int = 0) -> dict:
    key_list = jax.random.split(jax.random.key(seed), 14)
    return {
        "inputs": scatter_about(key_list[0], (MICRO, TOKENS, D), 1.0, 6.0, ((1, 16),)),
        "cotangent": noise_with(key_list[1], (MICRO, TOKENS, D), 1.0, 6.0, ((1, 16),), (1, 2, 16, 2.0)),
        "segments": jax.vmap(lambda own: jnp.searchsorted(jnp.cumsum(ragged(own, 4 * GROUPS, TOKENS, TOK_DEV, 2)), jnp.arange(TOKENS), side="right"))(jax.random.split(key_list[2], MICRO)).reshape((MICRO, TOKENS)).astype(jnp.int32),
        "routes": distinct(key_list[3], 2 * MICRO * TOKENS, EXPERTS, TOP, 512).reshape((2, MICRO, TOKENS, TOP)),
        "order": jax.vmap(lambda own: jax.random.permutation(own, TOK_DEV))(jax.random.split(key_list[4], 2 * MICRO * GROUPS)).reshape((2, MICRO, GROUPS, TOK_DEV)).astype(jnp.int32),
        "attn_gain": jnp.clip(1.0 + 0.15 * jax.random.normal(key_list[5], (2, D), jnp.float32), 0.25, 1.75).astype(jnp.bfloat16),
        "qkv_weight": scatter_about(key_list[6], (2, D, 3 * D), D ** -0.5, 0.21875, ((0, 2), (1, 16))),
        "position_bias": scatter_about(key_list[7], (2, DISTANCE_BUCKETS * ATTENTION_HEADS), 1.0, 4.0, ((0, 2), (1, 16))),
        "out_weight": scatter_about(key_list[8], (2, D, D), (D // 16) ** -0.5, 0.875, ((0, 2), (1, 16))),
        "moe_gain": jnp.clip(1.0 + 0.15 * jax.random.normal(key_list[9], (2, D), jnp.float32), 0.25, 1.75).astype(jnp.bfloat16),
        "router_weight": scatter_about(key_list[10], (2, D, EXPERTS), (2 * D) ** -0.5, 0.15625, ((0, 2), (1, 16))),
        "expert_in": scatter_about(key_list[11], (2, EXPERTS, D, FF), D ** -0.5, 0.21875, ((0, 2), (1, 8), (3, 2))),
        "expert_out": scatter_about(key_list[12], (2, EXPERTS, FF, D), FF ** -0.5, 0.109375, ((0, 2), (1, 8), (2, 2))),
    }


@jax.custom_vjp
def low(v):
    return lax.optimization_barrier(v.astype(jnp.bfloat16)).astype(jnp.float32)

@jax.custom_vjp
def low_back(v):
    return v

def low_keep(v):
    return (low(v), None)

def low_pass(kept, grad):
    return (grad,)

def back_keep(v):
    return (v, None)

def back_low(kept, grad):
    return (low(grad),)
low.defvjp(low_keep, low_pass)
low_back.defvjp(back_keep, back_low)
EPS = 1e-06
FULL_PRECISION = lax.Precision.HIGHEST

def thresholds():
    half_count = DISTANCE_BUCKETS // 2
    limits = []
    for level_index in range(1, DISTANCE_BUCKETS):
        if level_index < half_count:
            limits.append(level_index)
        else:
            ratio = (level_index - half_count) / half_count
            limits.append(int(math.ceil(half_count * (MAX_DIST / half_count) ** ratio)))
    return limits

def bucket_onehot(length):
    positions = jnp.arange(length, dtype=jnp.int32)
    distance = positions[:, None] - positions[None, :]
    bucket = jnp.zeros((length, length), jnp.int32)
    for threshold in thresholds():
        bucket = bucket + (distance >= threshold).astype(jnp.int32)
    levels = jnp.arange(DISTANCE_BUCKETS, dtype=jnp.int32)
    return (bucket[None, :, :] == levels[:, None, None]).astype(jnp.float32)

def matmul(left_side, right_side):
    return jnp.dot(left_side, right_side, precision=FULL_PRECISION, preferred_element_type=jnp.float32)

def norm_apply(values, gain_vector):
    factor = lax.rsqrt(lax.optimization_barrier(jnp.mean(values * values, axis=-1, keepdims=True)) + EPS)
    return values * factor * gain_vector

def gate_values(logits, routing):
    probabilities = jax.nn.softmax(logits, axis=-1)
    levels = jnp.arange(logits.shape[1], dtype=jnp.int32)
    pick_table = (routing[:, :, None] == levels[None, None, :]).astype(jnp.float32)
    chosen = lax.optimization_barrier(jnp.sum(probabilities[:, None, :] * pick_table, axis=2))
    return chosen / lax.optimization_barrier(jnp.sum(chosen, axis=1, keepdims=True))

def place_pairs(routing, priority, capacity, experts_all):
    length = routing.shape[0]
    pick_rank = jnp.arange(TOP, dtype=jnp.int32)
    pair_keys = (pick_rank[None, :] * length + priority[:, None]).reshape(-1)
    pair_experts = routing.reshape(-1)
    earlier = (pair_experts[:, None] == pair_experts[None, :]) & (pair_keys[None, :] < pair_keys[:, None])
    slot_rank = lax.optimization_barrier(jnp.sum(earlier.astype(jnp.int32), axis=1))
    return jnp.where(slot_rank < capacity, pair_experts * capacity + slot_rank, experts_all * capacity).astype(jnp.int32)

def layer(stream, segment, routing, priority, weights, bucket_indicator):
    attn_gain, qkv_w, relative_bias_matrix, out_w, moe_gain, router_w, w_in, w_out = weights
    length = stream.shape[0]
    normed_one = low(norm_apply(stream, attn_gain))
    qkv_rows = low_back(low(matmul(normed_one, qkv_w)))
    queries = qkv_rows[:, :D].reshape(length, ATTENTION_HEADS, HEAD_DIM)
    key_rows = qkv_rows[:, D:2 * D].reshape(length, ATTENTION_HEADS, HEAD_DIM)
    value_rows = qkv_rows[:, 2 * D:].reshape(length, ATTENTION_HEADS, HEAD_DIM)
    relative_position_bias = jnp.einsum('rgx,rn->ngx', bucket_indicator, relative_bias_matrix.reshape(DISTANCE_BUCKETS, ATTENTION_HEADS), precision=FULL_PRECISION)
    scores = jnp.einsum('qhd,khd->hqk', queries, key_rows, precision=FULL_PRECISION) * (1.0 / math.sqrt(HEAD_DIM)) + relative_position_bias
    scores = low_back(scores)
    positions = jnp.arange(length, dtype=jnp.int32)
    allowed = (positions[None, :] <= positions[:, None]) & (segment[None, :] == segment[:, None])
    scores = jnp.where(allowed[None], scores, -1e+30)
    attention = low(jax.nn.softmax(scores, axis=-1))
    context = jnp.einsum('hqk,khd->qhd', attention, value_rows, precision=FULL_PRECISION).reshape(length, D)
    context = low_back(low(context))
    residual = stream + low_back(matmul(context, out_w))
    moe_in = low(norm_apply(residual, moe_gain))
    logits = low_back(matmul(moe_in, router_w))
    gate_share = gate_values(logits, routing)
    slot_index = place_pairs(routing, priority, CAP, EXPERTS)
    slot_rows = jnp.zeros((EXPERTS * CAP + 1, D), jnp.float32).at[slot_index].add(jnp.repeat(moe_in, TOP, axis=0))
    dispatched = low_back(slot_rows[:EXPERTS * CAP].reshape(EXPERTS, CAP, D))
    hidden_pre = low_back(jnp.einsum('ecd,edf->ecf', dispatched, w_in, precision=FULL_PRECISION))
    hidden = low(jax.nn.gelu(hidden_pre, approximate=False))
    expert_rows = low_back(low(jnp.einsum('ecf,efd->ecd', hidden, w_out, precision=FULL_PRECISION)))
    flat_rows = jnp.concatenate([expert_rows.reshape(EXPERTS * CAP, D), jnp.zeros((1, D), jnp.float32)], axis=0)
    picked = flat_rows[slot_index].reshape(length, TOP, D)
    return residual + lax.optimization_barrier(jnp.sum(gate_share[:, :, None] * picked, axis=1))

def two_layers(stream, middle, first_layer, second_layer, segment, route_pair, order_pair, bucket_indicator):
    first_out = layer(stream, segment, route_pair[0], order_pair[0], first_layer, bucket_indicator)
    entering = low_back(low(first_out)) + middle
    second_out = layer(entering, segment, route_pair[1], order_pair[1], second_layer, bucket_indicator)
    return (first_out, second_out)

def reference(inputs, cotangent, segments, routes, order, attn_gain, qkv_weight, position_bias, out_weight, moe_gain, router_weight, expert_in, expert_out):
    block_count = MICRO * N_ROW * N_COL
    arrays = (attn_gain, qkv_weight, position_bias, out_weight, moe_gain, router_weight, expert_in, expert_out)
    first_layer = tuple((weight_array[0].astype(jnp.float32) for weight_array in arrays))
    second_layer = tuple((weight_array[1].astype(jnp.float32) for weight_array in arrays))
    bucket_indicator = bucket_onehot(TOK_DEV)
    stream_blocks = inputs.reshape(block_count, TOK_DEV, D)
    cot_blocks = cotangent.reshape(block_count, TOK_DEV, D)
    segment_blocks = segments.reshape(block_count, TOK_DEV)
    route_blocks = jnp.moveaxis(routes.reshape(2, block_count, TOK_DEV, TOP), 0, 1)
    order_blocks = jnp.moveaxis(order.reshape(2, block_count, TOK_DEV), 0, 1)
    zero_grads = jax.tree.map(jnp.zeros_like, (first_layer, second_layer))

    def accumulate(bucket_sums, block_data):
        stream_block, cot_block, segment_block, route_block, order_block = block_data
        stream_wide = stream_block.astype(jnp.float32)
        middle = jnp.zeros_like(stream_wide)

        def forward_pass(stream_in, middle_in, first_in, second_in):
            return two_layers(stream_in, middle_in, first_in, second_in, segment_block, route_block, order_block, bucket_indicator)
        results, pull_back = jax.vjp(forward_pass, stream_wide, middle, first_layer, second_layer)
        input_grad, middle_grad, first_grad, second_grad = pull_back((jnp.zeros_like(stream_wide), cot_block.astype(jnp.float32)))
        bucket_sums = jax.tree.map(jnp.add, bucket_sums, (first_grad, second_grad))
        return (bucket_sums, (results[0].astype(jnp.bfloat16), results[1].astype(jnp.bfloat16), input_grad, middle_grad))
    bucket_sums, (first_out, second_out, input_grad, middle_grad) = lax.scan(accumulate, zero_grads, (stream_blocks, cot_blocks, segment_blocks, route_blocks, order_blocks))
    layer_out = jnp.stack([first_out, second_out]).reshape(2, MICRO, TOK_DEV * N_ROW * N_COL, D)
    layer_in_grad = jnp.stack([input_grad, middle_grad]).reshape(2, MICRO, TOK_DEV * N_ROW * N_COL, D)
    stacked = [jnp.stack([bucket_sums[0][place], bucket_sums[1][place]]) for place in range(8)]
    return (layer_out, layer_in_grad, stacked[0], stacked[1], stacked[2], stacked[3], stacked[4], stacked[5], stacked[6], stacked[7])
```

```python
from functools import partial
import math
from types import SimpleNamespace

import jax
import jax.numpy as jnp
import numpy as np
from jax import lax
from jax.experimental import pallas as pl
from jax.experimental.pallas import tpu as pltpu
from jax.sharding import PartitionSpec as P

TOP = 2
DISTANCE_BUCKETS = 32
MAX_DIST = 128
EPS = 1e-06
MESH = pl.DeviceIdType.MESH
F32 = jnp.float32
BF16 = jnp.bfloat16
MIB = 1 << 20


class Geometry:
    def __init__(self, micro, length, width, heads, experts_all, local_experts, hidden, row_count, col_count):
        self.micro, self.length, self.width, self.heads, self.hidden = micro, length, width, heads, hidden
        self.tall = -(-heads // 8) * 8
        self.capacity = max(2, (5 * length * TOP + 4 * experts_all - 1) // (4 * experts_all))
        self.local_experts = local_experts
        self.experts_all = experts_all
        self.rows, self.cols = row_count, col_count
        self.cores = 2 if row_count % 2 == 0 else 1
        self.chips = row_count // self.cores
        main = self.capacity // 16 * 16
        rest = self.capacity - main
        self.share = main // local_experts if 0 < rest <= main // local_experts else 0
        if rest and not self.share:
            main += 16
        self.main = main
        self.first = 1 if self.share else 0
        self.units = local_experts + self.first
        self.slots = row_count * self.units * main
        self.sources = row_count * col_count
        self.expert_rows = self.sources * (main + self.share)

    def bases(self):
        expert = np.arange(self.experts_all)
        owner, local = expert // self.local_experts, expert % self.local_experts
        main = ((self.first + local) * self.rows + owner) * self.main
        tail = owner * self.main + local * self.share
        both = np.stack([main, tail]).astype(np.float32)
        return np.pad(both, ((0, 0), (0, 128 - self.experts_all)))


def buckets(length):
    distance = np.arange(length)
    bucket = np.zeros(length, np.int64)
    half = DISTANCE_BUCKETS // 2
    for level in range(1, DISTANCE_BUCKETS):
        if level < half:
            limit = level
        else:
            limit = int(math.ceil(half * (MAX_DIST / half) ** ((level - half) / half)))
        bucket += distance >= limit
    return (np.arange(DISTANCE_BUCKETS)[:, None] == bucket[None, :]).astype(np.float32)


def mm(left, right, contract):
    return lax.dot_general(
        left, right, (((contract[0],), (contract[1],)), ((), ())), preferred_element_type=F32
    )


def iota(shape, axis):
    return lax.broadcasted_iota(jnp.int32, shape, axis)


def norm_factor(values):
    return lax.rsqrt(jnp.mean(values * values, axis=-1, keepdims=True) + EPS)


def gelu_pair(x):
    density = jnp.exp(-0.5 * x * x)
    t = 1.0 / (1.0 + (0.3275911 * math.sqrt(0.5)) * jnp.abs(x))
    poly = 0.5 * 1.061405429
    for coefficient in (-1.453152027, 1.421413741, -0.284496736, 0.254829592):
        poly = poly * t + 0.5 * coefficient
    beyond = poly * t * density
    cdf = jnp.where(x >= 0, 1.0 - beyond, beyond)
    return x * cdf, cdf + x * density * (1.0 / math.sqrt(2.0 * math.pi))


def slot_onehots(aux, slots):
    positions = iota((aux.shape[0], slots), 1).astype(F32)
    return [(aux[:, 2 + c : 3 + c] == positions) for c in range(TOP)]


def vmem_grant(scratch, spare):
    held = 0
    for ref in scratch:
        if getattr(ref, "memory_space", None) == pltpu.VMEM:
            held += math.prod(ref.shape) * jnp.dtype(ref.dtype).itemsize
    return -(-held // MIB) + spare


def fits(*scratches):
    return vmem_grant([ref for scratch in scratches for ref in scratch.values()], 11) <= 62


def vmem_spec():
    return pl.BlockSpec(memory_space=pltpu.VMEM)


def hbm_spec():
    return pl.BlockSpec(memory_space=pltpu.HBM)


def in_hbm(array):
    return pltpu.with_memory_space_constraint(array, pltpu.HBM)


def shape(dims, kind):
    return jax.ShapeDtypeStruct(dims, kind)


def launch(body, near=None, held=None, outs=None, kept=None, state=None, scratch=None, spare=10, cost=None, **params):
    near, held, outs, kept, scratch = (dict(part or {}) for part in (near, held, outs, kept, scratch))
    state = {} if state is None else state
    old = [name for name in kept if name in state]
    names_in, names_out = list(near) + list(held), list(outs) + list(kept)

    def kernel(*refs):
        refs = list(refs)
        given, refs = refs[: len(names_in)], refs[len(names_in) + len(old) :]
        body(SimpleNamespace(**dict(zip(names_in + names_out + list(scratch), given + refs))))

    out_shapes = list(outs.values()) + [pltpu.HBM(dims, kind) for dims, kind in kept.values()]
    plain = [isinstance(out, jax.ShapeDtypeStruct) for out in out_shapes]
    estimate = {}
    if cost is not None:
        estimate["cost_estimate"] = pl.CostEstimate(flops=cost[0], bytes_accessed=cost[1], transcendentals=0)
    results = pl.pallas_call(
        kernel,
        out_shape=out_shapes,
        in_specs=[vmem_spec()] * len(near) + [hbm_spec()] * (len(held) + len(old)),
        out_specs=[vmem_spec() if near_by else hbm_spec() for near_by in plain],
        scratch_shapes=list(scratch.values()),
        input_output_aliases={len(names_in) + i: names_out.index(name) for i, name in enumerate(old)},
        compiler_params=pltpu.CompilerParams(
            vmem_limit_bytes=vmem_grant(scratch.values(), spare) * MIB, **params
        ),
        **estimate,
    )(*near.values(), *map(in_hbm, held.values()), *(in_hbm(state[name]) for name in old))
    results = dict(zip(names_out, results))
    for name in kept:
        state[name] = results.pop(name)
    return results


def of_micro(rows, m):
    if isinstance(m, int):
        return rows[m : m + 1]
    row = rows[0:1]
    for i in range(1, rows.shape[0]):
        row = jnp.where(m == i, rows[i : i + 1], row)
    return row


def as_column(row):
    return jnp.broadcast_to(row, (8, row.shape[1])).T[:, 0:1]


class Copies:
    def __init__(self, sems):
        self.sems, self.count, self.open = sems, 0, []

    def load(self, source, target):
        copy = pltpu.make_async_copy(source, target, self.sems.at[self.count])
        self.count += 1
        copy.start()
        return copy

    def save(self, source, target):
        self.open.append(self.load(source, target))

    def wait(self):
        for copy in self.open:
            copy.wait()


def remote(source, target, send, receive, where):
    return pltpu.make_async_remote_copy(
        src_ref=source, dst_ref=target, send_sem=send, recv_sem=receive, device_id=where, device_id_type=MESH
    )


def forward_micro(geo, tick):
    if tick == 0:
        return 0
    return geo.micro - 1 if tick == geo.micro else tick - lax.axis_index("section")


def backward_micro(geo, step):
    if step == 0:
        return geo.micro - 1
    return 0 if step == geo.micro else geo.micro - step - lax.axis_index("section")


class Across:
    def __init__(self, sender, sems, at=0):
        self.section = lax.axis_index("section")
        self.sender, self.other = sender, {"section": 1 - self.section}
        self.send_sem, self.recv_sem = sems.at[at], sems.at[at + 1]

    def greet(self):
        pl.semaphore_signal(pltpu.get_barrier_semaphore(), inc=1, device_id=self.other, device_id_type=MESH)

    def copy(self, source, target):
        return remote(source, target, self.send_sem, self.recv_sem, self.other)

    def send(self, source, target):
        @pl.when(self.section == self.sender)
        def _():
            self.copy(source, target).start()

    def sent(self, source, target):
        @pl.when(self.section == self.sender)
        def _():
            self.copy(source, target).wait_send()

    def take(self, target):
        @pl.when(self.section != self.sender)
        def _():
            self.copy(target, target).wait_recv()


def prepare(experts_all, at):
    heads, length = at.bias.shape[:2]
    rows = at.small[...].astype(F32).T
    at.gains[...] = rows[experts_all : experts_all + 2]
    picked = (at.head_pick[...] * rows[experts_all + 2 : experts_all + 3]).astype(BF16)
    by_distance = mm(picked, at.spread[...], (1, 0))
    for h in range(heads):
        block = by_distance[h : h + 1, :]
        step = 1
        while step < length:
            block = jnp.concatenate([block, pltpu.roll(block, step, 1)], axis=0)
            step *= 2
        at.bias[h] = block.astype(BF16)


def diagonal_sums(block):
    length = block.shape[1]
    size = block.shape[0] // 2
    while size >= 1:
        block = block[:size] + pltpu.roll(block[size:], length - size, 1)
        size //= 2
    return block


def only_section(geo, tick):
    return {0: 0, geo.micro: 1}.get(tick)


def where_active(active, body, at):
    if active is None:
        body(at)
    else:
        pl.when(lax.axis_index("section") == active)(partial(body, at))


def dense_forward_part(geo, tick, at, copies, enter, across, loaded, fused=True):
    length, width, heads = geo.length, geo.width, geo.heads
    size = width // heads
    per = 128 // size
    m = forward_micro(geo, tick)
    packed_qkv = copies.load(at.packed.at[:, pl.ds(0, 3 * width)], at.qkv_w)
    if tick == 0:
        copies.load(at.inputs.at[m], at.stream).wait()
    else:
        first = lax.axis_index("section") == 0
        own = pltpu.make_async_copy(at.inputs.at[m], at.stream, at.stream_sem)
        if tick == 1:
            enter()
            across.send(at.out.at[0] if fused else at.out_before.at[0], at.stream_in)
        else:
            came = pltpu.make_async_copy(at.received, at.stream, at.stream_sem)

        @pl.when(first)
        def _():
            own.start()
            own.wait()

        if tick == 1:
            across.take(at.stream_in)

            @pl.when(jnp.logical_not(first))
            def _():
                at.stream[...] = at.stream_in[...]
        else:

            @pl.when(jnp.logical_not(first))
            def _():
                came.start()
                came.wait()

    packed_rest = copies.load(at.packed.at[:, pl.ds(3 * width, width + 128)], at.rest_w)
    bias_load = copies.load(at.bias, at.bias_here)
    copies.save(at.stream, at.kept_stream.at[m])
    stream = at.stream[...].astype(F32)
    at.normed[...] = (stream * norm_factor(stream) * at.gains[0:1, :]).astype(BF16)
    copies.save(at.normed, at.kept_normed.at[m])
    packed_qkv.wait()
    at.qkv[...] = mm(at.normed[...], at.qkv_w[...], (1, 0)).astype(BF16)
    copies.save(at.qkv, at.kept_qkv.at[m])
    key_at, query_at = iota((length, length), 0), iota((length, length), 1)
    segments = of_micro(at.segments[...], m).astype(F32)
    allowed = (key_at <= query_at) & (as_column(segments) == segments)
    which = iota((length, 128), 1) // size
    head_row = iota((128, length), 0) // size
    scale = 1.0 / math.sqrt(size)
    zero = jnp.zeros((length, 128), BF16)
    bias_load.wait()
    for j in range(width // 128):
        queries = at.qkv[:, 128 * j : 128 * (j + 1)]
        keys = at.qkv[:, width + 128 * j : width + 128 * (j + 1)]
        values = at.qkv[:, 2 * width + 128 * j : 2 * width + 128 * (j + 1)]
        turned_values = values.astype(F32).T
        context = jnp.zeros((128, length), F32)
        for part in range(per):
            h = j * per + part
            own = which == part
            scores = mm(jnp.where(own, keys, zero), queries, (1, 1)) * scale + at.bias_here[h].astype(F32)
            scores = jnp.where(allowed, scores, -1e30)
            exponent = jnp.exp(scores - jnp.max(scores, axis=0, keepdims=True))
            prob = (exponent * (1.0 / jnp.sum(exponent, axis=0, keepdims=True))).astype(BF16)
            at.prob[h] = prob
            own_values = jnp.where(head_row == part, turned_values, 0.0).astype(BF16)
            context = context + mm(own_values, prob, (1, 0))
        at.context[:, 128 * j : 128 * (j + 1)] = context.T.astype(BF16)
        heads_here = pl.ds(j * per, per)
        copies.save(at.prob.at[heads_here], at.kept_prob.at[m, heads_here])
    copies.save(at.context, at.kept_context.at[m])
    packed_rest.wait()
    loaded()
    residual = stream + mm(at.context[...], at.rest_w[:, :width], (1, 0))
    at.residual[...] = residual
    copies.save(at.residual, at.kept_residual.at[m])
    moe_in = (residual * norm_factor(residual) * at.gains[1:2, :]).astype(BF16)
    at.moe_in[...] = moe_in
    copies.save(at.moe_in, at.kept_moe_in.at[m])
    logits = mm(moe_in, at.rest_w[:, width:], (1, 0))
    expert_at = iota(logits.shape, 1)
    picks = [(as_column(at.routes[0, m, c : c + 1, :].astype(F32)) == expert_at.astype(F32)).astype(F32) for c in range(TOP)]
    chosen = [jnp.sum(pick * logits, axis=1, keepdims=True) for pick in picks]
    top = jnp.maximum(chosen[0], chosen[1])
    powers = [jnp.exp(value - top) for value in chosen]
    total = powers[0] + powers[1]
    shares = [power / total for power in powers]
    order = of_micro(at.order[0, :, 0, :], m).astype(F32)
    before = (order < as_column(order)).astype(BF16)
    counts = [mm(before, pick.astype(BF16), (1, 0)) for pick in picks]
    counts[1] = counts[1] + jnp.sum(picks[0], axis=0, keepdims=True)
    slots = []
    for pick, count in zip(picks, counts):
        rank = jnp.sum(pick * count, axis=1, keepdims=True)
        main = jnp.sum(pick * at.bases[0:1, :], axis=1, keepdims=True)
        tail = jnp.sum(pick * at.bases[1:2, :], axis=1, keepdims=True)
        place = jnp.where(rank < geo.main, main + rank, tail + rank - geo.main)
        slots.append(jnp.where(rank < geo.capacity, place, -1.0))
    lane = iota((length, 128), 1)
    aux = jnp.zeros((length, 128), F32)
    for place, value in enumerate(shares + slots):
        aux = jnp.where(lane == place, value, aux)
    at.aux[...] = aux
    copies.save(at.aux, at.kept_aux.at[m])
    first, second = slot_onehots(aux, geo.slots)
    at.slots[...] = mm((first | second).astype(BF16), moe_in, (0, 0)).astype(BF16).reshape(at.slots.shape)


def dense_forward_body(geo, tick, at):
    across = Across(0, at.across_sems) if tick == 1 else None
    if across:
        across.greet()

    def enter():
        pl.semaphore_wait(pltpu.get_barrier_semaphore(), 1)

    copies = Copies(at.sems)
    dense_forward_part(geo, tick, at, copies, enter, across, lambda: None, fused=False)
    copies.save(at.slots, at.slot_rows)
    copies.wait()
    if across:
        across.sent(at.out_before.at[0], at.stream_in)


def dense_forward_scratch(geo, tick):
    length, width, heads = geo.length, geo.width, geo.heads
    scratch = dict(
        stream=pltpu.VMEM((length, width), BF16),
        qkv_w=pltpu.VMEM((width, 3 * width), BF16),
        rest_w=pltpu.VMEM((width, width + 128), BF16),
        bias_here=pltpu.VMEM((heads, length, length), BF16),
        normed=pltpu.VMEM((length, width), BF16),
        qkv=pltpu.VMEM((length, 3 * width), BF16),
        prob=pltpu.VMEM((heads, length, length), BF16),
        context=pltpu.VMEM((length, width), BF16),
        residual=pltpu.VMEM((length, width), F32),
        moe_in=pltpu.VMEM((length, width), BF16),
        aux=pltpu.VMEM((length, 128), F32),
        slots=pltpu.VMEM((geo.units, geo.rows, geo.main, width), BF16),
        sems=pltpu.SemaphoreType.DMA((16 + width // 128,)),
        stream_sem=pltpu.SemaphoreType.DMA,
        across_sems=pltpu.SemaphoreType.DMA((4,)),
    )
    if tick == 1:
        scratch["stream_in"] = pltpu.VMEM((length, width), BF16)
    return scratch


def dense_forward_refs(geo, tick, given, state, received):
    micro, length, width, heads = geo.micro, geo.length, geo.width, geo.heads
    near = {name: given[name] for name in ("segments", "order", "routes", "gains", "bases")}
    held = dict(packed=given["packed"], bias=given["bias"], inputs=given["inputs"])
    if tick > 1:
        held["received"] = received
    kept = dict(
        kept_stream=((micro, length, width), BF16),
        kept_normed=((micro, length, width), BF16),
        kept_qkv=((micro, length, 3 * width), BF16),
        kept_prob=((micro, heads, length, length), BF16),
        kept_context=((micro, length, width), BF16),
        kept_residual=((micro, length, width), F32),
        kept_moe_in=((micro, length, width), BF16),
        kept_aux=((micro, length, 128), F32),
    )
    return near, held, kept


def dense_forward(geo, tick, given, state, received):
    near, held, kept = dense_forward_refs(geo, tick, given, state, received)
    params = {}
    if tick == 1:
        held["out_before"] = state["out"]
        params = dict(collective_id=5 + 2 * geo.micro, has_side_effects=True)
    return launch(
        partial(where_active, only_section(geo, tick), partial(dense_forward_body, geo, tick)),
        near=near,
        held=held,
        outs=dict(slot_rows=pltpu.HBM((geo.units, geo.rows, geo.main, geo.width), BF16)),
        kept=kept,
        state=state,
        scratch=dense_forward_scratch(geo, tick),
        cost=(2_000_000_000, 14_000_000),
        **params,
    )["slot_rows"]


def combine(home, aux, result, picked_ref):
    for c, onehot in enumerate(slot_onehots(aux, home.shape[0])):
        picked = mm(onehot.astype(BF16), home, (1, 0))
        picked_ref[c] = picked.astype(BF16)
        result = result + aux[:, c : c + 1] * picked
    return result


def spread(incoming, aux, picked_ref, slots):
    lane = iota((aux.shape[0], 128), 1)
    gates = jnp.zeros(lane.shape, F32)
    total = 0.0
    for c, onehot in enumerate(slot_onehots(aux, slots)):
        gate = jnp.sum(picked_ref[c].astype(F32) * incoming, axis=1, keepdims=True)
        gates = jnp.where(lane == c, gate, gates)
        total = total + mm(onehot.astype(BF16), (aux[:, c : c + 1] * incoming).astype(BF16), (0, 0))
    return gates, total.astype(BF16)


def expert_picker(geo, e):
    dims = (geo.sources * geo.share, geo.sources * geo.main)
    own, place = iota(dims, 0), iota(dims, 1)
    return (place == own // geo.share * geo.main + e * geo.share + own % geo.share).astype(BF16)


class Exchange:
    def __init__(self, geo, at, x, active=None):
        self.geo, self.x, self.at = geo, x, at
        self.relay = geo.chips // 2 if active is not None and geo.chips > 1 else None
        self.near_rows = geo.cores
        self.ahead = 2 if self.relay else 1
        self.peers = geo.cols - 1
        self.other = {"section": 1 - lax.axis_index("section")}
        self.r, self.c = lax.axis_index("row"), lax.axis_index("col")
        self.z, self.core = self.r // geo.cores, self.r % geo.cores
        self.partner = self.z * geo.cores + (self.core + 1) % geo.cores

    def far(self, direct):
        return [k for k in range(1, self.geo.chips) if direct or k != self.relay]

    def far_rows(self, direct):
        return self.geo.cores * len(self.far(direct))

    def kinds(self):
        first = self.geo.first if self.relay else 0
        return [(pl.ds(at, n), direct) for at, n, direct in ((0, first, True), (first, self.geo.units - first, False)) if n]

    def chip(self, k):
        return (self.z + k + self.geo.chips) % self.geo.chips

    def row(self, k, d):
        return self.partner if k == 0 else self.chip(k) * self.geo.cores + d

    def col(self, j):
        return (self.c + j + self.geo.cols) % self.geo.cols

    def rows(self, k):
        return pl.ds(self.chip(k) * self.geo.cores, self.geo.cores)

    def others(self, k):
        return range(self.geo.cores - 1) if k == 0 else range(self.geo.cores)

    def greet(self):
        barrier = pltpu.get_barrier_semaphore()
        for k in range(self.geo.chips):
            for d in self.others(k):
                pl.semaphore_signal(barrier, inc=1, device_id={"row": self.row(k, d)}, device_id_type=MESH)
        for j in range(1, self.geo.cols):
            pl.semaphore_signal(barrier, inc=1, device_id={"col": self.col(j)}, device_id_type=MESH)
        if self.relay:
            pl.semaphore_signal(barrier, inc=1, device_id=self.other, device_id_type=MESH)

    def await_greetings(self, more):
        more = more + (1 if self.relay else 0)
        pl.semaphore_wait(pltpu.get_barrier_semaphore(), self.geo.rows + self.geo.cols - 2 + more)

    def came(self, block, sem):
        remote(block, block, self.at.done, sem, self.other).wait_recv()

    def left(self, block, sem):
        remote(block, block, sem, self.at.done, self.other).wait_send()


    def own(self, u):
        return pltpu.make_async_copy(
            self.x.at[u, self.r], self.at.inbox.at[u, self.c, self.r], self.at.own_sem.at[u]
        )

    def kind(self, u):
        if not (self.relay and self.geo.first):
            return 0
        return int(u < self.geo.first) if isinstance(u, int) else (u + self.geo.units - 1) // self.geo.units * -1 + 1

    def send(self, u, k):
        for d in self.others(k):
            remote(
                self.x.at[u, self.row(k, d)], self.at.inbox.at[u, self.c, self.r], self.at.in_send.at[self.kind(u)],
                self.at.in_recv.at[u, k], {"row": self.row(k, d)},
            ).start()

    def send_out(self, u):
        if self.relay:
            remote(
                self.x.at[u, self.rows(self.relay)], self.at.via_x.at[u], self.at.via_send,
                self.at.via_x_recv.at[u], self.other,
            ).start()

    def hand_over(self, u, k):
        block = self.at.inbox.at[u, self.c, self.rows(-k)]
        for j in range(1, self.geo.cols):
            remote(block, block, self.at.pass_send.at[u], self.at.pass_recv.at[u], {"col": self.col(j)}).start()

    def each(self, body):
        lax.fori_loop(0, self.geo.units, lambda u, carry: (body(u), carry)[1], 0)

    def open(self):
        for u in range(min(self.ahead, self.geo.units)):
            direct = u < self.geo.first
            for k in self.far(direct):
                self.send(u, k)
            if not direct:
                self.send_out(u)

        def body(u):
            self.own(u).start()
            self.send(u, 0)

        self.each(body)
        for u in range(min(3, self.geo.units)):
            self.pass_on_own(u)

    def pass_on_own(self, u):
        self.own(u).wait()
        if self.geo.cores > 1:
            self.came(self.at.inbox.at[u, self.c, pl.ds(0, 1)], self.at.in_recv.at[u, 0])
        self.hand_over(u, 0)

    def pass_on(self, u, direct=False):
        @pl.when(u + self.ahead < self.geo.units)
        def _():
            self.send_out(u + self.ahead)

        for k in self.far(direct):
            self.came(self.at.inbox.at[u, self.c, self.rows(-k)], self.at.in_recv.at[u, k])

            @pl.when(u + self.ahead < self.geo.units)
            def _():
                if k in self.far(False):
                    self.send(u + self.ahead, k)

            self.hand_over(u, k)

        @pl.when(u + 3 < self.geo.units)
        def _():
            self.pass_on_own(u + 3)

    def collect(self, u, direct=False):
        if self.peers:
            block = self.at.inbox.at[u, pl.ds(0, self.peers), pl.ds(0, self.near_rows + self.far_rows(direct))]
            self.came(block, self.at.pass_recv.at[u])
            self.left(block, self.at.pass_send.at[u])
        if self.relay and not direct:
            self.came(self.at.inbox.at[u, :, pl.ds(0, self.geo.cores)], self.at.into_recv.at[u])


    def send_parts(self, u, far, direct=False):
        if far and self.relay and not direct:
            for j in range(self.geo.cols):
                remote(
                    self.at.inbox.at[u, self.col(j), self.rows(self.relay)], self.at.via_part.at[u, j],
                    self.at.via_part_send, self.at.via_part_recv.at[u], self.other,
                ).start()
        for k in self.far(direct) if far else (0,):
            for j in range(1, self.geo.cols):
                remote(
                    self.at.inbox.at[u, self.col(j), self.rows(k)], self.at.arrived.at[u, j - 1, self.rows(k)],
                    self.at.out_send.at[self.kind(u)], self.at.out_recv.at[u, int(far)], {"col": self.col(j)},
                ).start()

    def send_home(self, u, far, direct=False):
        count = self.far_rows(direct) if far else self.near_rows
        if self.peers and count:
            self.came(self.at.arrived.at[u, :, pl.ds(0, count)], self.at.out_recv.at[u, int(far)])
        for k in self.far(direct) if far else (0,):
            rows = self.rows(k)
            total = self.at.inbox[u, self.c, rows].astype(F32)
            for j in range(1, self.geo.cols):
                total = total + self.at.arrived[u, j - 1, rows].astype(F32)
            self.at.stage[u, rows] = total.astype(BF16)
            for d in self.others(k):
                remote(
                    self.at.stage.at[u, self.row(k, d)], self.at.home.at[u, self.r], self.at.home_send.at[self.kind(u)],
                    self.at.home_recv.at[self.kind(u)], {"row": self.row(k, d)},
                ).start()
            if k == 0:
                self.at.home[u, self.r] = self.at.stage[u, self.r]

    def finish(self):
        at, cores = self.at, self.geo.cores
        for units, direct in self.kinds():
            sent_rows = self.far_rows(direct) + cores - 1
            if sent_rows:
                block = at.home.at[units, pl.ds(0, sent_rows)]
                self.came(block, at.home_recv.at[int(direct)])
                self.left(block, at.home_send.at[int(direct)])
                self.left(block, at.in_send.at[int(direct)])
            if self.peers:
                block = at.arrived.at[units, :, pl.ds(0, self.near_rows + self.far_rows(direct))]
                self.left(block, at.out_send.at[int(direct)])
            if self.relay and not direct:
                self.came(at.home.at[units, pl.ds(0, cores)], at.home_in_recv)
                self.left(at.via_x.at[units], at.via_send)
                self.left(at.via_part.at[units], at.via_part_send)


    def along(self, u, d, source, target, at):
        where = {"row": self.row(self.relay, d)}
        return remote(
            source.at[u, d], target.at[u, self.core], self.at.core_sems.at[at, u, d],
            self.at.core_sems.at[at + 1, u, self.core], where,
        )

    def along_came(self, u, d, target, at):
        self.came(target.at[u, d], self.at.core_sems.at[at + 1, u, d])

    def across(self, u, j):
        return remote(
            self.at.via_z.at[u], self.at.via_y.at[u, j - 1], self.at.via_sems.at[2, u, j], self.at.via_sems.at[3, u, j],
            {"col": self.col(j)},
        )

    def into(self, u, j):
        source = self.at.via_y.at[u, j - 1] if j else self.at.via_z.at[u]
        target = self.at.inbox.at[u, self.col(-j), self.rows(-self.relay)]
        return remote(source, target, self.at.via_sems.at[0, u, j], self.at.into_recv.at[u], self.other)

    def part_across(self, u, j):
        return remote(
            self.at.via_part.at[u, j], self.at.via_sum.at[u, j - 1], self.at.via_sems.at[4, u, j],
            self.at.via_sems.at[5, u, j], {"col": self.col(j)},
        )

    def home_in(self, u):
        return remote(
            self.at.via_home.at[u], self.at.home.at[u, self.rows(-self.relay)], self.at.via_sems.at[1, u, 0],
            self.at.home_in_recv, self.other,
        )

    def carry(self):
        geo, at = self.geo, self.at
        cores, columns = range(geo.cores), range(1, geo.cols)

        def rows_out(u):
            self.came(at.via_x.at[u], at.via_x_recv.at[u])
            for d in cores:
                self.along(u, d, at.via_x, at.via_z, 0).start()

        def rows_on(u):
            for d in cores:
                self.along_came(u, d, at.via_z, 0)
            self.into(u, 0).start()
            for j in columns:
                self.across(u, j).start()

        def rows_in(u):
            for j in columns:
                self.across(u, j).wait_recv()
                self.into(u, j).start()

        def parts_out(u):
            self.came(at.via_part.at[u], at.via_part_recv.at[u])
            for j in columns:
                self.part_across(u, j).start()

        def parts_on(u):
            total = at.via_part[u, 0].astype(F32)
            for j in columns:
                self.part_across(u, j).wait_recv()
                total = total + at.via_sum[u, j - 1].astype(F32)
            at.via_total[u] = total.astype(BF16)
            for d in cores:
                self.along(u, d, at.via_total, at.via_home, 2).start()

        def parts_in(u):
            for d in cores:
                self.along_came(u, d, at.via_home, 2)
            self.home_in(u).start()

        units = list(range(geo.first, geo.units))
        for steps in ((rows_out, rows_on, rows_in), (parts_out, parts_on, parts_in)):
            for t in range(len(units) + 2):
                for lag, work in enumerate(steps):
                    if 0 <= t - lag < len(units):
                        work(units[t - lag])
        for u in units:
            for d in cores:
                self.along(u, d, at.via_x, at.via_z, 0).wait_send()
                self.along(u, d, at.via_total, at.via_home, 2).wait_send()
            for j in range(geo.cols):
                self.into(u, j).wait_send()
            for j in columns:
                self.across(u, j).wait_send()
                self.part_across(u, j).wait_send()
            self.home_in(u).wait_send()


def run_experts(geo, exchange, rows, total, shared, loads, expert, saves):
    first, count = geo.first, geo.sources * geo.main
    inbox = exchange.at.inbox
    width = inbox.shape[-1]
    exchange.open()
    if first:
        exchange.pass_on(0, True)
    exchange.pass_on(first)
    if first:
        exchange.collect(0, True)
        shared[...] = jnp.zeros(shared.shape, F32)

    def step(e, carry):
        u = e + first
        slot = e % 2

        @pl.when(e + 1 < geo.local_experts)
        def _():
            exchange.pass_on(u + 1)

        exchange.collect(u)

        @pl.when(e >= 2)
        def _():
            for copy in saves(e - 2, slot):
                copy.wait()

        rows[slot, :count] = inbox[u].reshape(count, width)
        if first:
            picker = expert_picker(geo, e)
            tail = inbox[0].reshape(count, width)
            rows[slot, count:] = mm(picker, tail, (1, 0)).astype(BF16)
        for copy in loads(e):
            copy.wait()
        expert(e, slot)
        for copy in saves(e, slot):
            copy.start()
        inbox[u] = total[:count].astype(BF16).reshape(inbox.shape[1:])
        exchange.send_parts(u, True)
        if first:
            shared[...] += mm(picker, total[count:].astype(BF16), (0, 0))

        @pl.when(e >= 1)
        def _():
            exchange.send_home(u - 1, True)
            if exchange.relay:
                exchange.send_parts(u - 1, False)

        return carry

    lax.fori_loop(0, geo.local_experts, step, 0)
    if first:
        inbox[0] = shared[...].astype(BF16).reshape(inbox.shape[1:])
        exchange.send_parts(0, True, True)
    for u in range(geo.units):
        if not exchange.relay or u < first or u == geo.units - 1:
            exchange.send_parts(u, False)
    exchange.send_home(geo.units - 1, True)
    if first:
        exchange.send_home(0, True, True)
    exchange.each(lambda u: exchange.send_home(u, False))
    for e in range(max(0, geo.local_experts - 2), geo.local_experts):
        for copy in saves(e, e % 2):
            copy.wait()
    exchange.finish()


def share_work(exchange, active, work):
    if not exchange.relay:
        work()
        return
    section = lax.axis_index("section")
    pl.when(section == active)(work)

    @pl.when(section != active)
    def _():
        exchange.await_greetings(0)
        exchange.carry()


def start_loads(geo, loads):
    for e in range(geo.local_experts):
        for copy in loads(e):
            copy.start()


def forward_body(geo, tick, tile, fused, at):
    m = forward_micro(geo, tick)
    take, send = fused and tick == 1, 1 <= tick < geo.micro
    active = only_section(geo, tick)
    exchange = Exchange(geo, at, at.slots if fused else at.slot_rows, active)
    exchange.greet()
    across_in, across_out = Across(0, at.across_sems, 2), Across(0, at.across_sems)
    if take or send:
        across_out.greet()
    w_in, w_out = at.w_in_here, at.w_out_here

    def loads(e):
        return (
            pltpu.make_async_copy(at.w_in.at[e], w_in.at[e], at.load_sem.at[e, 0]),
            pltpu.make_async_copy(at.w_out.at[e], w_out.at[e], at.load_sem.at[e, 1]),
        )

    def saves(e, slot):
        return (
            pltpu.make_async_copy(at.rows.at[slot], at.kept_rows.at[m, e], at.save_sem.at[slot, 0]),
            pltpu.make_async_copy(at.wide.at[slot], at.kept_hidden.at[m, e], at.save_sem.at[slot, 1]),
            pltpu.make_async_copy(at.slope.at[slot], at.kept_slope.at[m, e], at.save_sem.at[slot, 2]),
        )

    def expert(e, slot):
        for f in range(0, geo.hidden, tile):
            value, derivative = gelu_pair(mm(at.rows[slot], w_in[e, :, f : f + tile], (1, 0)))
            value = value.astype(BF16)
            at.wide[slot, :, f : f + tile] = value
            at.slope[slot, :, f : f + tile] = derivative.astype(BF16)
            product = mm(value, w_out[e, f : f + tile, :], (1, 0))
            at.total[...] = product if f == 0 else at.total[...] + product

    def enter():
        exchange.await_greetings(int(take or send))

    def work():
        copies = Copies(at.sems)
        if fused:
            dense_forward_part(geo, tick, at, copies, enter, across_in, lambda: start_loads(geo, loads))
            if not take:
                enter()
        else:
            start_loads(geo, loads)
            aux_load = copies.load(at.kept_aux.at[m], at.aux)
            residual_load = copies.load(at.kept_residual.at[m], at.residual)
            enter()
        run_experts(geo, exchange, at.rows, at.total, at.shared, loads, expert, saves)
        if not fused:
            aux_load.wait()
            residual_load.wait()
        home = at.home[...].reshape(geo.slots, geo.width)
        at.result[...] = combine(home, at.aux[...], at.residual[...], at.picked).astype(BF16)
        if send:
            across_out.send(at.result, at.received_out)
        copies.save(at.result, at.out.at[m])
        copies.save(at.picked, at.kept_picked.at[m])
        copies.wait()
        if take:
            across_in.sent(at.out.at[0], at.stream_in)
        if send:
            across_out.take(at.received_out)
            across_out.sent(at.result, at.received_out)

    share_work(exchange, active, work)


def backward_body(geo, step, tile, fused, at):
    m = backward_micro(geo, step)
    take, send = step == 1, fused and 1 <= step < geo.micro
    active = only_section(geo, geo.micro - step)
    exchange = Exchange(geo, at, at.slot_grad, active)
    exchange.greet()
    first = lax.axis_index("section") == 0
    across, across_out = Across(1, at.across_sems), Across(1, at.across_sems, 2)
    if take or send:
        across.greet()
    w_in, w_out = at.w_in_here, at.w_out_here

    def loads(e):
        return (
            pltpu.make_async_copy(at.w_out.at[e], w_out.at[e], at.load_sem.at[e, 1]),
            pltpu.make_async_copy(at.kept_slope.at[m, e], at.slope.at[e], at.load_sem.at[e, 2]),
            pltpu.make_async_copy(at.w_in.at[e], w_in.at[e], at.load_sem.at[e, 0]),
        )

    def saves(e, slot):
        return (
            pltpu.make_async_copy(at.rows.at[slot], at.kept_seen.at[m, e], at.save_sem.at[slot, 0]),
            pltpu.make_async_copy(at.wide.at[slot], at.kept_pre.at[m, e], at.save_sem.at[slot, 1]),
        )

    def expert(e, slot):
        for f in range(0, geo.hidden, tile):
            grad = mm(at.rows[slot], w_out[e, f : f + tile, :], (1, 1))
            value = (grad * at.slope[e, :, f : f + tile].astype(F32)).astype(BF16)
            at.wide[slot, :, f : f + tile] = value
            product = mm(value, w_in[e, :, f : f + tile], (1, 1))
            at.total[...] = product if f == 0 else at.total[...] + product

    def incoming_load():
        own = pltpu.make_async_copy(at.cotangent.at[m], at.incoming_here, at.incoming_sem)
        if step == 0:
            return [own], [own]
        if step == 1:
            return [], [own]
        return [pltpu.make_async_copy(at.received, at.incoming_here, at.incoming_sem)], [own]

    def of_sections(action):
        early, late = incoming_load()

        @pl.when(first)
        def _():
            for copy in early:
                getattr(copy, action)()

        @pl.when(jnp.logical_not(first))
        def _():
            for copy in late:
                getattr(copy, action)()

    def work():
        copies = Copies(at.sems)
        picked_load = copies.load(at.kept_picked.at[m], at.picked)
        aux_load = copies.load(at.kept_aux.at[m], at.aux)
        of_sections("start")
        start_loads(geo, loads)
        dense_loads = dense_backward_loads(geo, m, at, copies) if fused else None
        exchange.await_greetings(int(take or send))
        if take:
            across.send(at.sent, at.incoming_far)
            across.take(at.incoming_far)

            @pl.when(first)
            def _():
                at.incoming_here[...] = at.incoming_far[...]

        of_sections("wait")
        picked_load.wait()
        aux_load.wait()
        at.incoming[...] = at.incoming_here[...]
        gates, slot_grad = spread(at.incoming_here[...].astype(F32), at.aux[...], at.picked, geo.slots)
        at.gates[...] = gates
        at.slot_grad[...] = slot_grad.reshape(at.slot_grad.shape)
        run_experts(geo, exchange, at.rows, at.total, at.shared, loads, expert, saves)
        first_slots, second_slots = slot_onehots(at.aux[...], geo.slots)
        home = at.home[...].reshape(geo.slots, geo.width)
        at.moe_grad[...] = mm((first_slots | second_slots).astype(BF16), home, (1, 0))
        if fused:
            dense_backward_part(geo, step, at, copies, dense_loads, lambda: None, across_out if send else None)
        if take:
            across.sent(at.sent, at.incoming_far)

    share_work(exchange, active, work)


def tile_of(hidden, limit):
    return limit if hidden % limit == 0 else hidden


def experts_scratch(geo, slope_slots):
    rows, local, width, hidden = geo.expert_rows, geo.local_experts, geo.width, geo.hidden
    steps = max(1, geo.cols - 1)
    one = pltpu.SemaphoreType.DMA
    two = pltpu.SemaphoreType.DMA((2,))
    unit = pltpu.SemaphoreType.DMA((geo.units,))
    return dict(
        inbox=pltpu.VMEM((geo.units, geo.cols, geo.rows, geo.main, width), BF16),
        arrived=pltpu.VMEM((geo.units, steps, geo.rows, geo.main, width), BF16),
        stage=pltpu.VMEM((geo.units, geo.rows, geo.main, width), BF16),
        home=pltpu.VMEM((geo.units, geo.rows, geo.main, width), BF16),
        picked=pltpu.VMEM((TOP, geo.length, width), BF16),
        aux=pltpu.VMEM((geo.length, 128), F32),
        rows=pltpu.VMEM((2, rows, width), BF16),
        wide=pltpu.VMEM((2, rows, hidden), BF16),
        slope=pltpu.VMEM((slope_slots, rows, hidden), BF16),
        w_in_here=pltpu.VMEM((local, width, hidden), BF16),
        w_out_here=pltpu.VMEM((local, hidden, width), BF16),
        total=pltpu.VMEM((rows, width), F32),
        shared=pltpu.VMEM((geo.sources * geo.main if geo.share else 16, width), F32),
        via_x=pltpu.VMEM((geo.units, geo.cores, geo.main, width), BF16),
        via_z=pltpu.VMEM((geo.units, geo.cores, geo.main, width), BF16),
        via_y=pltpu.VMEM((geo.units, steps, geo.cores, geo.main, width), BF16),
        via_part=pltpu.VMEM((geo.units, geo.cols, geo.cores, geo.main, width), BF16),
        via_sum=pltpu.VMEM((geo.units, steps, geo.cores, geo.main, width), BF16),
        via_total=pltpu.VMEM((geo.units, geo.cores, geo.main, width), BF16),
        via_home=pltpu.VMEM((geo.units, geo.cores, geo.main, width), BF16),
        via_sems=pltpu.SemaphoreType.DMA((6, geo.units, geo.cols)),
        core_sems=pltpu.SemaphoreType.DMA((4, geo.units, geo.cores)),
        own_sem=unit, pass_send=unit, pass_recv=unit, into_recv=unit, via_x_recv=unit, via_part_recv=unit,
        in_send=two, out_send=two, home_send=two, home_recv=two, home_in_recv=one, via_send=one, via_part_send=one,
        done=one,
        in_recv=pltpu.SemaphoreType.DMA((geo.units, geo.chips)),
        out_recv=pltpu.SemaphoreType.DMA((geo.units, 2)),
        load_sem=pltpu.SemaphoreType.DMA((local, 3)),
        save_sem=pltpu.SemaphoreType.DMA((2, 3)),
        sems=pltpu.SemaphoreType.DMA((6,)),
        across_sems=pltpu.SemaphoreType.DMA((4,)),
    )


def experts_cost(geo):
    weights = geo.local_experts * geo.hidden * geo.width
    return (4 * geo.expert_rows * weights, 4 * weights)


def forward_scratch(geo):
    scratch = experts_scratch(geo, 2)
    scratch["residual"] = pltpu.VMEM((geo.length, geo.width), F32)
    scratch["result"] = pltpu.VMEM((geo.length, geo.width), BF16)
    return scratch


def forward_tick(geo, tick, given, state, received):
    micro, length, width = geo.micro, geo.length, geo.width
    rows, local, hidden = geo.expert_rows, geo.local_experts, geo.hidden
    dense, scratch = dense_forward_scratch(geo, tick), forward_scratch(geo)
    fused = fits(dense, scratch)
    near, kept = {}, {}
    held = dict(w_in=given["w_in"], w_out=given["w_out"])
    if fused:
        near, dense_held, kept = dense_forward_refs(geo, tick, given, state, received)
        held.update(dense_held)
        scratch.update(dense)
    else:
        held["slot_rows"] = dense_forward(geo, tick, given, state, received)
        held.update(kept_aux=state["kept_aux"], kept_residual=state["kept_residual"])
    kept.update(
        out=((micro, length, width), BF16),
        kept_picked=((micro, TOP, length, width), BF16),
        kept_rows=((micro, local, rows, width), BF16),
        kept_hidden=((micro, local, rows, hidden), BF16),
        kept_slope=((micro, local, rows, hidden), BF16),
    )
    results = launch(
        partial(forward_body, geo, tick, tile_of(hidden, 512), fused),
        near=near,
        held=held,
        outs=dict(received_out=pltpu.HBM((length, width), BF16)) if 1 <= tick < micro else {},
        kept=kept,
        state=state,
        scratch=scratch,
        cost=experts_cost(geo),
        collective_id=3 + tick,
        has_side_effects=True,
    )
    return results.get("received_out")


def backward_step(geo, step, given, state, sent, received):
    micro, length, width = geo.micro, geo.length, geo.width
    rows, local, hidden = geo.expert_rows, geo.local_experts, geo.hidden
    scratch = experts_scratch(geo, local)
    scratch["slot_grad"] = pltpu.VMEM((geo.units, geo.rows, geo.main, width), BF16)
    scratch["incoming_here"] = pltpu.VMEM((length, width), BF16)
    scratch["incoming_sem"] = pltpu.SemaphoreType.DMA
    held = dict(
        cotangent=given["cotangent"], w_in=given["w_in"], w_out=given["w_out"], kept_aux=state["kept_aux"],
        kept_picked=state["kept_picked"], kept_slope=state["kept_slope"],
    )
    if step == 1:
        held["sent"] = sent
        scratch["incoming_far"] = pltpu.VMEM((length, width), BF16)
    elif step:
        held["received"] = received
    between = dict(
        moe_grad=shape((length, width), F32), gates=shape((length, 128), F32), incoming=shape((length, width), BF16)
    )
    dense = dense_backward_scratch(geo)
    near, outs, kept = {}, between, {}
    between_scratch = {name: pltpu.VMEM(one.shape, one.dtype) for name, one in between.items()}
    fused = fits(scratch, dense, between_scratch)
    if fused:
        near, dense_held, outs, kept = dense_backward_refs(geo, step, given, state)
        held.update(dense_held)
        scratch.update(dense)
        scratch.update(between_scratch)
    kept.update(
        kept_seen=((micro, local, rows, width), BF16),
        kept_pre=((micro, local, rows, hidden), BF16),
    )
    results = launch(
        partial(backward_body, geo, step, tile_of(hidden, 512), fused),
        near=near,
        held=held,
        outs=outs,
        kept=kept,
        state=state,
        scratch=scratch,
        cost=experts_cost(geo),
        collective_id=4 + micro + step,
        has_side_effects=True,
    )
    return results if fused else dense_backward(geo, step, results, given, state)


class Shards:
    def __init__(self, geo):
        self.cores, self.chips, self.cols = geo.cores, geo.chips, geo.cols
        r, self.c = lax.axis_index("row"), lax.axis_index("col")
        self.z, self.core = r // self.cores, r % self.cores

    def chip(self, k):
        return (self.z + k + self.chips) % self.chips

    def col(self, j):
        return (self.c + j + self.cols) % self.cols

    def row(self, z, other=0):
        return z * self.cores + (self.core + other) % self.cores

    def greet(self):
        barrier = pltpu.get_barrier_semaphore()
        targets = [{"row": self.row(self.chip(k))} for k in range(1, self.chips)]
        targets += [{"col": self.col(j)} for j in range(1, self.cols)]
        targets += [{"row": self.row(self.z, 1)}] * (self.cores - 1)
        for target in targets:
            pl.semaphore_signal(barrier, inc=1, device_id=target, device_id_type=MESH)
        self.greeted = len(targets)

    def await_greetings(self):
        pl.semaphore_wait(pltpu.get_barrier_semaphore(), self.greeted)


def gather_kernel(geo, pieces, qkv, out, router, gain_one, gain_two, terms, all_ref, small, own_sems, z_send, z_recv,
                  y_send, y_recv, core_send, core_recv):
    at = Shards(geo)
    at.greet()
    share, total = all_ref.shape[2:]
    narrow, wide = out.shape[1], qkv.shape[1]
    mine = all_ref.at[at.row(at.z), at.c]
    copies = Copies(own_sems)
    copies.save(qkv, mine.at[:, pl.ds(0, wide)])
    copies.save(out, mine.at[:, pl.ds(wide, narrow)])
    experts_all, count = router.shape[1], terms.shape[1]

    def unit(dims, shift=0):
        return (iota(dims, 0) + shift == iota(dims, 1)).astype(BF16)

    columns = mm(router[...], unit((experts_all, 128)), (1, 0))
    long_terms = mm(terms[...], unit((count, share)), (1, 0)).astype(BF16)
    for k, row in enumerate((gain_one[...], gain_two[...], long_terms)):
        columns = columns + mm(row, unit((1, 128), experts_all + k), (0, 0))
    small[...] = columns.astype(BF16)
    copies.save(small, mine.at[:, pl.ds(wide + narrow, 128)])
    copies.wait()
    at.await_greetings()
    step = total // pieces

    def block(k, j, h):
        return all_ref.at[at.row(at.chip(-k)), at.col(-j), :, pl.ds(h * step, step)]

    def pass_z(k, h):
        own = block(0, 0, h)
        remote(own, own, z_send, z_recv.at[h, k - 1], {"row": at.row(at.chip(k))}).start()

    def pass_y(k, h):
        for j in range(1, at.cols):
            one = block(k, 0, h)
            remote(one, one, y_send, y_recv.at[h, k, j - 1], {"col": at.col(j)}).start()

    def pass_core(k, j, h):
        if at.cores > 1:
            one = block(k, j, h)
            remote(one, one, core_send, core_recv, {"row": at.row(at.z, 1)}).start()

    def came(one, sem):
        remote(one, one, core_send, sem, {"row": at.row(at.z, 1)}).wait_recv()

    def left(one, sem):
        remote(one, one, sem, core_recv, {"row": at.row(at.z, 1)}).wait_send()

    def take_y(h):
        for k in range(at.chips):
            for j in range(1, at.cols):
                came(block(k, j, h), y_recv.at[h, k, j - 1])
                pass_core(k, j, h)

    for k in range(1, at.chips):
        pass_z(k, 0)
    for h in range(pieces):
        pass_y(0, h)
    for h in range(pieces):
        pass_core(0, 0, h)
    for h in range(pieces):
        for k in range(1, at.chips):
            came(block(k, 0, h), z_recv.at[h, k - 1])
            if h + 1 < pieces:
                pass_z(k, h + 1)
            pass_y(k, h)
            pass_core(k, 0, h)
        if h:
            take_y(h - 1)
    take_y(pieces - 1)
    if at.cores > 1:
        came(all_ref.at[pl.ds(0, at.chips)], core_recv)
        left(all_ref.at[pl.ds(0, at.chips)], core_send)
    if at.chips > 1:
        left(all_ref.at[pl.ds(0, at.chips - 1), 0], z_send)
    if at.cols > 1:
        left(all_ref.at[pl.ds(0, at.chips), pl.ds(0, at.cols - 1)], y_send)


def shard_sems(geo):
    chips = geo.chips
    z = pltpu.SemaphoreType.DMA((max(1, chips - 1),))
    y = pltpu.SemaphoreType.DMA((chips, max(1, geo.cols - 1)))
    core = pltpu.SemaphoreType.DMA((chips, geo.cols))
    return chips, z, y, core


def gather_shards(geo, qkv, out, router, gain_one, gain_two, terms):
    share, total = qkv.shape[0], qkv.shape[1] + out.shape[1] + 128
    pieces = 5 if total % 640 == 0 else 1
    one = pltpu.SemaphoreType.DMA
    return pl.pallas_call(
        partial(gather_kernel, geo, pieces),
        out_shape=pltpu.HBM((geo.rows, geo.cols, share, total), BF16),
        in_specs=[hbm_spec()] * 2 + [vmem_spec()] * 4,
        out_specs=hbm_spec(),
        scratch_shapes=[
            pltpu.VMEM((share, 128), BF16),
            pltpu.SemaphoreType.DMA((3,)),
            one, pltpu.SemaphoreType.DMA((pieces, max(1, geo.chips - 1))),
            one, pltpu.SemaphoreType.DMA((pieces, geo.chips, max(1, geo.cols - 1))),
            one, one,
        ],
        compiler_params=pltpu.CompilerParams(collective_id=1, has_side_effects=True),
    )(in_hbm(qkv), in_hbm(out), router, gain_one, gain_two, terms)


def reduce_kernel(geo, part_ref, out_ref, from_core, from_col, from_chip, pair, column, core_send, core_recv,
                  y_send, y_recv, z_send, z_recv):
    at = Shards(geo)
    at.greet()
    at.await_greetings()
    order = list(range(1, at.chips)) + [0]
    started = []

    def start(copy):
        copy.start()
        started.append(copy)

    def to_core(k):
        return remote(
            part_ref.at[at.row(at.chip(k), 1)], from_core.at[k], core_send.at[k, 0], core_recv.at[k, 0],
            {"row": at.row(at.z, 1)},
        )

    def to_col(k, j):
        return remote(
            pair.at[k, at.col(j)], from_col.at[k, j - 1], y_send.at[k, j - 1], y_recv.at[k, j - 1],
            {"col": at.col(j)},
        )

    def to_chip(k):
        return remote(
            column.at[k - 1], from_chip.at[k - 1], z_send.at[k - 1], z_recv.at[k - 1],
            {"row": at.row(at.chip(k))},
        )

    if at.cores > 1:
        for k in order:
            start(to_core(k))

    def sum_cores(k):
        total = part_ref[at.row(at.chip(k))].astype(F32)
        if at.cores > 1:
            to_core(k).wait_recv()
            total = total + from_core[k].astype(F32)
        pair[k] = total.astype(BF16)
        for j in range(1, at.cols):
            start(to_col(k, j))

    def sum_cols(k):
        total = pair[k, at.c].astype(F32)
        for j in range(1, at.cols):
            to_col(k, j).wait_recv()
            total = total + from_col[k, j - 1].astype(F32)
        if k:
            column[k - 1] = total.astype(BF16)
            start(to_chip(k))
        else:
            out_ref[...] = total

    for step, k in enumerate(order):
        sum_cores(k)
        if step:
            sum_cols(order[step - 1])
    sum_cols(order[-1])
    for k in range(1, at.chips):
        to_chip(k).wait_recv()
        out_ref[...] += from_chip[k - 1].astype(F32)
    for copy in started:
        copy.wait_send()


def reduce_shards(geo, parts):
    chips, z, y, core = shard_sems(geo)
    rows, cols, share, width = parts.shape
    steps = max(1, cols - 1)
    return pl.pallas_call(
        partial(reduce_kernel, geo),
        out_shape=shape((share, width), F32),
        in_specs=[vmem_spec()],
        out_specs=vmem_spec(),
        scratch_shapes=[
            pltpu.VMEM((chips, cols, share, width), BF16),
            pltpu.VMEM((chips, steps, share, width), BF16),
            pltpu.VMEM((max(1, chips - 1), share, width), BF16),
            pltpu.VMEM((chips, cols, share, width), BF16),
            pltpu.VMEM((max(1, chips - 1), share, width), BF16),
            core, core, y, y, z, z,
        ],
        compiler_params=pltpu.CompilerParams(
            vmem_limit_bytes=32 * MIB, collective_id=2, has_side_effects=True
        ),
    )(parts)


def expert_weights_kernel(experts_all, rows, pre, hidden, seen, packed, in_grad, out_grad, qkv, out, router, one, two,
                          terms):
    def product(left, right):
        left, right = (ref[:, 0].reshape(-1, ref.shape[-1]) for ref in (left, right))
        return mm(left, right, (0, 0))

    in_grad[0, 0] = product(rows, pre)
    out_grad[0, 0] = product(hidden, seen)

    @pl.when((pl.program_id(0) == 0) & (pl.program_id(1) == 0))
    def _():
        wide, narrow = qkv.shape[2], out.shape[2]
        qkv[0] = packed[:, :wide]
        out[0] = packed[:, wide : wide + narrow]
        small = packed[:, wide + narrow :]
        router[0] = small[:, :experts_all]
        pick = (iota((8, 128), 0) + experts_all == iota((8, 128), 1)).astype(F32)
        lines = lax.dot_general(
            pick, small, (((1,), (1,)), ((), ())), precision=lax.Precision.HIGHEST, preferred_element_type=F32
        )
        one[...] = lines[0:1]
        two[...] = lines[1:2]
        terms[...] = lines[2:3, : terms.shape[1]]


def expert_weights(geo, state, packed, terms):
    micro, local, count, width, hidden = geo.micro, geo.local_experts, geo.expert_rows, geo.width, geo.hidden
    tile = tile_of(hidden, 768)
    narrow = pl.BlockSpec((micro, 1, count, width), lambda e, f: (0, e, 0, 0))
    wide = pl.BlockSpec((micro, 1, count, tile), lambda e, f: (0, e, 0, f))
    flops = 4 * micro * local * count * width * hidden
    share = packed.shape[0]
    small = [(1, share, 3 * width), (1, share, width), (1, share, geo.experts_all), (1, share), (1, share), (1, terms)]

    def whole(dims):
        return pl.BlockSpec(dims, lambda e, f: (0,) * len(dims))

    return pl.pallas_call(
        partial(expert_weights_kernel, geo.experts_all),
        out_shape=[shape((1, local, width, hidden), F32), shape((1, local, hidden, width), F32)]
        + [shape(dims, F32) for dims in small],
        grid=(local, hidden // tile),
        in_specs=[narrow, wide, wide, narrow, whole(packed.shape)],
        out_specs=[
            pl.BlockSpec((1, 1, width, tile), lambda e, f: (0, e, 0, f)),
            pl.BlockSpec((1, 1, tile, width), lambda e, f: (0, e, f, 0)),
        ]
        + [whole(dims) for dims in small],
        compiler_params=pltpu.CompilerParams(vmem_limit_bytes=48 * MIB),
        cost_estimate=pl.CostEstimate(
            flops=flops, bytes_accessed=8 * local * hidden * width, transcendentals=0
        ),
    )(*(in_hbm(state[name]) for name in ("kept_rows", "kept_pre", "kept_hidden", "kept_seen")), packed)


def norm_backward(values, gain, grad):
    factor = norm_factor(values)
    unit = values * factor
    weighted = grad * gain
    inner = jnp.mean(weighted * unit, axis=-1, keepdims=True)
    return factor * (weighted - unit * inner), jnp.sum(grad * unit, axis=0, keepdims=True)


def dense_backward_loads(geo, m, at, copies):
    width = geo.width
    return dict(
        rest=copies.load(at.packed.at[:, pl.ds(3 * width, width + 128)], at.rest_w),
        residual=copies.load(at.kept_residual.at[m], at.residual),
        qkv=copies.load(at.kept_qkv.at[m], at.qkv),
        prob=copies.load(at.kept_prob.at[m], at.prob),
        stream=copies.load(at.kept_stream.at[m], at.stream),
        qkv_w=copies.load(at.packed.at[:, pl.ds(0, 3 * width)], at.qkv_w),
    )


def dense_backward_part(geo, step, at, copies, loads, enter, across):
    length, width, heads = geo.length, geo.width, geo.heads
    size = width // heads
    per = 128 // size
    m = backward_micro(geo, step)
    send = across is not None
    aux = at.aux[...]
    slope = aux[:, 0:1] * aux[:, 1:2] * (at.gates[:, 0:1] - at.gates[:, 1:2])
    expert_at = iota((length, 128), 1).astype(F32)
    logit_grad = (
        jnp.where(as_column(at.routes[0, m, 0:1, :].astype(F32)) == expert_at, slope, 0.0)
        - jnp.where(as_column(at.routes[0, m, 1:2, :].astype(F32)) == expert_at, slope, 0.0)
    ).astype(BF16)
    at.logit[...] = logit_grad
    copies.save(at.logit, at.kept_logit.at[m])
    loads["rest"].wait()
    moe_grad = at.moe_grad[...] + mm(logit_grad, at.rest_w[:, width:], (1, 1))
    loads["residual"].wait()
    part, gain_two = norm_backward(at.residual[...], at.gains[1:2, :], moe_grad)
    residual_grad = at.incoming[...].astype(F32) + part
    at.branch[...] = residual_grad.astype(BF16)
    copies.save(at.branch, at.kept_branch.at[m])
    at.context_grad[...] = mm(at.branch[...], at.rest_w[:, :width], (1, 1)).astype(BF16)
    which = iota((length, 128), 1) // size
    head_row = iota((128, length), 0) // size
    scale = 1.0 / math.sqrt(size)
    zero = jnp.zeros((length, 128), BF16)
    loads["qkv"].wait()
    loads["prob"].wait()
    at.sums[...] = jnp.zeros(at.sums.shape, F32)
    for j in range(width // 128):
        places = [slice(base * width + 128 * j, base * width + 128 * (j + 1)) for base in range(3)]
        queries, keys, values = (at.qkv[:, place] for place in places)
        grad = at.context_grad[:, places[0]]
        turned_keys = keys.astype(F32).T
        totals = [jnp.zeros(dims, F32) for dims in ((128, length), (length, 128), (length, 128))]
        for part_at in range(per):
            h = j * per + part_at
            own = which == part_at
            own_grad = jnp.where(own, grad, zero)
            prob = at.prob[h]
            prob_grad = mm(values, own_grad, (1, 1))
            weighted = prob.astype(F32)
            shift = jnp.sum(weighted * prob_grad, axis=0, keepdims=True)
            score_grad = (weighted * (prob_grad - shift)).astype(BF16)
            at.sums[h : h + 1, :] = diagonal_sums(score_grad.astype(F32))
            own_keys = jnp.where(head_row == part_at, turned_keys, 0.0).astype(BF16)
            totals[0] = totals[0] + mm(own_keys, score_grad, (1, 0))
            totals[1] = totals[1] + mm(score_grad, jnp.where(own, queries, zero), (1, 0))
            totals[2] = totals[2] + mm(prob, own_grad, (1, 0))
        at.qkv_grad[:, places[0]] = (totals[0].T * scale).astype(BF16)
        at.qkv_grad[:, places[1]] = (totals[1] * scale).astype(BF16)
        at.qkv_grad[:, places[2]] = totals[2].astype(BF16)
    copies.save(at.qkv_grad, at.kept_qkv_grad.at[m])
    copies.save(at.sums, at.kept_sums.at[m])
    loads["qkv_w"].wait()
    normed_grad = mm(at.qkv_grad[...], at.qkv_w[...], (1, 1))
    loads["stream"].wait()
    part, gain_one = norm_backward(at.stream[...].astype(F32), at.gains[0:1, :], normed_grad)
    at.gain_parts[...] = jnp.zeros(at.gain_parts.shape, F32)
    at.gain_parts[0:1, :] = gain_one
    at.gain_parts[1:2, :] = gain_two
    copies.save(at.gain_parts, at.kept_gains.at[m])
    in_grad = residual_grad + part
    at.in_grad_here[...] = in_grad
    copies.save(at.in_grad_here, at.in_grad.at[m])
    if step < geo.micro:
        at.sent_here[...] = in_grad.astype(BF16)
    if send:
        enter()
        across.send(at.sent_here, at.received_out)
    elif step < geo.micro:
        copies.save(at.sent_here, at.sent_out)
    copies.wait()
    if send:
        across.take(at.received_out)
        across.sent(at.sent_here, at.received_out)


def dense_backward_body(geo, step, at):
    send = 1 <= step < geo.micro
    across = Across(1, at.across_sems) if send else None
    if send:
        across.greet()

    def enter():
        pl.semaphore_wait(pltpu.get_barrier_semaphore(), 1)

    m = backward_micro(geo, step)
    copies = Copies(at.sems)
    aux_load = copies.load(at.kept_aux.at[m], at.aux)
    loads = dense_backward_loads(geo, m, at, copies)
    aux_load.wait()
    dense_backward_part(geo, step, at, copies, loads, enter, across)


def dense_backward_scratch(geo):
    length, width, heads = geo.length, geo.width, geo.heads
    return dict(
        aux=pltpu.VMEM((length, 128), F32),
        rest_w=pltpu.VMEM((width, width + 128), BF16),
        qkv_w=pltpu.VMEM((width, 3 * width), BF16),
        residual=pltpu.VMEM((length, width), F32),
        qkv=pltpu.VMEM((length, 3 * width), BF16),
        prob=pltpu.VMEM((heads, length, length), BF16),
        stream=pltpu.VMEM((length, width), BF16),
        logit=pltpu.VMEM((length, 128), BF16),
        branch=pltpu.VMEM((length, width), BF16),
        context_grad=pltpu.VMEM((length, width), BF16),
        qkv_grad=pltpu.VMEM((length, 3 * width), BF16),
        sums=pltpu.VMEM((geo.tall, length), F32),
        gain_parts=pltpu.VMEM((8, width), F32),
        in_grad_here=pltpu.VMEM((length, width), F32),
        sent_here=pltpu.VMEM((length, width), BF16),
        sems=pltpu.SemaphoreType.DMA((20,)),
        across_sems=pltpu.SemaphoreType.DMA((4,)),
    )


def dense_backward_refs(geo, step, given, state):
    micro, length, width = geo.micro, geo.length, geo.width
    outs = {}
    if 1 <= step < micro:
        outs["received_out"] = pltpu.HBM((length, width), BF16)
    elif step < micro:
        outs["sent_out"] = pltpu.HBM((length, width), BF16)
    names = ("kept_aux", "kept_residual", "kept_qkv", "kept_prob", "kept_stream")
    held = dict({name: state[name] for name in names}, packed=given["packed"])
    kept = dict(
        in_grad=((micro, length, width), F32),
        kept_branch=((micro, length, width), BF16),
        kept_qkv_grad=((micro, length, 3 * width), BF16),
        kept_logit=((micro, length, 128), BF16),
        kept_gains=((micro, 8, width), F32),
        kept_sums=((micro, geo.tall, length), F32),
    )
    return dict(routes=given["routes"], gains=given["gains"]), held, outs, kept


def dense_backward(geo, step, near, given, state):
    more, held, outs, kept = dense_backward_refs(geo, step, given, state)
    params = {}
    if 1 <= step < geo.micro:
        params = dict(collective_id=5 + 2 * geo.micro + step, has_side_effects=True)
    return launch(
        partial(where_active, only_section(geo, geo.micro - step), partial(dense_backward_body, geo, step)),
        near=dict(near, **more),
        held=held,
        outs=outs,
        kept=kept,
        state=state,
        scratch=dense_backward_scratch(geo),
        cost=(3_000_000_000, 14_000_000),
        **params,
    )


DENSE_GRADS = ("normed", "qkv_grad", "context", "branch", "moe_in", "logit")


def dense_weights_body(geo, at):
    width = geo.width
    copies = Copies(at.sems)
    loads = {}
    for name in DENSE_GRADS + ("gains", "sums"):
        loads[name] = copies.load(getattr(at, "kept_" + name), getattr(at, name))

    def product(left, right):
        left, right = (ref[...].reshape(-1, ref.shape[-1]) for ref in (left, right))
        return mm(left, right, (0, 0))

    def ready(*names):
        for name in names:
            loads[name].wait()

    ready("normed", "qkv_grad")
    normed = at.normed[...].reshape(-1, width)
    for j in range(0, 3 * width, width):
        grad = at.qkv_grad[:, :, j : j + width].reshape(-1, width)
        at.part[:, j : j + width] = mm(normed, grad, (0, 0)).astype(BF16)
    ready("context", "branch")
    at.part[:, 3 * width : 4 * width] = product(at.context, at.branch).astype(BF16)
    ready("moe_in", "logit", "gains", "sums")
    small = product(at.moe_in, at.logit)
    by_term = lax.dot_general(
        jnp.sum(at.sums[...], axis=0), at.spread[...].astype(F32), (((1,), (1,)), ((), ())),
        precision=lax.Precision.HIGHEST, preferred_element_type=F32,
    )
    bias_row = jnp.sum(by_term[: geo.heads] * at.head_pick[...], axis=0, keepdims=True)
    gain_rows = jnp.sum(at.gains[...], axis=0)
    place = iota((128, width), 0)
    rows = jnp.zeros((128, width), F32)
    for k, row in enumerate((gain_rows[0:1], gain_rows[1:2], bias_row)):
        rows = jnp.where(place == geo.experts_all + k, row, rows)
    at.part[:, 4 * width :] = (small + rows.T).astype(BF16)


def dense_weights(geo, head_pick, spread_table, state):
    held = {"kept_" + name: state["kept_" + name] for name in DENSE_GRADS}
    scratch = {name: pltpu.VMEM(held["kept_" + name].shape, BF16) for name in DENSE_GRADS}
    return launch(
        partial(dense_weights_body, geo),
        near=dict(head_pick=head_pick, spread=spread_table),
        held=dict(held, kept_gains=state["kept_gains"], kept_sums=state["kept_sums"]),
        outs=dict(part=shape((geo.width, 4 * geo.width + 128), BF16)),
        scratch=dict(
            scratch, sems=pltpu.SemaphoreType.DMA((len(DENSE_GRADS) + 2,)),
            gains=pltpu.VMEM(state["kept_gains"].shape, F32), sums=pltpu.VMEM(state["kept_sums"].shape, F32),
        ),
        spare=24,
        cost=(3_000_000_000, 10_000_000),
    )["part"]


def on_device(
    inputs, cotangent, segments, routes, order, attn_gain, qkv_weight, position_bias, out_weight, moe_gain,
    router_weight, expert_in, expert_out,
):
    micro, length, width = inputs.shape
    local_experts, hidden = expert_in.shape[1], expert_in.shape[3]
    experts_all = router_weight.shape[2]
    row_count, col_count = lax.axis_size("row"), lax.axis_size("col")
    devices = row_count * col_count
    share = width // devices
    terms = position_bias.shape[1]
    heads = terms * devices // DISTANCE_BUCKETS
    geo = Geometry(micro, length, width, heads, experts_all, local_experts, hidden, row_count, col_count)
    packed = gather_shards(
        geo, qkv_weight[0], out_weight[0], router_weight[0], attn_gain, moe_gain, position_bias
    ).reshape(width, -1)
    indicator = buckets(length)
    row_at = np.arange(width)
    term_at = np.where(row_at % share < terms, row_at // share * terms + row_at % share, -1)
    head_pick = jnp.asarray((term_at % heads == np.arange(heads)[:, None]) & (term_at >= 0), F32)
    spread_table = jnp.asarray(indicator[np.maximum(term_at, 0) // heads], BF16)
    prepared = launch(
        partial(prepare, experts_all),
        near=dict(small=packed[:, 4 * width :], head_pick=head_pick, spread=spread_table),
        outs=dict(gains=shape((2, width), F32), bias=shape((heads, length, length), BF16)),
        cost=(50_000_000, 6_000_000),
    )
    given = dict(
        prepared, packed=packed, inputs=inputs, cotangent=cotangent, w_in=expert_in[0], w_out=expert_out[0],
        segments=segments, order=order, routes=jnp.swapaxes(routes, 2, 3),
        bases=jnp.asarray(geo.bases()),
    )
    state = {}
    received = None
    for tick in range(micro + 1):
        received = forward_tick(geo, tick, given, state, received)
    sent = received = None
    for step in range(micro + 1):
        passed = backward_step(geo, step, given, state, sent, received)
        sent, received = passed.get("sent_out"), passed.get("received_out")
    part = dense_weights(geo, head_pick, spread_table, state)
    packed = reduce_shards(geo, part.reshape(row_count, col_count, share, -1))
    expert_in_grad, expert_out_grad, qkv, out, router, gain_one, gain_two, bias = expert_weights(
        geo, state, packed, terms
    )
    return (
        state["out"][None], state["in_grad"][None], gain_one, qkv, bias, out, gain_two, router, expert_in_grad,
        expert_out_grad,
    )


def solution(mesh):
    tokens = ("row", "col")
    return jax.shard_map(
        on_device,
        mesh=mesh,
        in_specs=(
            P(None, tokens, None),
            P(None, tokens, None),
            P(None, tokens),
            P("section", None, tokens, None),
            P("section", None, tokens, None),
            P("section", tokens),
            P("section", tokens, None),
            P("section", tokens),
            P("section", tokens, None),
            P("section", tokens),
            P("section", tokens, None),
            P("section", "row", None, "col"),
            P("section", "row", "col", None),
        ),
        out_specs=(
            P("section", None, tokens, None),
            P("section", None, tokens, None),
            P("section", tokens),
            P("section", tokens, None),
            P("section", tokens),
            P("section", tokens, None),
            P("section", tokens),
            P("section", tokens, None),
            P("section", "row", None, "col"),
            P("section", "row", "col", None),
        ),
        check_vma=False,
    )
```

```python
from functools import partial
import math
from types import SimpleNamespace

import jax
import jax.numpy as jnp
import numpy as np
from jax import lax
from jax.experimental import pallas as pl
from jax.experimental.pallas import tpu as pltpu
from jax.sharding import PartitionSpec as P

TOP = 2
DISTANCE_BUCKETS = 32
MAX_DIST = 128
EPS = 1e-06
MESH = pl.DeviceIdType.MESH
F32 = jnp.float32
BF16 = jnp.bfloat16
MIB = 1 << 20


class Geometry:
    def __init__(self, micro, length, width, heads, experts_all, local_experts, hidden, row_count, col_count):
        self.micro, self.length, self.width, self.heads, self.hidden = micro, length, width, heads, hidden
        self.tall = -(-heads // 8) * 8
        self.capacity = max(2, (5 * length * TOP + 4 * experts_all - 1) // (4 * experts_all))
        self.local_experts = local_experts
        self.experts_all = experts_all
        self.rows, self.cols = row_count, col_count
        self.cores = 2 if row_count % 2 == 0 else 1
        self.chips = row_count // self.cores
        main = self.capacity // 16 * 16
        rest = self.capacity - main
        self.share = main // local_experts if 0 < rest <= main // local_experts else 0
        if rest and not self.share:
            main += 16
        self.main = main
        self.first = 1 if self.share else 0
        self.units = local_experts + self.first
        self.slots = row_count * self.units * main
        self.sources = row_count * col_count
        self.expert_rows = self.sources * (main + self.share)

    def bases(self):
        expert = np.arange(self.experts_all)
        owner, local = expert // self.local_experts, expert % self.local_experts
        main = ((self.first + local) * self.rows + owner) * self.main
        tail = owner * self.main + local * self.share
        both = np.stack([main, tail]).astype(np.float32)
        return np.pad(both, ((0, 0), (0, 128 - self.experts_all)))


def buckets(length):
    distance = np.arange(length)
    bucket = np.zeros(length, np.int64)
    half = DISTANCE_BUCKETS // 2
    for level in range(1, DISTANCE_BUCKETS):
        if level < half:
            limit = level
        else:
            limit = int(math.ceil(half * (MAX_DIST / half) ** ((level - half) / half)))
        bucket += distance >= limit
    return (np.arange(DISTANCE_BUCKETS)[:, None] == bucket[None, :]).astype(np.float32)


def mm(left, right, contract):
    return lax.dot_general(
        left, right, (((contract[0],), (contract[1],)), ((), ())), preferred_element_type=F32
    )


def iota(shape, axis):
    return lax.broadcasted_iota(jnp.int32, shape, axis)


def norm_factor(values):
    return lax.rsqrt(jnp.mean(values * values, axis=-1, keepdims=True) + EPS)


def gelu_pair(x):
    density = jnp.exp(-0.5 * x * x)
    t = 1.0 / (1.0 + (0.3275911 * math.sqrt(0.5)) * jnp.abs(x))
    poly = 0.5 * 1.061405429
    for coefficient in (-1.453152027, 1.421413741, -0.284496736, 0.254829592):
        poly = poly * t + 0.5 * coefficient
    beyond = poly * t * density
    cdf = jnp.where(x >= 0, 1.0 - beyond, beyond)
    return x * cdf, cdf + x * density * (1.0 / math.sqrt(2.0 * math.pi))


def slot_onehots(aux, slots):
    positions = iota((aux.shape[0], slots), 1).astype(F32)
    return [(aux[:, 2 + c : 3 + c] == positions) for c in range(TOP)]


def vmem_grant(scratch, spare):
    held = 0
    for ref in scratch:
        if getattr(ref, "memory_space", None) == pltpu.VMEM:
            held += math.prod(ref.shape) * jnp.dtype(ref.dtype).itemsize
    return -(-held // MIB) + spare


def fits(*scratches):
    return vmem_grant([ref for scratch in scratches for ref in scratch.values()], 11) <= 62


def vmem_spec():
    return pl.BlockSpec(memory_space=pltpu.VMEM)


def hbm_spec():
    return pl.BlockSpec(memory_space=pltpu.HBM)


def in_hbm(array):
    return pltpu.with_memory_space_constraint(array, pltpu.HBM)


def shape(dims, kind):
    return jax.ShapeDtypeStruct(dims, kind)


def launch(body, near=None, held=None, outs=None, kept=None, state=None, scratch=None, spare=10, cost=None, **params):
    near, held, outs, kept, scratch = (dict(part or {}) for part in (near, held, outs, kept, scratch))
    state = {} if state is None else state
    old = [name for name in kept if name in state]
    names_in, names_out = list(near) + list(held), list(outs) + list(kept)

    def kernel(*refs):
        refs = list(refs)
        given, refs = refs[: len(names_in)], refs[len(names_in) + len(old) :]
        body(SimpleNamespace(**dict(zip(names_in + names_out + list(scratch), given + refs))))

    out_shapes = list(outs.values()) + [pltpu.HBM(dims, kind) for dims, kind in kept.values()]
    plain = [isinstance(out, jax.ShapeDtypeStruct) for out in out_shapes]
    estimate = {}
    if cost is not None:
        estimate["cost_estimate"] = pl.CostEstimate(flops=cost[0], bytes_accessed=cost[1], transcendentals=0)
    results = pl.pallas_call(
        kernel,
        out_shape=out_shapes,
        in_specs=[vmem_spec()] * len(near) + [hbm_spec()] * (len(held) + len(old)),
        out_specs=[vmem_spec() if near_by else hbm_spec() for near_by in plain],
        scratch_shapes=list(scratch.values()),
        input_output_aliases={len(names_in) + i: names_out.index(name) for i, name in enumerate(old)},
        compiler_params=pltpu.CompilerParams(
            vmem_limit_bytes=vmem_grant(scratch.values(), spare) * MIB, **params
        ),
        **estimate,
    )(*near.values(), *map(in_hbm, held.values()), *(in_hbm(state[name]) for name in old))
    results = dict(zip(names_out, results))
    for name in kept:
        state[name] = results.pop(name)
    return results


def of_micro(rows, m):
    if isinstance(m, int):
        return rows[m : m + 1]
    row = rows[0:1]
    for i in range(1, rows.shape[0]):
        row = jnp.where(m == i, rows[i : i + 1], row)
    return row


def as_column(row):
    return jnp.broadcast_to(row, (8, row.shape[1])).T[:, 0:1]


class Copies:
    def __init__(self, sems):
        self.sems, self.count, self.open = sems, 0, []

    def load(self, source, target):
        copy = pltpu.make_async_copy(source, target, self.sems.at[self.count])
        self.count += 1
        copy.start()
        return copy

    def save(self, source, target):
        self.open.append(self.load(source, target))

    def wait(self):
        for copy in self.open:
            copy.wait()


def remote(source, target, send, receive, where):
    return pltpu.make_async_remote_copy(
        src_ref=source, dst_ref=target, send_sem=send, recv_sem=receive, device_id=where, device_id_type=MESH
    )


def forward_micro(geo, tick):
    if tick == 0:
        return 0
    return geo.micro - 1 if tick == geo.micro else tick - lax.axis_index("section")


def backward_micro(geo, step):
    if step == 0:
        return geo.micro - 1
    return 0 if step == geo.micro else geo.micro - step - lax.axis_index("section")


class Across:
    def __init__(self, sender, sems, at=0):
        self.section = lax.axis_index("section")
        self.sender, self.other = sender, {"section": 1 - self.section}
        self.send_sem, self.recv_sem = sems.at[at], sems.at[at + 1]

    def greet(self):
        pl.semaphore_signal(pltpu.get_barrier_semaphore(), inc=1, device_id=self.other, device_id_type=MESH)

    def copy(self, source, target):
        return remote(source, target, self.send_sem, self.recv_sem, self.other)

    def send(self, source, target):
        @pl.when(self.section == self.sender)
        def _():
            self.copy(source, target).start()

    def sent(self, source, target):
        @pl.when(self.section == self.sender)
        def _():
            self.copy(source, target).wait_send()

    def take(self, target):
        @pl.when(self.section != self.sender)
        def _():
            self.copy(target, target).wait_recv()


def prepare(experts_all, at):
    heads, length = at.bias_here.shape[:2]
    width = at.small.shape[0]
    copies = Copies(at.sems)
    copies.load(at.packed.at[:, pl.ds(4 * width, 128)], at.small).wait()
    rows = at.small[...].astype(F32).T
    at.gains_here[0:2, :] = rows[experts_all : experts_all + 2]
    copies.save(at.gains_here, at.gains)
    picked = (at.head_pick[...] * rows[experts_all + 2 : experts_all + 3]).astype(BF16)
    by_distance = mm(picked, at.spread[...], (1, 0))
    for h in range(heads):
        block = by_distance[h : h + 1, :]
        step = 1
        while step < length:
            block = jnp.concatenate([block, pltpu.roll(block, step, 1)], axis=0)
            step *= 2
        at.bias_here[h] = block.astype(BF16)
    copies.save(at.bias_here, at.bias)
    copies.wait()


def diagonal_sums(block):
    length = block.shape[1]
    size = block.shape[0] // 2
    while size >= 1:
        block = block[:size] + pltpu.roll(block[size:], length - size, 1)
        size //= 2
    return block


def only_section(geo, tick):
    return {0: 0, geo.micro: 1}.get(tick)


def where_active(active, body, at):
    if active is None:
        body(at)
    else:
        pl.when(lax.axis_index("section") == active)(partial(body, at))


def dense_forward_part(geo, tick, at, copies, enter, across, loaded, fused=True):
    length, width, heads = geo.length, geo.width, geo.heads
    size = width // heads
    per = 128 // size
    m = forward_micro(geo, tick)
    gains_load = copies.load(at.gains, at.gains_here)
    thirds = [pl.ds(third * width, width) for third in range(3)]
    packed_qkv = [copies.load(at.packed.at[:, third], at.qkv_w.at[:, third]) for third in thirds]
    if tick == 0:
        copies.load(at.inputs.at[m], at.stream).wait()
    else:
        first = lax.axis_index("section") == 0
        own = pltpu.make_async_copy(at.inputs.at[m], at.stream, at.stream_sem)
        if tick == 1:
            enter()
            across.send(at.out.at[0] if fused else at.out_before.at[0], at.stream_in)
        else:
            came = pltpu.make_async_copy(at.received, at.stream, at.stream_sem)

        @pl.when(first)
        def _():
            own.start()
            own.wait()

        if tick == 1:
            across.take(at.stream_in)

            @pl.when(jnp.logical_not(first))
            def _():
                at.stream[...] = at.stream_in[...]
        else:

            @pl.when(jnp.logical_not(first))
            def _():
                came.start()
                came.wait()

    packed_rest = copies.load(at.packed.at[:, pl.ds(3 * width, width + 128)], at.rest_w)
    bias_load = copies.load(at.bias, at.bias_here)
    copies.save(at.stream, at.kept_stream.at[m])
    stream = at.stream[...].astype(F32)
    gains_load.wait()
    at.normed[...] = (stream * norm_factor(stream) * at.gains_here[0:1, :]).astype(BF16)
    copies.save(at.normed, at.kept_normed.at[m])
    for third, load in zip(thirds, packed_qkv):
        load.wait()
        at.qkv[:, third] = mm(at.normed[...], at.qkv_w[:, third], (1, 0)).astype(BF16)
    copies.save(at.qkv, at.kept_qkv.at[m])
    key_at, query_at = iota((length, length), 0), iota((length, length), 1)
    segments = of_micro(at.segments[...], m).astype(F32)
    allowed = (key_at <= query_at) & (as_column(segments) == segments)
    which = iota((length, 128), 1) // size
    head_row = iota((128, length), 0) // size
    scale = 1.0 / math.sqrt(size)
    zero = jnp.zeros((length, 128), BF16)
    bias_load.wait()
    for j in range(width // 128):
        queries = at.qkv[:, 128 * j : 128 * (j + 1)]
        keys = at.qkv[:, width + 128 * j : width + 128 * (j + 1)]
        values = at.qkv[:, 2 * width + 128 * j : 2 * width + 128 * (j + 1)]
        turned_values = values.astype(F32).T
        context = jnp.zeros((128, length), F32)
        for part in range(per):
            h = j * per + part
            own = which == part
            scores = mm(jnp.where(own, keys, zero), queries, (1, 1)) * scale + at.bias_here[h].astype(F32)
            scores = jnp.where(allowed, scores, -1e30)
            exponent = jnp.exp(scores - jnp.max(scores, axis=0, keepdims=True))
            prob = (exponent * (1.0 / jnp.sum(exponent, axis=0, keepdims=True))).astype(BF16)
            at.prob[h] = prob
            own_values = jnp.where(head_row == part, turned_values, 0.0).astype(BF16)
            context = context + mm(own_values, prob, (1, 0))
        at.context[:, 128 * j : 128 * (j + 1)] = context.T.astype(BF16)
        heads_here = pl.ds(j * per, per)
        copies.save(at.prob.at[heads_here], at.kept_prob.at[m, heads_here])
    copies.save(at.context, at.kept_context.at[m])
    packed_rest.wait()
    loaded()
    residual = stream + mm(at.context[...], at.rest_w[:, :width], (1, 0))
    at.residual[...] = residual
    copies.save(at.residual, at.kept_residual.at[m])
    moe_in = (residual * norm_factor(residual) * at.gains_here[1:2, :]).astype(BF16)
    at.moe_in[...] = moe_in
    copies.save(at.moe_in, at.kept_moe_in.at[m])
    logits = mm(moe_in, at.rest_w[:, width:], (1, 0))
    expert_at = iota(logits.shape, 1)
    picks = [(as_column(at.routes[0, m, c : c + 1, :].astype(F32)) == expert_at.astype(F32)).astype(F32) for c in range(TOP)]
    chosen = [jnp.sum(pick * logits, axis=1, keepdims=True) for pick in picks]
    top = jnp.maximum(chosen[0], chosen[1])
    powers = [jnp.exp(value - top) for value in chosen]
    total = powers[0] + powers[1]
    shares = [power / total for power in powers]
    order = of_micro(at.order[0, :, 0, :], m).astype(F32)
    before = (order < as_column(order)).astype(BF16)
    counts = [mm(before, pick.astype(BF16), (1, 0)) for pick in picks]
    counts[1] = counts[1] + jnp.sum(picks[0], axis=0, keepdims=True)
    slots = []
    for pick, count in zip(picks, counts):
        rank = jnp.sum(pick * count, axis=1, keepdims=True)
        main = jnp.sum(pick * at.bases[0:1, :], axis=1, keepdims=True)
        tail = jnp.sum(pick * at.bases[1:2, :], axis=1, keepdims=True)
        place = jnp.where(rank < geo.main, main + rank, tail + rank - geo.main)
        slots.append(jnp.where(rank < geo.capacity, place, -1.0))
    lane = iota((length, 128), 1)
    aux = jnp.zeros((length, 128), F32)
    for place, value in enumerate(shares + slots):
        aux = jnp.where(lane == place, value, aux)
    at.aux[...] = aux
    copies.save(at.aux, at.kept_aux.at[m])
    first, second = slot_onehots(aux, geo.slots)
    at.slots[...] = mm((first | second).astype(BF16), moe_in, (0, 0)).astype(BF16).reshape(at.slots.shape)


def dense_forward_body(geo, tick, at):
    across = Across(0, at.across_sems) if tick == 1 else None
    if across:
        across.greet()

    def enter():
        pl.semaphore_wait(pltpu.get_barrier_semaphore(), 1)

    copies = Copies(at.sems)
    dense_forward_part(geo, tick, at, copies, enter, across, lambda: None, fused=False)
    copies.save(at.slots, at.slot_rows)
    copies.wait()
    if across:
        across.sent(at.out_before.at[0], at.stream_in)


def dense_forward_scratch(geo, tick):
    length, width, heads = geo.length, geo.width, geo.heads
    scratch = dict(
        stream=pltpu.VMEM((length, width), BF16),
        qkv_w=pltpu.VMEM((width, 3 * width), BF16),
        rest_w=pltpu.VMEM((width, width + 128), BF16),
        bias_here=pltpu.VMEM((heads, length, length), BF16),
        normed=pltpu.VMEM((length, width), BF16),
        qkv=pltpu.VMEM((length, 3 * width), BF16),
        prob=pltpu.VMEM((heads, length, length), BF16),
        context=pltpu.VMEM((length, width), BF16),
        residual=pltpu.VMEM((length, width), F32),
        moe_in=pltpu.VMEM((length, width), BF16),
        aux=pltpu.VMEM((length, 128), F32),
        slots=pltpu.VMEM((geo.units, geo.rows, geo.main, width), BF16),
        gains_here=pltpu.VMEM((8, width), F32),
        sems=pltpu.SemaphoreType.DMA((20 + width // 128,)),
        stream_sem=pltpu.SemaphoreType.DMA,
        across_sems=pltpu.SemaphoreType.DMA((4,)),
    )
    if tick == 1:
        scratch["stream_in"] = pltpu.VMEM((length, width), BF16)
    return scratch


def dense_forward_refs(geo, tick, given, state, received):
    micro, length, width, heads = geo.micro, geo.length, geo.width, geo.heads
    near = {name: given[name] for name in ("segments", "order", "routes", "bases")}
    held = {name: given[name] for name in ("packed", "bias", "inputs", "gains")}
    if tick > 1:
        held["received"] = received
    kept = dict(
        kept_stream=((micro, length, width), BF16),
        kept_normed=((micro, length, width), BF16),
        kept_qkv=((micro, length, 3 * width), BF16),
        kept_prob=((micro, heads, length, length), BF16),
        kept_context=((micro, length, width), BF16),
        kept_residual=((micro, length, width), F32),
        kept_moe_in=((micro, length, width), BF16),
        kept_aux=((micro, length, 128), F32),
    )
    return near, held, kept


def dense_forward(geo, tick, given, state, received):
    near, held, kept = dense_forward_refs(geo, tick, given, state, received)
    params = {}
    if tick == 1:
        held["out_before"] = state["out"]
        params = dict(collective_id=5 + 2 * geo.micro, has_side_effects=True)
    return launch(
        partial(where_active, only_section(geo, tick), partial(dense_forward_body, geo, tick)),
        near=near,
        held=held,
        outs=dict(slot_rows=pltpu.HBM((geo.units, geo.rows, geo.main, geo.width), BF16)),
        kept=kept,
        state=state,
        scratch=dense_forward_scratch(geo, tick),
        cost=(2_000_000_000, 14_000_000),
        **params,
    )["slot_rows"]


def combine(home, aux, result, picked_ref):
    for c, onehot in enumerate(slot_onehots(aux, home.shape[0])):
        picked = mm(onehot.astype(BF16), home, (1, 0))
        picked_ref[c] = picked.astype(BF16)
        result = result + aux[:, c : c + 1] * picked
    return result


def spread(incoming, aux, slots):
    total = 0.0
    for c, onehot in enumerate(slot_onehots(aux, slots)):
        total = total + mm(onehot.astype(BF16), (aux[:, c : c + 1] * incoming).astype(BF16), (0, 0))
    return total.astype(BF16)


def gate_gradients(incoming, picked_ref):
    lane = iota((incoming.shape[0], 128), 1)
    gates = jnp.zeros(lane.shape, F32)
    for c in range(TOP):
        gate = jnp.sum(picked_ref[c].astype(F32) * incoming, axis=1, keepdims=True)
        gates = jnp.where(lane == c, gate, gates)
    return gates


def expert_picker(geo, e):
    dims = (geo.sources * geo.share, geo.sources * geo.main)
    own, place = iota(dims, 0), iota(dims, 1)
    return (place == own // geo.share * geo.main + e * geo.share + own % geo.share).astype(BF16)


class Exchange:
    def __init__(self, geo, at, x, active=None):
        self.geo, self.x, self.at = geo, x, at
        self.relay = geo.chips // 2 if active is not None and geo.chips > 1 else None
        self.near_rows = geo.cores
        self.ahead = 2 if self.relay else 1
        self.peers = geo.cols - 1
        self.other = {"section": 1 - lax.axis_index("section")}
        self.r, self.c = lax.axis_index("row"), lax.axis_index("col")
        self.z, self.core = self.r // geo.cores, self.r % geo.cores
        self.partner = self.z * geo.cores + (self.core + 1) % geo.cores

    def far(self, direct):
        return [k for k in range(1, self.geo.chips) if direct or k != self.relay]

    def far_rows(self, direct):
        return self.geo.cores * len(self.far(direct))

    def kinds(self):
        first = self.geo.first if self.relay else 0
        return [(pl.ds(at, n), direct) for at, n, direct in ((0, first, True), (first, self.geo.units - first, False)) if n]

    def chip(self, k):
        return (self.z + k + self.geo.chips) % self.geo.chips

    def row(self, k, d):
        return self.partner if k == 0 else self.chip(k) * self.geo.cores + d

    def col(self, j):
        return (self.c + j + self.geo.cols) % self.geo.cols

    def rows(self, k):
        return pl.ds(self.chip(k) * self.geo.cores, self.geo.cores)

    def others(self, k):
        return range(self.geo.cores - 1) if k == 0 else range(self.geo.cores)

    def greet(self):
        barrier = pltpu.get_barrier_semaphore()
        for k in range(self.geo.chips):
            for d in self.others(k):
                pl.semaphore_signal(barrier, inc=1, device_id={"row": self.row(k, d)}, device_id_type=MESH)
        for j in range(1, self.geo.cols):
            pl.semaphore_signal(barrier, inc=1, device_id={"col": self.col(j)}, device_id_type=MESH)
        if self.relay:
            pl.semaphore_signal(barrier, inc=1, device_id=self.other, device_id_type=MESH)

    def await_greetings(self, more):
        more = more + (1 if self.relay else 0)
        pl.semaphore_wait(pltpu.get_barrier_semaphore(), self.geo.rows + self.geo.cols - 2 + more)

    def came(self, block, sem):
        remote(block, block, self.at.done, sem, self.other).wait_recv()

    def left(self, block, sem):
        remote(block, block, sem, self.at.done, self.other).wait_send()


    def own(self, u):
        return pltpu.make_async_copy(
            self.x.at[u, self.r], self.at.inbox.at[u, self.c, self.r], self.at.own_sem.at[u]
        )

    def kind(self, u):
        if not (self.relay and self.geo.first):
            return 0
        return int(u < self.geo.first) if isinstance(u, int) else (u + self.geo.units - 1) // self.geo.units * -1 + 1

    def send(self, u, k):
        for d in self.others(k):
            remote(
                self.x.at[u, self.row(k, d)], self.at.inbox.at[u, self.c, self.r], self.at.in_send.at[self.kind(u)],
                self.at.in_recv.at[u, k], {"row": self.row(k, d)},
            ).start()

    def send_out(self, u):
        if self.relay:
            remote(
                self.x.at[u, self.rows(self.relay)], self.at.via_x.at[u], self.at.via_send,
                self.at.via_x_recv.at[u], self.other,
            ).start()

    def hand_over(self, u, k):
        block = self.at.inbox.at[u, self.c, self.rows(-k)]
        for j in range(1, self.geo.cols):
            remote(block, block, self.at.pass_send.at[u], self.at.pass_recv.at[u], {"col": self.col(j)}).start()

    def each(self, body):
        lax.fori_loop(0, self.geo.units, lambda u, carry: (body(u), carry)[1], 0)

    def open(self):
        for u in range(min(self.ahead, self.geo.units)):
            direct = u < self.geo.first
            for k in self.far(direct):
                self.send(u, k)
            if not direct:
                self.send_out(u)

        def body(u):
            self.own(u).start()
            self.send(u, 0)

        self.each(body)
        for u in range(min(3, self.geo.units)):
            self.pass_on_own(u)

    def pass_on_own(self, u):
        self.own(u).wait()
        if self.geo.cores > 1:
            self.came(self.at.inbox.at[u, self.c, pl.ds(0, 1)], self.at.in_recv.at[u, 0])
        self.hand_over(u, 0)

    def pass_on(self, u, direct=False):
        @pl.when(u + self.ahead < self.geo.units)
        def _():
            self.send_out(u + self.ahead)

        for k in self.far(direct):
            self.came(self.at.inbox.at[u, self.c, self.rows(-k)], self.at.in_recv.at[u, k])

            @pl.when(u + self.ahead < self.geo.units)
            def _():
                if k in self.far(False):
                    self.send(u + self.ahead, k)

            self.hand_over(u, k)

        @pl.when(u + 3 < self.geo.units)
        def _():
            self.pass_on_own(u + 3)

    def collect(self, u, direct=False):
        if self.peers:
            block = self.at.inbox.at[u, pl.ds(0, self.peers), pl.ds(0, self.near_rows + self.far_rows(direct))]
            self.came(block, self.at.pass_recv.at[u])
            self.left(block, self.at.pass_send.at[u])
        if self.relay and not direct:
            self.came(self.at.inbox.at[u, :, pl.ds(0, self.geo.cores)], self.at.into_recv.at[u])


    def send_parts(self, u, far, direct=False):
        if far and self.relay and not direct:
            for j in range(self.geo.cols):
                remote(
                    self.at.inbox.at[u, self.col(j), self.rows(self.relay)], self.at.via_part.at[u, j],
                    self.at.via_part_send, self.at.via_part_recv.at[u], self.other,
                ).start()
        for k in self.far(direct) if far else (0,):
            for j in range(1, self.geo.cols):
                remote(
                    self.at.inbox.at[u, self.col(j), self.rows(k)], self.at.arrived.at[u, j - 1, self.rows(k)],
                    self.at.out_send.at[self.kind(u)], self.at.out_recv.at[u, int(far)], {"col": self.col(j)},
                ).start()

    def send_home(self, u, far, direct=False):
        count = self.far_rows(direct) if far else self.near_rows
        if self.peers and count:
            self.came(self.at.arrived.at[u, :, pl.ds(0, count)], self.at.out_recv.at[u, int(far)])
        for k in self.far(direct) if far else (0,):
            rows = self.rows(k)
            total = self.at.inbox[u, self.c, rows].astype(F32)
            for j in range(1, self.geo.cols):
                total = total + self.at.arrived[u, j - 1, rows].astype(F32)
            self.at.stage[u, rows] = total.astype(BF16)
            for d in self.others(k):
                remote(
                    self.at.stage.at[u, self.row(k, d)], self.at.home.at[u, self.r], self.at.home_send.at[self.kind(u)],
                    self.at.home_recv.at[self.kind(u)], {"row": self.row(k, d)},
                ).start()
            if k == 0:
                self.at.home[u, self.r] = self.at.stage[u, self.r]

    def finish(self):
        at, cores = self.at, self.geo.cores
        for units, direct in self.kinds():
            sent_rows = self.far_rows(direct) + cores - 1
            if sent_rows:
                block = at.home.at[units, pl.ds(0, sent_rows)]
                self.came(block, at.home_recv.at[int(direct)])
                self.left(block, at.home_send.at[int(direct)])
                self.left(block, at.in_send.at[int(direct)])
            if self.peers:
                block = at.arrived.at[units, :, pl.ds(0, self.near_rows + self.far_rows(direct))]
                self.left(block, at.out_send.at[int(direct)])
            if self.relay and not direct:
                self.came(at.home.at[units, pl.ds(0, cores)], at.home_in_recv)
                self.left(at.via_x.at[units], at.via_send)
                self.left(at.via_part.at[units], at.via_part_send)


    def along(self, u, d, source, target, at):
        where = {"row": self.row(self.relay, d)}
        return remote(
            source.at[u, d], target.at[u, self.core], self.at.core_sems.at[at, u, d],
            self.at.core_sems.at[at + 1, u, self.core], where,
        )

    def along_came(self, u, d, target, at):
        self.came(target.at[u, d], self.at.core_sems.at[at + 1, u, d])

    def across(self, u, j):
        return remote(
            self.at.via_z.at[u], self.at.via_y.at[u, j - 1], self.at.via_sems.at[2, u, j], self.at.via_sems.at[3, u, j],
            {"col": self.col(j)},
        )

    def into(self, u, j):
        source = self.at.via_y.at[u, j - 1] if j else self.at.via_z.at[u]
        target = self.at.inbox.at[u, self.col(-j), self.rows(-self.relay)]
        return remote(source, target, self.at.via_sems.at[0, u, j], self.at.into_recv.at[u], self.other)

    def part_across(self, u, j):
        return remote(
            self.at.via_part.at[u, j], self.at.via_sum.at[u, j - 1], self.at.via_sems.at[4, u, j],
            self.at.via_sems.at[5, u, j], {"col": self.col(j)},
        )

    def home_in(self, u):
        return remote(
            self.at.via_home.at[u], self.at.home.at[u, self.rows(-self.relay)], self.at.via_sems.at[1, u, 0],
            self.at.home_in_recv, self.other,
        )

    def carry(self):
        geo, at = self.geo, self.at
        cores, columns = range(geo.cores), range(1, geo.cols)

        def rows_out(u):
            self.came(at.via_x.at[u], at.via_x_recv.at[u])
            for d in cores:
                self.along(u, d, at.via_x, at.via_z, 0).start()

        def rows_on(u):
            for d in cores:
                self.along_came(u, d, at.via_z, 0)
            self.into(u, 0).start()
            for j in columns:
                self.across(u, j).start()

        def rows_in(u):
            for j in columns:
                self.across(u, j).wait_recv()
                self.into(u, j).start()

        def parts_out(u):
            self.came(at.via_part.at[u], at.via_part_recv.at[u])
            for j in columns:
                self.part_across(u, j).start()

        def parts_on(u):
            total = at.via_part[u, 0].astype(F32)
            for j in columns:
                self.part_across(u, j).wait_recv()
                total = total + at.via_sum[u, j - 1].astype(F32)
            at.via_total[u] = total.astype(BF16)
            for d in cores:
                self.along(u, d, at.via_total, at.via_home, 2).start()

        def parts_in(u):
            for d in cores:
                self.along_came(u, d, at.via_home, 2)
            self.home_in(u).start()

        units = list(range(geo.first, geo.units))
        for steps in ((rows_out, rows_on, rows_in), (parts_out, parts_on, parts_in)):
            for t in range(len(units) + 2):
                for lag, work in enumerate(steps):
                    if 0 <= t - lag < len(units):
                        work(units[t - lag])
        for u in units:
            for d in cores:
                self.along(u, d, at.via_x, at.via_z, 0).wait_send()
                self.along(u, d, at.via_total, at.via_home, 2).wait_send()
            for j in range(geo.cols):
                self.into(u, j).wait_send()
            for j in columns:
                self.across(u, j).wait_send()
                self.part_across(u, j).wait_send()
            self.home_in(u).wait_send()


def run_experts(geo, exchange, rows, total, shared, loads, expert, saves, opened=lambda: None):
    first, count = geo.first, geo.sources * geo.main
    inbox = exchange.at.inbox
    width = inbox.shape[-1]
    exchange.open()
    opened()
    if first:
        exchange.pass_on(0, True)
    exchange.pass_on(first)
    if first:
        exchange.collect(0, True)
        shared[...] = jnp.zeros(shared.shape, F32)

    def step(e, carry):
        u = e + first
        slot = e % 2

        @pl.when(e + 1 < geo.local_experts)
        def _():
            exchange.pass_on(u + 1)

        exchange.collect(u)

        @pl.when(e >= 2)
        def _():
            for copy in saves(e - 2, slot):
                copy.wait()

        rows[slot, :count] = inbox[u].reshape(count, width)
        if first:
            picker = expert_picker(geo, e)
            tail = inbox[0].reshape(count, width)
            rows[slot, count:] = mm(picker, tail, (1, 0)).astype(BF16)
        for copy in loads(e):
            copy.wait()
        expert(e, slot)
        for copy in saves(e, slot):
            copy.start()
        inbox[u] = total[:count].astype(BF16).reshape(inbox.shape[1:])
        exchange.send_parts(u, True)
        if first:
            shared[...] += mm(picker, total[count:].astype(BF16), (0, 0))

        @pl.when(e >= 1)
        def _():
            exchange.send_home(u - 1, True)
            if exchange.relay:
                exchange.send_parts(u - 1, False)

        return carry

    lax.fori_loop(0, geo.local_experts, step, 0)
    if first:
        inbox[0] = shared[...].astype(BF16).reshape(inbox.shape[1:])
        exchange.send_parts(0, True, True)
    for u in range(geo.units):
        if not exchange.relay or u < first or u == geo.units - 1:
            exchange.send_parts(u, False)
    exchange.send_home(geo.units - 1, True)
    if first:
        exchange.send_home(0, True, True)
    exchange.each(lambda u: exchange.send_home(u, False))
    for e in range(max(0, geo.local_experts - 2), geo.local_experts):
        for copy in saves(e, e % 2):
            copy.wait()
    exchange.finish()


def share_work(exchange, active, work):
    if not exchange.relay:
        work()
        return
    section = lax.axis_index("section")
    pl.when(section == active)(work)

    @pl.when(section != active)
    def _():
        exchange.await_greetings(0)
        exchange.carry()


def start_loads(geo, loads):
    for e in range(geo.local_experts):
        for copy in loads(e):
            copy.start()


def forward_body(geo, tick, tile, fused, at):
    m = forward_micro(geo, tick)
    take, send = fused and tick == 1, 1 <= tick < geo.micro
    active = only_section(geo, tick)
    exchange = Exchange(geo, at, at.slots if fused else at.slot_rows, active)
    exchange.greet()
    across_in, across_out = Across(0, at.across_sems, 2), Across(0, at.across_sems)
    if take or send:
        across_out.greet()
    w_in, w_out = at.w_in_here, at.w_out_here

    def loads(e):
        return (
            pltpu.make_async_copy(at.w_in.at[e], w_in.at[e], at.load_sem.at[e, 0]),
            pltpu.make_async_copy(at.w_out.at[e], w_out.at[e], at.load_sem.at[e, 1]),
        )

    def saves(e, slot):
        return (
            pltpu.make_async_copy(at.rows.at[slot], at.kept_rows.at[m, e], at.save_sem.at[slot, 0]),
            pltpu.make_async_copy(at.wide.at[slot], at.kept_hidden.at[m, e], at.save_sem.at[slot, 1]),
            pltpu.make_async_copy(at.slope.at[slot], at.kept_slope.at[m, e], at.save_sem.at[slot, 2]),
        )

    def expert(e, slot):
        for f in range(0, geo.hidden, tile):
            value, derivative = gelu_pair(mm(at.rows[slot], w_in[e, :, f : f + tile], (1, 0)))
            value = value.astype(BF16)
            at.wide[slot, :, f : f + tile] = value
            at.slope[slot, :, f : f + tile] = derivative.astype(BF16)
            product = mm(value, w_out[e, f : f + tile, :], (1, 0))
            at.total[...] = product if f == 0 else at.total[...] + product

    def enter():
        exchange.await_greetings(int(take or send))

    def work():
        copies = Copies(at.sems)
        if fused:
            dense_forward_part(geo, tick, at, copies, enter, across_in, lambda: start_loads(geo, loads))
            if not take:
                enter()
        else:
            start_loads(geo, loads)
            aux_load = copies.load(at.kept_aux.at[m], at.aux)
            residual_load = copies.load(at.kept_residual.at[m], at.residual)
            enter()
        run_experts(geo, exchange, at.rows, at.total, at.shared, loads, expert, saves)
        if not fused:
            aux_load.wait()
            residual_load.wait()
        home = at.home[...].reshape(geo.slots, geo.width)
        at.result[...] = combine(home, at.aux[...], at.residual[...], at.picked).astype(BF16)
        if send:
            across_out.send(at.result, at.received_out)
        copies.save(at.result, at.out.at[m])
        copies.save(at.picked, at.kept_picked.at[m])
        copies.wait()
        if take:
            across_in.sent(at.out.at[0], at.stream_in)
        if send:
            across_out.take(at.received_out)
            across_out.sent(at.result, at.received_out)

    share_work(exchange, active, work)


def backward_body(geo, step, tile, fused, at):
    m = backward_micro(geo, step)
    take, send = step == 1, fused and 1 <= step < geo.micro
    active = only_section(geo, geo.micro - step)
    exchange = Exchange(geo, at, at.slot_grad, active)
    exchange.greet()
    first = lax.axis_index("section") == 0
    across, across_out = Across(1, at.across_sems), Across(1, at.across_sems, 2)
    if take or send:
        across.greet()
    w_in, w_out = at.w_in_here, at.w_out_here

    def loads(e):
        return (
            pltpu.make_async_copy(at.w_out.at[e], w_out.at[e], at.load_sem.at[e, 1]),
            pltpu.make_async_copy(at.kept_slope.at[m, e], at.slope.at[e], at.load_sem.at[e, 2]),
            pltpu.make_async_copy(at.w_in.at[e], w_in.at[e], at.load_sem.at[e, 0]),
        )

    def saves(e, slot):
        return (
            pltpu.make_async_copy(at.rows.at[slot], at.kept_seen.at[m, e], at.save_sem.at[slot, 0]),
            pltpu.make_async_copy(at.wide.at[slot], at.kept_pre.at[m, e], at.save_sem.at[slot, 1]),
        )

    def expert(e, slot):
        for f in range(0, geo.hidden, tile):
            grad = mm(at.rows[slot], w_out[e, f : f + tile, :], (1, 1))
            value = (grad * at.slope[e, :, f : f + tile].astype(F32)).astype(BF16)
            at.wide[slot, :, f : f + tile] = value
            product = mm(value, w_in[e, :, f : f + tile], (1, 1))
            at.total[...] = product if f == 0 else at.total[...] + product

    def incoming_load():
        own = pltpu.make_async_copy(at.cotangent.at[m], at.incoming_here, at.incoming_sem)
        if step == 0:
            return [own], [own]
        if step == 1:
            return [], [own]
        return [pltpu.make_async_copy(at.received, at.incoming_here, at.incoming_sem)], [own]

    def of_sections(action):
        early, late = incoming_load()

        @pl.when(first)
        def _():
            for copy in early:
                getattr(copy, action)()

        @pl.when(jnp.logical_not(first))
        def _():
            for copy in late:
                getattr(copy, action)()

    def work():
        copies = Copies(at.sems)
        picked_load = copies.load(at.kept_picked.at[m], at.picked)
        aux_load = copies.load(at.kept_aux.at[m], at.aux)
        of_sections("start")
        start_loads(geo, loads)
        dense_loads = dense_backward_loads(geo, m, at, copies) if fused else None
        exchange.await_greetings(int(take or send))
        if take:
            across.send(at.sent, at.incoming_far)
            across.take(at.incoming_far)

            @pl.when(first)
            def _():
                at.incoming_here[...] = at.incoming_far[...]

        of_sections("wait")
        aux_load.wait()
        slot_grad = spread(at.incoming_here[...].astype(F32), at.aux[...], geo.slots)
        at.slot_grad[...] = slot_grad.reshape(at.slot_grad.shape)

        def opened():
            picked_load.wait()
            at.incoming[...] = at.incoming_here[...]
            at.gates[...] = gate_gradients(at.incoming_here[...].astype(F32), at.picked)

        run_experts(geo, exchange, at.rows, at.total, at.shared, loads, expert, saves, opened)
        first_slots, second_slots = slot_onehots(at.aux[...], geo.slots)
        home = at.home[...].reshape(geo.slots, geo.width)
        at.moe_grad[...] = mm((first_slots | second_slots).astype(BF16), home, (1, 0))
        if fused:
            dense_backward_part(geo, step, at, copies, dense_loads, lambda: None, across_out if send else None)
        if take:
            across.sent(at.sent, at.incoming_far)

    share_work(exchange, active, work)


def tile_of(hidden, limit):
    return limit if hidden % limit == 0 else hidden


def experts_scratch(geo, slope_slots):
    rows, local, width, hidden = geo.expert_rows, geo.local_experts, geo.width, geo.hidden
    steps = max(1, geo.cols - 1)
    one = pltpu.SemaphoreType.DMA
    two = pltpu.SemaphoreType.DMA((2,))
    unit = pltpu.SemaphoreType.DMA((geo.units,))
    return dict(
        inbox=pltpu.VMEM((geo.units, geo.cols, geo.rows, geo.main, width), BF16),
        arrived=pltpu.VMEM((geo.units, steps, geo.rows, geo.main, width), BF16),
        stage=pltpu.VMEM((geo.units, geo.rows, geo.main, width), BF16),
        home=pltpu.VMEM((geo.units, geo.rows, geo.main, width), BF16),
        picked=pltpu.VMEM((TOP, geo.length, width), BF16),
        aux=pltpu.VMEM((geo.length, 128), F32),
        rows=pltpu.VMEM((2, rows, width), BF16),
        wide=pltpu.VMEM((2, rows, hidden), BF16),
        slope=pltpu.VMEM((slope_slots, rows, hidden), BF16),
        w_in_here=pltpu.VMEM((local, width, hidden), BF16),
        w_out_here=pltpu.VMEM((local, hidden, width), BF16),
        total=pltpu.VMEM((rows, width), F32),
        shared=pltpu.VMEM((geo.sources * geo.main if geo.share else 16, width), F32),
        via_x=pltpu.VMEM((geo.units, geo.cores, geo.main, width), BF16),
        via_z=pltpu.VMEM((geo.units, geo.cores, geo.main, width), BF16),
        via_y=pltpu.VMEM((geo.units, steps, geo.cores, geo.main, width), BF16),
        via_part=pltpu.VMEM((geo.units, geo.cols, geo.cores, geo.main, width), BF16),
        via_sum=pltpu.VMEM((geo.units, steps, geo.cores, geo.main, width), BF16),
        via_total=pltpu.VMEM((geo.units, geo.cores, geo.main, width), BF16),
        via_home=pltpu.VMEM((geo.units, geo.cores, geo.main, width), BF16),
        via_sems=pltpu.SemaphoreType.DMA((6, geo.units, geo.cols)),
        core_sems=pltpu.SemaphoreType.DMA((4, geo.units, geo.cores)),
        own_sem=unit, pass_send=unit, pass_recv=unit, into_recv=unit, via_x_recv=unit, via_part_recv=unit,
        in_send=two, out_send=two, home_send=two, home_recv=two, home_in_recv=one, via_send=one, via_part_send=one,
        done=one,
        in_recv=pltpu.SemaphoreType.DMA((geo.units, geo.chips)),
        out_recv=pltpu.SemaphoreType.DMA((geo.units, 2)),
        load_sem=pltpu.SemaphoreType.DMA((local, 3)),
        save_sem=pltpu.SemaphoreType.DMA((2, 3)),
        sems=pltpu.SemaphoreType.DMA((6,)),
        across_sems=pltpu.SemaphoreType.DMA((4,)),
    )


def experts_cost(geo):
    weights = geo.local_experts * geo.hidden * geo.width
    return (4 * geo.expert_rows * weights, 4 * weights)


def forward_scratch(geo):
    scratch = experts_scratch(geo, 2)
    scratch["residual"] = pltpu.VMEM((geo.length, geo.width), F32)
    scratch["result"] = pltpu.VMEM((geo.length, geo.width), BF16)
    return scratch


def forward_tick(geo, tick, given, state, received):
    micro, length, width = geo.micro, geo.length, geo.width
    rows, local, hidden = geo.expert_rows, geo.local_experts, geo.hidden
    dense, scratch = dense_forward_scratch(geo, tick), forward_scratch(geo)
    fused = fits(dense, scratch)
    near, kept = {}, {}
    held = dict(w_in=given["w_in"], w_out=given["w_out"])
    if fused:
        near, dense_held, kept = dense_forward_refs(geo, tick, given, state, received)
        held.update(dense_held)
        scratch.update(dense)
    else:
        held["slot_rows"] = dense_forward(geo, tick, given, state, received)
        held.update(kept_aux=state["kept_aux"], kept_residual=state["kept_residual"])
    kept.update(
        out=((micro, length, width), BF16),
        kept_picked=((micro, TOP, length, width), BF16),
        kept_rows=((micro, local, rows, width), BF16),
        kept_hidden=((micro, local, rows, hidden), BF16),
        kept_slope=((micro, local, rows, hidden), BF16),
    )
    results = launch(
        partial(forward_body, geo, tick, tile_of(hidden, 768), fused),
        near=near,
        held=held,
        outs=dict(received_out=pltpu.HBM((length, width), BF16)) if 1 <= tick < micro else {},
        kept=kept,
        state=state,
        scratch=scratch,
        cost=experts_cost(geo),
        collective_id=3 + tick,
        has_side_effects=True,
    )
    return results.get("received_out")


def backward_step(geo, step, given, state, sent, received):
    micro, length, width = geo.micro, geo.length, geo.width
    rows, local, hidden = geo.expert_rows, geo.local_experts, geo.hidden
    scratch = experts_scratch(geo, local)
    scratch["slot_grad"] = pltpu.VMEM((geo.units, geo.rows, geo.main, width), BF16)
    scratch["incoming_here"] = pltpu.VMEM((length, width), BF16)
    scratch["incoming_sem"] = pltpu.SemaphoreType.DMA
    held = dict(
        cotangent=given["cotangent"], w_in=given["w_in"], w_out=given["w_out"], kept_aux=state["kept_aux"],
        kept_picked=state["kept_picked"], kept_slope=state["kept_slope"],
    )
    if step == 1:
        held["sent"] = sent
        scratch["incoming_far"] = pltpu.VMEM((length, width), BF16)
    elif step:
        held["received"] = received
    between = dict(
        moe_grad=shape((length, width), F32), gates=shape((length, 128), F32), incoming=shape((length, width), BF16)
    )
    dense = dense_backward_scratch(geo)
    near, outs, kept = {}, between, {}
    between_scratch = {name: pltpu.VMEM(one.shape, one.dtype) for name, one in between.items()}
    fused = fits(scratch, dense, between_scratch)
    if fused:
        near, dense_held, outs, kept = dense_backward_refs(geo, step, given, state)
        held.update(dense_held)
        scratch.update(dense)
        scratch.update(between_scratch)
    kept.update(
        kept_seen=((micro, local, rows, width), BF16),
        kept_pre=((micro, local, rows, hidden), BF16),
    )
    results = launch(
        partial(backward_body, geo, step, tile_of(hidden, 768), fused),
        near=near,
        held=held,
        outs=outs,
        kept=kept,
        state=state,
        scratch=scratch,
        cost=experts_cost(geo),
        collective_id=4 + micro + step,
        has_side_effects=True,
    )
    return results if fused else dense_backward(geo, step, results, given, state)


class Shards:
    def __init__(self, geo):
        self.cores, self.chips, self.cols = geo.cores, geo.chips, geo.cols
        r, self.c = lax.axis_index("row"), lax.axis_index("col")
        self.z, self.core = r // self.cores, r % self.cores

    def chip(self, k):
        return (self.z + k + self.chips) % self.chips

    def col(self, j):
        return (self.c + j + self.cols) % self.cols

    def row(self, z, other=0):
        return z * self.cores + (self.core + other) % self.cores

    def greet(self):
        barrier = pltpu.get_barrier_semaphore()
        targets = [{"row": self.row(self.chip(k))} for k in range(1, self.chips)]
        targets += [{"col": self.col(j)} for j in range(1, self.cols)]
        targets += [{"row": self.row(self.z, 1)}] * (self.cores - 1)
        for target in targets:
            pl.semaphore_signal(barrier, inc=1, device_id=target, device_id_type=MESH)
        self.greeted = len(targets)

    def await_greetings(self):
        pl.semaphore_wait(pltpu.get_barrier_semaphore(), self.greeted)


def gather_kernel(geo, pieces, qkv, out, router, gain_one, gain_two, terms, all_ref, small, own_sems, z_send, z_recv,
                  y_send, y_recv, core_send, core_recv):
    at = Shards(geo)
    at.greet()
    share, total = all_ref.shape[2:]
    narrow, wide = out.shape[1], qkv.shape[1]
    mine = all_ref.at[at.row(at.z), at.c]
    copies = Copies(own_sems)
    copies.save(qkv, mine.at[:, pl.ds(0, wide)])
    copies.save(out, mine.at[:, pl.ds(wide, narrow)])
    experts_all, count = router.shape[0], terms.shape[1]

    def unit(dims, shift=0):
        return (iota(dims, 0) + shift == iota(dims, 1)).astype(BF16)

    columns = mm(router[...], unit((experts_all, 128)), (0, 0))
    long_terms = mm(terms[...], unit((count, share)), (1, 0)).astype(BF16)
    for k, row in enumerate((gain_one[...], gain_two[...], long_terms)):
        columns = columns + mm(row, unit((1, 128), experts_all + k), (0, 0))
    small[...] = columns.astype(BF16)
    copies.save(small, mine.at[:, pl.ds(wide + narrow, 128)])
    copies.wait()
    at.await_greetings()
    step = total // pieces

    def block(k, j, h):
        return all_ref.at[at.row(at.chip(-k)), at.col(-j), :, pl.ds(h * step, step)]

    def pass_z(k, h):
        own = block(0, 0, h)
        remote(own, own, z_send, z_recv.at[h, k - 1], {"row": at.row(at.chip(k))}).start()

    def pass_y(k, h):
        for j in range(1, at.cols):
            one = block(k, 0, h)
            remote(one, one, y_send, y_recv.at[h, k, j - 1], {"col": at.col(j)}).start()

    def pass_core(k, j, h):
        if at.cores > 1:
            one = block(k, j, h)
            remote(one, one, core_send, core_recv, {"row": at.row(at.z, 1)}).start()

    def came(one, sem):
        remote(one, one, core_send, sem, {"row": at.row(at.z, 1)}).wait_recv()

    def left(one, sem):
        remote(one, one, sem, core_recv, {"row": at.row(at.z, 1)}).wait_send()

    def take_y(h):
        for k in range(at.chips):
            for j in range(1, at.cols):
                came(block(k, j, h), y_recv.at[h, k, j - 1])
                pass_core(k, j, h)

    for k in range(1, at.chips):
        pass_z(k, 0)
    for h in range(pieces):
        pass_y(0, h)
    for h in range(pieces):
        pass_core(0, 0, h)
    for h in range(pieces):
        for k in range(1, at.chips):
            came(block(k, 0, h), z_recv.at[h, k - 1])
            if h + 1 < pieces:
                pass_z(k, h + 1)
            pass_y(k, h)
            pass_core(k, 0, h)
        if h:
            take_y(h - 1)
    take_y(pieces - 1)
    if at.cores > 1:
        came(all_ref.at[pl.ds(0, at.chips)], core_recv)
        left(all_ref.at[pl.ds(0, at.chips)], core_send)
    if at.chips > 1:
        left(all_ref.at[pl.ds(0, at.chips - 1), 0], z_send)
    if at.cols > 1:
        left(all_ref.at[pl.ds(0, at.chips), pl.ds(0, at.cols - 1)], y_send)


def gather_shards(geo, qkv, out, router, gain_one, gain_two, terms):
    share, total = qkv.shape[0], qkv.shape[1] + out.shape[1] + 128
    pieces = 5 if total % 640 == 0 else 1
    one = pltpu.SemaphoreType.DMA
    return pl.pallas_call(
        partial(gather_kernel, geo, pieces),
        out_shape=pltpu.HBM((geo.rows, geo.cols, share, total), BF16),
        in_specs=[hbm_spec()] * 2 + [vmem_spec()] * 4,
        out_specs=hbm_spec(),
        scratch_shapes=[
            pltpu.VMEM((share, 128), BF16),
            pltpu.SemaphoreType.DMA((3,)),
            one, pltpu.SemaphoreType.DMA((pieces, max(1, geo.chips - 1))),
            one, pltpu.SemaphoreType.DMA((pieces, geo.chips, max(1, geo.cols - 1))),
            one, one,
        ],
        compiler_params=pltpu.CompilerParams(collective_id=1, has_side_effects=True),
    )(in_hbm(qkv), in_hbm(out), router, gain_one, gain_two, terms)


def reduce_part(shards, refs):
    at = shards
    part_ref, out_ref = refs.part, refs.shard
    from_core, from_col, from_chip, pair, column = refs.from_core, refs.from_col, refs.from_chip, refs.pair, refs.column
    core_send, core_recv, y_send, y_recv, z_send, z_recv = (
        refs.core_send, refs.core_recv, refs.y_send, refs.y_recv, refs.z_send, refs.z_recv
    )
    order = list(range(1, at.chips)) + [0]
    started = []

    def start(copy):
        copy.start()
        started.append(copy)

    def to_core(k):
        return remote(
            part_ref.at[at.row(at.chip(k), 1)], from_core.at[k], core_send.at[k, 0], core_recv.at[k, 0],
            {"row": at.row(at.z, 1)},
        )

    def to_col(k, j):
        return remote(
            pair.at[k, at.col(j)], from_col.at[k, j - 1], y_send.at[k, j - 1], y_recv.at[k, j - 1],
            {"col": at.col(j)},
        )

    def to_chip(k):
        return remote(
            column.at[k - 1], from_chip.at[k - 1], z_send.at[k - 1], z_recv.at[k - 1],
            {"row": at.row(at.chip(k))},
        )

    if at.cores > 1:
        for k in order:
            start(to_core(k))

    def sum_cores(k):
        total = part_ref[at.row(at.chip(k))].astype(F32)
        if at.cores > 1:
            to_core(k).wait_recv()
            total = total + from_core[k].astype(F32)
        pair[k] = total.astype(BF16)
        for j in range(1, at.cols):
            start(to_col(k, j))

    def sum_cols(k):
        total = pair[k, at.c].astype(F32)
        for j in range(1, at.cols):
            to_col(k, j).wait_recv()
            total = total + from_col[k, j - 1].astype(F32)
        if k:
            column[k - 1] = total.astype(BF16)
            start(to_chip(k))
        else:
            out_ref[...] = total

    for step, k in enumerate(order):
        sum_cores(k)
        if step:
            sum_cols(order[step - 1])
    sum_cols(order[-1])
    for k in range(1, at.chips):
        to_chip(k).wait_recv()
        out_ref[...] += from_chip[k - 1].astype(F32)
    for copy in started:
        copy.wait_send()


def reduce_scratch(geo, share, width):
    chips, steps, far = geo.chips, max(1, geo.cols - 1), max(1, geo.chips - 1)
    z = pltpu.SemaphoreType.DMA((far,))
    y = pltpu.SemaphoreType.DMA((chips, steps))
    core = pltpu.SemaphoreType.DMA((chips, geo.cols))
    return dict(
        from_core=pltpu.VMEM((chips, geo.cols, share, width), BF16),
        from_col=pltpu.VMEM((chips, steps, share, width), BF16),
        from_chip=pltpu.VMEM((far, share, width), BF16),
        pair=pltpu.VMEM((chips, geo.cols, share, width), BF16),
        column=pltpu.VMEM((far, share, width), BF16),
        core_send=core, core_recv=core, y_send=y, y_recv=y, z_send=z, z_recv=z,
    )


def expert_weights_kernel(experts_all, rows, pre, hidden, seen, packed, in_grad, out_grad, qkv, out, router, one, two,
                          terms):
    def product(left, right):
        left, right = (ref[:, 0].reshape(-1, ref.shape[-1]) for ref in (left, right))
        return mm(left, right, (0, 0))

    in_grad[0, 0] = product(rows, pre)
    out_grad[0, 0] = product(hidden, seen)

    @pl.when((pl.program_id(0) == 0) & (pl.program_id(1) == 0))
    def _():
        wide, narrow = qkv.shape[2], out.shape[2]
        qkv[0] = packed[:, :wide]
        out[0] = packed[:, wide : wide + narrow]
        small = packed[:, wide + narrow :]
        dims = (experts_all + 8, 128)
        pick = (iota(dims, 0) == iota(dims, 1)).astype(F32)
        lines = lax.dot_general(
            pick, small, (((1,), (1,)), ((), ())), precision=lax.Precision.HIGHEST, preferred_element_type=F32
        )
        router[0] = lines[:experts_all]
        one[...] = lines[experts_all : experts_all + 1]
        two[...] = lines[experts_all + 1 : experts_all + 2]
        terms[...] = lines[experts_all + 2 : experts_all + 3, : terms.shape[1]]


def expert_weights(geo, state, packed, terms):
    micro, local, count, width, hidden = geo.micro, geo.local_experts, geo.expert_rows, geo.width, geo.hidden
    tile = tile_of(hidden, 768)
    narrow = pl.BlockSpec((micro, 1, count, width), lambda e, f: (0, e, 0, 0))
    wide = pl.BlockSpec((micro, 1, count, tile), lambda e, f: (0, e, 0, f))
    flops = 4 * micro * local * count * width * hidden
    share = packed.shape[0]
    small = [(1, share, 3 * width), (1, share, width), (1, geo.experts_all, share), (1, share), (1, share), (1, terms)]

    def whole(dims):
        return pl.BlockSpec(dims, lambda e, f: (0,) * len(dims))

    return pl.pallas_call(
        partial(expert_weights_kernel, geo.experts_all),
        out_shape=[shape((1, local, width, hidden), F32), shape((1, local, hidden, width), F32)]
        + [shape(dims, F32) for dims in small],
        grid=(local, hidden // tile),
        in_specs=[narrow, wide, wide, narrow, whole(packed.shape)],
        out_specs=[
            pl.BlockSpec((1, 1, width, tile), lambda e, f: (0, e, 0, f)),
            pl.BlockSpec((1, 1, tile, width), lambda e, f: (0, e, f, 0)),
        ]
        + [whole(dims) for dims in small],
        compiler_params=pltpu.CompilerParams(vmem_limit_bytes=48 * MIB),
        cost_estimate=pl.CostEstimate(
            flops=flops, bytes_accessed=8 * local * hidden * width, transcendentals=0
        ),
    )(*(in_hbm(state[name]) for name in ("kept_rows", "kept_pre", "kept_hidden", "kept_seen")), packed)


def norm_backward(values, gain, grad):
    factor = norm_factor(values)
    unit = values * factor
    weighted = grad * gain
    inner = jnp.mean(weighted * unit, axis=-1, keepdims=True)
    return factor * (weighted - unit * inner), jnp.sum(grad * unit, axis=0, keepdims=True)


def dense_backward_loads(geo, m, at, copies):
    width = geo.width
    return dict(
        rest=copies.load(at.packed.at[:, pl.ds(3 * width, width + 128)], at.rest_w),
        gains=copies.load(at.gains, at.gains_here),
        residual=copies.load(at.kept_residual.at[m], at.residual),
        qkv=copies.load(at.kept_qkv.at[m], at.qkv),
        prob=copies.load(at.kept_prob.at[m], at.prob),
        stream=copies.load(at.kept_stream.at[m], at.stream),
        qkv_w=copies.load(at.packed.at[:, pl.ds(0, 3 * width)], at.qkv_w),
    )


def dense_backward_part(geo, step, at, copies, loads, enter, across):
    length, width, heads = geo.length, geo.width, geo.heads
    size = width // heads
    per = 128 // size
    m = backward_micro(geo, step)
    send = across is not None
    aux = at.aux[...]
    slope = aux[:, 0:1] * aux[:, 1:2] * (at.gates[:, 0:1] - at.gates[:, 1:2])
    expert_at = iota((length, 128), 1).astype(F32)
    logit_grad = (
        jnp.where(as_column(at.routes[0, m, 0:1, :].astype(F32)) == expert_at, slope, 0.0)
        - jnp.where(as_column(at.routes[0, m, 1:2, :].astype(F32)) == expert_at, slope, 0.0)
    ).astype(BF16)
    at.logit[...] = logit_grad
    copies.save(at.logit, at.kept_logit.at[m])
    loads["rest"].wait()
    moe_grad = at.moe_grad[...] + mm(logit_grad, at.rest_w[:, width:], (1, 1))
    loads["residual"].wait()
    loads["gains"].wait()
    part, gain_two = norm_backward(at.residual[...], at.gains_here[1:2, :], moe_grad)
    residual_grad = at.incoming[...].astype(F32) + part
    at.branch[...] = residual_grad.astype(BF16)
    copies.save(at.branch, at.kept_branch.at[m])
    at.context_grad[...] = mm(at.branch[...], at.rest_w[:, :width], (1, 1)).astype(BF16)
    which = iota((length, 128), 1) // size
    head_row = iota((128, length), 0) // size
    scale = 1.0 / math.sqrt(size)
    zero = jnp.zeros((length, 128), BF16)
    loads["qkv"].wait()
    loads["prob"].wait()
    at.sums[...] = jnp.zeros(at.sums.shape, F32)
    for j in range(width // 128):
        places = [slice(base * width + 128 * j, base * width + 128 * (j + 1)) for base in range(3)]
        queries, keys, values = (at.qkv[:, place] for place in places)
        grad = at.context_grad[:, places[0]]
        turned_keys = keys.astype(F32).T
        totals = [jnp.zeros(dims, F32) for dims in ((128, length), (length, 128), (length, 128))]
        for part_at in range(per):
            h = j * per + part_at
            own = which == part_at
            own_grad = jnp.where(own, grad, zero)
            prob = at.prob[h]
            prob_grad = mm(values, own_grad, (1, 1))
            weighted = prob.astype(F32)
            shift = jnp.sum(weighted * prob_grad, axis=0, keepdims=True)
            score_grad = (weighted * (prob_grad - shift)).astype(BF16)
            at.sums[h : h + 1, :] = diagonal_sums(score_grad.astype(F32))
            own_keys = jnp.where(head_row == part_at, turned_keys, 0.0).astype(BF16)
            totals[0] = totals[0] + mm(own_keys, score_grad, (1, 0))
            totals[1] = totals[1] + mm(score_grad, jnp.where(own, queries, zero), (1, 0))
            totals[2] = totals[2] + mm(prob, own_grad, (1, 0))
        at.qkv_grad[:, places[0]] = (totals[0].T * scale).astype(BF16)
        at.qkv_grad[:, places[1]] = (totals[1] * scale).astype(BF16)
        at.qkv_grad[:, places[2]] = totals[2].astype(BF16)
    copies.save(at.qkv_grad, at.kept_qkv_grad.at[m])
    copies.save(at.sums, at.kept_sums.at[m])
    loads["qkv_w"].wait()
    normed_grad = mm(at.qkv_grad[...], at.qkv_w[...], (1, 1))
    loads["stream"].wait()
    part, gain_one = norm_backward(at.stream[...].astype(F32), at.gains_here[0:1, :], normed_grad)
    at.gain_parts[...] = jnp.zeros(at.gain_parts.shape, F32)
    at.gain_parts[0:1, :] = gain_one
    at.gain_parts[1:2, :] = gain_two
    copies.save(at.gain_parts, at.kept_gains.at[m])
    in_grad = residual_grad + part
    at.in_grad_here[...] = in_grad
    copies.save(at.in_grad_here, at.in_grad.at[m])
    if step < geo.micro:
        at.sent_here[...] = in_grad.astype(BF16)
    if send:
        enter()
        across.send(at.sent_here, at.received_out)
    elif step < geo.micro:
        copies.save(at.sent_here, at.sent_out)
    copies.wait()
    if send:
        across.take(at.received_out)
        across.sent(at.sent_here, at.received_out)


def dense_backward_body(geo, step, at):
    send = 1 <= step < geo.micro
    across = Across(1, at.across_sems) if send else None
    if send:
        across.greet()

    def enter():
        pl.semaphore_wait(pltpu.get_barrier_semaphore(), 1)

    m = backward_micro(geo, step)
    copies = Copies(at.sems)
    aux_load = copies.load(at.kept_aux.at[m], at.aux)
    loads = dense_backward_loads(geo, m, at, copies)
    aux_load.wait()
    dense_backward_part(geo, step, at, copies, loads, enter, across)


def dense_backward_scratch(geo):
    length, width, heads = geo.length, geo.width, geo.heads
    return dict(
        aux=pltpu.VMEM((length, 128), F32),
        rest_w=pltpu.VMEM((width, width + 128), BF16),
        qkv_w=pltpu.VMEM((width, 3 * width), BF16),
        residual=pltpu.VMEM((length, width), F32),
        qkv=pltpu.VMEM((length, 3 * width), BF16),
        prob=pltpu.VMEM((heads, length, length), BF16),
        stream=pltpu.VMEM((length, width), BF16),
        logit=pltpu.VMEM((length, 128), BF16),
        branch=pltpu.VMEM((length, width), BF16),
        context_grad=pltpu.VMEM((length, width), BF16),
        qkv_grad=pltpu.VMEM((length, 3 * width), BF16),
        sums=pltpu.VMEM((geo.tall, length), F32),
        gain_parts=pltpu.VMEM((8, width), F32),
        in_grad_here=pltpu.VMEM((length, width), F32),
        gains_here=pltpu.VMEM((8, width), F32),
        sent_here=pltpu.VMEM((length, width), BF16),
        sems=pltpu.SemaphoreType.DMA((20,)),
        across_sems=pltpu.SemaphoreType.DMA((4,)),
    )


def dense_backward_refs(geo, step, given, state):
    micro, length, width = geo.micro, geo.length, geo.width
    outs = {}
    if 1 <= step < micro:
        outs["received_out"] = pltpu.HBM((length, width), BF16)
    elif step < micro:
        outs["sent_out"] = pltpu.HBM((length, width), BF16)
    names = ("kept_aux", "kept_residual", "kept_qkv", "kept_prob", "kept_stream")
    held = dict({name: state[name] for name in names}, packed=given["packed"], gains=given["gains"])
    kept = dict(
        in_grad=((micro, length, width), F32),
        kept_branch=((micro, length, width), BF16),
        kept_qkv_grad=((micro, length, 3 * width), BF16),
        kept_logit=((micro, length, 128), BF16),
        kept_gains=((micro, 8, width), F32),
        kept_sums=((micro, geo.tall, length), F32),
    )
    return dict(routes=given["routes"]), held, outs, kept


def dense_backward(geo, step, near, given, state):
    more, held, outs, kept = dense_backward_refs(geo, step, given, state)
    params = {}
    if 1 <= step < geo.micro:
        params = dict(collective_id=5 + 2 * geo.micro + step, has_side_effects=True)
    return launch(
        partial(where_active, only_section(geo, geo.micro - step), partial(dense_backward_body, geo, step)),
        near=dict(near, **more),
        held=held,
        outs=outs,
        kept=kept,
        state=state,
        scratch=dense_backward_scratch(geo),
        cost=(3_000_000_000, 14_000_000),
        **params,
    )


DENSE_GRADS = ("normed", "qkv_grad", "context", "branch", "moe_in", "logit")


def dense_weights_body(geo, at):
    width = geo.width
    copies = Copies(at.sems)
    loads = {}
    for name in DENSE_GRADS + ("gains", "sums"):
        loads[name] = copies.load(getattr(at, "kept_" + name), getattr(at, name))

    def product(left, right):
        left, right = (ref[...].reshape(-1, ref.shape[-1]) for ref in (left, right))
        return mm(left, right, (0, 0))

    def ready(*names):
        for name in names:
            loads[name].wait()

    def put(places, block):
        block = block.astype(BF16)
        if len(at.part.shape) == 4:
            at.part[:, :, :, places] = block.reshape(at.part.shape[:3] + block.shape[1:])
        else:
            at.part[:, places] = block

    ready("normed", "qkv_grad")
    normed = at.normed[...].reshape(-1, width)
    for j in range(0, 3 * width, width):
        grad = at.qkv_grad[:, :, j : j + width].reshape(-1, width)
        put(slice(j, j + width), mm(normed, grad, (0, 0)))
    ready("context", "branch")
    put(slice(3 * width, 4 * width), product(at.context, at.branch))
    ready("moe_in", "logit", "gains", "sums")
    small = product(at.moe_in, at.logit)
    by_term = lax.dot_general(
        jnp.sum(at.sums[...], axis=0), at.spread[...].astype(F32), (((1,), (1,)), ((), ())),
        precision=lax.Precision.HIGHEST, preferred_element_type=F32,
    )
    bias_row = jnp.sum(by_term[: geo.heads] * at.head_pick[...], axis=0, keepdims=True)
    gain_rows = jnp.sum(at.gains[...], axis=0)
    place = iota((128, width), 0)
    rows = jnp.zeros((128, width), F32)
    for k, row in enumerate((gain_rows[0:1], gain_rows[1:2], bias_row)):
        rows = jnp.where(place == geo.experts_all + k, row, rows)
    put(slice(4 * width, None), small + rows.T)


def reduce_body(geo, at):
    shards = Shards(geo)
    shards.greet()
    dense_weights_body(geo, at)
    shards.await_greetings()
    reduce_part(shards, at)


def dense_weights(geo, head_pick, spread_table, state):
    held = {"kept_" + name: state["kept_" + name] for name in DENSE_GRADS + ("gains", "sums")}
    scratch = {name: pltpu.VMEM(held["kept_" + name].shape, BF16) for name in DENSE_GRADS}
    scratch.update(
        sems=pltpu.SemaphoreType.DMA((len(DENSE_GRADS) + 2,)),
        gains=pltpu.VMEM(state["kept_gains"].shape, F32), sums=pltpu.VMEM(state["kept_sums"].shape, F32),
    )
    share, total = geo.width // geo.sources, 4 * geo.width + 128
    parts = (geo.rows, geo.cols, share, total)
    fused = share % 16 == 0
    outs = dict(shard=shape((share, total), F32)) if fused else dict(part=shape((geo.width, total), BF16))
    params = {}
    if fused:
        scratch.update(reduce_scratch(geo, share, total), part=pltpu.VMEM(parts, BF16))
        params = dict(collective_id=2, has_side_effects=True)
    results = launch(
        partial(reduce_body if fused else dense_weights_body, geo),
        near=dict(head_pick=head_pick, spread=spread_table),
        held=held,
        outs=outs,
        scratch=scratch,
        spare=24,
        cost=(3_000_000_000, 10_000_000),
        **params,
    )
    if fused:
        return results["shard"]

    def body(at):
        shards = Shards(geo)
        shards.greet()
        shards.await_greetings()
        reduce_part(shards, at)

    return launch(
        body,
        near=dict(part=results["part"].reshape(parts)),
        outs=dict(shard=shape((share, total), F32)),
        scratch=reduce_scratch(geo, share, total),
        collective_id=2,
        has_side_effects=True,
    )["shard"]


def on_device(
    inputs, cotangent, segments, routes, order, attn_gain, qkv_weight, position_bias, out_weight, moe_gain,
    router_weight, expert_in, expert_out,
):
    micro, length, width = inputs.shape
    local_experts, hidden = expert_in.shape[1], expert_in.shape[3]
    experts_all = router_weight.shape[2]
    row_count, col_count = lax.axis_size("row"), lax.axis_size("col")
    devices = row_count * col_count
    share = width // devices
    terms = position_bias.shape[1]
    heads = terms * devices // DISTANCE_BUCKETS
    geo = Geometry(micro, length, width, heads, experts_all, local_experts, hidden, row_count, col_count)
    packed = gather_shards(
        geo, qkv_weight[0], out_weight[0], router_weight[0].T, attn_gain, moe_gain, position_bias
    ).reshape(width, -1)
    indicator = buckets(length)
    row_at = np.arange(width)
    term_at = np.where(row_at % share < terms, row_at // share * terms + row_at % share, -1)
    head_pick = jnp.asarray((term_at % heads == np.arange(heads)[:, None]) & (term_at >= 0), F32)
    spread_table = jnp.asarray(indicator[np.maximum(term_at, 0) // heads], BF16)
    prepared = launch(
        partial(prepare, experts_all),
        near=dict(head_pick=head_pick, spread=spread_table),
        held=dict(packed=packed),
        outs=dict(gains=pltpu.HBM((8, width), F32), bias=pltpu.HBM((heads, length, length), BF16)),
        scratch=dict(
            small=pltpu.VMEM((width, 128), BF16), gains_here=pltpu.VMEM((8, width), F32),
            bias_here=pltpu.VMEM((heads, length, length), BF16), sems=pltpu.SemaphoreType.DMA((3,)),
        ),
        cost=(50_000_000, 6_000_000),
    )
    given = dict(
        prepared, packed=packed, inputs=inputs, cotangent=cotangent, w_in=expert_in[0], w_out=expert_out[0],
        segments=segments, order=order, routes=jnp.swapaxes(routes, 2, 3),
        bases=jnp.asarray(geo.bases()),
    )
    state = {}
    received = None
    for tick in range(micro + 1):
        received = forward_tick(geo, tick, given, state, received)
    sent = received = None
    for step in range(micro + 1):
        passed = backward_step(geo, step, given, state, sent, received)
        sent, received = passed.get("sent_out"), passed.get("received_out")
    packed = dense_weights(geo, head_pick, spread_table, state)
    expert_in_grad, expert_out_grad, qkv, out, router, gain_one, gain_two, bias = expert_weights(
        geo, state, packed, terms
    )
    return (
        state["out"][None], state["in_grad"][None], gain_one, qkv, bias, out, gain_two,
        jnp.swapaxes(router, 1, 2), expert_in_grad,
        expert_out_grad,
    )


def solution(mesh):
    tokens = ("row", "col")
    return jax.shard_map(
        on_device,
        mesh=mesh,
        in_specs=(
            P(None, tokens, None),
            P(None, tokens, None),
            P(None, tokens),
            P("section", None, tokens, None),
            P("section", None, tokens, None),
            P("section", tokens),
            P("section", tokens, None),
            P("section", tokens),
            P("section", tokens, None),
            P("section", tokens),
            P("section", tokens, None),
            P("section", "row", None, "col"),
            P("section", "row", "col", None),
        ),
        out_specs=(
            P("section", None, tokens, None),
            P("section", None, tokens, None),
            P("section", tokens),
            P("section", tokens, None),
            P("section", tokens),
            P("section", tokens, None),
            P("section", tokens),
            P("section", tokens, None),
            P("section", "row", None, "col"),
            P("section", "row", "col", None),
        ),
        check_vma=False,
    )
```

```python
from functools import partial
import math
from types import SimpleNamespace

import jax
import jax.numpy as jnp
import numpy as np
from jax import lax
from jax.experimental import pallas as pl
from jax.experimental.pallas import tpu as pltpu
from jax.sharding import PartitionSpec as P

TOP = 2
DISTANCE_BUCKETS = 32
MAX_DIST = 128
EPS = 1e-06
MESH = pl.DeviceIdType.MESH
F32 = jnp.float32
BF16 = jnp.bfloat16
MIB = 1 << 20


class Geometry:
    def __init__(self, micro, length, width, heads, experts_all, local_experts, hidden, row_count, col_count):
        self.micro, self.length, self.width, self.heads, self.hidden = micro, length, width, heads, hidden
        self.tall = -(-heads // 8) * 8
        self.capacity = max(2, (5 * length * TOP + 4 * experts_all - 1) // (4 * experts_all))
        self.local_experts = local_experts
        self.experts_all = experts_all
        self.rows, self.cols = row_count, col_count
        self.cores = 2 if row_count % 2 == 0 else 1
        self.chips = row_count // self.cores
        main = self.capacity // 16 * 16
        rest = self.capacity - main
        self.share = main // local_experts if 0 < rest <= main // local_experts else 0
        if rest and not self.share:
            main += 16
        self.main = main
        self.first = 1 if self.share else 0
        self.units = local_experts + self.first
        self.slots = row_count * self.units * main
        self.sources = row_count * col_count
        self.expert_rows = self.sources * (main + self.share)

    def bases(self):
        expert = np.arange(self.experts_all)
        owner, local = expert // self.local_experts, expert % self.local_experts
        main = ((self.first + local) * self.rows + owner) * self.main
        tail = owner * self.main + local * self.share
        both = np.stack([main, tail]).astype(np.float32)
        return np.pad(both, ((0, 0), (0, 128 - self.experts_all)))


def buckets(length):
    distance = np.arange(length)
    bucket = np.zeros(length, np.int64)
    half = DISTANCE_BUCKETS // 2
    for level in range(1, DISTANCE_BUCKETS):
        if level < half:
            limit = level
        else:
            limit = int(math.ceil(half * (MAX_DIST / half) ** ((level - half) / half)))
        bucket += distance >= limit
    return (np.arange(DISTANCE_BUCKETS)[:, None] == bucket[None, :]).astype(np.float32)


def mm(left, right, contract):
    return lax.dot_general(
        left, right, (((contract[0],), (contract[1],)), ((), ())), preferred_element_type=F32
    )


def iota(shape, axis):
    return lax.broadcasted_iota(jnp.int32, shape, axis)


def norm_factor(values):
    return lax.rsqrt(jnp.mean(values * values, axis=-1, keepdims=True) + EPS)


def gelu_pair(x):
    density = jnp.exp(-0.5 * x * x)
    t = 1.0 / (1.0 + (0.3275911 * math.sqrt(0.5)) * jnp.abs(x))
    poly = 0.5 * 1.061405429
    for coefficient in (-1.453152027, 1.421413741, -0.284496736, 0.254829592):
        poly = poly * t + 0.5 * coefficient
    beyond = poly * t * density
    cdf = jnp.where(x >= 0, 1.0 - beyond, beyond)
    return x * cdf, cdf + x * density * (1.0 / math.sqrt(2.0 * math.pi))


def slot_onehots(aux, slots):
    positions = iota((aux.shape[0], slots), 1).astype(F32)
    return [(aux[:, 2 + c : 3 + c] == positions) for c in range(TOP)]


def vmem_grant(scratch, spare):
    held = 0
    for ref in scratch:
        if getattr(ref, "memory_space", None) == pltpu.VMEM:
            held += math.prod(ref.shape) * jnp.dtype(ref.dtype).itemsize
    return -(-held // MIB) + spare


def fits(*scratches):
    return vmem_grant([ref for scratch in scratches for ref in scratch.values()], 11) <= 62


def vmem_spec():
    return pl.BlockSpec(memory_space=pltpu.VMEM)


def hbm_spec():
    return pl.BlockSpec(memory_space=pltpu.HBM)


def in_hbm(array):
    return pltpu.with_memory_space_constraint(array, pltpu.HBM)


def shape(dims, kind):
    return jax.ShapeDtypeStruct(dims, kind)


def launch(body, near=None, held=None, outs=None, kept=None, state=None, scratch=None, spare=10, cost=None, **params):
    near, held, outs, kept, scratch = (dict(part or {}) for part in (near, held, outs, kept, scratch))
    state = {} if state is None else state
    old = [name for name in kept if name in state]
    names_in, names_out = list(near) + list(held), list(outs) + list(kept)

    def kernel(*refs):
        refs = list(refs)
        given, refs = refs[: len(names_in)], refs[len(names_in) + len(old) :]
        body(SimpleNamespace(**dict(zip(names_in + names_out + list(scratch), given + refs))))

    out_shapes = list(outs.values()) + [pltpu.HBM(dims, kind) for dims, kind in kept.values()]
    plain = [isinstance(out, jax.ShapeDtypeStruct) for out in out_shapes]
    estimate = {}
    if cost is not None:
        estimate["cost_estimate"] = pl.CostEstimate(flops=cost[0], bytes_accessed=cost[1], transcendentals=0)
    results = pl.pallas_call(
        kernel,
        out_shape=out_shapes,
        in_specs=[vmem_spec()] * len(near) + [hbm_spec()] * (len(held) + len(old)),
        out_specs=[vmem_spec() if near_by else hbm_spec() for near_by in plain],
        scratch_shapes=list(scratch.values()),
        input_output_aliases={len(names_in) + i: names_out.index(name) for i, name in enumerate(old)},
        compiler_params=pltpu.CompilerParams(
            vmem_limit_bytes=vmem_grant(scratch.values(), spare) * MIB, **params
        ),
        **estimate,
    )(*near.values(), *map(in_hbm, held.values()), *(in_hbm(state[name]) for name in old))
    results = dict(zip(names_out, results))
    for name in kept:
        state[name] = results.pop(name)
    return results


def of_micro(rows, m):
    if isinstance(m, int):
        return rows[m : m + 1]
    row = rows[0:1]
    for i in range(1, rows.shape[0]):
        row = jnp.where(m == i, rows[i : i + 1], row)
    return row


def as_column(row):
    return jnp.broadcast_to(row, (8, row.shape[1])).T[:, 0:1]


class Copies:
    def __init__(self, sems):
        self.sems, self.count, self.open = sems, 0, []

    def load(self, source, target):
        copy = pltpu.make_async_copy(source, target, self.sems.at[self.count])
        self.count += 1
        copy.start()
        return copy

    def save(self, source, target):
        self.open.append(self.load(source, target))

    def wait(self):
        for copy in self.open:
            copy.wait()


def remote(source, target, send, receive, where):
    return pltpu.make_async_remote_copy(
        src_ref=source, dst_ref=target, send_sem=send, recv_sem=receive, device_id=where, device_id_type=MESH
    )


def forward_micro(geo, tick):
    if tick == 0:
        return 0
    return geo.micro - 1 if tick == geo.micro else tick - lax.axis_index("section")


def backward_micro(geo, step):
    if step == 0:
        return geo.micro - 1
    return 0 if step == geo.micro else geo.micro - step - lax.axis_index("section")


class Across:
    def __init__(self, sender, sems, at=0):
        self.section = lax.axis_index("section")
        self.sender, self.other = sender, {"section": 1 - self.section}
        self.send_sem, self.recv_sem = sems.at[at], sems.at[at + 1]

    def greet(self):
        pl.semaphore_signal(pltpu.get_barrier_semaphore(), inc=1, device_id=self.other, device_id_type=MESH)

    def copy(self, source, target):
        return remote(source, target, self.send_sem, self.recv_sem, self.other)

    def send(self, source, target):
        @pl.when(self.section == self.sender)
        def _():
            self.copy(source, target).start()

    def sent(self, source, target):
        @pl.when(self.section == self.sender)
        def _():
            self.copy(source, target).wait_send()

    def take(self, target):
        @pl.when(self.section != self.sender)
        def _():
            self.copy(target, target).wait_recv()


def prepare(experts_all, at):
    heads, length = at.bias_here.shape[:2]
    width = at.small.shape[0]
    copies = Copies(at.sems)
    copies.load(at.packed.at[:, pl.ds(4 * width, 128)], at.small).wait()
    rows = at.small[...].astype(F32).T
    at.gains_here[0:2, :] = rows[experts_all : experts_all + 2]
    copies.save(at.gains_here, at.gains)
    picked = (at.head_pick[...] * rows[experts_all + 2 : experts_all + 3]).astype(BF16)
    by_distance = mm(picked, at.spread[...], (1, 0))
    for h in range(heads):
        block = by_distance[h : h + 1, :]
        step = 1
        while step < length:
            block = jnp.concatenate([block, pltpu.roll(block, step, 1)], axis=0)
            step *= 2
        at.bias_here[h] = block.astype(BF16)
    copies.save(at.bias_here, at.bias)
    copies.wait()


def diagonal_sums(block):
    length = block.shape[1]
    size = block.shape[0] // 2
    while size >= 1:
        block = block[:size] + pltpu.roll(block[size:], length - size, 1)
        size //= 2
    return block


def only_section(geo, tick):
    return {0: 0, geo.micro: 1}.get(tick)


def where_active(active, body, at):
    if active is None:
        body(at)
    else:
        pl.when(lax.axis_index("section") == active)(partial(body, at))


def dense_forward_part(geo, tick, at, copies, enter, across, loaded, fused=True):
    length, width, heads = geo.length, geo.width, geo.heads
    size = width // heads
    per = 128 // size
    m = forward_micro(geo, tick)
    gains_load = copies.load(at.gains, at.gains_here)
    thirds = [pl.ds(third * width, width) for third in range(3)]
    packed_qkv = [copies.load(at.packed.at[:, third], at.qkv_w.at[:, third]) for third in thirds]
    if tick == 0:
        copies.load(at.inputs.at[m], at.stream).wait()
    else:
        first = lax.axis_index("section") == 0
        own = pltpu.make_async_copy(at.inputs.at[m], at.stream, at.stream_sem)
        if tick == 1:
            enter()
            across.send(at.out.at[0] if fused else at.out_before.at[0], at.stream_in)
        else:
            came = pltpu.make_async_copy(at.received, at.stream, at.stream_sem)

        @pl.when(first)
        def _():
            own.start()
            own.wait()

        if tick == 1:
            across.take(at.stream_in)

            @pl.when(jnp.logical_not(first))
            def _():
                at.stream[...] = at.stream_in[...]
        else:

            @pl.when(jnp.logical_not(first))
            def _():
                came.start()
                came.wait()

    packed_rest = copies.load(at.packed.at[:, pl.ds(3 * width, width + 128)], at.rest_w)
    bias_load = copies.load(at.bias, at.bias_here)
    copies.save(at.stream, at.kept_stream.at[m])
    stream = at.stream[...].astype(F32)
    gains_load.wait()
    at.normed[...] = (stream * norm_factor(stream) * at.gains_here[0:1, :]).astype(BF16)
    copies.save(at.normed, at.kept_normed.at[m])
    for third, load in zip(thirds, packed_qkv):
        load.wait()
        at.qkv[:, third] = mm(at.normed[...], at.qkv_w[:, third], (1, 0)).astype(BF16)
    copies.save(at.qkv, at.kept_qkv.at[m])
    key_at, query_at = iota((length, length), 0), iota((length, length), 1)
    segments = of_micro(at.segments[...], m).astype(F32)
    allowed = (key_at <= query_at) & (as_column(segments) == segments)
    which = iota((length, 128), 1) // size
    head_row = iota((128, length), 0) // size
    scale = 1.0 / math.sqrt(size)
    zero = jnp.zeros((length, 128), BF16)
    bias_load.wait()
    for j in range(width // 128):
        queries = at.qkv[:, 128 * j : 128 * (j + 1)]
        keys = at.qkv[:, width + 128 * j : width + 128 * (j + 1)]
        values = at.qkv[:, 2 * width + 128 * j : 2 * width + 128 * (j + 1)]
        turned_values = values.astype(F32).T
        context = jnp.zeros((128, length), F32)
        for part in range(per):
            h = j * per + part
            own = which == part
            scores = mm(jnp.where(own, keys, zero), queries, (1, 1)) * scale + at.bias_here[h].astype(F32)
            scores = jnp.where(allowed, scores, -1e30)
            exponent = jnp.exp(scores - jnp.max(scores, axis=0, keepdims=True))
            prob = (exponent * (1.0 / jnp.sum(exponent, axis=0, keepdims=True))).astype(BF16)
            at.prob[h] = prob
            own_values = jnp.where(head_row == part, turned_values, 0.0).astype(BF16)
            context = context + mm(own_values, prob, (1, 0))
        at.context[:, 128 * j : 128 * (j + 1)] = context.T.astype(BF16)
    copies.save(at.prob, at.kept_prob.at[m])
    copies.save(at.context, at.kept_context.at[m])
    packed_rest.wait()
    loaded()
    residual = stream + mm(at.context[...], at.rest_w[:, :width], (1, 0))
    at.residual[...] = residual
    copies.save(at.residual, at.kept_residual.at[m])
    moe_in = (residual * norm_factor(residual) * at.gains_here[1:2, :]).astype(BF16)
    at.moe_in[...] = moe_in
    copies.save(at.moe_in, at.kept_moe_in.at[m])
    logits = mm(moe_in, at.rest_w[:, width:], (1, 0))
    expert_at = iota(logits.shape, 1)
    picks = [(as_column(at.routes[0, m, c : c + 1, :].astype(F32)) == expert_at.astype(F32)).astype(F32) for c in range(TOP)]
    chosen = [jnp.sum(pick * logits, axis=1, keepdims=True) for pick in picks]
    top = jnp.maximum(chosen[0], chosen[1])
    powers = [jnp.exp(value - top) for value in chosen]
    total = powers[0] + powers[1]
    shares = [power / total for power in powers]
    order = of_micro(at.order[0, :, 0, :], m).astype(F32)
    before = (order < as_column(order)).astype(BF16)
    counts = [mm(before, pick.astype(BF16), (1, 0)) for pick in picks]
    counts[1] = counts[1] + jnp.sum(picks[0], axis=0, keepdims=True)
    slots = []
    for pick, count in zip(picks, counts):
        rank = jnp.sum(pick * count, axis=1, keepdims=True)
        main = jnp.sum(pick * at.bases[0:1, :], axis=1, keepdims=True)
        tail = jnp.sum(pick * at.bases[1:2, :], axis=1, keepdims=True)
        place = jnp.where(rank < geo.main, main + rank, tail + rank - geo.main)
        slots.append(jnp.where(rank < geo.capacity, place, -1.0))
    lane = iota((length, 128), 1)
    aux = jnp.zeros((length, 128), F32)
    for place, value in enumerate(shares + slots):
        aux = jnp.where(lane == place, value, aux)
    at.aux[...] = aux
    copies.save(at.aux, at.kept_aux.at[m])
    first, second = slot_onehots(aux, geo.slots)
    at.slots[...] = mm((first | second).astype(BF16), moe_in, (0, 0)).astype(BF16).reshape(at.slots.shape)


def dense_forward_body(geo, tick, at):
    across = Across(0, at.across_sems) if tick == 1 else None
    if across:
        across.greet()

    def enter():
        pl.semaphore_wait(pltpu.get_barrier_semaphore(), 1)

    copies = Copies(at.sems)
    dense_forward_part(geo, tick, at, copies, enter, across, lambda: None, fused=False)
    copies.save(at.slots, at.slot_rows)
    copies.wait()
    if across:
        across.sent(at.out_before.at[0], at.stream_in)


def dense_forward_scratch(geo, tick):
    length, width, heads = geo.length, geo.width, geo.heads
    scratch = dict(
        stream=pltpu.VMEM((length, width), BF16),
        qkv_w=pltpu.VMEM((width, 3 * width), BF16),
        rest_w=pltpu.VMEM((width, width + 128), BF16),
        bias_here=pltpu.VMEM((heads, length, length), BF16),
        normed=pltpu.VMEM((length, width), BF16),
        qkv=pltpu.VMEM((length, 3 * width), BF16),
        prob=pltpu.VMEM((heads, length, length), BF16),
        context=pltpu.VMEM((length, width), BF16),
        residual=pltpu.VMEM((length, width), F32),
        moe_in=pltpu.VMEM((length, width), BF16),
        aux=pltpu.VMEM((length, 128), F32),
        slots=pltpu.VMEM((geo.units, geo.rows, geo.main, width), BF16),
        gains_here=pltpu.VMEM((8, width), F32),
        sems=pltpu.SemaphoreType.DMA((20 + width // 128,)),
        stream_sem=pltpu.SemaphoreType.DMA,
        across_sems=pltpu.SemaphoreType.DMA((4,)),
    )
    if tick == 1:
        scratch["stream_in"] = pltpu.VMEM((length, width), BF16)
    return scratch


def dense_forward_refs(geo, tick, given, state, received):
    micro, length, width, heads = geo.micro, geo.length, geo.width, geo.heads
    near = {name: given[name] for name in ("segments", "order", "routes", "bases")}
    held = {name: given[name] for name in ("packed", "bias", "inputs", "gains")}
    if tick > 1:
        held["received"] = received
    kept = dict(
        kept_stream=((micro, length, width), BF16),
        kept_normed=((micro, length, width), BF16),
        kept_qkv=((micro, length, 3 * width), BF16),
        kept_prob=((micro, heads, length, length), BF16),
        kept_context=((micro, length, width), BF16),
        kept_residual=((micro, length, width), F32),
        kept_moe_in=((micro, length, width), BF16),
        kept_aux=((micro, length, 128), F32),
    )
    return near, held, kept


def dense_forward(geo, tick, given, state, received):
    near, held, kept = dense_forward_refs(geo, tick, given, state, received)
    params = {}
    if tick == 1:
        held["out_before"] = state["out"]
        params = dict(collective_id=5 + 2 * geo.micro, has_side_effects=True)
    return launch(
        partial(where_active, only_section(geo, tick), partial(dense_forward_body, geo, tick)),
        near=near,
        held=held,
        outs=dict(slot_rows=pltpu.HBM((geo.units, geo.rows, geo.main, geo.width), BF16)),
        kept=kept,
        state=state,
        scratch=dense_forward_scratch(geo, tick),
        cost=(2_000_000_000, 14_000_000),
        **params,
    )["slot_rows"]


def combine(home, aux, result, picked_ref):
    for c, onehot in enumerate(slot_onehots(aux, home.shape[0])):
        picked = mm(onehot.astype(BF16), home, (1, 0))
        picked_ref[c] = picked.astype(BF16)
        result = result + aux[:, c : c + 1] * picked
    return result


def spread(incoming, aux, slots):
    total = 0.0
    for c, onehot in enumerate(slot_onehots(aux, slots)):
        total = total + mm(onehot.astype(BF16), (aux[:, c : c + 1] * incoming).astype(BF16), (0, 0))
    return total.astype(BF16)


def gate_gradients(incoming, picked_ref):
    lane = iota((incoming.shape[0], 128), 1)
    gates = jnp.zeros(lane.shape, F32)
    for c in range(TOP):
        gate = jnp.sum(picked_ref[c].astype(F32) * incoming, axis=1, keepdims=True)
        gates = jnp.where(lane == c, gate, gates)
    return gates


def expert_picker(geo, e):
    dims = (geo.sources * geo.share, geo.sources * geo.main)
    own, place = iota(dims, 0), iota(dims, 1)
    return (place == own // geo.share * geo.main + e * geo.share + own % geo.share).astype(BF16)


class Exchange:
    def __init__(self, geo, at, x, active=None):
        self.geo, self.x, self.at = geo, x, at
        self.relay = geo.chips // 2 if active is not None and geo.chips > 1 else None
        self.near_rows = geo.cores
        self.ahead = 2 if self.relay else 1
        self.peers = geo.cols - 1
        self.other = {"section": 1 - lax.axis_index("section")}
        self.r, self.c = lax.axis_index("row"), lax.axis_index("col")
        self.z, self.core = self.r // geo.cores, self.r % geo.cores
        self.partner = self.z * geo.cores + (self.core + 1) % geo.cores

    def far(self, direct):
        chips = sorted(range(1, self.geo.chips), key=lambda k: abs(2 * k - self.geo.chips))
        return [k for k in chips if direct or k != self.relay]

    def far_rows(self, direct):
        return self.geo.cores * len(self.far(direct))

    def kinds(self):
        first = self.geo.first if self.relay else 0
        return [(pl.ds(at, n), direct) for at, n, direct in ((0, first, True), (first, self.geo.units - first, False)) if n]

    def chip(self, k):
        return (self.z + k + self.geo.chips) % self.geo.chips

    def row(self, k, d):
        return self.partner if k == 0 else self.chip(k) * self.geo.cores + d

    def col(self, j):
        return (self.c + j + self.geo.cols) % self.geo.cols

    def rows(self, k):
        return pl.ds(self.chip(k) * self.geo.cores, self.geo.cores)

    def others(self, k):
        return range(self.geo.cores - 1) if k == 0 else range(self.geo.cores)

    def greet(self):
        barrier = pltpu.get_barrier_semaphore()
        for k in range(self.geo.chips):
            for d in self.others(k):
                pl.semaphore_signal(barrier, inc=1, device_id={"row": self.row(k, d)}, device_id_type=MESH)
        for j in range(1, self.geo.cols):
            pl.semaphore_signal(barrier, inc=1, device_id={"col": self.col(j)}, device_id_type=MESH)
        if self.relay:
            pl.semaphore_signal(barrier, inc=1, device_id=self.other, device_id_type=MESH)

    def await_greetings(self, more):
        more = more + (1 if self.relay else 0)
        pl.semaphore_wait(pltpu.get_barrier_semaphore(), self.geo.rows + self.geo.cols - 2 + more)

    def came(self, block, sem):
        remote(block, block, self.at.done, sem, self.other).wait_recv()

    def left(self, block, sem):
        remote(block, block, sem, self.at.done, self.other).wait_send()


    def own(self, u):
        return pltpu.make_async_copy(
            self.x.at[u, self.r], self.at.inbox.at[u, self.c, self.r], self.at.own_sem.at[u]
        )

    def kind(self, u):
        if not (self.relay and self.geo.first):
            return 0
        return int(u < self.geo.first) if isinstance(u, int) else (u + self.geo.units - 1) // self.geo.units * -1 + 1

    def send(self, u, k):
        for d in self.others(k):
            remote(
                self.x.at[u, self.row(k, d)], self.at.inbox.at[u, self.c, self.r], self.at.in_send.at[self.kind(u)],
                self.at.in_recv.at[u, k], {"row": self.row(k, d)},
            ).start()

    def send_out(self, u):
        if self.relay:
            remote(
                self.x.at[u, self.rows(self.relay)], self.at.via_x.at[u], self.at.via_send,
                self.at.via_x_recv.at[u], self.other,
            ).start()

    def hand_over(self, u, k):
        block = self.at.inbox.at[u, self.c, self.rows(-k)]
        for j in range(1, self.geo.cols):
            remote(block, block, self.at.pass_send.at[u], self.at.pass_recv.at[u], {"col": self.col(j)}).start()

    def each(self, body):
        lax.fori_loop(0, self.geo.units, lambda u, carry: (body(u), carry)[1], 0)

    def open(self):
        for u in range(min(self.ahead, self.geo.units)):
            direct = u < self.geo.first
            for k in self.far(direct):
                self.send(u, k)
            if not direct:
                self.send_out(u)

        def body(u):
            self.own(u).start()
            self.send(u, 0)

        self.each(body)
        for u in range(min(3, self.geo.units)):
            self.pass_on_own(u)

    def pass_on_own(self, u):
        self.own(u).wait()
        if self.geo.cores > 1:
            self.came(self.at.inbox.at[u, self.c, pl.ds(0, 1)], self.at.in_recv.at[u, 0])
        self.hand_over(u, 0)

    def pass_on(self, u, direct=False):
        @pl.when(u + self.ahead < self.geo.units)
        def _():
            self.send_out(u + self.ahead)

        for k in self.far(direct):
            self.came(self.at.inbox.at[u, self.c, self.rows(-k)], self.at.in_recv.at[u, k])

            @pl.when(u + self.ahead < self.geo.units)
            def _():
                if k in self.far(False):
                    self.send(u + self.ahead, k)

            self.hand_over(u, k)

        @pl.when(u + 3 < self.geo.units)
        def _():
            self.pass_on_own(u + 3)

    def collect(self, u, direct=False):
        if self.peers:
            block = self.at.inbox.at[u, pl.ds(0, self.peers), pl.ds(0, self.near_rows + self.far_rows(direct))]
            self.came(block, self.at.pass_recv.at[u])
            self.left(block, self.at.pass_send.at[u])
        if self.relay and not direct:
            self.came(self.at.inbox.at[u, :, pl.ds(0, self.geo.cores)], self.at.into_recv.at[u])


    def send_parts(self, u, far, direct=False):
        if far and self.relay and not direct:
            for j in range(self.geo.cols):
                remote(
                    self.at.inbox.at[u, self.col(j), self.rows(self.relay)], self.at.via_part.at[u, j],
                    self.at.via_part_send, self.at.via_part_recv.at[u], self.other,
                ).start()
        for k in self.far(direct) if far else (0,):
            for j in range(1, self.geo.cols):
                remote(
                    self.at.inbox.at[u, self.col(j), self.rows(k)], self.at.arrived.at[u, j - 1, self.rows(k)],
                    self.at.out_send.at[self.kind(u)], self.at.out_recv.at[u, k], {"col": self.col(j)},
                ).start()

    def send_home(self, u, far, direct=False):
        for k in self.far(direct) if far else (0,):
            rows = self.rows(k)
            if self.peers:
                self.came(self.at.arrived.at[u, :, rows], self.at.out_recv.at[u, k])
            total = self.at.inbox[u, self.c, rows].astype(F32)
            for j in range(1, self.geo.cols):
                total = total + self.at.arrived[u, j - 1, rows].astype(F32)
            self.at.stage[u, rows] = total.astype(BF16)
            for d in self.others(k):
                remote(
                    self.at.stage.at[u, self.row(k, d)], self.at.home.at[u, self.r], self.at.home_send.at[self.kind(u)],
                    self.at.home_recv.at[self.kind(u)], {"row": self.row(k, d)},
                ).start()
            if k == 0:
                self.at.home[u, self.r] = self.at.stage[u, self.r]

    def finish(self):
        at, cores = self.at, self.geo.cores
        for units, direct in self.kinds():
            sent_rows = self.far_rows(direct) + cores - 1
            if sent_rows:
                block = at.home.at[units, pl.ds(0, sent_rows)]
                self.came(block, at.home_recv.at[int(direct)])
                self.left(block, at.home_send.at[int(direct)])
                self.left(block, at.in_send.at[int(direct)])
            if self.peers:
                block = at.arrived.at[units, :, pl.ds(0, self.near_rows + self.far_rows(direct))]
                self.left(block, at.out_send.at[int(direct)])
            if self.relay and not direct:
                self.came(at.home.at[units, pl.ds(0, cores)], at.home_in_recv)
                self.left(at.via_x.at[units], at.via_send)
                self.left(at.via_part.at[units], at.via_part_send)


    def along(self, u, d, source, target, at):
        where = {"row": self.row(self.relay, d)}
        return remote(
            source.at[u, d], target.at[u, self.core], self.at.core_sems.at[at, u, d],
            self.at.core_sems.at[at + 1, u, self.core], where,
        )

    def along_came(self, u, d, target, at):
        self.came(target.at[u, d], self.at.core_sems.at[at + 1, u, d])

    def across(self, u, j):
        return remote(
            self.at.via_z.at[u], self.at.via_y.at[u, j - 1], self.at.via_sems.at[2, u, j], self.at.via_sems.at[3, u, j],
            {"col": self.col(j)},
        )

    def into(self, u, j):
        source = self.at.via_y.at[u, j - 1] if j else self.at.via_z.at[u]
        target = self.at.inbox.at[u, self.col(-j), self.rows(-self.relay)]
        return remote(source, target, self.at.via_sems.at[0, u, j], self.at.into_recv.at[u], self.other)

    def part_across(self, u, j):
        return remote(
            self.at.via_part.at[u, j], self.at.via_sum.at[u, j - 1], self.at.via_sems.at[4, u, j],
            self.at.via_sems.at[5, u, j], {"col": self.col(j)},
        )

    def home_in(self, u):
        return remote(
            self.at.via_home.at[u], self.at.home.at[u, self.rows(-self.relay)], self.at.via_sems.at[1, u, 0],
            self.at.home_in_recv, self.other,
        )

    def carry(self):
        geo, at = self.geo, self.at
        cores, columns = range(geo.cores), range(1, geo.cols)

        def rows_out(u):
            self.came(at.via_x.at[u], at.via_x_recv.at[u])
            for d in cores:
                self.along(u, d, at.via_x, at.via_z, 0).start()

        def rows_on(u):
            for d in cores:
                self.along_came(u, d, at.via_z, 0)
            self.into(u, 0).start()
            for j in columns:
                self.across(u, j).start()

        def rows_in(u):
            for j in columns:
                self.across(u, j).wait_recv()
                self.into(u, j).start()

        def parts_out(u):
            self.came(at.via_part.at[u], at.via_part_recv.at[u])
            for j in columns:
                self.part_across(u, j).start()

        def parts_on(u):
            total = at.via_part[u, 0].astype(F32)
            for j in columns:
                self.part_across(u, j).wait_recv()
                total = total + at.via_sum[u, j - 1].astype(F32)
            at.via_total[u] = total.astype(BF16)
            for d in cores:
                self.along(u, d, at.via_total, at.via_home, 2).start()

        def parts_in(u):
            for d in cores:
                self.along_came(u, d, at.via_home, 2)
            self.home_in(u).start()

        units = list(range(geo.first, geo.units))
        for steps in ((rows_out, rows_on, rows_in), (parts_out, parts_on, parts_in)):
            for t in range(len(units) + 2):
                for lag, work in enumerate(steps):
                    if 0 <= t - lag < len(units):
                        work(units[t - lag])
        for u in units:
            for d in cores:
                self.along(u, d, at.via_x, at.via_z, 0).wait_send()
                self.along(u, d, at.via_total, at.via_home, 2).wait_send()
            for j in range(geo.cols):
                self.into(u, j).wait_send()
            for j in columns:
                self.across(u, j).wait_send()
                self.part_across(u, j).wait_send()
            self.home_in(u).wait_send()


def run_experts(geo, exchange, rows, total, shared, loads, expert, saves, opened=lambda: None):
    first, count = geo.first, geo.sources * geo.main
    inbox = exchange.at.inbox
    width = inbox.shape[-1]
    exchange.open()
    opened()
    if first:
        exchange.pass_on(0, True)
    exchange.pass_on(first)
    if first:
        exchange.collect(0, True)
        shared[...] = jnp.zeros(shared.shape, F32)

    def step(e, carry):
        u = e + first
        slot = e % 2

        @pl.when(e + 1 < geo.local_experts)
        def _():
            exchange.pass_on(u + 1)

        exchange.collect(u)

        @pl.when(e >= 2)
        def _():
            for copy in saves(e - 2, slot):
                copy.wait()

        rows[slot, :count] = inbox[u].reshape(count, width)
        if first:
            picker = expert_picker(geo, e)
            tail = inbox[0].reshape(count, width)
            rows[slot, count:] = mm(picker, tail, (1, 0)).astype(BF16)
        for copy in loads(e):
            copy.wait()
        expert(e, slot)
        for copy in saves(e, slot):
            copy.start()
        inbox[u] = total[:count].astype(BF16).reshape(inbox.shape[1:])
        exchange.send_parts(u, True)
        if first:
            shared[...] += mm(picker, total[count:].astype(BF16), (0, 0))

        @pl.when(e >= 1)
        def _():
            exchange.send_home(u - 1, True)
            if exchange.relay:
                exchange.send_parts(u - 1, False)

        return carry

    lax.fori_loop(0, geo.local_experts, step, 0)
    if first:
        inbox[0] = shared[...].astype(BF16).reshape(inbox.shape[1:])
        exchange.send_parts(0, True, True)
    near = [u for u in range(geo.units) if not exchange.relay or u < first or u == geo.units - 1]
    half = len(near) // 2
    exchange.send_home(geo.units - 1, True)
    for u in near[half:]:
        exchange.send_parts(u, False)
    if first:
        exchange.send_home(0, True, True)
    for u in near[:half]:
        exchange.send_parts(u, False)
    exchange.each(lambda u: exchange.send_home(u, False))
    for e in range(max(0, geo.local_experts - 2), geo.local_experts):
        for copy in saves(e, e % 2):
            copy.wait()
    exchange.finish()


def share_work(exchange, active, work):
    if not exchange.relay:
        work()
        return
    section = lax.axis_index("section")
    pl.when(section == active)(work)

    @pl.when(section != active)
    def _():
        exchange.await_greetings(0)
        exchange.carry()


def start_loads(geo, loads):
    for e in range(geo.local_experts):
        for copy in loads(e):
            copy.start()


def forward_body(geo, tick, tile, fused, at):
    m = forward_micro(geo, tick)
    take, send = fused and tick == 1, 1 <= tick < geo.micro
    active = only_section(geo, tick)
    exchange = Exchange(geo, at, at.slots if fused else at.slot_rows, active)
    exchange.greet()
    across_in, across_out = Across(0, at.across_sems, 2), Across(0, at.across_sems)
    if take or send:
        across_out.greet()
    w_in, w_out = at.w_in_here, at.w_out_here

    def loads(e):
        return (
            pltpu.make_async_copy(at.w_in.at[e], w_in.at[e], at.load_sem.at[e, 0]),
            pltpu.make_async_copy(at.w_out.at[e], w_out.at[e], at.load_sem.at[e, 1]),
        )

    def saves(e, slot):
        return (
            pltpu.make_async_copy(at.rows.at[slot], at.kept_rows.at[m, e], at.save_sem.at[slot, 0]),
            pltpu.make_async_copy(at.wide.at[slot], at.kept_hidden.at[m, e], at.save_sem.at[slot, 1]),
            pltpu.make_async_copy(at.slope.at[slot], at.kept_slope.at[m, e], at.save_sem.at[slot, 2]),
        )

    def expert(e, slot):
        for f in range(0, geo.hidden, tile):
            value, derivative = gelu_pair(mm(at.rows[slot], w_in[e, :, f : f + tile], (1, 0)))
            value = value.astype(BF16)
            at.wide[slot, :, f : f + tile] = value
            at.slope[slot, :, f : f + tile] = derivative.astype(BF16)
            product = mm(value, w_out[e, f : f + tile, :], (1, 0))
            at.total[...] = product if f == 0 else at.total[...] + product

    def enter():
        exchange.await_greetings(int(take or send))

    def work():
        copies = Copies(at.sems)
        if fused:
            dense_forward_part(geo, tick, at, copies, enter, across_in, lambda: start_loads(geo, loads))
            if not take:
                enter()
        else:
            start_loads(geo, loads)
            aux_load = copies.load(at.kept_aux.at[m], at.aux)
            residual_load = copies.load(at.kept_residual.at[m], at.residual)
            enter()
        run_experts(geo, exchange, at.rows, at.total, at.shared, loads, expert, saves)
        if not fused:
            aux_load.wait()
            residual_load.wait()
        home = at.home[...].reshape(geo.slots, geo.width)
        at.result[...] = combine(home, at.aux[...], at.residual[...], at.picked).astype(BF16)
        if send:
            across_out.send(at.result, at.received_out)
        copies.save(at.result, at.out.at[m])
        copies.save(at.picked, at.kept_picked.at[m])
        copies.wait()
        if take:
            across_in.sent(at.out.at[0], at.stream_in)
        if send:
            across_out.take(at.received_out)
            across_out.sent(at.result, at.received_out)

    share_work(exchange, active, work)


def backward_body(geo, step, tile, fused, at):
    m = backward_micro(geo, step)
    take, send = step == 1, fused and 1 <= step < geo.micro
    active = only_section(geo, geo.micro - step)
    exchange = Exchange(geo, at, at.slot_grad, active)
    exchange.greet()
    first = lax.axis_index("section") == 0
    across, across_out = Across(1, at.across_sems), Across(1, at.across_sems, 2)
    if take or send:
        across.greet()
    w_in, w_out = at.w_in_here, at.w_out_here

    def loads(e):
        return (
            pltpu.make_async_copy(at.w_out.at[e], w_out.at[e], at.load_sem.at[e, 1]),
            pltpu.make_async_copy(at.kept_slope.at[m, e], at.slope.at[e], at.load_sem.at[e, 2]),
            pltpu.make_async_copy(at.w_in.at[e], w_in.at[e], at.load_sem.at[e, 0]),
        )

    def saves(e, slot):
        return (
            pltpu.make_async_copy(at.rows.at[slot], at.kept_seen.at[m, e], at.save_sem.at[slot, 0]),
            pltpu.make_async_copy(at.wide.at[slot], at.kept_pre.at[m, e], at.save_sem.at[slot, 1]),
        )

    def expert(e, slot):
        for f in range(0, geo.hidden, tile):
            grad = mm(at.rows[slot], w_out[e, f : f + tile, :], (1, 1))
            value = (grad * at.slope[e, :, f : f + tile].astype(F32)).astype(BF16)
            at.wide[slot, :, f : f + tile] = value
            product = mm(value, w_in[e, :, f : f + tile], (1, 1))
            at.total[...] = product if f == 0 else at.total[...] + product

    def incoming_load():
        own = pltpu.make_async_copy(at.cotangent.at[m], at.incoming_here, at.incoming_sem)
        if step == 0:
            return [own], [own]
        if step == 1:
            return [], [own]
        return [pltpu.make_async_copy(at.received, at.incoming_here, at.incoming_sem)], [own]

    def of_sections(action):
        early, late = incoming_load()

        @pl.when(first)
        def _():
            for copy in early:
                getattr(copy, action)()

        @pl.when(jnp.logical_not(first))
        def _():
            for copy in late:
                getattr(copy, action)()

    def work():
        copies = Copies(at.sems)
        picked_load = copies.load(at.kept_picked.at[m], at.picked)
        aux_load = copies.load(at.kept_aux.at[m], at.aux)
        of_sections("start")
        start_loads(geo, loads)
        dense_loads = dense_backward_loads(geo, m, at, copies) if fused else None
        exchange.await_greetings(int(take or send))
        if take:
            across.send(at.sent, at.incoming_far)
            across.take(at.incoming_far)

            @pl.when(first)
            def _():
                at.incoming_here[...] = at.incoming_far[...]

        of_sections("wait")
        aux_load.wait()
        slot_grad = spread(at.incoming_here[...].astype(F32), at.aux[...], geo.slots)
        at.slot_grad[...] = slot_grad.reshape(at.slot_grad.shape)

        def opened():
            picked_load.wait()
            at.incoming[...] = at.incoming_here[...]
            at.gates[...] = gate_gradients(at.incoming_here[...].astype(F32), at.picked)

        run_experts(geo, exchange, at.rows, at.total, at.shared, loads, expert, saves, opened)
        first_slots, second_slots = slot_onehots(at.aux[...], geo.slots)
        home = at.home[...].reshape(geo.slots, geo.width)
        at.moe_grad[...] = mm((first_slots | second_slots).astype(BF16), home, (1, 0))
        if fused:
            dense_backward_part(geo, step, at, copies, dense_loads, lambda: None, across_out if send else None)
        if take:
            across.sent(at.sent, at.incoming_far)

    share_work(exchange, active, work)


def tile_of(hidden, limit):
    return limit if hidden % limit == 0 else hidden


def experts_scratch(geo, slope_slots):
    rows, local, width, hidden = geo.expert_rows, geo.local_experts, geo.width, geo.hidden
    steps = max(1, geo.cols - 1)
    one = pltpu.SemaphoreType.DMA
    two = pltpu.SemaphoreType.DMA((2,))
    unit = pltpu.SemaphoreType.DMA((geo.units,))
    return dict(
        inbox=pltpu.VMEM((geo.units, geo.cols, geo.rows, geo.main, width), BF16),
        arrived=pltpu.VMEM((geo.units, steps, geo.rows, geo.main, width), BF16),
        stage=pltpu.VMEM((geo.units, geo.rows, geo.main, width), BF16),
        home=pltpu.VMEM((geo.units, geo.rows, geo.main, width), BF16),
        picked=pltpu.VMEM((TOP, geo.length, width), BF16),
        aux=pltpu.VMEM((geo.length, 128), F32),
        rows=pltpu.VMEM((2, rows, width), BF16),
        wide=pltpu.VMEM((2, rows, hidden), BF16),
        slope=pltpu.VMEM((slope_slots, rows, hidden), BF16),
        w_in_here=pltpu.VMEM((local, width, hidden), BF16),
        w_out_here=pltpu.VMEM((local, hidden, width), BF16),
        total=pltpu.VMEM((rows, width), F32),
        shared=pltpu.VMEM((geo.sources * geo.main if geo.share else 16, width), F32),
        via_x=pltpu.VMEM((geo.units, geo.cores, geo.main, width), BF16),
        via_z=pltpu.VMEM((geo.units, geo.cores, geo.main, width), BF16),
        via_y=pltpu.VMEM((geo.units, steps, geo.cores, geo.main, width), BF16),
        via_part=pltpu.VMEM((geo.units, geo.cols, geo.cores, geo.main, width), BF16),
        via_sum=pltpu.VMEM((geo.units, steps, geo.cores, geo.main, width), BF16),
        via_total=pltpu.VMEM((geo.units, geo.cores, geo.main, width), BF16),
        via_home=pltpu.VMEM((geo.units, geo.cores, geo.main, width), BF16),
        via_sems=pltpu.SemaphoreType.DMA((6, geo.units, geo.cols)),
        core_sems=pltpu.SemaphoreType.DMA((4, geo.units, geo.cores)),
        own_sem=unit, pass_send=unit, pass_recv=unit, into_recv=unit, via_x_recv=unit, via_part_recv=unit,
        in_send=two, out_send=two, home_send=two, home_recv=two, home_in_recv=one, via_send=one, via_part_send=one,
        done=one,
        in_recv=pltpu.SemaphoreType.DMA((geo.units, geo.chips)),
        out_recv=pltpu.SemaphoreType.DMA((geo.units, geo.chips)),
        load_sem=pltpu.SemaphoreType.DMA((local, 3)),
        save_sem=pltpu.SemaphoreType.DMA((2, 3)),
        sems=pltpu.SemaphoreType.DMA((6,)),
        across_sems=pltpu.SemaphoreType.DMA((4,)),
    )


def experts_cost(geo):
    weights = geo.local_experts * geo.hidden * geo.width
    return (4 * geo.expert_rows * weights, 4 * weights)


def forward_scratch(geo):
    scratch = experts_scratch(geo, 2)
    scratch["residual"] = pltpu.VMEM((geo.length, geo.width), F32)
    scratch["result"] = pltpu.VMEM((geo.length, geo.width), BF16)
    return scratch


def forward_tick(geo, tick, given, state, received):
    micro, length, width = geo.micro, geo.length, geo.width
    rows, local, hidden = geo.expert_rows, geo.local_experts, geo.hidden
    dense, scratch = dense_forward_scratch(geo, tick), forward_scratch(geo)
    fused = fits(dense, scratch)
    near, kept = {}, {}
    held = dict(w_in=given["w_in"], w_out=given["w_out"])
    if fused:
        near, dense_held, kept = dense_forward_refs(geo, tick, given, state, received)
        held.update(dense_held)
        scratch.update(dense)
    else:
        held["slot_rows"] = dense_forward(geo, tick, given, state, received)
        held.update(kept_aux=state["kept_aux"], kept_residual=state["kept_residual"])
    kept.update(
        out=((micro, length, width), BF16),
        kept_picked=((micro, TOP, length, width), BF16),
        kept_rows=((micro, local, rows, width), BF16),
        kept_hidden=((micro, local, rows, hidden), BF16),
        kept_slope=((micro, local, rows, hidden), BF16),
    )
    results = launch(
        partial(forward_body, geo, tick, tile_of(hidden, 768), fused),
        near=near,
        held=held,
        outs=dict(received_out=pltpu.HBM((length, width), BF16)) if 1 <= tick < micro else {},
        kept=kept,
        state=state,
        scratch=scratch,
        cost=experts_cost(geo),
        collective_id=3 + tick,
        has_side_effects=True,
    )
    return results.get("received_out")


def backward_step(geo, step, given, state, sent, received):
    micro, length, width = geo.micro, geo.length, geo.width
    rows, local, hidden = geo.expert_rows, geo.local_experts, geo.hidden
    scratch = experts_scratch(geo, local)
    scratch["slot_grad"] = pltpu.VMEM((geo.units, geo.rows, geo.main, width), BF16)
    scratch["incoming_here"] = pltpu.VMEM((length, width), BF16)
    scratch["incoming_sem"] = pltpu.SemaphoreType.DMA
    held = dict(
        cotangent=given["cotangent"], w_in=given["w_in"], w_out=given["w_out"], kept_aux=state["kept_aux"],
        kept_picked=state["kept_picked"], kept_slope=state["kept_slope"],
    )
    if step == 1:
        held["sent"] = sent
        scratch["incoming_far"] = pltpu.VMEM((length, width), BF16)
    elif step:
        held["received"] = received
    between = dict(
        moe_grad=shape((length, width), F32), gates=shape((length, 128), F32), incoming=shape((length, width), BF16)
    )
    dense = dense_backward_scratch(geo)
    near, outs, kept = {}, between, {}
    between_scratch = {name: pltpu.VMEM(one.shape, one.dtype) for name, one in between.items()}
    fused = fits(scratch, dense, between_scratch)
    if fused:
        near, dense_held, outs, kept = dense_backward_refs(geo, step, given, state)
        held.update(dense_held)
        scratch.update(dense)
        scratch.update(between_scratch)
    kept.update(
        kept_seen=((micro, local, rows, width), BF16),
        kept_pre=((micro, local, rows, hidden), BF16),
    )
    results = launch(
        partial(backward_body, geo, step, tile_of(hidden, 768), fused),
        near=near,
        held=held,
        outs=outs,
        kept=kept,
        state=state,
        scratch=scratch,
        cost=experts_cost(geo),
        collective_id=4 + micro + step,
        has_side_effects=True,
    )
    return results if fused else dense_backward(geo, step, results, given, state)


class Shards:
    def __init__(self, geo):
        self.cores, self.chips, self.cols = geo.cores, geo.chips, geo.cols
        r, self.c = lax.axis_index("row"), lax.axis_index("col")
        self.z, self.core = r // self.cores, r % self.cores

    def chip(self, k):
        return (self.z + k + self.chips) % self.chips

    def col(self, j):
        return (self.c + j + self.cols) % self.cols

    def row(self, z, other=0):
        return z * self.cores + (self.core + other) % self.cores

    def greet(self):
        barrier = pltpu.get_barrier_semaphore()
        targets = [{"row": self.row(self.chip(k))} for k in range(1, self.chips)]
        targets += [{"col": self.col(j)} for j in range(1, self.cols)]
        targets += [{"row": self.row(self.z, 1)}] * (self.cores - 1)
        for target in targets:
            pl.semaphore_signal(barrier, inc=1, device_id=target, device_id_type=MESH)
        self.greeted = len(targets)

    def await_greetings(self):
        pl.semaphore_wait(pltpu.get_barrier_semaphore(), self.greeted)


def gather_kernel(geo, pieces, qkv, out, router, gain_one, gain_two, terms, all_ref, small, own_sems, z_send, z_recv,
                  y_send, y_recv, core_send, core_recv):
    at = Shards(geo)
    at.greet()
    share, total = all_ref.shape[2:]
    narrow, wide = out.shape[1], qkv.shape[1]
    mine = all_ref.at[at.row(at.z), at.c]
    copies = Copies(own_sems)
    copies.save(qkv, mine.at[:, pl.ds(0, wide)])
    copies.save(out, mine.at[:, pl.ds(wide, narrow)])
    experts_all, count = router.shape[0], terms.shape[1]

    def unit(dims, shift=0):
        return (iota(dims, 0) + shift == iota(dims, 1)).astype(BF16)

    columns = mm(router[...], unit((experts_all, 128)), (0, 0))
    long_terms = mm(terms[...], unit((count, share)), (1, 0)).astype(BF16)
    for k, row in enumerate((gain_one[...], gain_two[...], long_terms)):
        columns = columns + mm(row, unit((1, 128), experts_all + k), (0, 0))
    small[...] = columns.astype(BF16)
    copies.save(small, mine.at[:, pl.ds(wide + narrow, 128)])
    copies.wait()
    at.await_greetings()
    step = total // pieces

    def block(k, j, h):
        return all_ref.at[at.row(at.chip(-k)), at.col(-j), :, pl.ds(h * step, step)]

    def pass_z(k, h):
        own = block(0, 0, h)
        remote(own, own, z_send, z_recv.at[h, k - 1], {"row": at.row(at.chip(k))}).start()

    def pass_y(k, h):
        for j in range(1, at.cols):
            one = block(k, 0, h)
            remote(one, one, y_send, y_recv.at[h, k, j - 1], {"col": at.col(j)}).start()

    def pass_core(k, j, h):
        if at.cores > 1:
            one = block(k, j, h)
            remote(one, one, core_send, core_recv, {"row": at.row(at.z, 1)}).start()

    def came(one, sem):
        remote(one, one, core_send, sem, {"row": at.row(at.z, 1)}).wait_recv()

    def left(one, sem):
        remote(one, one, sem, core_recv, {"row": at.row(at.z, 1)}).wait_send()

    def take_y(h):
        for k in range(at.chips):
            for j in range(1, at.cols):
                came(block(k, j, h), y_recv.at[h, k, j - 1])
                pass_core(k, j, h)

    ahead = min(2, pieces)
    for h in range(ahead):
        for k in range(1, at.chips):
            pass_z(k, h)
    for h in range(pieces):
        pass_y(0, h)
    for h in range(pieces):
        pass_core(0, 0, h)
    for h in range(pieces):
        for k in range(1, at.chips):
            came(block(k, 0, h), z_recv.at[h, k - 1])
            if h + ahead < pieces:
                pass_z(k, h + ahead)
            pass_y(k, h)
            pass_core(k, 0, h)
        if h:
            take_y(h - 1)
    take_y(pieces - 1)
    if at.cores > 1:
        came(all_ref.at[pl.ds(0, at.chips)], core_recv)
        left(all_ref.at[pl.ds(0, at.chips)], core_send)
    if at.chips > 1:
        left(all_ref.at[pl.ds(0, at.chips - 1), 0], z_send)
    if at.cols > 1:
        left(all_ref.at[pl.ds(0, at.chips), pl.ds(0, at.cols - 1)], y_send)


def gather_shards(geo, qkv, out, router, gain_one, gain_two, terms):
    share, total = qkv.shape[0], qkv.shape[1] + out.shape[1] + 128
    pieces = 5 if total % 640 == 0 else 1
    one = pltpu.SemaphoreType.DMA
    return pl.pallas_call(
        partial(gather_kernel, geo, pieces),
        out_shape=pltpu.HBM((geo.rows, geo.cols, share, total), BF16),
        in_specs=[hbm_spec()] * 2 + [vmem_spec()] * 4,
        out_specs=hbm_spec(),
        scratch_shapes=[
            pltpu.VMEM((share, 128), BF16),
            pltpu.SemaphoreType.DMA((3,)),
            one, pltpu.SemaphoreType.DMA((pieces, max(1, geo.chips - 1))),
            one, pltpu.SemaphoreType.DMA((pieces, geo.chips, max(1, geo.cols - 1))),
            one, one,
        ],
        compiler_params=pltpu.CompilerParams(collective_id=1, has_side_effects=True),
    )(in_hbm(qkv), in_hbm(out), router, gain_one, gain_two, terms)


def reduce_part(shards, refs):
    at = shards
    part_ref, out_ref = refs.part, refs.shard
    from_core, from_col, from_chip, pair, column = refs.from_core, refs.from_col, refs.from_chip, refs.pair, refs.column
    core_send, core_recv, y_send, y_recv, z_send, z_recv = (
        refs.core_send, refs.core_recv, refs.y_send, refs.y_recv, refs.z_send, refs.z_recv
    )
    order = list(range(1, at.chips)) + [0]
    started = []

    def start(copy):
        copy.start()
        started.append(copy)

    def to_core(k):
        return remote(
            part_ref.at[at.row(at.chip(k), 1)], from_core.at[k], core_send.at[k, 0], core_recv.at[k, 0],
            {"row": at.row(at.z, 1)},
        )

    def to_col(k, j):
        return remote(
            pair.at[k, at.col(j)], from_col.at[k, j - 1], y_send.at[k, j - 1], y_recv.at[k, j - 1],
            {"col": at.col(j)},
        )

    def to_chip(k):
        return remote(
            column.at[k - 1], from_chip.at[k - 1], z_send.at[k - 1], z_recv.at[k - 1],
            {"row": at.row(at.chip(k))},
        )

    if at.cores > 1:
        for k in order:
            start(to_core(k))

    def sum_cores(k):
        total = part_ref[at.row(at.chip(k))].astype(F32)
        if at.cores > 1:
            to_core(k).wait_recv()
            total = total + from_core[k].astype(F32)
        pair[k] = total.astype(BF16)
        for j in range(1, at.cols):
            start(to_col(k, j))

    def sum_cols(k):
        total = pair[k, at.c].astype(F32)
        for j in range(1, at.cols):
            to_col(k, j).wait_recv()
            total = total + from_col[k, j - 1].astype(F32)
        if k:
            column[k - 1] = total.astype(BF16)
            start(to_chip(k))
        else:
            out_ref[...] = total

    for step, k in enumerate(order):
        sum_cores(k)
        if step:
            sum_cols(order[step - 1])
    sum_cols(order[-1])
    for k in range(1, at.chips):
        to_chip(k).wait_recv()
        out_ref[...] += from_chip[k - 1].astype(F32)
    for copy in started:
        copy.wait_send()


def reduce_scratch(geo, share, width):
    chips, steps, far = geo.chips, max(1, geo.cols - 1), max(1, geo.chips - 1)
    z = pltpu.SemaphoreType.DMA((far,))
    y = pltpu.SemaphoreType.DMA((chips, steps))
    core = pltpu.SemaphoreType.DMA((chips, geo.cols))
    return dict(
        from_core=pltpu.VMEM((chips, geo.cols, share, width), BF16),
        from_col=pltpu.VMEM((chips, steps, share, width), BF16),
        from_chip=pltpu.VMEM((far, share, width), BF16),
        pair=pltpu.VMEM((chips, geo.cols, share, width), BF16),
        column=pltpu.VMEM((far, share, width), BF16),
        core_send=core, core_recv=core, y_send=y, y_recv=y, z_send=z, z_recv=z,
    )


def expert_weights_kernel(experts_all, rows, pre, hidden, seen, packed, in_grad, out_grad, qkv, out, router, one, two,
                          terms):
    def product(left, right):
        left, right = (ref[:, 0].reshape(-1, ref.shape[-1]) for ref in (left, right))
        return mm(left, right, (0, 0))

    in_grad[0, 0] = product(rows, pre)
    out_grad[0, 0] = product(hidden, seen)

    @pl.when((pl.program_id(0) == 0) & (pl.program_id(1) == 0))
    def _():
        wide, narrow = qkv.shape[2], out.shape[2]
        qkv[0] = packed[:, :wide]
        out[0] = packed[:, wide : wide + narrow]
        small = packed[:, wide + narrow :]
        dims = (experts_all + 8, 128)
        pick = (iota(dims, 0) == iota(dims, 1)).astype(F32)
        lines = lax.dot_general(
            pick, small, (((1,), (1,)), ((), ())), precision=lax.Precision.HIGHEST, preferred_element_type=F32
        )
        router[0] = lines[:experts_all]
        one[...] = lines[experts_all : experts_all + 1]
        two[...] = lines[experts_all + 1 : experts_all + 2]
        terms[...] = lines[experts_all + 2 : experts_all + 3, : terms.shape[1]]


def expert_weights(geo, state, packed, terms):
    micro, local, count, width, hidden = geo.micro, geo.local_experts, geo.expert_rows, geo.width, geo.hidden
    tile = tile_of(hidden, 768)
    narrow = pl.BlockSpec((micro, 1, count, width), lambda e, f: (0, e, 0, 0))
    wide = pl.BlockSpec((micro, 1, count, tile), lambda e, f: (0, e, 0, f))
    flops = 4 * micro * local * count * width * hidden
    share = packed.shape[0]
    small = [(1, share, 3 * width), (1, share, width), (1, geo.experts_all, share), (1, share), (1, share), (1, terms)]

    def whole(dims):
        return pl.BlockSpec(dims, lambda e, f: (0,) * len(dims))

    return pl.pallas_call(
        partial(expert_weights_kernel, geo.experts_all),
        out_shape=[shape((1, local, width, hidden), F32), shape((1, local, hidden, width), F32)]
        + [shape(dims, F32) for dims in small],
        grid=(local, hidden // tile),
        in_specs=[narrow, wide, wide, narrow, whole(packed.shape)],
        out_specs=[
            pl.BlockSpec((1, 1, width, tile), lambda e, f: (0, e, 0, f)),
            pl.BlockSpec((1, 1, tile, width), lambda e, f: (0, e, f, 0)),
        ]
        + [whole(dims) for dims in small],
        compiler_params=pltpu.CompilerParams(vmem_limit_bytes=48 * MIB),
        cost_estimate=pl.CostEstimate(
            flops=flops, bytes_accessed=8 * local * hidden * width, transcendentals=0
        ),
    )(*(in_hbm(state[name]) for name in ("kept_rows", "kept_pre", "kept_hidden", "kept_seen")), packed)


def norm_backward(values, gain, grad):
    factor = norm_factor(values)
    unit = values * factor
    weighted = grad * gain
    inner = jnp.mean(weighted * unit, axis=-1, keepdims=True)
    return factor * (weighted - unit * inner), jnp.sum(grad * unit, axis=0, keepdims=True)


def dense_backward_loads(geo, m, at, copies):
    width = geo.width
    return dict(
        rest=copies.load(at.packed.at[:, pl.ds(3 * width, width + 128)], at.rest_w),
        gains=copies.load(at.gains, at.gains_here),
        residual=copies.load(at.kept_residual.at[m], at.residual),
        qkv=copies.load(at.kept_qkv.at[m], at.qkv),
        prob=copies.load(at.kept_prob.at[m], at.prob),
        stream=copies.load(at.kept_stream.at[m], at.stream),
        qkv_w=copies.load(at.packed.at[:, pl.ds(0, 3 * width)], at.qkv_w),
    )


def dense_backward_part(geo, step, at, copies, loads, enter, across):
    length, width, heads = geo.length, geo.width, geo.heads
    size = width // heads
    per = 128 // size
    m = backward_micro(geo, step)
    send = across is not None
    aux = at.aux[...]
    slope = aux[:, 0:1] * aux[:, 1:2] * (at.gates[:, 0:1] - at.gates[:, 1:2])
    expert_at = iota((length, 128), 1).astype(F32)
    logit_grad = (
        jnp.where(as_column(at.routes[0, m, 0:1, :].astype(F32)) == expert_at, slope, 0.0)
        - jnp.where(as_column(at.routes[0, m, 1:2, :].astype(F32)) == expert_at, slope, 0.0)
    ).astype(BF16)
    at.logit[...] = logit_grad
    copies.save(at.logit, at.kept_logit.at[m])
    loads["rest"].wait()
    moe_grad = at.moe_grad[...] + mm(logit_grad, at.rest_w[:, width:], (1, 1))
    loads["residual"].wait()
    loads["gains"].wait()
    part, gain_two = norm_backward(at.residual[...], at.gains_here[1:2, :], moe_grad)
    residual_grad = at.incoming[...].astype(F32) + part
    at.branch[...] = residual_grad.astype(BF16)
    copies.save(at.branch, at.kept_branch.at[m])
    at.context_grad[...] = mm(at.branch[...], at.rest_w[:, :width], (1, 1)).astype(BF16)
    which = iota((length, 128), 1) // size
    head_row = iota((128, length), 0) // size
    scale = 1.0 / math.sqrt(size)
    zero = jnp.zeros((length, 128), BF16)
    loads["qkv"].wait()
    loads["prob"].wait()
    at.sums[...] = jnp.zeros(at.sums.shape, F32)
    for j in range(width // 128):
        places = [slice(base * width + 128 * j, base * width + 128 * (j + 1)) for base in range(3)]
        queries, keys, values = (at.qkv[:, place] for place in places)
        grad = at.context_grad[:, places[0]]
        turned_keys = keys.astype(F32).T
        totals = [jnp.zeros(dims, F32) for dims in ((128, length), (length, 128), (length, 128))]
        for part_at in range(per):
            h = j * per + part_at
            own = which == part_at
            own_grad = jnp.where(own, grad, zero)
            prob = at.prob[h]
            prob_grad = mm(values, own_grad, (1, 1))
            weighted = prob.astype(F32)
            shift = jnp.sum(weighted * prob_grad, axis=0, keepdims=True)
            score_grad = (weighted * (prob_grad - shift)).astype(BF16)
            at.sums[h : h + 1, :] = diagonal_sums(score_grad.astype(F32))
            own_keys = jnp.where(head_row == part_at, turned_keys, 0.0).astype(BF16)
            totals[0] = totals[0] + mm(own_keys, score_grad, (1, 0))
            totals[1] = totals[1] + mm(score_grad, jnp.where(own, queries, zero), (1, 0))
            totals[2] = totals[2] + mm(prob, own_grad, (1, 0))
        at.qkv_grad[:, places[0]] = (totals[0].T * scale).astype(BF16)
        at.qkv_grad[:, places[1]] = (totals[1] * scale).astype(BF16)
        at.qkv_grad[:, places[2]] = totals[2].astype(BF16)
    copies.save(at.qkv_grad, at.kept_qkv_grad.at[m])
    copies.save(at.sums, at.kept_sums.at[m])
    loads["qkv_w"].wait()
    normed_grad = mm(at.qkv_grad[...], at.qkv_w[...], (1, 1))
    loads["stream"].wait()
    part, gain_one = norm_backward(at.stream[...].astype(F32), at.gains_here[0:1, :], normed_grad)
    at.gain_parts[...] = jnp.zeros(at.gain_parts.shape, F32)
    at.gain_parts[0:1, :] = gain_one
    at.gain_parts[1:2, :] = gain_two
    copies.save(at.gain_parts, at.kept_gains.at[m])
    in_grad = residual_grad + part
    at.in_grad_here[...] = in_grad
    copies.save(at.in_grad_here, at.in_grad.at[m])
    if step < geo.micro:
        at.sent_here[...] = in_grad.astype(BF16)
    if send:
        enter()
        across.send(at.sent_here, at.received_out)
    elif step < geo.micro:
        copies.save(at.sent_here, at.sent_out)
    copies.wait()
    if send:
        across.take(at.received_out)
        across.sent(at.sent_here, at.received_out)


def dense_backward_body(geo, step, at):
    send = 1 <= step < geo.micro
    across = Across(1, at.across_sems) if send else None
    if send:
        across.greet()

    def enter():
        pl.semaphore_wait(pltpu.get_barrier_semaphore(), 1)

    m = backward_micro(geo, step)
    copies = Copies(at.sems)
    aux_load = copies.load(at.kept_aux.at[m], at.aux)
    loads = dense_backward_loads(geo, m, at, copies)
    aux_load.wait()
    dense_backward_part(geo, step, at, copies, loads, enter, across)


def dense_backward_scratch(geo):
    length, width, heads = geo.length, geo.width, geo.heads
    return dict(
        aux=pltpu.VMEM((length, 128), F32),
        rest_w=pltpu.VMEM((width, width + 128), BF16),
        qkv_w=pltpu.VMEM((width, 3 * width), BF16),
        residual=pltpu.VMEM((length, width), F32),
        qkv=pltpu.VMEM((length, 3 * width), BF16),
        prob=pltpu.VMEM((heads, length, length), BF16),
        stream=pltpu.VMEM((length, width), BF16),
        logit=pltpu.VMEM((length, 128), BF16),
        branch=pltpu.VMEM((length, width), BF16),
        context_grad=pltpu.VMEM((length, width), BF16),
        qkv_grad=pltpu.VMEM((length, 3 * width), BF16),
        sums=pltpu.VMEM((geo.tall, length), F32),
        gain_parts=pltpu.VMEM((8, width), F32),
        in_grad_here=pltpu.VMEM((length, width), F32),
        gains_here=pltpu.VMEM((8, width), F32),
        sent_here=pltpu.VMEM((length, width), BF16),
        sems=pltpu.SemaphoreType.DMA((20,)),
        across_sems=pltpu.SemaphoreType.DMA((4,)),
    )


def dense_backward_refs(geo, step, given, state):
    micro, length, width = geo.micro, geo.length, geo.width
    outs = {}
    if 1 <= step < micro:
        outs["received_out"] = pltpu.HBM((length, width), BF16)
    elif step < micro:
        outs["sent_out"] = pltpu.HBM((length, width), BF16)
    names = ("kept_aux", "kept_residual", "kept_qkv", "kept_prob", "kept_stream")
    held = dict({name: state[name] for name in names}, packed=given["packed"], gains=given["gains"])
    kept = dict(
        in_grad=((micro, length, width), F32),
        kept_branch=((micro, length, width), BF16),
        kept_qkv_grad=((micro, length, 3 * width), BF16),
        kept_logit=((micro, length, 128), BF16),
        kept_gains=((micro, 8, width), F32),
        kept_sums=((micro, geo.tall, length), F32),
    )
    return dict(routes=given["routes"]), held, outs, kept


def dense_backward(geo, step, near, given, state):
    more, held, outs, kept = dense_backward_refs(geo, step, given, state)
    params = {}
    if 1 <= step < geo.micro:
        params = dict(collective_id=5 + 2 * geo.micro + step, has_side_effects=True)
    return launch(
        partial(where_active, only_section(geo, geo.micro - step), partial(dense_backward_body, geo, step)),
        near=dict(near, **more),
        held=held,
        outs=outs,
        kept=kept,
        state=state,
        scratch=dense_backward_scratch(geo),
        cost=(3_000_000_000, 14_000_000),
        **params,
    )


DENSE_GRADS = ("normed", "qkv_grad", "context", "branch", "moe_in", "logit")


def dense_weights_body(geo, at):
    width = geo.width
    copies = Copies(at.sems)
    loads = {}
    for name in DENSE_GRADS + ("gains", "sums"):
        loads[name] = copies.load(getattr(at, "kept_" + name), getattr(at, name))

    def product(left, right):
        left, right = (ref[...].reshape(-1, ref.shape[-1]) for ref in (left, right))
        return mm(left, right, (0, 0))

    def ready(*names):
        for name in names:
            loads[name].wait()

    def put(places, block):
        block = block.astype(BF16)
        if len(at.part.shape) == 4:
            at.part[:, :, :, places] = block.reshape(at.part.shape[:3] + block.shape[1:])
        else:
            at.part[:, places] = block

    ready("normed", "qkv_grad")
    normed = at.normed[...].reshape(-1, width)
    for j in range(0, 3 * width, width):
        grad = at.qkv_grad[:, :, j : j + width].reshape(-1, width)
        put(slice(j, j + width), mm(normed, grad, (0, 0)))
    ready("context", "branch")
    put(slice(3 * width, 4 * width), product(at.context, at.branch))
    ready("moe_in", "logit", "gains", "sums")
    small = product(at.moe_in, at.logit)
    by_term = lax.dot_general(
        jnp.sum(at.sums[...], axis=0), at.spread[...].astype(F32), (((1,), (1,)), ((), ())),
        precision=lax.Precision.HIGHEST, preferred_element_type=F32,
    )
    bias_row = jnp.sum(by_term[: geo.heads] * at.head_pick[...], axis=0, keepdims=True)
    gain_rows = jnp.sum(at.gains[...], axis=0)
    place = iota((128, width), 0)
    rows = jnp.zeros((128, width), F32)
    for k, row in enumerate((gain_rows[0:1], gain_rows[1:2], bias_row)):
        rows = jnp.where(place == geo.experts_all + k, row, rows)
    put(slice(4 * width, None), small + rows.T)


def reduce_body(geo, at):
    shards = Shards(geo)
    shards.greet()
    dense_weights_body(geo, at)
    shards.await_greetings()
    reduce_part(shards, at)


def dense_weights(geo, head_pick, spread_table, state):
    held = {"kept_" + name: state["kept_" + name] for name in DENSE_GRADS + ("gains", "sums")}
    scratch = {name: pltpu.VMEM(held["kept_" + name].shape, BF16) for name in DENSE_GRADS}
    scratch.update(
        sems=pltpu.SemaphoreType.DMA((len(DENSE_GRADS) + 2,)),
        gains=pltpu.VMEM(state["kept_gains"].shape, F32), sums=pltpu.VMEM(state["kept_sums"].shape, F32),
    )
    share, total = geo.width // geo.sources, 4 * geo.width + 128
    parts = (geo.rows, geo.cols, share, total)
    fused = share % 16 == 0
    outs = dict(shard=shape((share, total), F32)) if fused else dict(part=shape((geo.width, total), BF16))
    params = {}
    if fused:
        scratch.update(reduce_scratch(geo, share, total), part=pltpu.VMEM(parts, BF16))
        params = dict(collective_id=2, has_side_effects=True)
    results = launch(
        partial(reduce_body if fused else dense_weights_body, geo),
        near=dict(head_pick=head_pick, spread=spread_table),
        held=held,
        outs=outs,
        scratch=scratch,
        spare=24,
        cost=(3_000_000_000, 10_000_000),
        **params,
    )
    if fused:
        return results["shard"]

    def body(at):
        shards = Shards(geo)
        shards.greet()
        shards.await_greetings()
        reduce_part(shards, at)

    return launch(
        body,
        near=dict(part=results["part"].reshape(parts)),
        outs=dict(shard=shape((share, total), F32)),
        scratch=reduce_scratch(geo, share, total),
        collective_id=2,
        has_side_effects=True,
    )["shard"]


def on_device(
    inputs, cotangent, segments, routes, order, attn_gain, qkv_weight, position_bias, out_weight, moe_gain,
    router_weight, expert_in, expert_out,
):
    micro, length, width = inputs.shape
    local_experts, hidden = expert_in.shape[1], expert_in.shape[3]
    experts_all = router_weight.shape[2]
    row_count, col_count = lax.axis_size("row"), lax.axis_size("col")
    devices = row_count * col_count
    share = width // devices
    terms = position_bias.shape[1]
    heads = terms * devices // DISTANCE_BUCKETS
    geo = Geometry(micro, length, width, heads, experts_all, local_experts, hidden, row_count, col_count)
    packed = gather_shards(
        geo, qkv_weight[0], out_weight[0], router_weight[0].T, attn_gain, moe_gain, position_bias
    ).reshape(width, -1)
    indicator = buckets(length)
    row_at = np.arange(width)
    term_at = np.where(row_at % share < terms, row_at // share * terms + row_at % share, -1)
    head_pick = jnp.asarray((term_at % heads == np.arange(heads)[:, None]) & (term_at >= 0), F32)
    spread_table = jnp.asarray(indicator[np.maximum(term_at, 0) // heads], BF16)
    prepared = launch(
        partial(prepare, experts_all),
        near=dict(head_pick=head_pick, spread=spread_table),
        held=dict(packed=packed),
        outs=dict(gains=pltpu.HBM((8, width), F32), bias=pltpu.HBM((heads, length, length), BF16)),
        scratch=dict(
            small=pltpu.VMEM((width, 128), BF16), gains_here=pltpu.VMEM((8, width), F32),
            bias_here=pltpu.VMEM((heads, length, length), BF16), sems=pltpu.SemaphoreType.DMA((3,)),
        ),
        cost=(50_000_000, 6_000_000),
    )
    given = dict(
        prepared, packed=packed, inputs=inputs, cotangent=cotangent, w_in=expert_in[0], w_out=expert_out[0],
        segments=segments, order=order, routes=jnp.swapaxes(routes, 2, 3),
        bases=jnp.asarray(geo.bases()),
    )
    state = {}
    received = None
    for tick in range(micro + 1):
        received = forward_tick(geo, tick, given, state, received)
    sent = received = None
    for step in range(micro + 1):
        passed = backward_step(geo, step, given, state, sent, received)
        sent, received = passed.get("sent_out"), passed.get("received_out")
    packed = dense_weights(geo, head_pick, spread_table, state)
    expert_in_grad, expert_out_grad, qkv, out, router, gain_one, gain_two, bias = expert_weights(
        geo, state, packed, terms
    )
    return (
        state["out"][None], state["in_grad"][None], gain_one, qkv, bias, out, gain_two,
        jnp.swapaxes(router, 1, 2), expert_in_grad,
        expert_out_grad,
    )


def solution(mesh):
    tokens = ("row", "col")
    return jax.shard_map(
        on_device,
        mesh=mesh,
        in_specs=(
            P(None, tokens, None),
            P(None, tokens, None),
            P(None, tokens),
            P("section", None, tokens, None),
            P("section", None, tokens, None),
            P("section", tokens),
            P("section", tokens, None),
            P("section", tokens),
            P("section", tokens, None),
            P("section", tokens),
            P("section", tokens, None),
            P("section", "row", None, "col"),
            P("section", "row", "col", None),
        ),
        out_specs=(
            P("section", None, tokens, None),
            P("section", None, tokens, None),
            P("section", tokens),
            P("section", tokens, None),
            P("section", tokens),
            P("section", tokens, None),
            P("section", tokens),
            P("section", tokens, None),
            P("section", "row", None, "col"),
            P("section", "row", "col", None),
        ),
        check_vma=False,
    )
```

```python
from functools import partial
import math
from types import SimpleNamespace

import jax
import jax.numpy as jnp
import numpy as np
from jax import lax
from jax.experimental import pallas as pl
from jax.experimental.pallas import tpu as pltpu
from jax.sharding import PartitionSpec as P

TOP = 2
DISTANCE_BUCKETS = 32
MAX_DIST = 128
EPS = 1e-06
MESH = pl.DeviceIdType.MESH
F32 = jnp.float32
BF16 = jnp.bfloat16
MIB = 1 << 20


class Geometry:
    def __init__(self, micro, length, width, heads, experts_all, local_experts, hidden, row_count, col_count):
        self.micro, self.length, self.width, self.heads, self.hidden = micro, length, width, heads, hidden
        self.tall = -(-heads // 8) * 8
        self.capacity = max(2, (5 * length * TOP + 4 * experts_all - 1) // (4 * experts_all))
        self.local_experts = local_experts
        self.experts_all = experts_all
        self.rows, self.cols = row_count, col_count
        self.cores = 2 if row_count % 2 == 0 else 1
        self.chips = row_count // self.cores
        main = self.capacity // 16 * 16
        rest = self.capacity - main
        self.share = main // local_experts if 0 < rest <= main // local_experts else 0
        if rest and not self.share:
            main += 16
        self.main = main
        self.first = 1 if self.share else 0
        self.units = local_experts + self.first
        self.slots = row_count * self.units * main
        self.sources = row_count * col_count
        self.expert_rows = self.sources * (main + self.share)

    def bases(self):
        expert = np.arange(self.experts_all)
        owner, local = expert // self.local_experts, expert % self.local_experts
        main = ((self.first + local) * self.rows + owner) * self.main
        tail = owner * self.main + local * self.share
        both = np.stack([main, tail]).astype(np.float32)
        return np.pad(both, ((0, 0), (0, 128 - self.experts_all)))


def buckets(length):
    distance = np.arange(length)
    bucket = np.zeros(length, np.int64)
    half = DISTANCE_BUCKETS // 2
    for level in range(1, DISTANCE_BUCKETS):
        if level < half:
            limit = level
        else:
            limit = int(math.ceil(half * (MAX_DIST / half) ** ((level - half) / half)))
        bucket += distance >= limit
    return (np.arange(DISTANCE_BUCKETS)[:, None] == bucket[None, :]).astype(np.float32)


def mm(left, right, contract):
    return lax.dot_general(
        left, right, (((contract[0],), (contract[1],)), ((), ())), preferred_element_type=F32
    )


def iota(shape, axis):
    return lax.broadcasted_iota(jnp.int32, shape, axis)


def norm_factor(values):
    return lax.rsqrt(jnp.mean(values * values, axis=-1, keepdims=True) + EPS)


def gelu_pair(x):
    density = jnp.exp(-0.5 * x * x)
    t = 1.0 / (1.0 + (0.3275911 * math.sqrt(0.5)) * jnp.abs(x))
    poly = 0.5 * 1.061405429
    for coefficient in (-1.453152027, 1.421413741, -0.284496736, 0.254829592):
        poly = poly * t + 0.5 * coefficient
    beyond = poly * t * density
    cdf = jnp.where(x >= 0, 1.0 - beyond, beyond)
    return x * cdf, cdf + x * density * (1.0 / math.sqrt(2.0 * math.pi))


def slot_onehots(aux, slots):
    positions = iota((aux.shape[0], slots), 1).astype(F32)
    return [(aux[:, 2 + c : 3 + c] == positions) for c in range(TOP)]


def vmem_grant(scratch, spare):
    held = 0
    for ref in scratch:
        if getattr(ref, "memory_space", None) == pltpu.VMEM:
            held += math.prod(ref.shape) * jnp.dtype(ref.dtype).itemsize
    return -(-held // MIB) + spare


def fits(*scratches):
    return vmem_grant([ref for scratch in scratches for ref in scratch.values()], 11) <= 62


def vmem_spec():
    return pl.BlockSpec(memory_space=pltpu.VMEM)


def hbm_spec():
    return pl.BlockSpec(memory_space=pltpu.HBM)


def in_hbm(array):
    return pltpu.with_memory_space_constraint(array, pltpu.HBM)


def shape(dims, kind):
    return jax.ShapeDtypeStruct(dims, kind)


def launch(body, near=None, held=None, outs=None, kept=None, state=None, scratch=None, spare=10, cost=None, **params):
    near, held, outs, kept, scratch = (dict(part or {}) for part in (near, held, outs, kept, scratch))
    state = {} if state is None else state
    old = [name for name in kept if name in state]
    names_in, names_out = list(near) + list(held), list(outs) + list(kept)

    def kernel(*refs):
        refs = list(refs)
        given, refs = refs[: len(names_in)], refs[len(names_in) + len(old) :]
        body(SimpleNamespace(**dict(zip(names_in + names_out + list(scratch), given + refs))))

    out_shapes = list(outs.values()) + [pltpu.HBM(dims, kind) for dims, kind in kept.values()]
    plain = [isinstance(out, jax.ShapeDtypeStruct) for out in out_shapes]
    estimate = {}
    if cost is not None:
        estimate["cost_estimate"] = pl.CostEstimate(flops=cost[0], bytes_accessed=cost[1], transcendentals=0)
    results = pl.pallas_call(
        kernel,
        out_shape=out_shapes,
        in_specs=[vmem_spec()] * len(near) + [hbm_spec()] * (len(held) + len(old)),
        out_specs=[vmem_spec() if near_by else hbm_spec() for near_by in plain],
        scratch_shapes=list(scratch.values()),
        input_output_aliases={len(names_in) + i: names_out.index(name) for i, name in enumerate(old)},
        compiler_params=pltpu.CompilerParams(
            vmem_limit_bytes=vmem_grant(scratch.values(), spare) * MIB, **params
        ),
        **estimate,
    )(*near.values(), *map(in_hbm, held.values()), *(in_hbm(state[name]) for name in old))
    results = dict(zip(names_out, results))
    for name in kept:
        state[name] = results.pop(name)
    return results


def of_micro(rows, m):
    if isinstance(m, int):
        return rows[m : m + 1]
    row = rows[0:1]
    for i in range(1, rows.shape[0]):
        row = jnp.where(m == i, rows[i : i + 1], row)
    return row


def as_column(row):
    return jnp.broadcast_to(row, (8, row.shape[1])).T[:, 0:1]


class Copies:
    def __init__(self, sems):
        self.sems, self.count, self.open = sems, 0, []

    def load(self, source, target):
        copy = pltpu.make_async_copy(source, target, self.sems.at[self.count])
        self.count += 1
        copy.start()
        return copy

    def save(self, source, target):
        self.open.append(self.load(source, target))

    def wait(self):
        for copy in self.open:
            copy.wait()


def remote(source, target, send, receive, where):
    return pltpu.make_async_remote_copy(
        src_ref=source, dst_ref=target, send_sem=send, recv_sem=receive, device_id=where, device_id_type=MESH
    )


def forward_micro(geo, tick):
    if tick == 0:
        return 0
    return geo.micro - 1 if tick == geo.micro else tick - lax.axis_index("section")


def backward_micro(geo, step):
    if step == 0:
        return geo.micro - 1
    return 0 if step == geo.micro else geo.micro - step - lax.axis_index("section")


class Across:
    def __init__(self, sender, sems, at=0):
        self.section = lax.axis_index("section")
        self.sender, self.other = sender, {"section": 1 - self.section}
        self.send_sem, self.recv_sem = sems.at[at], sems.at[at + 1]

    def greet(self):
        pl.semaphore_signal(pltpu.get_barrier_semaphore(), inc=1, device_id=self.other, device_id_type=MESH)

    def copy(self, source, target):
        return remote(source, target, self.send_sem, self.recv_sem, self.other)

    def send(self, source, target):
        @pl.when(self.section == self.sender)
        def _():
            self.copy(source, target).start()

    def sent(self, source, target):
        @pl.when(self.section == self.sender)
        def _():
            self.copy(source, target).wait_send()

    def take(self, target):
        @pl.when(self.section != self.sender)
        def _():
            self.copy(target, target).wait_recv()


def prepare(experts_all, at):
    heads, length = at.bias_here.shape[:2]
    width = at.small.shape[0]
    copies = Copies(at.sems)
    copies.load(at.packed.at[:, pl.ds(4 * width, 128)], at.small).wait()
    rows = at.small[...].astype(F32).T
    at.gains_here[0:2, :] = rows[experts_all : experts_all + 2]
    copies.save(at.gains_here, at.gains)
    picked = (at.head_pick[...] * rows[experts_all + 2 : experts_all + 3]).astype(BF16)
    by_distance = mm(picked, at.spread[...], (1, 0))
    for h in range(heads):
        block = by_distance[h : h + 1, :]
        step = 1
        while step < length:
            block = jnp.concatenate([block, pltpu.roll(block, step, 1)], axis=0)
            step *= 2
        at.bias_here[h] = block.astype(BF16)
    copies.save(at.bias_here, at.bias)
    copies.wait()


def diagonal_sums(block):
    length = block.shape[1]
    size = block.shape[0] // 2
    while size >= 1:
        block = block[:size] + pltpu.roll(block[size:], length - size, 1)
        size //= 2
    return block


def only_section(geo, tick):
    return {0: 0, geo.micro: 1}.get(tick)


def where_active(active, body, at):
    if active is None:
        body(at)
    else:
        pl.when(lax.axis_index("section") == active)(partial(body, at))


def dense_forward_part(geo, tick, at, copies, enter, across, loaded, fused=True):
    length, width, heads = geo.length, geo.width, geo.heads
    size = width // heads
    per = 128 // size
    m = forward_micro(geo, tick)
    gains_load = copies.load(at.gains, at.gains_here)
    thirds = [pl.ds(third * width, width) for third in range(3)]
    packed_qkv = [copies.load(at.packed.at[:, third], at.qkv_w.at[:, third]) for third in thirds]
    if tick == 0:
        copies.load(at.inputs.at[m], at.stream).wait()
    else:
        first = lax.axis_index("section") == 0
        own = pltpu.make_async_copy(at.inputs.at[m], at.stream, at.stream_sem)
        if tick == 1:
            enter()
            across.send(at.out.at[0] if fused else at.out_before.at[0], at.stream_in)
        else:
            came = pltpu.make_async_copy(at.received, at.stream, at.stream_sem)

        @pl.when(first)
        def _():
            own.start()
            own.wait()

        if tick == 1:
            across.take(at.stream_in)

            @pl.when(jnp.logical_not(first))
            def _():
                at.stream[...] = at.stream_in[...]
        else:

            @pl.when(jnp.logical_not(first))
            def _():
                came.start()
                came.wait()

    packed_rest = copies.load(at.packed.at[:, pl.ds(3 * width, width + 128)], at.rest_w)
    bias_load = copies.load(at.bias, at.bias_here)
    copies.save(at.stream, at.kept_stream.at[m])
    stream = at.stream[...].astype(F32)
    gains_load.wait()
    at.normed[...] = (stream * norm_factor(stream) * at.gains_here[0:1, :]).astype(BF16)
    copies.save(at.normed, at.kept_normed.at[m])
    for third, load in zip(thirds, packed_qkv):
        load.wait()
        at.qkv[:, third] = mm(at.normed[...], at.qkv_w[:, third], (1, 0)).astype(BF16)
    copies.save(at.qkv, at.kept_qkv.at[m])
    key_at, query_at = iota((length, length), 0), iota((length, length), 1)
    segments = of_micro(at.segments[...], m).astype(F32)
    allowed = (key_at <= query_at) & (as_column(segments) == segments)
    which = iota((length, 128), 1) // size
    head_row = iota((128, length), 0) // size
    scale = 1.0 / math.sqrt(size)
    zero = jnp.zeros((length, 128), BF16)
    bias_load.wait()
    for j in range(width // 128):
        queries = at.qkv[:, 128 * j : 128 * (j + 1)]
        keys = at.qkv[:, width + 128 * j : width + 128 * (j + 1)]
        values = at.qkv[:, 2 * width + 128 * j : 2 * width + 128 * (j + 1)]
        turned_values = values.astype(F32).T
        context = jnp.zeros((128, length), F32)
        for part in range(per):
            h = j * per + part
            own = which == part
            scores = mm(jnp.where(own, keys, zero), queries, (1, 1)) * scale + at.bias_here[h].astype(F32)
            scores = jnp.where(allowed, scores, -1e30)
            exponent = jnp.exp(scores - jnp.max(scores, axis=0, keepdims=True))
            prob = (exponent * (1.0 / jnp.sum(exponent, axis=0, keepdims=True))).astype(BF16)
            at.prob[h] = prob
            own_values = jnp.where(head_row == part, turned_values, 0.0).astype(BF16)
            context = context + mm(own_values, prob, (1, 0))
        at.context[:, 128 * j : 128 * (j + 1)] = context.T.astype(BF16)
    copies.save(at.prob, at.kept_prob.at[m])
    copies.save(at.context, at.kept_context.at[m])
    packed_rest.wait()
    loaded()
    residual = stream + mm(at.context[...], at.rest_w[:, :width], (1, 0))
    at.residual[...] = residual
    copies.save(at.residual, at.kept_residual.at[m])
    moe_in = (residual * norm_factor(residual) * at.gains_here[1:2, :]).astype(BF16)
    at.moe_in[...] = moe_in
    copies.save(at.moe_in, at.kept_moe_in.at[m])
    logits = mm(moe_in, at.rest_w[:, width:], (1, 0))
    expert_at = iota(logits.shape, 1)
    picks = [(as_column(at.routes[0, m, c : c + 1, :].astype(F32)) == expert_at.astype(F32)).astype(F32) for c in range(TOP)]
    chosen = [jnp.sum(pick * logits, axis=1, keepdims=True) for pick in picks]
    top = jnp.maximum(chosen[0], chosen[1])
    powers = [jnp.exp(value - top) for value in chosen]
    total = powers[0] + powers[1]
    shares = [power / total for power in powers]
    order = of_micro(at.order[0, :, 0, :], m).astype(F32)
    before = (order < as_column(order)).astype(BF16)
    counts = [mm(before, pick.astype(BF16), (1, 0)) for pick in picks]
    counts[1] = counts[1] + jnp.sum(picks[0], axis=0, keepdims=True)
    slots = []
    for pick, count in zip(picks, counts):
        rank = jnp.sum(pick * count, axis=1, keepdims=True)
        main = jnp.sum(pick * at.bases[0:1, :], axis=1, keepdims=True)
        tail = jnp.sum(pick * at.bases[1:2, :], axis=1, keepdims=True)
        place = jnp.where(rank < geo.main, main + rank, tail + rank - geo.main)
        slots.append(jnp.where(rank < geo.capacity, place, -1.0))
    lane = iota((length, 128), 1)
    aux = jnp.zeros((length, 128), F32)
    for place, value in enumerate(shares + slots):
        aux = jnp.where(lane == place, value, aux)
    at.aux[...] = aux
    copies.save(at.aux, at.kept_aux.at[m])
    first, second = slot_onehots(aux, geo.slots)
    at.slots[...] = mm((first | second).astype(BF16), moe_in, (0, 0)).astype(BF16).reshape(at.slots.shape)


def dense_forward_body(geo, tick, at):
    across = Across(0, at.across_sems) if tick == 1 else None
    if across:
        across.greet()

    def enter():
        pl.semaphore_wait(pltpu.get_barrier_semaphore(), 1)

    copies = Copies(at.sems)
    dense_forward_part(geo, tick, at, copies, enter, across, lambda: None, fused=False)
    copies.save(at.slots, at.slot_rows)
    copies.wait()
    if across:
        across.sent(at.out_before.at[0], at.stream_in)


def dense_forward_scratch(geo, tick):
    length, width, heads = geo.length, geo.width, geo.heads
    scratch = dict(
        stream=pltpu.VMEM((length, width), BF16),
        qkv_w=pltpu.VMEM((width, 3 * width), BF16),
        rest_w=pltpu.VMEM((width, width + 128), BF16),
        bias_here=pltpu.VMEM((heads, length, length), BF16),
        normed=pltpu.VMEM((length, width), BF16),
        qkv=pltpu.VMEM((length, 3 * width), BF16),
        prob=pltpu.VMEM((heads, length, length), BF16),
        context=pltpu.VMEM((length, width), BF16),
        residual=pltpu.VMEM((length, width), F32),
        moe_in=pltpu.VMEM((length, width), BF16),
        aux=pltpu.VMEM((length, 128), F32),
        slots=pltpu.VMEM((geo.units, geo.rows, geo.main, width), BF16),
        gains_here=pltpu.VMEM((8, width), F32),
        sems=pltpu.SemaphoreType.DMA((20 + width // 128,)),
        stream_sem=pltpu.SemaphoreType.DMA,
        across_sems=pltpu.SemaphoreType.DMA((4,)),
    )
    if tick == 1:
        scratch["stream_in"] = pltpu.VMEM((length, width), BF16)
    return scratch


def dense_forward_refs(geo, tick, given, state, received):
    micro, length, width, heads = geo.micro, geo.length, geo.width, geo.heads
    near = {name: given[name] for name in ("segments", "order", "routes", "bases")}
    held = {name: given[name] for name in ("packed", "bias", "inputs", "gains")}
    if tick > 1:
        held["received"] = received
    kept = dict(
        kept_stream=((micro, length, width), BF16),
        kept_normed=((micro, length, width), BF16),
        kept_qkv=((micro, length, 3 * width), BF16),
        kept_prob=((micro, heads, length, length), BF16),
        kept_context=((micro, length, width), BF16),
        kept_residual=((micro, length, width), F32),
        kept_moe_in=((micro, length, width), BF16),
        kept_aux=((micro, length, 128), F32),
    )
    return near, held, kept


def dense_forward(geo, tick, given, state, received):
    near, held, kept = dense_forward_refs(geo, tick, given, state, received)
    params = {}
    if tick == 1:
        held["out_before"] = state["out"]
        params = dict(collective_id=5 + 2 * geo.micro, has_side_effects=True)
    return launch(
        partial(where_active, only_section(geo, tick), partial(dense_forward_body, geo, tick)),
        near=near,
        held=held,
        outs=dict(slot_rows=pltpu.HBM((geo.units, geo.rows, geo.main, geo.width), BF16)),
        kept=kept,
        state=state,
        scratch=dense_forward_scratch(geo, tick),
        cost=(2_000_000_000, 14_000_000),
        **params,
    )["slot_rows"]


def combine(home, aux, result, picked_ref):
    for c, onehot in enumerate(slot_onehots(aux, home.shape[0])):
        picked = mm(onehot.astype(BF16), home, (1, 0))
        picked_ref[c] = picked.astype(BF16)
        result = result + aux[:, c : c + 1] * picked
    return result


def spread(incoming, aux, slots):
    total = 0.0
    for c, onehot in enumerate(slot_onehots(aux, slots)):
        total = total + mm(onehot.astype(BF16), (aux[:, c : c + 1] * incoming).astype(BF16), (0, 0))
    return total.astype(BF16)


def gate_gradients(incoming, picked_ref):
    lane = iota((incoming.shape[0], 128), 1)
    gates = jnp.zeros(lane.shape, F32)
    for c in range(TOP):
        gate = jnp.sum(picked_ref[c].astype(F32) * incoming, axis=1, keepdims=True)
        gates = jnp.where(lane == c, gate, gates)
    return gates


def expert_picker(geo, e):
    dims = (geo.sources * geo.share, geo.sources * geo.main)
    own, place = iota(dims, 0), iota(dims, 1)
    return (place == own // geo.share * geo.main + e * geo.share + own % geo.share).astype(BF16)


class Exchange:
    def __init__(self, geo, at, x, active=None):
        self.geo, self.x, self.at = geo, x, at
        self.relay = geo.chips // 2 if active is not None and geo.chips > 1 else None
        self.near_rows = geo.cores
        self.ahead = 2 if self.relay else 1
        self.peers = geo.cols - 1
        self.other = {"section": 1 - lax.axis_index("section")}
        self.r, self.c = lax.axis_index("row"), lax.axis_index("col")
        self.z, self.core = self.r // geo.cores, self.r % geo.cores
        self.partner = self.z * geo.cores + (self.core + 1) % geo.cores

    def far(self, direct):
        chips = sorted(range(1, self.geo.chips), key=lambda k: abs(2 * k - self.geo.chips))
        return [k for k in chips if direct or k != self.relay]

    def far_rows(self, direct):
        return self.geo.cores * len(self.far(direct))

    def kinds(self):
        first = self.geo.first if self.relay else 0
        return [(pl.ds(at, n), direct) for at, n, direct in ((0, first, True), (first, self.geo.units - first, False)) if n]

    def chip(self, k):
        return (self.z + k + self.geo.chips) % self.geo.chips

    def row(self, k, d):
        return self.partner if k == 0 else self.chip(k) * self.geo.cores + d

    def col(self, j):
        return (self.c + j + self.geo.cols) % self.geo.cols

    def rows(self, k):
        return pl.ds(self.chip(k) * self.geo.cores, self.geo.cores)

    def others(self, k):
        return range(self.geo.cores - 1) if k == 0 else range(self.geo.cores)

    def greet(self):
        barrier = pltpu.get_barrier_semaphore()
        for k in range(self.geo.chips):
            for d in self.others(k):
                pl.semaphore_signal(barrier, inc=1, device_id={"row": self.row(k, d)}, device_id_type=MESH)
        for j in range(1, self.geo.cols):
            pl.semaphore_signal(barrier, inc=1, device_id={"col": self.col(j)}, device_id_type=MESH)
        if self.relay:
            pl.semaphore_signal(barrier, inc=1, device_id=self.other, device_id_type=MESH)

    def await_greetings(self, more):
        more = more + (1 if self.relay else 0)
        pl.semaphore_wait(pltpu.get_barrier_semaphore(), self.geo.rows + self.geo.cols - 2 + more)

    def came(self, block, sem):
        remote(block, block, self.at.done, sem, self.other).wait_recv()

    def left(self, block, sem):
        remote(block, block, sem, self.at.done, self.other).wait_send()


    def own(self, u):
        return pltpu.make_async_copy(
            self.x.at[u, self.r], self.at.inbox.at[u, self.c, self.r], self.at.own_sem.at[u]
        )

    def kind(self, u):
        if not (self.relay and self.geo.first):
            return 0
        return int(u < self.geo.first) if isinstance(u, int) else (u + self.geo.units - 1) // self.geo.units * -1 + 1

    def send(self, u, k):
        for d in self.others(k):
            remote(
                self.x.at[u, self.row(k, d)], self.at.inbox.at[u, self.c, self.r], self.at.in_send.at[self.kind(u)],
                self.at.in_recv.at[u, k], {"row": self.row(k, d)},
            ).start()

    def send_out(self, u):
        if self.relay:
            remote(
                self.x.at[u, self.rows(self.relay)], self.at.via_x.at[u], self.at.via_send,
                self.at.via_x_recv.at[u], self.other,
            ).start()

    def hand_over(self, u, k):
        block = self.at.inbox.at[u, self.c, self.rows(-k)]
        for j in range(1, self.geo.cols):
            remote(block, block, self.at.pass_send.at[u], self.at.pass_recv.at[u], {"col": self.col(j)}).start()

    def each(self, body):
        lax.fori_loop(0, self.geo.units, lambda u, carry: (body(u), carry)[1], 0)

    def open(self):
        for u in range(min(self.ahead, self.geo.units)):
            direct = u < self.geo.first
            for k in self.far(direct):
                self.send(u, k)
            if not direct:
                self.send_out(u)

        def body(u):
            self.own(u).start()
            self.send(u, 0)

        self.each(body)
        for u in range(min(3, self.geo.units)):
            self.pass_on_own(u)

    def pass_on_own(self, u):
        self.own(u).wait()
        if self.geo.cores > 1:
            self.came(self.at.inbox.at[u, self.c, pl.ds(0, 1)], self.at.in_recv.at[u, 0])
        self.hand_over(u, 0)

    def pass_on(self, u, direct=False):
        @pl.when(u + self.ahead < self.geo.units)
        def _():
            self.send_out(u + self.ahead)

        for k in self.far(direct):
            self.came(self.at.inbox.at[u, self.c, self.rows(-k)], self.at.in_recv.at[u, k])

            @pl.when(u + self.ahead < self.geo.units)
            def _():
                if k in self.far(False):
                    self.send(u + self.ahead, k)

            self.hand_over(u, k)

        @pl.when(u + 3 < self.geo.units)
        def _():
            self.pass_on_own(u + 3)

    def collect(self, u, direct=False):
        if self.peers:
            block = self.at.inbox.at[u, pl.ds(0, self.peers), pl.ds(0, self.near_rows + self.far_rows(direct))]
            self.came(block, self.at.pass_recv.at[u])
            self.left(block, self.at.pass_send.at[u])
        if self.relay and not direct:
            self.came(self.at.inbox.at[u, :, pl.ds(0, self.geo.cores)], self.at.into_recv.at[u])


    def send_parts(self, u, far, direct=False):
        if far and self.relay and not direct:
            for j in range(self.geo.cols):
                remote(
                    self.at.inbox.at[u, self.col(j), self.rows(self.relay)], self.at.via_part.at[u, j],
                    self.at.via_part_send, self.at.via_part_recv.at[u], self.other,
                ).start()
        for k in self.far(direct) if far else (0,):
            for j in range(1, self.geo.cols):
                remote(
                    self.at.inbox.at[u, self.col(j), self.rows(k)], self.at.arrived.at[u, j - 1, self.rows(k)],
                    self.at.out_send.at[self.kind(u)], self.at.out_recv.at[u, k], {"col": self.col(j)},
                ).start()

    def send_home(self, u, far, direct=False):
        for k in self.far(direct) if far else (0,):
            rows = self.rows(k)
            if self.peers:
                self.came(self.at.arrived.at[u, :, rows], self.at.out_recv.at[u, k])
            total = self.at.inbox[u, self.c, rows].astype(F32)
            for j in range(1, self.geo.cols):
                total = total + self.at.arrived[u, j - 1, rows].astype(F32)
            self.at.stage[u, rows] = total.astype(BF16)
            for d in self.others(k):
                remote(
                    self.at.stage.at[u, self.row(k, d)], self.at.home.at[u, self.r], self.at.home_send.at[self.kind(u)],
                    self.at.home_recv.at[self.kind(u)], {"row": self.row(k, d)},
                ).start()
            if k == 0:
                self.at.home[u, self.r] = self.at.stage[u, self.r]

    def finish(self):
        at, cores = self.at, self.geo.cores
        for units, direct in self.kinds():
            sent_rows = self.far_rows(direct) + cores - 1
            if sent_rows:
                block = at.home.at[units, pl.ds(0, sent_rows)]
                self.came(block, at.home_recv.at[int(direct)])
                self.left(block, at.home_send.at[int(direct)])
                self.left(block, at.in_send.at[int(direct)])
            if self.peers:
                block = at.arrived.at[units, :, pl.ds(0, self.near_rows + self.far_rows(direct))]
                self.left(block, at.out_send.at[int(direct)])
            if self.relay and not direct:
                self.came(at.home.at[units, pl.ds(0, cores)], at.home_in_recv)
                self.left(at.via_x.at[units], at.via_send)
                self.left(at.via_part.at[units], at.via_part_send)


    def along(self, u, d, source, target, at):
        where = {"row": self.row(self.relay, d)}
        return remote(
            source.at[u, d], target.at[u, self.core], self.at.core_sems.at[at, u, d],
            self.at.core_sems.at[at + 1, u, self.core], where,
        )

    def along_came(self, u, d, target, at):
        self.came(target.at[u, d], self.at.core_sems.at[at + 1, u, d])

    def across(self, u, j):
        return remote(
            self.at.via_z.at[u], self.at.via_y.at[u, j - 1], self.at.via_sems.at[2, u, j], self.at.via_sems.at[3, u, j],
            {"col": self.col(j)},
        )

    def into(self, u, j):
        source = self.at.via_y.at[u, j - 1] if j else self.at.via_z.at[u]
        target = self.at.inbox.at[u, self.col(-j), self.rows(-self.relay)]
        return remote(source, target, self.at.via_sems.at[0, u, j], self.at.into_recv.at[u], self.other)

    def part_across(self, u, j):
        return remote(
            self.at.via_part.at[u, j], self.at.via_sum.at[u, j - 1], self.at.via_sems.at[4, u, j],
            self.at.via_sems.at[5, u, j], {"col": self.col(j)},
        )

    def home_in(self, u):
        return remote(
            self.at.via_home.at[u], self.at.home.at[u, self.rows(-self.relay)], self.at.via_sems.at[1, u, 0],
            self.at.home_in_recv, self.other,
        )

    def carry(self):
        geo, at = self.geo, self.at
        cores, columns = range(geo.cores), range(1, geo.cols)

        def rows_out(u):
            self.came(at.via_x.at[u], at.via_x_recv.at[u])
            for d in cores:
                self.along(u, d, at.via_x, at.via_z, 0).start()

        def rows_on(u):
            for d in cores:
                self.along_came(u, d, at.via_z, 0)
            self.into(u, 0).start()
            for j in columns:
                self.across(u, j).start()

        def rows_in(u):
            for j in columns:
                self.across(u, j).wait_recv()
                self.into(u, j).start()

        def parts_out(u):
            self.came(at.via_part.at[u], at.via_part_recv.at[u])
            for j in columns:
                self.part_across(u, j).start()

        def parts_on(u):
            total = at.via_part[u, 0].astype(F32)
            for j in columns:
                self.part_across(u, j).wait_recv()
                total = total + at.via_sum[u, j - 1].astype(F32)
            at.via_total[u] = total.astype(BF16)
            for d in cores:
                self.along(u, d, at.via_total, at.via_home, 2).start()

        def parts_in(u):
            for d in cores:
                self.along_came(u, d, at.via_home, 2)
            self.home_in(u).start()

        units = list(range(geo.first, geo.units))
        for steps in ((rows_out, rows_on, rows_in), (parts_out, parts_on, parts_in)):
            for t in range(len(units) + 2):
                for lag, work in enumerate(steps):
                    if 0 <= t - lag < len(units):
                        work(units[t - lag])
        for u in units:
            for d in cores:
                self.along(u, d, at.via_x, at.via_z, 0).wait_send()
                self.along(u, d, at.via_total, at.via_home, 2).wait_send()
            for j in range(geo.cols):
                self.into(u, j).wait_send()
            for j in columns:
                self.across(u, j).wait_send()
                self.part_across(u, j).wait_send()
            self.home_in(u).wait_send()


def run_experts(geo, exchange, rows, total, shared, loads, expert, saves, opened=lambda: None):
    first, count = geo.first, geo.sources * geo.main
    inbox = exchange.at.inbox
    width = inbox.shape[-1]
    exchange.open()
    opened()
    if first:
        exchange.pass_on(0, True)
    exchange.pass_on(first)
    if first:
        exchange.collect(0, True)
        shared[...] = jnp.zeros(shared.shape, F32)

    def step(e, carry):
        u = e + first
        slot = e % 2

        @pl.when(e + 1 < geo.local_experts)
        def _():
            exchange.pass_on(u + 1)

        exchange.collect(u)

        @pl.when(e >= 2)
        def _():
            for copy in saves(e - 2, slot):
                copy.wait()

        rows[slot, :count] = inbox[u].reshape(count, width)
        if first:
            picker = expert_picker(geo, e)
            tail = inbox[0].reshape(count, width)
            rows[slot, count:] = mm(picker, tail, (1, 0)).astype(BF16)
        for copy in loads(e):
            copy.wait()
        expert(e, slot)
        for copy in saves(e, slot):
            copy.start()
        inbox[u] = total[:count].astype(BF16).reshape(inbox.shape[1:])
        exchange.send_parts(u, True)
        if first:
            shared[...] += mm(picker, total[count:].astype(BF16), (0, 0))

        @pl.when(e >= 1)
        def _():
            exchange.send_home(u - 1, True)
            if exchange.relay:
                exchange.send_parts(u - 1, False)

        return carry

    lax.fori_loop(0, geo.local_experts, step, 0)
    if first:
        inbox[0] = shared[...].astype(BF16).reshape(inbox.shape[1:])
        exchange.send_parts(0, True, True)
    near = [u for u in range(geo.units) if not exchange.relay or u < first or u == geo.units - 1]
    half = len(near) // 2
    exchange.send_home(geo.units - 1, True)
    for u in near[half:]:
        exchange.send_parts(u, False)
    if first:
        exchange.send_home(0, True, True)
    for u in near[:half]:
        exchange.send_parts(u, False)
    exchange.each(lambda u: exchange.send_home(u, False))
    for e in range(max(0, geo.local_experts - 2), geo.local_experts):
        for copy in saves(e, e % 2):
            copy.wait()
    exchange.finish()


def share_work(exchange, active, work):
    if not exchange.relay:
        work()
        return
    section = lax.axis_index("section")
    pl.when(section == active)(work)

    @pl.when(section != active)
    def _():
        exchange.await_greetings(0)
        exchange.carry()


def start_loads(geo, loads):
    for e in range(geo.local_experts):
        for copy in loads(e):
            copy.start()


def forward_body(geo, tick, tile, fused, at):
    m = forward_micro(geo, tick)
    take, send = fused and tick == 1, 1 <= tick < geo.micro
    active = only_section(geo, tick)
    exchange = Exchange(geo, at, at.slots if fused else at.slot_rows, active)
    exchange.greet()
    across_in, across_out = Across(0, at.across_sems, 2), Across(0, at.across_sems)
    if take or send:
        across_out.greet()
    w_in, w_out = at.w_in_here, at.w_out_here

    def loads(e):
        return (
            pltpu.make_async_copy(at.w_in.at[e], w_in.at[e], at.load_sem.at[e, 0]),
            pltpu.make_async_copy(at.w_out.at[e], w_out.at[e], at.load_sem.at[e, 1]),
        )

    def saves(e, slot):
        return (
            pltpu.make_async_copy(at.rows.at[slot], at.kept_rows.at[m, e], at.save_sem.at[slot, 0]),
            pltpu.make_async_copy(at.wide.at[slot], at.kept_hidden.at[m, e], at.save_sem.at[slot, 1]),
            pltpu.make_async_copy(at.slope.at[slot], at.kept_slope.at[m, e], at.save_sem.at[slot, 2]),
        )

    def expert(e, slot):
        for f in range(0, geo.hidden, tile):
            value, derivative = gelu_pair(mm(at.rows[slot], w_in[e, :, f : f + tile], (1, 0)))
            value = value.astype(BF16)
            at.wide[slot, :, f : f + tile] = value
            at.slope[slot, :, f : f + tile] = derivative.astype(BF16)
            product = mm(value, w_out[e, f : f + tile, :], (1, 0))
            at.total[...] = product if f == 0 else at.total[...] + product

    def enter():
        exchange.await_greetings(int(take or send))

    def work():
        copies = Copies(at.sems)
        if fused:
            dense_forward_part(geo, tick, at, copies, enter, across_in, lambda: start_loads(geo, loads))
            if not take:
                enter()
        else:
            start_loads(geo, loads)
            aux_load = copies.load(at.kept_aux.at[m], at.aux)
            residual_load = copies.load(at.kept_residual.at[m], at.residual)
            enter()
        run_experts(geo, exchange, at.rows, at.total, at.shared, loads, expert, saves)
        if not fused:
            aux_load.wait()
            residual_load.wait()
        home = at.home[...].reshape(geo.slots, geo.width)
        at.result[...] = combine(home, at.aux[...], at.residual[...], at.picked).astype(BF16)
        if send:
            across_out.send(at.result, at.received_out)
        copies.save(at.result, at.out.at[m])
        copies.save(at.picked, at.kept_picked.at[m])
        copies.wait()
        if take:
            across_in.sent(at.out.at[0], at.stream_in)
        if send:
            across_out.take(at.received_out)
            across_out.sent(at.result, at.received_out)

    share_work(exchange, active, work)


def backward_body(geo, step, tile, fused, at):
    m = backward_micro(geo, step)
    take, send = step == 1, fused and 1 <= step < geo.micro
    active = only_section(geo, geo.micro - step)
    exchange = Exchange(geo, at, at.slot_grad, active)
    exchange.greet()
    first = lax.axis_index("section") == 0
    across, across_out = Across(1, at.across_sems), Across(1, at.across_sems, 2)
    if take or send:
        across.greet()
    w_in, w_out = at.w_in_here, at.w_out_here

    def loads(e):
        return (
            pltpu.make_async_copy(at.w_out.at[e], w_out.at[e], at.load_sem.at[e, 1]),
            pltpu.make_async_copy(at.kept_slope.at[m, e], at.slope.at[e], at.load_sem.at[e, 2]),
            pltpu.make_async_copy(at.w_in.at[e], w_in.at[e], at.load_sem.at[e, 0]),
        )

    def saves(e, slot):
        return (
            pltpu.make_async_copy(at.rows.at[slot], at.kept_seen.at[m, e], at.save_sem.at[slot, 0]),
            pltpu.make_async_copy(at.wide.at[slot], at.kept_pre.at[m, e], at.save_sem.at[slot, 1]),
        )

    def expert(e, slot):
        for f in range(0, geo.hidden, tile):
            grad = mm(at.rows[slot], w_out[e, f : f + tile, :], (1, 1))
            value = (grad * at.slope[e, :, f : f + tile].astype(F32)).astype(BF16)
            at.wide[slot, :, f : f + tile] = value
            product = mm(value, w_in[e, :, f : f + tile], (1, 1))
            at.total[...] = product if f == 0 else at.total[...] + product

    def incoming_load():
        own = pltpu.make_async_copy(at.cotangent.at[m], at.incoming_here, at.incoming_sem)
        if step == 0:
            return [own], [own]
        if step == 1:
            return [], [own]
        return [pltpu.make_async_copy(at.received, at.incoming_here, at.incoming_sem)], [own]

    def of_sections(action):
        early, late = incoming_load()

        @pl.when(first)
        def _():
            for copy in early:
                getattr(copy, action)()

        @pl.when(jnp.logical_not(first))
        def _():
            for copy in late:
                getattr(copy, action)()

    def work():
        copies = Copies(at.sems)
        picked_load = copies.load(at.kept_picked.at[m], at.picked)
        aux_load = copies.load(at.kept_aux.at[m], at.aux)
        of_sections("start")
        start_loads(geo, loads)
        dense_loads = dense_backward_loads(geo, m, at, copies) if fused else None
        exchange.await_greetings(int(take or send))
        if take:
            across.send(at.sent, at.incoming_far)
            across.take(at.incoming_far)

            @pl.when(first)
            def _():
                at.incoming_here[...] = at.incoming_far[...]

        of_sections("wait")
        aux_load.wait()
        slot_grad = spread(at.incoming_here[...].astype(F32), at.aux[...], geo.slots)
        at.slot_grad[...] = slot_grad.reshape(at.slot_grad.shape)

        def opened():
            picked_load.wait()
            at.incoming[...] = at.incoming_here[...]
            at.gates[...] = gate_gradients(at.incoming_here[...].astype(F32), at.picked)

        run_experts(geo, exchange, at.rows, at.total, at.shared, loads, expert, saves, opened)
        first_slots, second_slots = slot_onehots(at.aux[...], geo.slots)
        home = at.home[...].reshape(geo.slots, geo.width)
        at.moe_grad[...] = mm((first_slots | second_slots).astype(BF16), home, (1, 0))
        if fused:
            dense_backward_part(geo, step, at, copies, dense_loads, lambda: None, across_out if send else None)
        if take:
            across.sent(at.sent, at.incoming_far)

    share_work(exchange, active, work)


def tile_of(hidden, limit):
    return limit if hidden % limit == 0 else hidden


def experts_scratch(geo, slope_slots):
    rows, local, width, hidden = geo.expert_rows, geo.local_experts, geo.width, geo.hidden
    steps = max(1, geo.cols - 1)
    one = pltpu.SemaphoreType.DMA
    two = pltpu.SemaphoreType.DMA((2,))
    unit = pltpu.SemaphoreType.DMA((geo.units,))
    return dict(
        inbox=pltpu.VMEM((geo.units, geo.cols, geo.rows, geo.main, width), BF16),
        arrived=pltpu.VMEM((geo.units, steps, geo.rows, geo.main, width), BF16),
        stage=pltpu.VMEM((geo.units, geo.rows, geo.main, width), BF16),
        home=pltpu.VMEM((geo.units, geo.rows, geo.main, width), BF16),
        picked=pltpu.VMEM((TOP, geo.length, width), BF16),
        aux=pltpu.VMEM((geo.length, 128), F32),
        rows=pltpu.VMEM((2, rows, width), BF16),
        wide=pltpu.VMEM((2, rows, hidden), BF16),
        slope=pltpu.VMEM((slope_slots, rows, hidden), BF16),
        w_in_here=pltpu.VMEM((local, width, hidden), BF16),
        w_out_here=pltpu.VMEM((local, hidden, width), BF16),
        total=pltpu.VMEM((rows, width), F32),
        shared=pltpu.VMEM((geo.sources * geo.main if geo.share else 16, width), F32),
        via_x=pltpu.VMEM((geo.units, geo.cores, geo.main, width), BF16),
        via_z=pltpu.VMEM((geo.units, geo.cores, geo.main, width), BF16),
        via_y=pltpu.VMEM((geo.units, steps, geo.cores, geo.main, width), BF16),
        via_part=pltpu.VMEM((geo.units, geo.cols, geo.cores, geo.main, width), BF16),
        via_sum=pltpu.VMEM((geo.units, steps, geo.cores, geo.main, width), BF16),
        via_total=pltpu.VMEM((geo.units, geo.cores, geo.main, width), BF16),
        via_home=pltpu.VMEM((geo.units, geo.cores, geo.main, width), BF16),
        via_sems=pltpu.SemaphoreType.DMA((6, geo.units, geo.cols)),
        core_sems=pltpu.SemaphoreType.DMA((4, geo.units, geo.cores)),
        own_sem=unit, pass_send=unit, pass_recv=unit, into_recv=unit, via_x_recv=unit, via_part_recv=unit,
        in_send=two, out_send=two, home_send=two, home_recv=two, home_in_recv=one, via_send=one, via_part_send=one,
        done=one,
        in_recv=pltpu.SemaphoreType.DMA((geo.units, geo.chips)),
        out_recv=pltpu.SemaphoreType.DMA((geo.units, geo.chips)),
        load_sem=pltpu.SemaphoreType.DMA((local, 3)),
        save_sem=pltpu.SemaphoreType.DMA((2, 3)),
        sems=pltpu.SemaphoreType.DMA((6,)),
        across_sems=pltpu.SemaphoreType.DMA((4,)),
    )


def experts_cost(geo):
    weights = geo.local_experts * geo.hidden * geo.width
    return (4 * geo.expert_rows * weights, 4 * weights)


def forward_scratch(geo):
    scratch = experts_scratch(geo, 2)
    scratch["residual"] = pltpu.VMEM((geo.length, geo.width), F32)
    scratch["result"] = pltpu.VMEM((geo.length, geo.width), BF16)
    return scratch


def forward_tick(geo, tick, given, state, received):
    micro, length, width = geo.micro, geo.length, geo.width
    rows, local, hidden = geo.expert_rows, geo.local_experts, geo.hidden
    dense, scratch = dense_forward_scratch(geo, tick), forward_scratch(geo)
    fused = fits(dense, scratch)
    near, kept = {}, {}
    held = dict(w_in=given["w_in"], w_out=given["w_out"])
    if fused:
        near, dense_held, kept = dense_forward_refs(geo, tick, given, state, received)
        held.update(dense_held)
        scratch.update(dense)
    else:
        held["slot_rows"] = dense_forward(geo, tick, given, state, received)
        held.update(kept_aux=state["kept_aux"], kept_residual=state["kept_residual"])
    kept.update(
        out=((micro, length, width), BF16),
        kept_picked=((micro, TOP, length, width), BF16),
        kept_rows=((micro, local, rows, width), BF16),
        kept_hidden=((micro, local, rows, hidden), BF16),
        kept_slope=((micro, local, rows, hidden), BF16),
    )
    results = launch(
        partial(forward_body, geo, tick, tile_of(hidden, 768), fused),
        near=near,
        held=held,
        outs=dict(received_out=pltpu.HBM((length, width), BF16)) if 1 <= tick < micro else {},
        kept=kept,
        state=state,
        scratch=scratch,
        cost=experts_cost(geo),
        collective_id=3 + tick,
        has_side_effects=True,
    )
    return results.get("received_out")


def backward_step(geo, step, given, state, sent, received):
    micro, length, width = geo.micro, geo.length, geo.width
    rows, local, hidden = geo.expert_rows, geo.local_experts, geo.hidden
    scratch = experts_scratch(geo, local)
    scratch["slot_grad"] = pltpu.VMEM((geo.units, geo.rows, geo.main, width), BF16)
    scratch["incoming_here"] = pltpu.VMEM((length, width), BF16)
    scratch["incoming_sem"] = pltpu.SemaphoreType.DMA
    held = dict(
        cotangent=given["cotangent"], w_in=given["w_in"], w_out=given["w_out"], kept_aux=state["kept_aux"],
        kept_picked=state["kept_picked"], kept_slope=state["kept_slope"],
    )
    if step == 1:
        held["sent"] = sent
        scratch["incoming_far"] = pltpu.VMEM((length, width), BF16)
    elif step:
        held["received"] = received
    between = dict(
        moe_grad=shape((length, width), F32), gates=shape((length, 128), F32), incoming=shape((length, width), BF16)
    )
    dense = dense_backward_scratch(geo)
    near, outs, kept = {}, between, {}
    between_scratch = {name: pltpu.VMEM(one.shape, one.dtype) for name, one in between.items()}
    fused = fits(scratch, dense, between_scratch)
    if fused:
        near, dense_held, outs, kept = dense_backward_refs(geo, step, given, state)
        held.update(dense_held)
        scratch.update(dense)
        scratch.update(between_scratch)
    kept.update(
        kept_seen=((micro, local, rows, width), BF16),
        kept_pre=((micro, local, rows, hidden), BF16),
    )
    results = launch(
        partial(backward_body, geo, step, tile_of(hidden, 768), fused),
        near=near,
        held=held,
        outs=outs,
        kept=kept,
        state=state,
        scratch=scratch,
        cost=experts_cost(geo),
        collective_id=4 + micro + step,
        has_side_effects=True,
    )
    return results if fused else dense_backward(geo, step, results, given, state)


class Shards:
    def __init__(self, geo):
        self.cores, self.chips, self.cols = geo.cores, geo.chips, geo.cols
        r, self.c = lax.axis_index("row"), lax.axis_index("col")
        self.z, self.core = r // self.cores, r % self.cores

    def chip(self, k):
        return (self.z + k + self.chips) % self.chips

    def col(self, j):
        return (self.c + j + self.cols) % self.cols

    def row(self, z, other=0):
        return z * self.cores + (self.core + other) % self.cores

    def greet(self):
        barrier = pltpu.get_barrier_semaphore()
        targets = [{"row": self.row(self.chip(k))} for k in range(1, self.chips)]
        targets += [{"col": self.col(j)} for j in range(1, self.cols)]
        targets += [{"row": self.row(self.z, 1)}] * (self.cores - 1)
        for target in targets:
            pl.semaphore_signal(barrier, inc=1, device_id=target, device_id_type=MESH)
        self.greeted = len(targets)

    def await_greetings(self):
        pl.semaphore_wait(pltpu.get_barrier_semaphore(), self.greeted)


def gather_kernel(geo, pieces, qkv, out, router, gain_one, gain_two, terms, all_ref, small, own_sems, z_send, z_recv,
                  y_send, y_recv, core_send, core_recv):
    at = Shards(geo)
    at.greet()
    share, total = all_ref.shape[2:]
    narrow, wide = out.shape[1], qkv.shape[1]
    mine = all_ref.at[at.row(at.z), at.c]
    copies = Copies(own_sems)
    copies.save(qkv, mine.at[:, pl.ds(0, wide)])
    copies.save(out, mine.at[:, pl.ds(wide, narrow)])
    experts_all, count = router.shape[0], terms.shape[1]

    def unit(dims, shift=0):
        return (iota(dims, 0) + shift == iota(dims, 1)).astype(BF16)

    columns = mm(router[...], unit((experts_all, 128)), (0, 0))
    long_terms = mm(terms[...], unit((count, share)), (1, 0)).astype(BF16)
    for k, row in enumerate((gain_one[...], gain_two[...], long_terms)):
        columns = columns + mm(row, unit((1, 128), experts_all + k), (0, 0))
    small[...] = columns.astype(BF16)
    copies.save(small, mine.at[:, pl.ds(wide + narrow, 128)])
    copies.wait()
    at.await_greetings()
    step = total // pieces

    def block(k, j, h):
        return all_ref.at[at.row(at.chip(-k)), at.col(-j), :, pl.ds(h * step, step)]

    def pass_z(k, h):
        own = block(0, 0, h)
        remote(own, own, z_send, z_recv.at[h, k - 1], {"row": at.row(at.chip(k))}).start()

    def pass_y(k, h):
        for j in range(1, at.cols):
            one = block(k, 0, h)
            remote(one, one, y_send, y_recv.at[h, k, j - 1], {"col": at.col(j)}).start()

    def pass_core(k, j, h):
        if at.cores > 1:
            one = block(k, j, h)
            remote(one, one, core_send, core_recv, {"row": at.row(at.z, 1)}).start()

    def came(one, sem):
        remote(one, one, core_send, sem, {"row": at.row(at.z, 1)}).wait_recv()

    def left(one, sem):
        remote(one, one, sem, core_recv, {"row": at.row(at.z, 1)}).wait_send()

    def take_y(h):
        for k in range(at.chips):
            for j in range(1, at.cols):
                came(block(k, j, h), y_recv.at[h, k, j - 1])
                pass_core(k, j, h)

    ahead = min(2, pieces)
    for h in range(ahead):
        for k in range(1, at.chips):
            pass_z(k, h)
    for h in range(pieces):
        pass_y(0, h)
    for h in range(pieces):
        pass_core(0, 0, h)
    for h in range(pieces):
        for k in range(1, at.chips):
            came(block(k, 0, h), z_recv.at[h, k - 1])
            if h + ahead < pieces:
                pass_z(k, h + ahead)
            pass_y(k, h)
            pass_core(k, 0, h)
        if h:
            take_y(h - 1)
    take_y(pieces - 1)
    if at.cores > 1:
        came(all_ref.at[pl.ds(0, at.chips)], core_recv)
        left(all_ref.at[pl.ds(0, at.chips)], core_send)
    if at.chips > 1:
        left(all_ref.at[pl.ds(0, at.chips - 1), 0], z_send)
    if at.cols > 1:
        left(all_ref.at[pl.ds(0, at.chips), pl.ds(0, at.cols - 1)], y_send)


def gather_shards(geo, qkv, out, router, gain_one, gain_two, terms):
    share, total = qkv.shape[0], qkv.shape[1] + out.shape[1] + 128
    pieces = 5 if total % 640 == 0 else 1
    one = pltpu.SemaphoreType.DMA
    return pl.pallas_call(
        partial(gather_kernel, geo, pieces),
        out_shape=pltpu.HBM((geo.rows, geo.cols, share, total), BF16),
        in_specs=[hbm_spec()] * 2 + [vmem_spec()] * 4,
        out_specs=hbm_spec(),
        scratch_shapes=[
            pltpu.VMEM((share, 128), BF16),
            pltpu.SemaphoreType.DMA((3,)),
            one, pltpu.SemaphoreType.DMA((pieces, max(1, geo.chips - 1))),
            one, pltpu.SemaphoreType.DMA((pieces, geo.chips, max(1, geo.cols - 1))),
            one, one,
        ],
        compiler_params=pltpu.CompilerParams(collective_id=1, has_side_effects=True),
    )(in_hbm(qkv), in_hbm(out), router, gain_one, gain_two, terms)


def reduce_part(shards, refs):
    at = shards
    part_ref, out_ref = refs.part, refs.shard
    from_core, from_col, from_chip, pair, column = refs.from_core, refs.from_col, refs.from_chip, refs.pair, refs.column
    core_send, core_recv, y_send, y_recv, z_send, z_recv = (
        refs.core_send, refs.core_recv, refs.y_send, refs.y_recv, refs.z_send, refs.z_recv
    )
    order = list(range(1, at.chips)) + [0]
    started = []

    def start(copy):
        copy.start()
        started.append(copy)

    def to_core(k):
        return remote(
            part_ref.at[at.row(at.chip(k), 1)], from_core.at[k], core_send.at[k, 0], core_recv.at[k, 0],
            {"row": at.row(at.z, 1)},
        )

    def to_col(k, j):
        return remote(
            pair.at[k, at.col(j)], from_col.at[k, j - 1], y_send.at[k, j - 1], y_recv.at[k, j - 1],
            {"col": at.col(j)},
        )

    def to_chip(k):
        return remote(
            column.at[k - 1], from_chip.at[k - 1], z_send.at[k - 1], z_recv.at[k - 1],
            {"row": at.row(at.chip(k))},
        )

    if at.cores > 1:
        for k in order:
            start(to_core(k))

    def sum_cores(k):
        total = part_ref[at.row(at.chip(k))].astype(F32)
        if at.cores > 1:
            to_core(k).wait_recv()
            total = total + from_core[k].astype(F32)
        pair[k] = total.astype(BF16)
        for j in range(1, at.cols):
            start(to_col(k, j))

    def sum_cols(k):
        total = pair[k, at.c].astype(F32)
        for j in range(1, at.cols):
            to_col(k, j).wait_recv()
            total = total + from_col[k, j - 1].astype(F32)
        if k:
            column[k - 1] = total.astype(BF16)
            start(to_chip(k))
        else:
            out_ref[...] = total

    for step, k in enumerate(order):
        sum_cores(k)
        if step:
            sum_cols(order[step - 1])
    sum_cols(order[-1])
    for k in range(1, at.chips):
        to_chip(k).wait_recv()
        out_ref[...] += from_chip[k - 1].astype(F32)
    for copy in started:
        copy.wait_send()


def reduce_scratch(geo, share, width):
    chips, steps, far = geo.chips, max(1, geo.cols - 1), max(1, geo.chips - 1)
    z = pltpu.SemaphoreType.DMA((far,))
    y = pltpu.SemaphoreType.DMA((chips, steps))
    core = pltpu.SemaphoreType.DMA((chips, geo.cols))
    return dict(
        from_core=pltpu.VMEM((chips, geo.cols, share, width), BF16),
        from_col=pltpu.VMEM((chips, steps, share, width), BF16),
        from_chip=pltpu.VMEM((far, share, width), BF16),
        pair=pltpu.VMEM((chips, geo.cols, share, width), BF16),
        column=pltpu.VMEM((far, share, width), BF16),
        core_send=core, core_recv=core, y_send=y, y_recv=y, z_send=z, z_recv=z,
    )


def expert_weights_kernel(rows, pre, hidden, seen, in_grad, out_grad):
    def product(left, right):
        left, right = (ref[:, 0].reshape(-1, ref.shape[-1]) for ref in (left, right))
        return mm(left, right, (0, 0))

    in_grad[0, 0] = product(rows, pre)
    out_grad[0, 0] = product(hidden, seen)


def expert_weights(geo, state):
    micro, local, count, width, hidden = geo.micro, geo.local_experts, geo.expert_rows, geo.width, geo.hidden
    tile = tile_of(hidden, 768)
    narrow = pl.BlockSpec((micro, 1, count, width), lambda e, f: (0, e, 0, 0))
    wide = pl.BlockSpec((micro, 1, count, tile), lambda e, f: (0, e, 0, f))
    flops = 4 * micro * local * count * width * hidden
    return pl.pallas_call(
        expert_weights_kernel,
        out_shape=(shape((1, local, width, hidden), F32), shape((1, local, hidden, width), F32)),
        grid=(local, hidden // tile),
        in_specs=[narrow, wide, wide, narrow],
        out_specs=[
            pl.BlockSpec((1, 1, width, tile), lambda e, f: (0, e, 0, f)),
            pl.BlockSpec((1, 1, tile, width), lambda e, f: (0, e, f, 0)),
        ],
        compiler_params=pltpu.CompilerParams(vmem_limit_bytes=48 * MIB),
        cost_estimate=pl.CostEstimate(
            flops=flops, bytes_accessed=8 * local * hidden * width, transcendentals=0
        ),
    )(*(in_hbm(state[name]) for name in ("kept_rows", "kept_pre", "kept_hidden", "kept_seen")))


def norm_backward(values, gain, grad):
    factor = norm_factor(values)
    unit = values * factor
    weighted = grad * gain
    inner = jnp.mean(weighted * unit, axis=-1, keepdims=True)
    return factor * (weighted - unit * inner), jnp.sum(grad * unit, axis=0, keepdims=True)


def dense_backward_loads(geo, m, at, copies):
    width = geo.width
    return dict(
        rest=copies.load(at.packed.at[:, pl.ds(3 * width, width + 128)], at.rest_w),
        gains=copies.load(at.gains, at.gains_here),
        residual=copies.load(at.kept_residual.at[m], at.residual),
        qkv=copies.load(at.kept_qkv.at[m], at.qkv),
        prob=copies.load(at.kept_prob.at[m], at.prob),
        stream=copies.load(at.kept_stream.at[m], at.stream),
        qkv_w=copies.load(at.packed.at[:, pl.ds(0, 3 * width)], at.qkv_w),
    )


def dense_backward_part(geo, step, at, copies, loads, enter, across):
    length, width, heads = geo.length, geo.width, geo.heads
    size = width // heads
    per = 128 // size
    m = backward_micro(geo, step)
    send = across is not None
    aux = at.aux[...]
    slope = aux[:, 0:1] * aux[:, 1:2] * (at.gates[:, 0:1] - at.gates[:, 1:2])
    expert_at = iota((length, 128), 1).astype(F32)
    logit_grad = (
        jnp.where(as_column(at.routes[0, m, 0:1, :].astype(F32)) == expert_at, slope, 0.0)
        - jnp.where(as_column(at.routes[0, m, 1:2, :].astype(F32)) == expert_at, slope, 0.0)
    ).astype(BF16)
    at.logit[...] = logit_grad
    copies.save(at.logit, at.kept_logit.at[m])
    loads["rest"].wait()
    moe_grad = at.moe_grad[...] + mm(logit_grad, at.rest_w[:, width:], (1, 1))
    loads["residual"].wait()
    loads["gains"].wait()
    part, gain_two = norm_backward(at.residual[...], at.gains_here[1:2, :], moe_grad)
    residual_grad = at.incoming[...].astype(F32) + part
    at.branch[...] = residual_grad.astype(BF16)
    copies.save(at.branch, at.kept_branch.at[m])
    at.context_grad[...] = mm(at.branch[...], at.rest_w[:, :width], (1, 1)).astype(BF16)
    which = iota((length, 128), 1) // size
    head_row = iota((128, length), 0) // size
    scale = 1.0 / math.sqrt(size)
    zero = jnp.zeros((length, 128), BF16)
    loads["qkv"].wait()
    loads["prob"].wait()
    at.sums[...] = jnp.zeros(at.sums.shape, F32)
    for j in range(width // 128):
        places = [slice(base * width + 128 * j, base * width + 128 * (j + 1)) for base in range(3)]
        queries, keys, values = (at.qkv[:, place] for place in places)
        grad = at.context_grad[:, places[0]]
        turned_keys = keys.astype(F32).T
        totals = [jnp.zeros(dims, F32) for dims in ((128, length), (length, 128), (length, 128))]
        for part_at in range(per):
            h = j * per + part_at
            own = which == part_at
            own_grad = jnp.where(own, grad, zero)
            prob = at.prob[h]
            prob_grad = mm(values, own_grad, (1, 1))
            weighted = prob.astype(F32)
            shift = jnp.sum(weighted * prob_grad, axis=0, keepdims=True)
            score_grad = (weighted * (prob_grad - shift)).astype(BF16)
            at.sums[h : h + 1, :] = diagonal_sums(score_grad.astype(F32))
            own_keys = jnp.where(head_row == part_at, turned_keys, 0.0).astype(BF16)
            totals[0] = totals[0] + mm(own_keys, score_grad, (1, 0))
            totals[1] = totals[1] + mm(score_grad, jnp.where(own, queries, zero), (1, 0))
            totals[2] = totals[2] + mm(prob, own_grad, (1, 0))
        at.qkv_grad[:, places[0]] = (totals[0].T * scale).astype(BF16)
        at.qkv_grad[:, places[1]] = (totals[1] * scale).astype(BF16)
        at.qkv_grad[:, places[2]] = totals[2].astype(BF16)
    copies.save(at.qkv_grad, at.kept_qkv_grad.at[m])
    copies.save(at.sums, at.kept_sums.at[m])
    loads["qkv_w"].wait()
    normed_grad = mm(at.qkv_grad[...], at.qkv_w[...], (1, 1))
    loads["stream"].wait()
    part, gain_one = norm_backward(at.stream[...].astype(F32), at.gains_here[0:1, :], normed_grad)
    at.gain_parts[...] = jnp.zeros(at.gain_parts.shape, F32)
    at.gain_parts[0:1, :] = gain_one
    at.gain_parts[1:2, :] = gain_two
    copies.save(at.gain_parts, at.kept_gains.at[m])
    in_grad = residual_grad + part
    at.in_grad_here[...] = in_grad
    copies.save(at.in_grad_here, at.in_grad.at[m])
    if step < geo.micro:
        at.sent_here[...] = in_grad.astype(BF16)
    if send:
        enter()
        across.send(at.sent_here, at.received_out)
    elif step < geo.micro:
        copies.save(at.sent_here, at.sent_out)
    copies.wait()
    if send:
        across.take(at.received_out)
        across.sent(at.sent_here, at.received_out)


def dense_backward_body(geo, step, at):
    send = 1 <= step < geo.micro
    across = Across(1, at.across_sems) if send else None
    if send:
        across.greet()

    def enter():
        pl.semaphore_wait(pltpu.get_barrier_semaphore(), 1)

    m = backward_micro(geo, step)
    copies = Copies(at.sems)
    aux_load = copies.load(at.kept_aux.at[m], at.aux)
    loads = dense_backward_loads(geo, m, at, copies)
    aux_load.wait()
    dense_backward_part(geo, step, at, copies, loads, enter, across)


def dense_backward_scratch(geo):
    length, width, heads = geo.length, geo.width, geo.heads
    return dict(
        aux=pltpu.VMEM((length, 128), F32),
        rest_w=pltpu.VMEM((width, width + 128), BF16),
        qkv_w=pltpu.VMEM((width, 3 * width), BF16),
        residual=pltpu.VMEM((length, width), F32),
        qkv=pltpu.VMEM((length, 3 * width), BF16),
        prob=pltpu.VMEM((heads, length, length), BF16),
        stream=pltpu.VMEM((length, width), BF16),
        logit=pltpu.VMEM((length, 128), BF16),
        branch=pltpu.VMEM((length, width), BF16),
        context_grad=pltpu.VMEM((length, width), BF16),
        qkv_grad=pltpu.VMEM((length, 3 * width), BF16),
        sums=pltpu.VMEM((geo.tall, length), F32),
        gain_parts=pltpu.VMEM((8, width), F32),
        in_grad_here=pltpu.VMEM((length, width), F32),
        gains_here=pltpu.VMEM((8, width), F32),
        sent_here=pltpu.VMEM((length, width), BF16),
        sems=pltpu.SemaphoreType.DMA((20,)),
        across_sems=pltpu.SemaphoreType.DMA((4,)),
    )


def dense_backward_refs(geo, step, given, state):
    micro, length, width = geo.micro, geo.length, geo.width
    outs = {}
    if 1 <= step < micro:
        outs["received_out"] = pltpu.HBM((length, width), BF16)
    elif step < micro:
        outs["sent_out"] = pltpu.HBM((length, width), BF16)
    names = ("kept_aux", "kept_residual", "kept_qkv", "kept_prob", "kept_stream")
    held = dict({name: state[name] for name in names}, packed=given["packed"], gains=given["gains"])
    kept = dict(
        in_grad=((micro, length, width), F32),
        kept_branch=((micro, length, width), BF16),
        kept_qkv_grad=((micro, length, 3 * width), BF16),
        kept_logit=((micro, length, 128), BF16),
        kept_gains=((micro, 8, width), F32),
        kept_sums=((micro, geo.tall, length), F32),
    )
    return dict(routes=given["routes"]), held, outs, kept


def dense_backward(geo, step, near, given, state):
    more, held, outs, kept = dense_backward_refs(geo, step, given, state)
    params = {}
    if 1 <= step < geo.micro:
        params = dict(collective_id=5 + 2 * geo.micro + step, has_side_effects=True)
    return launch(
        partial(where_active, only_section(geo, geo.micro - step), partial(dense_backward_body, geo, step)),
        near=dict(near, **more),
        held=held,
        outs=outs,
        kept=kept,
        state=state,
        scratch=dense_backward_scratch(geo),
        cost=(3_000_000_000, 14_000_000),
        **params,
    )


DENSE_GRADS = ("normed", "qkv_grad", "context", "branch", "moe_in", "logit")


def dense_weights_body(geo, at):
    width = geo.width
    copies = Copies(at.sems)
    loads = {}
    for name in DENSE_GRADS + ("gains", "sums"):
        loads[name] = copies.load(getattr(at, "kept_" + name), getattr(at, name))

    def product(left, right):
        left, right = (ref[...].reshape(-1, ref.shape[-1]) for ref in (left, right))
        return mm(left, right, (0, 0))

    def ready(*names):
        for name in names:
            loads[name].wait()

    early = 2 * width

    def put(places, block):
        at.late[:, places] = block.astype(BF16)

    ready("normed", "qkv_grad")
    normed = at.normed[...].reshape(-1, width)

    def qkv_product(j):
        grad = at.qkv_grad[:, :, j : j + width].reshape(-1, width)
        return mm(normed, grad, (0, 0))

    put(slice(0, width), qkv_product(early))
    for j in range(0, early, width):
        block = qkv_product(j).astype(BF16)
        if len(at.part.shape) == 4:
            at.part[:, :, :, j : j + width] = block.reshape(at.part.shape[:3] + block.shape[1:])
        else:
            at.part[:, j : j + width] = block
    ready("context", "branch")
    put(slice(width, 2 * width), product(at.context, at.branch))
    ready("moe_in", "logit", "gains", "sums")
    small = product(at.moe_in, at.logit)
    by_term = lax.dot_general(
        jnp.sum(at.sums[...], axis=0), at.spread[...].astype(F32), (((1,), (1,)), ((), ())),
        precision=lax.Precision.HIGHEST, preferred_element_type=F32,
    )
    bias_row = jnp.sum(by_term[: geo.heads] * at.head_pick[...], axis=0, keepdims=True)
    gain_rows = jnp.sum(at.gains[...], axis=0)
    place = iota((128, width), 0)
    rows = jnp.zeros((128, width), F32)
    for k, row in enumerate((gain_rows[0:1], gain_rows[1:2], bias_row)):
        rows = jnp.where(place == geo.experts_all + k, row, rows)
    put(slice(2 * width, 2 * width + 128), small + rows.T)


def dense_weights(geo, head_pick, spread_table, state):
    held = {"kept_" + name: state["kept_" + name] for name in DENSE_GRADS + ("gains", "sums")}
    scratch = {name: pltpu.VMEM(held["kept_" + name].shape, BF16) for name in DENSE_GRADS}
    scratch.update(
        sems=pltpu.SemaphoreType.DMA((len(DENSE_GRADS) + 2,)),
        gains=pltpu.VMEM(state["kept_gains"].shape, F32), sums=pltpu.VMEM(state["kept_sums"].shape, F32),
    )
    share, width = geo.width // geo.sources, geo.width
    parts = (geo.rows, geo.cols, share, 2 * width)
    results = launch(
        partial(dense_weights_body, geo),
        near=dict(head_pick=head_pick, spread=spread_table),
        held=held,
        outs=dict(
            part=shape(parts if share % 16 == 0 else (width, 2 * width), BF16),
            late=shape((width, 2 * width + 128), BF16),
        ),
        scratch=scratch,
        spare=24,
        cost=(3_000_000_000, 10_000_000),
    )
    return results["part"].reshape(parts), results["late"]


def reduce_shards(geo, part):
    def body(at):
        shards = Shards(geo)
        shards.greet()
        shards.await_greetings()
        reduce_part(shards, at)

    share, total = part.shape[2:]
    return launch(
        body,
        near=dict(part=part),
        outs=dict(shard=shape((share, total), F32)),
        scratch=reduce_scratch(geo, share, total),
        collective_id=2,
        has_side_effects=True,
    )["shard"]


def on_device(
    inputs, cotangent, segments, routes, order, attn_gain, qkv_weight, position_bias, out_weight, moe_gain,
    router_weight, expert_in, expert_out,
):
    micro, length, width = inputs.shape
    local_experts, hidden = expert_in.shape[1], expert_in.shape[3]
    experts_all = router_weight.shape[2]
    row_count, col_count = lax.axis_size("row"), lax.axis_size("col")
    devices = row_count * col_count
    share = width // devices
    terms = position_bias.shape[1]
    heads = terms * devices // DISTANCE_BUCKETS
    geo = Geometry(micro, length, width, heads, experts_all, local_experts, hidden, row_count, col_count)
    packed = gather_shards(
        geo, qkv_weight[0], out_weight[0], router_weight[0].T, attn_gain, moe_gain, position_bias
    ).reshape(width, -1)
    indicator = buckets(length)
    row_at = np.arange(width)
    term_at = np.where(row_at % share < terms, row_at // share * terms + row_at % share, -1)
    head_pick = jnp.asarray((term_at % heads == np.arange(heads)[:, None]) & (term_at >= 0), F32)
    spread_table = jnp.asarray(indicator[np.maximum(term_at, 0) // heads], BF16)
    prepared = launch(
        partial(prepare, experts_all),
        near=dict(head_pick=head_pick, spread=spread_table),
        held=dict(packed=packed),
        outs=dict(gains=pltpu.HBM((8, width), F32), bias=pltpu.HBM((heads, length, length), BF16)),
        scratch=dict(
            small=pltpu.VMEM((width, 128), BF16), gains_here=pltpu.VMEM((8, width), F32),
            bias_here=pltpu.VMEM((heads, length, length), BF16), sems=pltpu.SemaphoreType.DMA((3,)),
        ),
        cost=(50_000_000, 6_000_000),
    )
    given = dict(
        prepared, packed=packed, inputs=inputs, cotangent=cotangent, w_in=expert_in[0], w_out=expert_out[0],
        segments=segments, order=order, routes=jnp.swapaxes(routes, 2, 3),
        bases=jnp.asarray(geo.bases()),
    )
    state = {}
    received = None
    for tick in range(micro + 1):
        received = forward_tick(geo, tick, given, state, received)
    sent = received = None
    for step in range(micro + 1):
        passed = backward_step(geo, step, given, state, sent, received)
        sent, received = passed.get("sent_out"), passed.get("received_out")
    part, late = dense_weights(geo, head_pick, spread_table, state)
    late = lax.psum_scatter(late, ("row", "col"), scatter_dimension=0, tiled=True)
    part = reduce_shards(geo, part)
    expert_in_grad, expert_out_grad = expert_weights(geo, state)
    late = late.astype(F32)
    small = late[:, 2 * width :]
    return (
        state["out"][None], state["in_grad"][None], small[:, experts_all][None],
        jnp.concatenate([part, late[:, :width]], axis=1)[None], small[:terms, experts_all + 2][None],
        late[None, :, width : 2 * width], small[:, experts_all + 1][None], small[None, :, :experts_all],
        expert_in_grad, expert_out_grad,
    )


def solution(mesh):
    tokens = ("row", "col")
    return jax.shard_map(
        on_device,
        mesh=mesh,
        in_specs=(
            P(None, tokens, None),
            P(None, tokens, None),
            P(None, tokens),
            P("section", None, tokens, None),
            P("section", None, tokens, None),
            P("section", tokens),
            P("section", tokens, None),
            P("section", tokens),
            P("section", tokens, None),
            P("section", tokens),
            P("section", tokens, None),
            P("section", "row", None, "col"),
            P("section", "row", "col", None),
        ),
        out_specs=(
            P("section", None, tokens, None),
            P("section", None, tokens, None),
            P("section", tokens),
            P("section", tokens, None),
            P("section", tokens),
            P("section", tokens, None),
            P("section", tokens),
            P("section", tokens, None),
            P("section", "row", None, "col"),
            P("section", "row", "col", None),
        ),
        check_vma=False,
    )
```

```python
from functools import partial
import math
from types import SimpleNamespace

import jax
import jax.numpy as jnp
import numpy as np
from jax import lax
from jax.experimental import pallas as pl
from jax.experimental.pallas import tpu as pltpu
from jax.sharding import PartitionSpec as P

TOP = 2
DISTANCE_BUCKETS = 32
MAX_DIST = 128
EPS = 1e-06
MESH = pl.DeviceIdType.MESH
F32 = jnp.float32
BF16 = jnp.bfloat16
MIB = 1 << 20


class Geometry:
    def __init__(self, micro, length, width, heads, experts_all, local_experts, hidden, row_count, col_count):
        self.micro, self.length, self.width, self.heads, self.hidden = micro, length, width, heads, hidden
        self.tall = -(-heads // 8) * 8
        self.capacity = max(2, (5 * length * TOP + 4 * experts_all - 1) // (4 * experts_all))
        self.local_experts = local_experts
        self.experts_all = experts_all
        self.rows, self.cols = row_count, col_count
        self.cores = 2 if row_count % 2 == 0 else 1
        self.chips = row_count // self.cores
        main = self.capacity // 16 * 16
        rest = self.capacity - main
        self.share = main // local_experts if 0 < rest <= main // local_experts else 0
        if rest and not self.share:
            main += 16
        self.main = main
        self.first = 1 if self.share else 0
        self.units = local_experts + self.first
        self.slots = row_count * self.units * main
        self.sources = row_count * col_count
        self.expert_rows = self.sources * (main + self.share)

    def bases(self):
        expert = np.arange(self.experts_all)
        owner, local = expert // self.local_experts, expert % self.local_experts
        main = ((self.first + local) * self.rows + owner) * self.main
        tail = owner * self.main + local * self.share
        both = np.stack([main, tail]).astype(np.float32)
        return np.pad(both, ((0, 0), (0, 128 - self.experts_all)))


def buckets(length):
    distance = np.arange(length)
    bucket = np.zeros(length, np.int64)
    half = DISTANCE_BUCKETS // 2
    for level in range(1, DISTANCE_BUCKETS):
        if level < half:
            limit = level
        else:
            limit = int(math.ceil(half * (MAX_DIST / half) ** ((level - half) / half)))
        bucket += distance >= limit
    return (np.arange(DISTANCE_BUCKETS)[:, None] == bucket[None, :]).astype(np.float32)


def mm(left, right, contract):
    return lax.dot_general(
        left, right, (((contract[0],), (contract[1],)), ((), ())), preferred_element_type=F32
    )


def iota(shape, axis):
    return lax.broadcasted_iota(jnp.int32, shape, axis)


def norm_factor(values):
    return lax.rsqrt(jnp.mean(values * values, axis=-1, keepdims=True) + EPS)


def gelu_pair(x):
    density = jnp.exp(-0.5 * x * x)
    t = 1.0 / (1.0 + (0.3275911 * math.sqrt(0.5)) * jnp.abs(x))
    poly = 0.5 * 1.061405429
    for coefficient in (-1.453152027, 1.421413741, -0.284496736, 0.254829592):
        poly = poly * t + 0.5 * coefficient
    beyond = poly * t * density
    cdf = jnp.where(x >= 0, 1.0 - beyond, beyond)
    return x * cdf, cdf + x * density * (1.0 / math.sqrt(2.0 * math.pi))


def slot_onehots(aux, slots):
    positions = iota((aux.shape[0], slots), 1).astype(F32)
    return [(aux[:, 2 + c : 3 + c] == positions) for c in range(TOP)]


def vmem_grant(scratch, spare):
    held = 0
    for ref in scratch:
        if getattr(ref, "memory_space", None) == pltpu.VMEM:
            held += math.prod(ref.shape) * jnp.dtype(ref.dtype).itemsize
    return -(-held // MIB) + spare


def fits(*scratches):
    return vmem_grant([ref for scratch in scratches for ref in scratch.values()], 11) <= 62


def vmem_spec():
    return pl.BlockSpec(memory_space=pltpu.VMEM)


def hbm_spec():
    return pl.BlockSpec(memory_space=pltpu.HBM)


def in_hbm(array):
    return pltpu.with_memory_space_constraint(array, pltpu.HBM)


def shape(dims, kind):
    return jax.ShapeDtypeStruct(dims, kind)


def launch(body, near=None, held=None, outs=None, kept=None, state=None, scratch=None, spare=10, cost=None, **params):
    near, held, outs, kept, scratch = (dict(part or {}) for part in (near, held, outs, kept, scratch))
    state = {} if state is None else state
    old = [name for name in kept if name in state]
    names_in, names_out = list(near) + list(held), list(outs) + list(kept)

    def kernel(*refs):
        refs = list(refs)
        given, refs = refs[: len(names_in)], refs[len(names_in) + len(old) :]
        body(SimpleNamespace(**dict(zip(names_in + names_out + list(scratch), given + refs))))

    out_shapes = list(outs.values()) + [pltpu.HBM(dims, kind) for dims, kind in kept.values()]
    plain = [isinstance(out, jax.ShapeDtypeStruct) for out in out_shapes]
    estimate = {}
    if cost is not None:
        estimate["cost_estimate"] = pl.CostEstimate(flops=cost[0], bytes_accessed=cost[1], transcendentals=0)
    results = pl.pallas_call(
        kernel,
        out_shape=out_shapes,
        in_specs=[vmem_spec()] * len(near) + [hbm_spec()] * (len(held) + len(old)),
        out_specs=[vmem_spec() if near_by else hbm_spec() for near_by in plain],
        scratch_shapes=list(scratch.values()),
        input_output_aliases={len(names_in) + i: names_out.index(name) for i, name in enumerate(old)},
        compiler_params=pltpu.CompilerParams(
            vmem_limit_bytes=vmem_grant(scratch.values(), spare) * MIB, **params
        ),
        **estimate,
    )(*near.values(), *map(in_hbm, held.values()), *(in_hbm(state[name]) for name in old))
    results = dict(zip(names_out, results))
    for name in kept:
        state[name] = results.pop(name)
    return results


def of_micro(rows, m):
    if isinstance(m, int):
        return rows[m : m + 1]
    row = rows[0:1]
    for i in range(1, rows.shape[0]):
        row = jnp.where(m == i, rows[i : i + 1], row)
    return row


def as_column(row):
    return jnp.broadcast_to(row, (8, row.shape[1])).T[:, 0:1]


class Copies:
    def __init__(self, sems):
        self.sems, self.count, self.open = sems, 0, []

    def load(self, source, target):
        copy = pltpu.make_async_copy(source, target, self.sems.at[self.count])
        self.count += 1
        copy.start()
        return copy

    def save(self, source, target):
        self.open.append(self.load(source, target))

    def wait(self):
        for copy in self.open:
            copy.wait()


def remote(source, target, send, receive, where):
    return pltpu.make_async_remote_copy(
        src_ref=source, dst_ref=target, send_sem=send, recv_sem=receive, device_id=where, device_id_type=MESH
    )


def forward_micro(geo, tick):
    if tick == 0:
        return 0
    return geo.micro - 1 if tick == geo.micro else tick - lax.axis_index("section")


def backward_micro(geo, step):
    if step == 0:
        return geo.micro - 1
    return 0 if step == geo.micro else geo.micro - step - lax.axis_index("section")


class Across:
    def __init__(self, sender, sems, at=0):
        self.section = lax.axis_index("section")
        self.sender, self.other = sender, {"section": 1 - self.section}
        self.send_sem, self.recv_sem = sems.at[at], sems.at[at + 1]

    def greet(self):
        pl.semaphore_signal(pltpu.get_barrier_semaphore(), inc=1, device_id=self.other, device_id_type=MESH)

    def copy(self, source, target):
        return remote(source, target, self.send_sem, self.recv_sem, self.other)

    def send(self, source, target):
        @pl.when(self.section == self.sender)
        def _():
            self.copy(source, target).start()

    def sent(self, source, target):
        @pl.when(self.section == self.sender)
        def _():
            self.copy(source, target).wait_send()

    def take(self, target):
        @pl.when(self.section != self.sender)
        def _():
            self.copy(target, target).wait_recv()


def prepare(experts_all, at):
    heads, length = at.bias_here.shape[:2]
    width = at.small.shape[0]
    copies = Copies(at.sems)
    copies.load(at.packed.at[:, pl.ds(4 * width, 128)], at.small).wait()
    rows = at.small[...].astype(F32).T
    at.gains_here[0:2, :] = rows[experts_all : experts_all + 2]
    copies.save(at.gains_here, at.gains)
    picked = (at.head_pick[...] * rows[experts_all + 2 : experts_all + 3]).astype(BF16)
    by_distance = mm(picked, at.spread[...], (1, 0))
    for h in range(heads):
        block = by_distance[h : h + 1, :]
        step = 1
        while step < length:
            block = jnp.concatenate([block, pltpu.roll(block, step, 1)], axis=0)
            step *= 2
        at.bias_here[h] = block.astype(BF16)
    copies.save(at.bias_here, at.bias)
    copies.wait()


def diagonal_sums(block):
    length = block.shape[1]
    size = block.shape[0] // 2
    while size >= 1:
        block = block[:size] + pltpu.roll(block[size:], length - size, 1)
        size //= 2
    return block


def only_section(geo, tick):
    return {0: 0, geo.micro: 1}.get(tick)


def where_active(active, body, at):
    if active is None:
        body(at)
    else:
        pl.when(lax.axis_index("section") == active)(partial(body, at))


def dense_forward_part(geo, tick, at, copies, enter, across, loaded, fused=True):
    length, width, heads = geo.length, geo.width, geo.heads
    size = width // heads
    per = 128 // size
    m = forward_micro(geo, tick)
    gains_load = copies.load(at.gains, at.gains_here)
    thirds = [pl.ds(third * width, width) for third in range(3)]
    packed_qkv = [copies.load(at.packed.at[:, third], at.qkv_w.at[:, third]) for third in thirds]
    if tick == 0:
        copies.load(at.inputs.at[m], at.stream).wait()
    else:
        first = lax.axis_index("section") == 0
        own = pltpu.make_async_copy(at.inputs.at[m], at.stream, at.stream_sem)
        if tick == 1:
            enter()
            across.send(at.out.at[0] if fused else at.out_before.at[0], at.stream_in)
        else:
            came = pltpu.make_async_copy(at.received, at.stream, at.stream_sem)

        @pl.when(first)
        def _():
            own.start()
            own.wait()

        if tick == 1:
            across.take(at.stream_in)

            @pl.when(jnp.logical_not(first))
            def _():
                at.stream[...] = at.stream_in[...]
        else:

            @pl.when(jnp.logical_not(first))
            def _():
                came.start()
                came.wait()

    packed_rest = copies.load(at.packed.at[:, pl.ds(3 * width, width + 128)], at.rest_w)
    bias_load = copies.load(at.bias, at.bias_here)
    copies.save(at.stream, at.kept_stream.at[m])
    stream = at.stream[...].astype(F32)
    gains_load.wait()
    at.normed[...] = (stream * norm_factor(stream) * at.gains_here[0:1, :]).astype(BF16)
    copies.save(at.normed, at.kept_normed.at[m])
    for third, load in zip(thirds, packed_qkv):
        load.wait()
        at.qkv[:, third] = mm(at.normed[...], at.qkv_w[:, third], (1, 0)).astype(BF16)
    copies.save(at.qkv, at.kept_qkv.at[m])
    key_at, query_at = iota((length, length), 0), iota((length, length), 1)
    segments = of_micro(at.segments[...], m).astype(F32)
    allowed = (key_at <= query_at) & (as_column(segments) == segments)
    which = iota((length, 128), 1) // size
    head_row = iota((128, length), 0) // size
    scale = 1.0 / math.sqrt(size)
    zero = jnp.zeros((length, 128), BF16)
    bias_load.wait()
    for j in range(width // 128):
        queries = at.qkv[:, 128 * j : 128 * (j + 1)]
        keys = at.qkv[:, width + 128 * j : width + 128 * (j + 1)]
        values = at.qkv[:, 2 * width + 128 * j : 2 * width + 128 * (j + 1)]
        turned_values = values.astype(F32).T
        context = jnp.zeros((128, length), F32)
        for part in range(per):
            h = j * per + part
            own = which == part
            scores = mm(jnp.where(own, keys, zero), queries, (1, 1)) * scale + at.bias_here[h].astype(F32)
            scores = jnp.where(allowed, scores, -1e30)
            exponent = jnp.exp(scores - jnp.max(scores, axis=0, keepdims=True))
            prob = (exponent * (1.0 / jnp.sum(exponent, axis=0, keepdims=True))).astype(BF16)
            at.prob[h] = prob
            own_values = jnp.where(head_row == part, turned_values, 0.0).astype(BF16)
            context = context + mm(own_values, prob, (1, 0))
        at.context[:, 128 * j : 128 * (j + 1)] = context.T.astype(BF16)
    copies.save(at.prob, at.kept_prob.at[m])
    copies.save(at.context, at.kept_context.at[m])
    packed_rest.wait()
    loaded()
    residual = stream + mm(at.context[...], at.rest_w[:, :width], (1, 0))
    at.residual[...] = residual
    copies.save(at.residual, at.kept_residual.at[m])
    moe_in = (residual * norm_factor(residual) * at.gains_here[1:2, :]).astype(BF16)
    at.moe_in[...] = moe_in
    copies.save(at.moe_in, at.kept_moe_in.at[m])
    logits = mm(moe_in, at.rest_w[:, width:], (1, 0))
    expert_at = iota(logits.shape, 1)
    picks = [(as_column(at.routes[0, m, c : c + 1, :].astype(F32)) == expert_at.astype(F32)).astype(F32) for c in range(TOP)]
    chosen = [jnp.sum(pick * logits, axis=1, keepdims=True) for pick in picks]
    top = jnp.maximum(chosen[0], chosen[1])
    powers = [jnp.exp(value - top) for value in chosen]
    total = powers[0] + powers[1]
    shares = [power / total for power in powers]
    order = of_micro(at.order[0, :, 0, :], m).astype(F32)
    before = (order < as_column(order)).astype(BF16)
    counts = [mm(before, pick.astype(BF16), (1, 0)) for pick in picks]
    counts[1] = counts[1] + jnp.sum(picks[0], axis=0, keepdims=True)
    slots = []
    for pick, count in zip(picks, counts):
        rank = jnp.sum(pick * count, axis=1, keepdims=True)
        main = jnp.sum(pick * at.bases[0:1, :], axis=1, keepdims=True)
        tail = jnp.sum(pick * at.bases[1:2, :], axis=1, keepdims=True)
        place = jnp.where(rank < geo.main, main + rank, tail + rank - geo.main)
        slots.append(jnp.where(rank < geo.capacity, place, -1.0))
    lane = iota((length, 128), 1)
    aux = jnp.zeros((length, 128), F32)
    for place, value in enumerate(shares + slots):
        aux = jnp.where(lane == place, value, aux)
    at.aux[...] = aux
    copies.save(at.aux, at.kept_aux.at[m])
    first, second = slot_onehots(aux, geo.slots)
    at.slots[...] = mm((first | second).astype(BF16), moe_in, (0, 0)).astype(BF16).reshape(at.slots.shape)


def dense_forward_body(geo, tick, at):
    across = Across(0, at.across_sems) if tick == 1 else None
    if across:
        across.greet()

    def enter():
        pl.semaphore_wait(pltpu.get_barrier_semaphore(), 1)

    copies = Copies(at.sems)
    dense_forward_part(geo, tick, at, copies, enter, across, lambda: None, fused=False)
    copies.save(at.slots, at.slot_rows)
    copies.wait()
    if across:
        across.sent(at.out_before.at[0], at.stream_in)


def dense_forward_scratch(geo, tick):
    length, width, heads = geo.length, geo.width, geo.heads
    scratch = dict(
        stream=pltpu.VMEM((length, width), BF16),
        qkv_w=pltpu.VMEM((width, 3 * width), BF16),
        rest_w=pltpu.VMEM((width, width + 128), BF16),
        bias_here=pltpu.VMEM((heads, length, length), BF16),
        normed=pltpu.VMEM((length, width), BF16),
        qkv=pltpu.VMEM((length, 3 * width), BF16),
        prob=pltpu.VMEM((heads, length, length), BF16),
        context=pltpu.VMEM((length, width), BF16),
        residual=pltpu.VMEM((length, width), F32),
        moe_in=pltpu.VMEM((length, width), BF16),
        aux=pltpu.VMEM((length, 128), F32),
        slots=pltpu.VMEM((geo.units, geo.rows, geo.main, width), BF16),
        gains_here=pltpu.VMEM((8, width), F32),
        sems=pltpu.SemaphoreType.DMA((20 + width // 128,)),
        stream_sem=pltpu.SemaphoreType.DMA,
        across_sems=pltpu.SemaphoreType.DMA((4,)),
    )
    if tick == 1:
        scratch["stream_in"] = pltpu.VMEM((length, width), BF16)
    return scratch


def dense_forward_refs(geo, tick, given, state, received):
    micro, length, width, heads = geo.micro, geo.length, geo.width, geo.heads
    near = {name: given[name] for name in ("segments", "order", "routes", "bases")}
    held = {name: given[name] for name in ("packed", "bias", "inputs", "gains")}
    if tick > 1:
        held["received"] = received
    kept = dict(
        kept_stream=((micro, length, width), BF16),
        kept_normed=((micro, length, width), BF16),
        kept_qkv=((micro, length, 3 * width), BF16),
        kept_prob=((micro, heads, length, length), BF16),
        kept_context=((micro, length, width), BF16),
        kept_residual=((micro, length, width), F32),
        kept_moe_in=((micro, length, width), BF16),
        kept_aux=((micro, length, 128), F32),
    )
    return near, held, kept


def dense_forward(geo, tick, given, state, received):
    near, held, kept = dense_forward_refs(geo, tick, given, state, received)
    params = {}
    if tick == 1:
        held["out_before"] = state["out"]
        params = dict(collective_id=5 + 2 * geo.micro, has_side_effects=True)
    return launch(
        partial(where_active, only_section(geo, tick), partial(dense_forward_body, geo, tick)),
        near=near,
        held=held,
        outs=dict(slot_rows=pltpu.HBM((geo.units, geo.rows, geo.main, geo.width), BF16)),
        kept=kept,
        state=state,
        scratch=dense_forward_scratch(geo, tick),
        cost=(2_000_000_000, 14_000_000),
        **params,
    )["slot_rows"]


def combine(home, aux, result, picked_ref):
    for c, onehot in enumerate(slot_onehots(aux, home.shape[0])):
        picked = mm(onehot.astype(BF16), home, (1, 0))
        picked_ref[c] = picked.astype(BF16)
        result = result + aux[:, c : c + 1] * picked
    return result


def spread(incoming, aux, slots):
    total = 0.0
    for c, onehot in enumerate(slot_onehots(aux, slots)):
        total = total + mm(onehot.astype(BF16), (aux[:, c : c + 1] * incoming).astype(BF16), (0, 0))
    return total.astype(BF16)


def gate_gradients(incoming, picked_ref):
    lane = iota((incoming.shape[0], 128), 1)
    gates = jnp.zeros(lane.shape, F32)
    for c in range(TOP):
        gate = jnp.sum(picked_ref[c].astype(F32) * incoming, axis=1, keepdims=True)
        gates = jnp.where(lane == c, gate, gates)
    return gates


def expert_picker(geo, e):
    dims = (geo.sources * geo.share, geo.sources * geo.main)
    own, place = iota(dims, 0), iota(dims, 1)
    return (place == own // geo.share * geo.main + e * geo.share + own % geo.share).astype(BF16)


class Exchange:
    def __init__(self, geo, at, x, active=None):
        self.geo, self.x, self.at = geo, x, at
        self.relay = geo.chips // 2 if active is not None and geo.chips > 1 else None
        self.near_rows = geo.cores
        self.ahead = 2 if self.relay else 1
        self.peers = geo.cols - 1
        self.other = {"section": 1 - lax.axis_index("section")}
        self.r, self.c = lax.axis_index("row"), lax.axis_index("col")
        self.z, self.core = self.r // geo.cores, self.r % geo.cores
        self.partner = self.z * geo.cores + (self.core + 1) % geo.cores

    def far(self, direct):
        chips = sorted(range(1, self.geo.chips), key=lambda k: abs(2 * k - self.geo.chips))
        return [k for k in chips if direct or k != self.relay]

    def far_rows(self, direct):
        return self.geo.cores * len(self.far(direct))

    def kinds(self):
        first = self.geo.first if self.relay else 0
        return [(pl.ds(at, n), direct) for at, n, direct in ((0, first, True), (first, self.geo.units - first, False)) if n]

    def chip(self, k):
        return (self.z + k + self.geo.chips) % self.geo.chips

    def row(self, k, d):
        return self.partner if k == 0 else self.chip(k) * self.geo.cores + d

    def col(self, j):
        return (self.c + j + self.geo.cols) % self.geo.cols

    def rows(self, k):
        return pl.ds(self.chip(k) * self.geo.cores, self.geo.cores)

    def others(self, k):
        return range(self.geo.cores - 1) if k == 0 else range(self.geo.cores)

    def greet(self):
        barrier = pltpu.get_barrier_semaphore()
        for k in range(self.geo.chips):
            for d in self.others(k):
                pl.semaphore_signal(barrier, inc=1, device_id={"row": self.row(k, d)}, device_id_type=MESH)
        for j in range(1, self.geo.cols):
            pl.semaphore_signal(barrier, inc=1, device_id={"col": self.col(j)}, device_id_type=MESH)
        if self.relay:
            pl.semaphore_signal(barrier, inc=1, device_id=self.other, device_id_type=MESH)

    def await_greetings(self, more):
        more = more + (1 if self.relay else 0)
        pl.semaphore_wait(pltpu.get_barrier_semaphore(), self.geo.rows + self.geo.cols - 2 + more)

    def came(self, block, sem):
        remote(block, block, self.at.done, sem, self.other).wait_recv()

    def left(self, block, sem):
        remote(block, block, sem, self.at.done, self.other).wait_send()


    def own(self, u):
        return pltpu.make_async_copy(
            self.x.at[u, self.r], self.at.inbox.at[u, self.c, self.r], self.at.own_sem.at[u]
        )

    def kind(self, u):
        if not (self.relay and self.geo.first):
            return 0
        return int(u < self.geo.first) if isinstance(u, int) else (u + self.geo.units - 1) // self.geo.units * -1 + 1

    def send(self, u, k):
        for d in self.others(k):
            remote(
                self.x.at[u, self.row(k, d)], self.at.inbox.at[u, self.c, self.r], self.at.in_send.at[self.kind(u)],
                self.at.in_recv.at[u, k], {"row": self.row(k, d)},
            ).start()

    def send_out(self, u):
        if self.relay:
            remote(
                self.x.at[u, self.rows(self.relay)], self.at.via_x.at[u], self.at.via_send,
                self.at.via_x_recv.at[u], self.other,
            ).start()

    def hand_over(self, u, k):
        block = self.at.inbox.at[u, self.c, self.rows(-k)]
        for j in range(1, self.geo.cols):
            remote(block, block, self.at.pass_send.at[u], self.at.pass_recv.at[u], {"col": self.col(j)}).start()

    def each(self, body):
        lax.fori_loop(0, self.geo.units, lambda u, carry: (body(u), carry)[1], 0)

    def open(self):
        for u in range(min(self.ahead, self.geo.units)):
            direct = u < self.geo.first
            for k in self.far(direct):
                self.send(u, k)
            if not direct:
                self.send_out(u)

        def body(u):
            self.own(u).start()
            self.send(u, 0)

        self.each(body)
        for u in range(min(3, self.geo.units)):
            self.pass_on_own(u)

    def pass_on_own(self, u):
        self.own(u).wait()
        if self.geo.cores > 1:
            self.came(self.at.inbox.at[u, self.c, pl.ds(0, 1)], self.at.in_recv.at[u, 0])
        self.hand_over(u, 0)

    def pass_on(self, u, direct=False):
        @pl.when(u + self.ahead < self.geo.units)
        def _():
            self.send_out(u + self.ahead)

        for k in self.far(direct):
            self.came(self.at.inbox.at[u, self.c, self.rows(-k)], self.at.in_recv.at[u, k])

            @pl.when(u + self.ahead < self.geo.units)
            def _():
                if k in self.far(False):
                    self.send(u + self.ahead, k)

            self.hand_over(u, k)

        @pl.when(u + 3 < self.geo.units)
        def _():
            self.pass_on_own(u + 3)

    def collect(self, u, direct=False):
        if self.peers:
            block = self.at.inbox.at[u, pl.ds(0, self.peers), pl.ds(0, self.near_rows + self.far_rows(direct))]
            self.came(block, self.at.pass_recv.at[u])
            self.left(block, self.at.pass_send.at[u])
        if self.relay and not direct:
            self.came(self.at.inbox.at[u, :, pl.ds(0, self.geo.cores)], self.at.into_recv.at[u])


    def send_parts(self, u, far, direct=False):
        if far and self.relay and not direct:
            for j in range(self.geo.cols):
                remote(
                    self.at.inbox.at[u, self.col(j), self.rows(self.relay)], self.at.via_part.at[u, j],
                    self.at.via_part_send, self.at.via_part_recv.at[u], self.other,
                ).start()
        for k in self.far(direct) if far else (0,):
            for j in range(1, self.geo.cols):
                remote(
                    self.at.inbox.at[u, self.col(j), self.rows(k)], self.at.arrived.at[u, j - 1, self.rows(k)],
                    self.at.out_send.at[self.kind(u)], self.at.out_recv.at[u, k], {"col": self.col(j)},
                ).start()

    def send_home(self, u, far, direct=False):
        for k in self.far(direct) if far else (0,):
            rows = self.rows(k)
            if self.peers:
                self.came(self.at.arrived.at[u, :, rows], self.at.out_recv.at[u, k])
            total = self.at.inbox[u, self.c, rows].astype(F32)
            for j in range(1, self.geo.cols):
                total = total + self.at.arrived[u, j - 1, rows].astype(F32)
            self.at.stage[u, rows] = total.astype(BF16)
            for d in self.others(k):
                remote(
                    self.at.stage.at[u, self.row(k, d)], self.at.home.at[u, self.r], self.at.home_send.at[self.kind(u)],
                    self.at.home_recv.at[self.kind(u)], {"row": self.row(k, d)},
                ).start()
            if k == 0:
                self.at.home[u, self.r] = self.at.stage[u, self.r]

    def finish(self):
        at, cores = self.at, self.geo.cores
        for units, direct in self.kinds():
            sent_rows = self.far_rows(direct) + cores - 1
            if sent_rows:
                block = at.home.at[units, pl.ds(0, sent_rows)]
                self.came(block, at.home_recv.at[int(direct)])
                self.left(block, at.home_send.at[int(direct)])
                self.left(block, at.in_send.at[int(direct)])
            if self.peers:
                block = at.arrived.at[units, :, pl.ds(0, self.near_rows + self.far_rows(direct))]
                self.left(block, at.out_send.at[int(direct)])
            if self.relay and not direct:
                self.came(at.home.at[units, pl.ds(0, cores)], at.home_in_recv)
                self.left(at.via_x.at[units], at.via_send)
                self.left(at.via_part.at[units], at.via_part_send)


    def along(self, u, d, source, target, at):
        where = {"row": self.row(self.relay, d)}
        return remote(
            source.at[u, d], target.at[u, self.core], self.at.core_sems.at[at, u, d],
            self.at.core_sems.at[at + 1, u, self.core], where,
        )

    def along_came(self, u, d, target, at):
        self.came(target.at[u, d], self.at.core_sems.at[at + 1, u, d])

    def across(self, u, j):
        return remote(
            self.at.via_z.at[u], self.at.via_y.at[u, j - 1], self.at.via_sems.at[2, u, j], self.at.via_sems.at[3, u, j],
            {"col": self.col(j)},
        )

    def into(self, u, j):
        source = self.at.via_y.at[u, j - 1] if j else self.at.via_z.at[u]
        target = self.at.inbox.at[u, self.col(-j), self.rows(-self.relay)]
        return remote(source, target, self.at.via_sems.at[0, u, j], self.at.into_recv.at[u], self.other)

    def part_across(self, u, j):
        return remote(
            self.at.via_part.at[u, j], self.at.via_sum.at[u, j - 1], self.at.via_sems.at[4, u, j],
            self.at.via_sems.at[5, u, j], {"col": self.col(j)},
        )

    def home_in(self, u):
        return remote(
            self.at.via_home.at[u], self.at.home.at[u, self.rows(-self.relay)], self.at.via_sems.at[1, u, 0],
            self.at.home_in_recv, self.other,
        )

    def carry(self):
        geo, at = self.geo, self.at
        cores, columns = range(geo.cores), range(1, geo.cols)

        def rows_out(u):
            self.came(at.via_x.at[u], at.via_x_recv.at[u])
            for d in cores:
                self.along(u, d, at.via_x, at.via_z, 0).start()

        def rows_on(u):
            for d in cores:
                self.along_came(u, d, at.via_z, 0)
            self.into(u, 0).start()
            for j in columns:
                self.across(u, j).start()

        def rows_in(u):
            for j in columns:
                self.across(u, j).wait_recv()
                self.into(u, j).start()

        def parts_out(u):
            self.came(at.via_part.at[u], at.via_part_recv.at[u])
            for j in columns:
                self.part_across(u, j).start()

        def parts_on(u):
            total = at.via_part[u, 0].astype(F32)
            for j in columns:
                self.part_across(u, j).wait_recv()
                total = total + at.via_sum[u, j - 1].astype(F32)
            at.via_total[u] = total.astype(BF16)
            for d in cores:
                self.along(u, d, at.via_total, at.via_home, 2).start()

        def parts_in(u):
            for d in cores:
                self.along_came(u, d, at.via_home, 2)
            self.home_in(u).start()

        units = list(range(geo.first, geo.units))
        for steps in ((rows_out, rows_on, rows_in), (parts_out, parts_on, parts_in)):
            for t in range(len(units) + 2):
                for lag, work in enumerate(steps):
                    if 0 <= t - lag < len(units):
                        work(units[t - lag])
        for u in units:
            for d in cores:
                self.along(u, d, at.via_x, at.via_z, 0).wait_send()
                self.along(u, d, at.via_total, at.via_home, 2).wait_send()
            for j in range(geo.cols):
                self.into(u, j).wait_send()
            for j in columns:
                self.across(u, j).wait_send()
                self.part_across(u, j).wait_send()
            self.home_in(u).wait_send()


def run_experts(geo, exchange, rows, total, shared, loads, expert, saves, opened=lambda: None):
    first, count = geo.first, geo.sources * geo.main
    inbox = exchange.at.inbox
    width = inbox.shape[-1]
    exchange.open()
    opened()
    if first:
        exchange.pass_on(0, True)
    exchange.pass_on(first)
    if first:
        exchange.collect(0, True)
        shared[...] = jnp.zeros(shared.shape, F32)

    def step(e, carry):
        u = e + first
        slot = e % 2

        @pl.when(e + 1 < geo.local_experts)
        def _():
            exchange.pass_on(u + 1)

        exchange.collect(u)

        @pl.when(e >= 2)
        def _():
            for copy in saves(e - 2, slot):
                copy.wait()

        rows[slot, :count] = inbox[u].reshape(count, width)
        if first:
            picker = expert_picker(geo, e)
            tail = inbox[0].reshape(count, width)
            rows[slot, count:] = mm(picker, tail, (1, 0)).astype(BF16)
        for copy in loads(e):
            copy.wait()
        expert(e, slot)
        for copy in saves(e, slot):
            copy.start()
        inbox[u] = total[:count].astype(BF16).reshape(inbox.shape[1:])
        exchange.send_parts(u, True)
        if first:
            shared[...] += mm(picker, total[count:].astype(BF16), (0, 0))

        @pl.when(e >= 1)
        def _():
            exchange.send_home(u - 1, True)
            if exchange.relay:
                exchange.send_parts(u - 1, False)

        return carry

    lax.fori_loop(0, geo.local_experts, step, 0)
    if first:
        inbox[0] = shared[...].astype(BF16).reshape(inbox.shape[1:])
        exchange.send_parts(0, True, True)
    near = [u for u in range(geo.units) if not exchange.relay or u < first or u == geo.units - 1]
    half = len(near) // 2
    exchange.send_home(geo.units - 1, True)
    for u in near[half:]:
        exchange.send_parts(u, False)
    if first:
        exchange.send_home(0, True, True)
    for u in near[:half]:
        exchange.send_parts(u, False)
    exchange.each(lambda u: exchange.send_home(u, False))
    for e in range(max(0, geo.local_experts - 2), geo.local_experts):
        for copy in saves(e, e % 2):
            copy.wait()
    exchange.finish()


def share_work(exchange, active, work):
    if not exchange.relay:
        work()
        return
    section = lax.axis_index("section")
    pl.when(section == active)(work)

    @pl.when(section != active)
    def _():
        exchange.await_greetings(0)
        exchange.carry()


def start_loads(geo, loads):
    for e in range(geo.local_experts):
        for copy in loads(e):
            copy.start()


def forward_body(geo, tick, tile, fused, at):
    m = forward_micro(geo, tick)
    take, send = fused and tick == 1, 1 <= tick < geo.micro
    active = only_section(geo, tick)
    exchange = Exchange(geo, at, at.slots if fused else at.slot_rows, active)
    exchange.greet()
    across_in, across_out = Across(0, at.across_sems, 2), Across(0, at.across_sems)
    if take or send:
        across_out.greet()
    w_in, w_out = at.w_in_here, at.w_out_here

    def loads(e):
        return (
            pltpu.make_async_copy(at.w_in.at[e], w_in.at[e], at.load_sem.at[e, 0]),
            pltpu.make_async_copy(at.w_out.at[e], w_out.at[e], at.load_sem.at[e, 1]),
        )

    def saves(e, slot):
        return (
            pltpu.make_async_copy(at.rows.at[slot], at.kept_rows.at[m, e], at.save_sem.at[slot, 0]),
            pltpu.make_async_copy(at.wide.at[slot], at.kept_hidden.at[m, e], at.save_sem.at[slot, 1]),
            pltpu.make_async_copy(at.slope.at[slot], at.kept_slope.at[m, e], at.save_sem.at[slot, 2]),
        )

    def expert(e, slot):
        for f in range(0, geo.hidden, tile):
            value, derivative = gelu_pair(mm(at.rows[slot], w_in[e, :, f : f + tile], (1, 0)))
            value = value.astype(BF16)
            at.wide[slot, :, f : f + tile] = value
            at.slope[slot, :, f : f + tile] = derivative.astype(BF16)
            product = mm(value, w_out[e, f : f + tile, :], (1, 0))
            at.total[...] = product if f == 0 else at.total[...] + product

    def enter():
        exchange.await_greetings(int(take or send))

    def work():
        copies = Copies(at.sems)
        if fused:
            dense_forward_part(geo, tick, at, copies, enter, across_in, lambda: start_loads(geo, loads))
            if not take:
                enter()
        else:
            start_loads(geo, loads)
            aux_load = copies.load(at.kept_aux.at[m], at.aux)
            residual_load = copies.load(at.kept_residual.at[m], at.residual)
            enter()
        run_experts(geo, exchange, at.rows, at.total, at.shared, loads, expert, saves)
        if not fused:
            aux_load.wait()
            residual_load.wait()
        home = at.home[...].reshape(geo.slots, geo.width)
        at.result[...] = combine(home, at.aux[...], at.residual[...], at.picked).astype(BF16)
        if send:
            across_out.send(at.result, at.received_out)
        copies.save(at.result, at.out.at[m])
        copies.save(at.picked, at.kept_picked.at[m])
        copies.wait()
        if take:
            across_in.sent(at.out.at[0], at.stream_in)
        if send:
            across_out.take(at.received_out)
            across_out.sent(at.result, at.received_out)

    share_work(exchange, active, work)


def backward_body(geo, step, tile, fused, at):
    m = backward_micro(geo, step)
    take, send = step == 1, fused and 1 <= step < geo.micro
    active = only_section(geo, geo.micro - step)
    exchange = Exchange(geo, at, at.slot_grad, active)
    exchange.greet()
    first = lax.axis_index("section") == 0
    across, across_out = Across(1, at.across_sems), Across(1, at.across_sems, 2)
    if take or send:
        across.greet()
    w_in, w_out = at.w_in_here, at.w_out_here

    def loads(e):
        return (
            pltpu.make_async_copy(at.w_out.at[e], w_out.at[e], at.load_sem.at[e, 1]),
            pltpu.make_async_copy(at.kept_slope.at[m, e], at.slope.at[e], at.load_sem.at[e, 2]),
            pltpu.make_async_copy(at.w_in.at[e], w_in.at[e], at.load_sem.at[e, 0]),
        )

    def saves(e, slot):
        return (
            pltpu.make_async_copy(at.rows.at[slot], at.kept_seen.at[m, e], at.save_sem.at[slot, 0]),
            pltpu.make_async_copy(at.wide.at[slot], at.kept_pre.at[m, e], at.save_sem.at[slot, 1]),
        )

    def expert(e, slot):
        for f in range(0, geo.hidden, tile):
            grad = mm(at.rows[slot], w_out[e, f : f + tile, :], (1, 1))
            value = (grad * at.slope[e, :, f : f + tile].astype(F32)).astype(BF16)
            at.wide[slot, :, f : f + tile] = value
            product = mm(value, w_in[e, :, f : f + tile], (1, 1))
            at.total[...] = product if f == 0 else at.total[...] + product

    def incoming_load():
        own = pltpu.make_async_copy(at.cotangent.at[m], at.incoming_here, at.incoming_sem)
        if step == 0:
            return [own], [own]
        if step == 1:
            return [], [own]
        return [pltpu.make_async_copy(at.received, at.incoming_here, at.incoming_sem)], [own]

    def of_sections(action):
        early, late = incoming_load()

        @pl.when(first)
        def _():
            for copy in early:
                getattr(copy, action)()

        @pl.when(jnp.logical_not(first))
        def _():
            for copy in late:
                getattr(copy, action)()

    def work():
        copies = Copies(at.sems)
        picked_load = copies.load(at.kept_picked.at[m], at.picked)
        aux_load = copies.load(at.kept_aux.at[m], at.aux)
        of_sections("start")
        start_loads(geo, loads)
        dense_loads = dense_backward_loads(geo, m, at, copies) if fused else None
        exchange.await_greetings(int(take or send))
        if take:
            across.send(at.sent, at.incoming_far)
            across.take(at.incoming_far)

            @pl.when(first)
            def _():
                at.incoming_here[...] = at.incoming_far[...]

        of_sections("wait")
        aux_load.wait()
        slot_grad = spread(at.incoming_here[...].astype(F32), at.aux[...], geo.slots)
        at.slot_grad[...] = slot_grad.reshape(at.slot_grad.shape)

        def opened():
            picked_load.wait()
            at.incoming[...] = at.incoming_here[...]
            at.gates[...] = gate_gradients(at.incoming_here[...].astype(F32), at.picked)

        run_experts(geo, exchange, at.rows, at.total, at.shared, loads, expert, saves, opened)
        first_slots, second_slots = slot_onehots(at.aux[...], geo.slots)
        home = at.home[...].reshape(geo.slots, geo.width)
        at.moe_grad[...] = mm((first_slots | second_slots).astype(BF16), home, (1, 0))
        if fused:
            dense_backward_part(geo, step, at, copies, dense_loads, lambda: None, across_out if send else None)
        if take:
            across.sent(at.sent, at.incoming_far)

    share_work(exchange, active, work)


def tile_of(hidden, limit):
    return limit if hidden % limit == 0 else hidden


def experts_scratch(geo, slope_slots):
    rows, local, width, hidden = geo.expert_rows, geo.local_experts, geo.width, geo.hidden
    steps = max(1, geo.cols - 1)
    one = pltpu.SemaphoreType.DMA
    two = pltpu.SemaphoreType.DMA((2,))
    unit = pltpu.SemaphoreType.DMA((geo.units,))
    return dict(
        inbox=pltpu.VMEM((geo.units, geo.cols, geo.rows, geo.main, width), BF16),
        arrived=pltpu.VMEM((geo.units, steps, geo.rows, geo.main, width), BF16),
        stage=pltpu.VMEM((geo.units, geo.rows, geo.main, width), BF16),
        home=pltpu.VMEM((geo.units, geo.rows, geo.main, width), BF16),
        picked=pltpu.VMEM((TOP, geo.length, width), BF16),
        aux=pltpu.VMEM((geo.length, 128), F32),
        rows=pltpu.VMEM((2, rows, width), BF16),
        wide=pltpu.VMEM((2, rows, hidden), BF16),
        slope=pltpu.VMEM((slope_slots, rows, hidden), BF16),
        w_in_here=pltpu.VMEM((local, width, hidden), BF16),
        w_out_here=pltpu.VMEM((local, hidden, width), BF16),
        total=pltpu.VMEM((rows, width), F32),
        shared=pltpu.VMEM((geo.sources * geo.main if geo.share else 16, width), F32),
        via_x=pltpu.VMEM((geo.units, geo.cores, geo.main, width), BF16),
        via_z=pltpu.VMEM((geo.units, geo.cores, geo.main, width), BF16),
        via_y=pltpu.VMEM((geo.units, steps, geo.cores, geo.main, width), BF16),
        via_part=pltpu.VMEM((geo.units, geo.cols, geo.cores, geo.main, width), BF16),
        via_sum=pltpu.VMEM((geo.units, steps, geo.cores, geo.main, width), BF16),
        via_total=pltpu.VMEM((geo.units, geo.cores, geo.main, width), BF16),
        via_home=pltpu.VMEM((geo.units, geo.cores, geo.main, width), BF16),
        via_sems=pltpu.SemaphoreType.DMA((6, geo.units, geo.cols)),
        core_sems=pltpu.SemaphoreType.DMA((4, geo.units, geo.cores)),
        own_sem=unit, pass_send=unit, pass_recv=unit, into_recv=unit, via_x_recv=unit, via_part_recv=unit,
        in_send=two, out_send=two, home_send=two, home_recv=two, home_in_recv=one, via_send=one, via_part_send=one,
        done=one,
        in_recv=pltpu.SemaphoreType.DMA((geo.units, geo.chips)),
        out_recv=pltpu.SemaphoreType.DMA((geo.units, geo.chips)),
        load_sem=pltpu.SemaphoreType.DMA((local, 3)),
        save_sem=pltpu.SemaphoreType.DMA((2, 3)),
        sems=pltpu.SemaphoreType.DMA((6,)),
        across_sems=pltpu.SemaphoreType.DMA((4,)),
    )


def experts_cost(geo):
    weights = geo.local_experts * geo.hidden * geo.width
    return (4 * geo.expert_rows * weights, 4 * weights)


def forward_scratch(geo):
    scratch = experts_scratch(geo, 2)
    scratch["residual"] = pltpu.VMEM((geo.length, geo.width), F32)
    scratch["result"] = pltpu.VMEM((geo.length, geo.width), BF16)
    return scratch


def forward_tick(geo, tick, given, state, received):
    micro, length, width = geo.micro, geo.length, geo.width
    rows, local, hidden = geo.expert_rows, geo.local_experts, geo.hidden
    dense, scratch = dense_forward_scratch(geo, tick), forward_scratch(geo)
    fused = fits(dense, scratch)
    near, kept = {}, {}
    held = dict(w_in=given["w_in"], w_out=given["w_out"])
    if fused:
        near, dense_held, kept = dense_forward_refs(geo, tick, given, state, received)
        held.update(dense_held)
        scratch.update(dense)
    else:
        held["slot_rows"] = dense_forward(geo, tick, given, state, received)
        held.update(kept_aux=state["kept_aux"], kept_residual=state["kept_residual"])
    kept.update(
        out=((micro, length, width), BF16),
        kept_picked=((micro, TOP, length, width), BF16),
        kept_rows=((micro, local, rows, width), BF16),
        kept_hidden=((micro, local, rows, hidden), BF16),
        kept_slope=((micro, local, rows, hidden), BF16),
    )
    results = launch(
        partial(forward_body, geo, tick, tile_of(hidden, 768), fused),
        near=near,
        held=held,
        outs=dict(received_out=pltpu.HBM((length, width), BF16)) if 1 <= tick < micro else {},
        kept=kept,
        state=state,
        scratch=scratch,
        cost=experts_cost(geo),
        collective_id=3 + tick,
        has_side_effects=True,
    )
    return results.get("received_out")


def backward_step(geo, step, given, state, sent, received):
    micro, length, width = geo.micro, geo.length, geo.width
    rows, local, hidden = geo.expert_rows, geo.local_experts, geo.hidden
    scratch = experts_scratch(geo, local)
    scratch["slot_grad"] = pltpu.VMEM((geo.units, geo.rows, geo.main, width), BF16)
    scratch["incoming_here"] = pltpu.VMEM((length, width), BF16)
    scratch["incoming_sem"] = pltpu.SemaphoreType.DMA
    held = dict(
        cotangent=given["cotangent"], w_in=given["w_in"], w_out=given["w_out"], kept_aux=state["kept_aux"],
        kept_picked=state["kept_picked"], kept_slope=state["kept_slope"],
    )
    if step == 1:
        held["sent"] = sent
        scratch["incoming_far"] = pltpu.VMEM((length, width), BF16)
    elif step:
        held["received"] = received
    between = dict(
        moe_grad=shape((length, width), F32), gates=shape((length, 128), F32), incoming=shape((length, width), BF16)
    )
    dense = dense_backward_scratch(geo)
    near, outs, kept = {}, between, {}
    between_scratch = {name: pltpu.VMEM(one.shape, one.dtype) for name, one in between.items()}
    fused = fits(scratch, dense, between_scratch)
    if fused:
        near, dense_held, outs, kept = dense_backward_refs(geo, step, given, state)
        held.update(dense_held)
        scratch.update(dense)
        scratch.update(between_scratch)
    kept.update(
        kept_seen=((micro, local, rows, width), BF16),
        kept_pre=((micro, local, rows, hidden), BF16),
    )
    results = launch(
        partial(backward_body, geo, step, tile_of(hidden, 768), fused),
        near=near,
        held=held,
        outs=outs,
        kept=kept,
        state=state,
        scratch=scratch,
        cost=experts_cost(geo),
        collective_id=4 + micro + step,
        has_side_effects=True,
    )
    return results if fused else dense_backward(geo, step, results, given, state)


class Shards:
    def __init__(self, geo):
        self.cores, self.chips, self.cols = geo.cores, geo.chips, geo.cols
        r, self.c = lax.axis_index("row"), lax.axis_index("col")
        self.z, self.core = r // self.cores, r % self.cores

    def chip(self, k):
        return (self.z + k + self.chips) % self.chips

    def col(self, j):
        return (self.c + j + self.cols) % self.cols

    def row(self, z, other=0):
        return z * self.cores + (self.core + other) % self.cores

    def greet(self):
        barrier = pltpu.get_barrier_semaphore()
        targets = [{"row": self.row(self.chip(k))} for k in range(1, self.chips)]
        targets += [{"col": self.col(j)} for j in range(1, self.cols)]
        targets += [{"row": self.row(self.z, 1)}] * (self.cores - 1)
        for target in targets:
            pl.semaphore_signal(barrier, inc=1, device_id=target, device_id_type=MESH)
        self.greeted = len(targets)

    def await_greetings(self):
        pl.semaphore_wait(pltpu.get_barrier_semaphore(), self.greeted)


def gather_kernel(geo, pieces, qkv, out, router, gain_one, gain_two, terms, all_ref, small, own_sems, z_send, z_recv,
                  y_send, y_recv, core_send, core_recv):
    at = Shards(geo)
    at.greet()
    share, total = all_ref.shape[2:]
    narrow, wide = out.shape[1], qkv.shape[1]
    mine = all_ref.at[at.row(at.z), at.c]
    copies = Copies(own_sems)
    copies.save(qkv, mine.at[:, pl.ds(0, wide)])
    copies.save(out, mine.at[:, pl.ds(wide, narrow)])
    experts_all, count = router.shape[0], terms.shape[1]

    def unit(dims, shift=0):
        return (iota(dims, 0) + shift == iota(dims, 1)).astype(BF16)

    columns = mm(router[...], unit((experts_all, 128)), (0, 0))
    long_terms = mm(terms[...], unit((count, share)), (1, 0)).astype(BF16)
    for k, row in enumerate((gain_one[...], gain_two[...], long_terms)):
        columns = columns + mm(row, unit((1, 128), experts_all + k), (0, 0))
    small[...] = columns.astype(BF16)
    copies.save(small, mine.at[:, pl.ds(wide + narrow, 128)])
    copies.wait()
    at.await_greetings()
    step = total // pieces

    def block(k, j, h):
        return all_ref.at[at.row(at.chip(-k)), at.col(-j), :, pl.ds(h * step, step)]

    def pass_z(k, h):
        own = block(0, 0, h)
        remote(own, own, z_send, z_recv.at[h, k - 1], {"row": at.row(at.chip(k))}).start()

    def pass_y(k, h):
        for j in range(1, at.cols):
            one = block(k, 0, h)
            remote(one, one, y_send, y_recv.at[h, k, j - 1], {"col": at.col(j)}).start()

    def pass_core(k, j, h):
        if at.cores > 1:
            one = block(k, j, h)
            remote(one, one, core_send, core_recv, {"row": at.row(at.z, 1)}).start()

    def came(one, sem):
        remote(one, one, core_send, sem, {"row": at.row(at.z, 1)}).wait_recv()

    def left(one, sem):
        remote(one, one, sem, core_recv, {"row": at.row(at.z, 1)}).wait_send()

    def take_y(h):
        for k in range(at.chips):
            for j in range(1, at.cols):
                came(block(k, j, h), y_recv.at[h, k, j - 1])
                pass_core(k, j, h)

    ahead = min(2, pieces)
    for h in range(ahead):
        for k in range(1, at.chips):
            pass_z(k, h)
    for h in range(pieces):
        pass_y(0, h)
    for h in range(pieces):
        pass_core(0, 0, h)
    for h in range(pieces):
        for k in range(1, at.chips):
            came(block(k, 0, h), z_recv.at[h, k - 1])
            if h + ahead < pieces:
                pass_z(k, h + ahead)
            pass_y(k, h)
            pass_core(k, 0, h)
        if h:
            take_y(h - 1)
    take_y(pieces - 1)
    if at.cores > 1:
        came(all_ref.at[pl.ds(0, at.chips)], core_recv)
        left(all_ref.at[pl.ds(0, at.chips)], core_send)
    if at.chips > 1:
        left(all_ref.at[pl.ds(0, at.chips - 1), 0], z_send)
    if at.cols > 1:
        left(all_ref.at[pl.ds(0, at.chips), pl.ds(0, at.cols - 1)], y_send)


def gather_shards(geo, qkv, out, router, gain_one, gain_two, terms):
    share, total = qkv.shape[0], qkv.shape[1] + out.shape[1] + 128
    pieces = 5 if total % 640 == 0 else 1
    one = pltpu.SemaphoreType.DMA
    return pl.pallas_call(
        partial(gather_kernel, geo, pieces),
        out_shape=pltpu.HBM((geo.rows, geo.cols, share, total), BF16),
        in_specs=[hbm_spec()] * 2 + [vmem_spec()] * 4,
        out_specs=hbm_spec(),
        scratch_shapes=[
            pltpu.VMEM((share, 128), BF16),
            pltpu.SemaphoreType.DMA((3,)),
            one, pltpu.SemaphoreType.DMA((pieces, max(1, geo.chips - 1))),
            one, pltpu.SemaphoreType.DMA((pieces, geo.chips, max(1, geo.cols - 1))),
            one, one,
        ],
        compiler_params=pltpu.CompilerParams(collective_id=1, has_side_effects=True),
    )(in_hbm(qkv), in_hbm(out), router, gain_one, gain_two, terms)


def reduce_part(shards, refs, groups):
    at = shards
    started = []

    def start(copy):
        copy.start()
        started.append(copy)

    def to_core(g, k):
        return remote(
            refs.part.at[at.row(at.chip(k), 1), :, :, lanes[g]], refs.from_core.at[k, :, :, lanes[g]],
            refs.core_send.at[g, k], refs.core_recv.at[g, k], {"row": at.row(at.z, 1)},
        )

    def to_col(g, k, j):
        return remote(
            refs.pair.at[k, at.col(j), :, lanes[g]], refs.from_col.at[k, j - 1, :, lanes[g]],
            refs.y_send.at[g, k, j - 1], refs.y_recv.at[g, k, j - 1], {"col": at.col(j)},
        )

    def to_chip(g, k):
        return remote(
            refs.column.at[k - 1, :, lanes[g]], refs.from_chip.at[k - 1, :, lanes[g]], refs.z_send.at[g, k - 1],
            refs.z_recv.at[g, k - 1], {"row": at.row(at.chip(k))},
        )

    def sum_cores(g, k):
        total = refs.part[at.row(at.chip(k)), :, :, lanes[g]].astype(F32)
        if at.cores > 1:
            to_core(g, k).wait_recv()
            total = total + refs.from_core[k, :, :, lanes[g]].astype(F32)
        refs.pair[k, :, :, lanes[g]] = total.astype(BF16)
        for j in range(1, at.cols):
            start(to_col(g, k, j))

    def sum_cols(g, k):
        total = refs.pair[k, at.c, :, lanes[g]].astype(F32)
        for j in range(1, at.cols):
            to_col(g, k, j).wait_recv()
            total = total + refs.from_col[k, j - 1, :, lanes[g]].astype(F32)
        if k:
            refs.column[k - 1, :, lanes[g]] = total.astype(BF16)
            start(to_chip(g, k))
        else:
            refs.shard[:, lanes[g]] = total

    lanes, waiting = [], []

    def advance(g, k):
        sum_cores(g, k)
        waiting.append((g, k))
        if len(waiting) > 2:
            sum_cols(*waiting.pop(0))

    far = sorted(range(1, at.chips), key=lambda k: abs(2 * k - at.chips))
    for places in groups:
        lanes.append(places)
        g = len(lanes) - 1
        if at.cores > 1:
            for k in far + [0]:
                start(to_core(g, k))
        if g:
            for k in far:
                advance(g - 1, k)
    for k in far:
        advance(len(lanes) - 1, k)
    for g in range(len(lanes)):
        advance(g, 0)
    while waiting:
        sum_cols(*waiting.pop(0))
    for g in range(len(lanes)):
        for k in far:
            to_chip(g, k).wait_recv()
            refs.shard[:, lanes[g]] += refs.from_chip[k - 1, :, lanes[g]].astype(F32)
    for copy in started:
        copy.wait_send()


def reduce_scratch(geo, share, width):
    chips, steps, far = geo.chips, max(1, geo.cols - 1), max(1, geo.chips - 1)
    z = pltpu.SemaphoreType.DMA((4, far))
    y = pltpu.SemaphoreType.DMA((4, chips, steps))
    core = pltpu.SemaphoreType.DMA((4, chips))
    return dict(
        from_core=pltpu.VMEM((chips, geo.cols, share, width), BF16),
        from_col=pltpu.VMEM((chips, steps, share, width), BF16),
        from_chip=pltpu.VMEM((far, share, width), BF16),
        pair=pltpu.VMEM((chips, geo.cols, share, width), BF16),
        column=pltpu.VMEM((far, share, width), BF16),
        core_send=core, core_recv=core, y_send=y, y_recv=y, z_send=z, z_recv=z,
    )


def expert_weights_kernel(experts_all, rows, pre, hidden, seen, packed, in_grad, out_grad, qkv, out, router, one, two,
                          terms):
    def product(left, right):
        left, right = (ref[:, 0].reshape(-1, ref.shape[-1]) for ref in (left, right))
        return mm(left, right, (0, 0))

    in_grad[0, 0] = product(rows, pre)
    out_grad[0, 0] = product(hidden, seen)

    @pl.when((pl.program_id(0) == 0) & (pl.program_id(1) == 0))
    def _():
        wide, narrow = qkv.shape[2], out.shape[2]
        qkv[0] = packed[:, :wide]
        out[0] = packed[:, wide : wide + narrow]
        small = packed[:, wide + narrow :]
        dims = (experts_all + 8, 128)
        pick = (iota(dims, 0) == iota(dims, 1)).astype(F32)
        lines = lax.dot_general(
            pick, small, (((1,), (1,)), ((), ())), precision=lax.Precision.HIGHEST, preferred_element_type=F32
        )
        router[0] = lines[:experts_all]
        one[...] = lines[experts_all : experts_all + 1]
        two[...] = lines[experts_all + 1 : experts_all + 2]
        terms[...] = lines[experts_all + 2 : experts_all + 3, : terms.shape[1]]


def expert_weights(geo, state, packed, terms):
    micro, local, count, width, hidden = geo.micro, geo.local_experts, geo.expert_rows, geo.width, geo.hidden
    tile = tile_of(hidden, 768)
    narrow = pl.BlockSpec((micro, 1, count, width), lambda e, f: (0, e, 0, 0))
    wide = pl.BlockSpec((micro, 1, count, tile), lambda e, f: (0, e, 0, f))
    flops = 4 * micro * local * count * width * hidden
    share = packed.shape[0]
    small = [(1, share, 3 * width), (1, share, width), (1, geo.experts_all, share), (1, share), (1, share), (1, terms)]

    def whole(dims):
        return pl.BlockSpec(dims, lambda e, f: (0,) * len(dims))

    return pl.pallas_call(
        partial(expert_weights_kernel, geo.experts_all),
        out_shape=[shape((1, local, width, hidden), F32), shape((1, local, hidden, width), F32)]
        + [shape(dims, F32) for dims in small],
        grid=(local, hidden // tile),
        in_specs=[narrow, wide, wide, narrow, whole(packed.shape)],
        out_specs=[
            pl.BlockSpec((1, 1, width, tile), lambda e, f: (0, e, 0, f)),
            pl.BlockSpec((1, 1, tile, width), lambda e, f: (0, e, f, 0)),
        ]
        + [whole(dims) for dims in small],
        compiler_params=pltpu.CompilerParams(vmem_limit_bytes=48 * MIB),
        cost_estimate=pl.CostEstimate(
            flops=flops, bytes_accessed=8 * local * hidden * width, transcendentals=0
        ),
    )(*(in_hbm(state[name]) for name in ("kept_rows", "kept_pre", "kept_hidden", "kept_seen")), packed)


def norm_backward(values, gain, grad):
    factor = norm_factor(values)
    unit = values * factor
    weighted = grad * gain
    inner = jnp.mean(weighted * unit, axis=-1, keepdims=True)
    return factor * (weighted - unit * inner), jnp.sum(grad * unit, axis=0, keepdims=True)


def dense_backward_loads(geo, m, at, copies):
    width = geo.width
    return dict(
        rest=copies.load(at.packed.at[:, pl.ds(3 * width, width + 128)], at.rest_w),
        gains=copies.load(at.gains, at.gains_here),
        residual=copies.load(at.kept_residual.at[m], at.residual),
        qkv=copies.load(at.kept_qkv.at[m], at.qkv),
        prob=copies.load(at.kept_prob.at[m], at.prob),
        stream=copies.load(at.kept_stream.at[m], at.stream),
        qkv_w=copies.load(at.packed.at[:, pl.ds(0, 3 * width)], at.qkv_w),
    )


def dense_backward_part(geo, step, at, copies, loads, enter, across):
    length, width, heads = geo.length, geo.width, geo.heads
    size = width // heads
    per = 128 // size
    m = backward_micro(geo, step)
    send = across is not None
    aux = at.aux[...]
    slope = aux[:, 0:1] * aux[:, 1:2] * (at.gates[:, 0:1] - at.gates[:, 1:2])
    expert_at = iota((length, 128), 1).astype(F32)
    logit_grad = (
        jnp.where(as_column(at.routes[0, m, 0:1, :].astype(F32)) == expert_at, slope, 0.0)
        - jnp.where(as_column(at.routes[0, m, 1:2, :].astype(F32)) == expert_at, slope, 0.0)
    ).astype(BF16)
    at.logit[...] = logit_grad
    copies.save(at.logit, at.kept_logit.at[m])
    loads["rest"].wait()
    moe_grad = at.moe_grad[...] + mm(logit_grad, at.rest_w[:, width:], (1, 1))
    loads["residual"].wait()
    loads["gains"].wait()
    part, gain_two = norm_backward(at.residual[...], at.gains_here[1:2, :], moe_grad)
    residual_grad = at.incoming[...].astype(F32) + part
    at.branch[...] = residual_grad.astype(BF16)
    copies.save(at.branch, at.kept_branch.at[m])
    at.context_grad[...] = mm(at.branch[...], at.rest_w[:, :width], (1, 1)).astype(BF16)
    which = iota((length, 128), 1) // size
    head_row = iota((128, length), 0) // size
    scale = 1.0 / math.sqrt(size)
    zero = jnp.zeros((length, 128), BF16)
    loads["qkv"].wait()
    loads["prob"].wait()
    at.sums[...] = jnp.zeros(at.sums.shape, F32)
    for j in range(width // 128):
        places = [slice(base * width + 128 * j, base * width + 128 * (j + 1)) for base in range(3)]
        queries, keys, values = (at.qkv[:, place] for place in places)
        grad = at.context_grad[:, places[0]]
        turned_keys = keys.astype(F32).T
        totals = [jnp.zeros(dims, F32) for dims in ((128, length), (length, 128), (length, 128))]
        for part_at in range(per):
            h = j * per + part_at
            own = which == part_at
            own_grad = jnp.where(own, grad, zero)
            prob = at.prob[h]
            prob_grad = mm(values, own_grad, (1, 1))
            weighted = prob.astype(F32)
            shift = jnp.sum(weighted * prob_grad, axis=0, keepdims=True)
            score_grad = (weighted * (prob_grad - shift)).astype(BF16)
            at.sums[h : h + 1, :] = diagonal_sums(score_grad.astype(F32))
            own_keys = jnp.where(head_row == part_at, turned_keys, 0.0).astype(BF16)
            totals[0] = totals[0] + mm(own_keys, score_grad, (1, 0))
            totals[1] = totals[1] + mm(score_grad, jnp.where(own, queries, zero), (1, 0))
            totals[2] = totals[2] + mm(prob, own_grad, (1, 0))
        at.qkv_grad[:, places[0]] = (totals[0].T * scale).astype(BF16)
        at.qkv_grad[:, places[1]] = (totals[1] * scale).astype(BF16)
        at.qkv_grad[:, places[2]] = totals[2].astype(BF16)
    copies.save(at.qkv_grad, at.kept_qkv_grad.at[m])
    copies.save(at.sums, at.kept_sums.at[m])
    loads["qkv_w"].wait()
    normed_grad = mm(at.qkv_grad[...], at.qkv_w[...], (1, 1))
    loads["stream"].wait()
    part, gain_one = norm_backward(at.stream[...].astype(F32), at.gains_here[0:1, :], normed_grad)
    at.gain_parts[...] = jnp.zeros(at.gain_parts.shape, F32)
    at.gain_parts[0:1, :] = gain_one
    at.gain_parts[1:2, :] = gain_two
    copies.save(at.gain_parts, at.kept_gains.at[m])
    in_grad = residual_grad + part
    at.in_grad_here[...] = in_grad
    copies.save(at.in_grad_here, at.in_grad.at[m])
    if step < geo.micro:
        at.sent_here[...] = in_grad.astype(BF16)
    if send:
        enter()
        across.send(at.sent_here, at.received_out)
    elif step < geo.micro:
        copies.save(at.sent_here, at.sent_out)
    copies.wait()
    if send:
        across.take(at.received_out)
        across.sent(at.sent_here, at.received_out)


def dense_backward_body(geo, step, at):
    send = 1 <= step < geo.micro
    across = Across(1, at.across_sems) if send else None
    if send:
        across.greet()

    def enter():
        pl.semaphore_wait(pltpu.get_barrier_semaphore(), 1)

    m = backward_micro(geo, step)
    copies = Copies(at.sems)
    aux_load = copies.load(at.kept_aux.at[m], at.aux)
    loads = dense_backward_loads(geo, m, at, copies)
    aux_load.wait()
    dense_backward_part(geo, step, at, copies, loads, enter, across)


def dense_backward_scratch(geo):
    length, width, heads = geo.length, geo.width, geo.heads
    return dict(
        aux=pltpu.VMEM((length, 128), F32),
        rest_w=pltpu.VMEM((width, width + 128), BF16),
        qkv_w=pltpu.VMEM((width, 3 * width), BF16),
        residual=pltpu.VMEM((length, width), F32),
        qkv=pltpu.VMEM((length, 3 * width), BF16),
        prob=pltpu.VMEM((heads, length, length), BF16),
        stream=pltpu.VMEM((length, width), BF16),
        logit=pltpu.VMEM((length, 128), BF16),
        branch=pltpu.VMEM((length, width), BF16),
        context_grad=pltpu.VMEM((length, width), BF16),
        qkv_grad=pltpu.VMEM((length, 3 * width), BF16),
        sums=pltpu.VMEM((geo.tall, length), F32),
        gain_parts=pltpu.VMEM((8, width), F32),
        in_grad_here=pltpu.VMEM((length, width), F32),
        gains_here=pltpu.VMEM((8, width), F32),
        sent_here=pltpu.VMEM((length, width), BF16),
        sems=pltpu.SemaphoreType.DMA((20,)),
        across_sems=pltpu.SemaphoreType.DMA((4,)),
    )


def dense_backward_refs(geo, step, given, state):
    micro, length, width = geo.micro, geo.length, geo.width
    outs = {}
    if 1 <= step < micro:
        outs["received_out"] = pltpu.HBM((length, width), BF16)
    elif step < micro:
        outs["sent_out"] = pltpu.HBM((length, width), BF16)
    names = ("kept_aux", "kept_residual", "kept_qkv", "kept_prob", "kept_stream")
    held = dict({name: state[name] for name in names}, packed=given["packed"], gains=given["gains"])
    kept = dict(
        in_grad=((micro, length, width), F32),
        kept_branch=((micro, length, width), BF16),
        kept_qkv_grad=((micro, length, 3 * width), BF16),
        kept_logit=((micro, length, 128), BF16),
        kept_gains=((micro, 8, width), F32),
        kept_sums=((micro, geo.tall, length), F32),
    )
    return dict(routes=given["routes"]), held, outs, kept


def dense_backward(geo, step, near, given, state):
    more, held, outs, kept = dense_backward_refs(geo, step, given, state)
    params = {}
    if 1 <= step < geo.micro:
        params = dict(collective_id=5 + 2 * geo.micro + step, has_side_effects=True)
    return launch(
        partial(where_active, only_section(geo, geo.micro - step), partial(dense_backward_body, geo, step)),
        near=dict(near, **more),
        held=held,
        outs=outs,
        kept=kept,
        state=state,
        scratch=dense_backward_scratch(geo),
        cost=(3_000_000_000, 14_000_000),
        **params,
    )


DENSE_GRADS = ("normed", "qkv_grad", "context", "branch", "moe_in", "logit")


def dense_weights_groups(geo, at):
    width = geo.width
    copies = Copies(at.sems)
    loads = {}
    for name in DENSE_GRADS + ("gains", "sums"):
        loads[name] = copies.load(getattr(at, "kept_" + name), getattr(at, name))

    def product(left, right):
        left, right = (ref[...].reshape(-1, ref.shape[-1]) for ref in (left, right))
        return mm(left, right, (0, 0))

    def ready(*names):
        for name in names:
            loads[name].wait()

    def put(places, block):
        block = block.astype(BF16)
        if len(at.part.shape) == 4:
            at.part[:, :, :, places] = block.reshape(at.part.shape[:3] + block.shape[1:])
        else:
            at.part[:, places] = block

    ready("normed", "qkv_grad")
    normed = at.normed[...].reshape(-1, width)
    for j in range(0, 3 * width, width):
        grad = at.qkv_grad[:, :, j : j + width].reshape(-1, width)
        put(slice(j, j + width), mm(normed, grad, (0, 0)))
        yield slice(j, j + width)
    ready("context", "branch")
    put(slice(3 * width, 4 * width), product(at.context, at.branch))
    ready("moe_in", "logit", "gains", "sums")
    small = product(at.moe_in, at.logit)
    by_term = lax.dot_general(
        jnp.sum(at.sums[...], axis=0), at.spread[...].astype(F32), (((1,), (1,)), ((), ())),
        precision=lax.Precision.HIGHEST, preferred_element_type=F32,
    )
    bias_row = jnp.sum(by_term[: geo.heads] * at.head_pick[...], axis=0, keepdims=True)
    gain_rows = jnp.sum(at.gains[...], axis=0)
    place = iota((128, width), 0)
    rows = jnp.zeros((128, width), F32)
    for k, row in enumerate((gain_rows[0:1], gain_rows[1:2], bias_row)):
        rows = jnp.where(place == geo.experts_all + k, row, rows)
    put(slice(4 * width, 4 * width + 128), small + rows.T)
    yield slice(3 * width, 4 * width + 128)


def dense_weights_body(geo, at):
    for _ in dense_weights_groups(geo, at):
        pass


def reduce_body(geo, at):
    shards = Shards(geo)
    shards.greet()

    def groups():
        for g, places in enumerate(dense_weights_groups(geo, at)):
            if g == 0:
                shards.await_greetings()
            yield places

    reduce_part(shards, at, groups())


def dense_weights(geo, head_pick, spread_table, state):
    held = {"kept_" + name: state["kept_" + name] for name in DENSE_GRADS + ("gains", "sums")}
    scratch = {name: pltpu.VMEM(held["kept_" + name].shape, BF16) for name in DENSE_GRADS}
    scratch.update(
        sems=pltpu.SemaphoreType.DMA((len(DENSE_GRADS) + 2,)),
        gains=pltpu.VMEM(state["kept_gains"].shape, F32), sums=pltpu.VMEM(state["kept_sums"].shape, F32),
    )
    share, total = geo.width // geo.sources, 4 * geo.width + 128
    parts = (geo.rows, geo.cols, share, total)
    fused = share % 16 == 0
    outs = dict(shard=shape((share, total), F32)) if fused else dict(part=shape((geo.width, total), BF16))
    params = {}
    if fused:
        scratch.update(reduce_scratch(geo, share, total), part=pltpu.VMEM(parts, BF16))
        params = dict(collective_id=2, has_side_effects=True)
    results = launch(
        partial(reduce_body if fused else dense_weights_body, geo),
        near=dict(head_pick=head_pick, spread=spread_table),
        held=held,
        outs=outs,
        scratch=scratch,
        spare=24,
        cost=(3_000_000_000, 10_000_000),
        **params,
    )
    if fused:
        return results["shard"]

    def body(at):
        shards = Shards(geo)
        shards.greet()
        shards.await_greetings()
        reduce_part(shards, at, [slice(0, total)])

    return launch(
        body,
        near=dict(part=results["part"].reshape(parts)),
        outs=dict(shard=shape((share, total), F32)),
        scratch=reduce_scratch(geo, share, total),
        collective_id=2,
        has_side_effects=True,
    )["shard"]


def on_device(
    inputs, cotangent, segments, routes, order, attn_gain, qkv_weight, position_bias, out_weight, moe_gain,
    router_weight, expert_in, expert_out,
):
    micro, length, width = inputs.shape
    local_experts, hidden = expert_in.shape[1], expert_in.shape[3]
    experts_all = router_weight.shape[2]
    row_count, col_count = lax.axis_size("row"), lax.axis_size("col")
    devices = row_count * col_count
    share = width // devices
    terms = position_bias.shape[1]
    heads = terms * devices // DISTANCE_BUCKETS
    geo = Geometry(micro, length, width, heads, experts_all, local_experts, hidden, row_count, col_count)
    packed = gather_shards(
        geo, qkv_weight[0], out_weight[0], router_weight[0].T, attn_gain, moe_gain, position_bias
    ).reshape(width, -1)
    indicator = buckets(length)
    row_at = np.arange(width)
    term_at = np.where(row_at % share < terms, row_at // share * terms + row_at % share, -1)
    head_pick = jnp.asarray((term_at % heads == np.arange(heads)[:, None]) & (term_at >= 0), F32)
    spread_table = jnp.asarray(indicator[np.maximum(term_at, 0) // heads], BF16)
    prepared = launch(
        partial(prepare, experts_all),
        near=dict(head_pick=head_pick, spread=spread_table),
        held=dict(packed=packed),
        outs=dict(gains=pltpu.HBM((8, width), F32), bias=pltpu.HBM((heads, length, length), BF16)),
        scratch=dict(
            small=pltpu.VMEM((width, 128), BF16), gains_here=pltpu.VMEM((8, width), F32),
            bias_here=pltpu.VMEM((heads, length, length), BF16), sems=pltpu.SemaphoreType.DMA((3,)),
        ),
        cost=(50_000_000, 6_000_000),
    )
    given = dict(
        prepared, packed=packed, inputs=inputs, cotangent=cotangent, w_in=expert_in[0], w_out=expert_out[0],
        segments=segments, order=order, routes=jnp.swapaxes(routes, 2, 3),
        bases=jnp.asarray(geo.bases()),
    )
    state = {}
    received = None
    for tick in range(micro + 1):
        received = forward_tick(geo, tick, given, state, received)
    sent = received = None
    for step in range(micro + 1):
        passed = backward_step(geo, step, given, state, sent, received)
        sent, received = passed.get("sent_out"), passed.get("received_out")
    packed = dense_weights(geo, head_pick, spread_table, state)
    expert_in_grad, expert_out_grad, qkv, out, router, gain_one, gain_two, bias = expert_weights(
        geo, state, packed, terms
    )
    return (
        state["out"][None], state["in_grad"][None], gain_one, qkv, bias, out, gain_two,
        jnp.swapaxes(router, 1, 2), expert_in_grad,
        expert_out_grad,
    )


def solution(mesh):
    tokens = ("row", "col")
    return jax.shard_map(
        on_device,
        mesh=mesh,
        in_specs=(
            P(None, tokens, None),
            P(None, tokens, None),
            P(None, tokens),
            P("section", None, tokens, None),
            P("section", None, tokens, None),
            P("section", tokens),
            P("section", tokens, None),
            P("section", tokens),
            P("section", tokens, None),
            P("section", tokens),
            P("section", tokens, None),
            P("section", "row", None, "col"),
            P("section", "row", "col", None),
        ),
        out_specs=(
            P("section", None, tokens, None),
            P("section", None, tokens, None),
            P("section", tokens),
            P("section", tokens, None),
            P("section", tokens),
            P("section", tokens, None),
            P("section", tokens),
            P("section", tokens, None),
            P("section", "row", None, "col"),
            P("section", "row", "col", None),
        ),
        check_vma=False,
    )
```

```python
from functools import partial
import math
from types import SimpleNamespace

import jax
import jax.numpy as jnp
import numpy as np
from jax import lax
from jax.experimental import pallas as pl
from jax.experimental.pallas import tpu as pltpu
from jax.sharding import PartitionSpec as P

TOP = 2
DISTANCE_BUCKETS = 32
MAX_DIST = 128
EPS = 1e-06
MESH = pl.DeviceIdType.MESH
F32 = jnp.float32
BF16 = jnp.bfloat16
MIB = 1 << 20


class Geometry:
    def __init__(self, micro, length, width, heads, experts_all, local_experts, hidden, row_count, col_count):
        self.micro, self.length, self.width, self.heads, self.hidden = micro, length, width, heads, hidden
        self.tall = -(-heads // 8) * 8
        self.capacity = max(2, (5 * length * TOP + 4 * experts_all - 1) // (4 * experts_all))
        self.local_experts = local_experts
        self.experts_all = experts_all
        self.rows, self.cols = row_count, col_count
        self.cores = 2 if row_count % 2 == 0 else 1
        self.chips = row_count // self.cores
        main = self.capacity // 16 * 16
        rest = self.capacity - main
        self.share = main // local_experts if 0 < rest <= main // local_experts else 0
        if rest and not self.share:
            main += 16
        self.main = main
        self.first = 1 if self.share else 0
        self.units = local_experts + self.first
        self.slots = row_count * self.units * main
        self.sources = row_count * col_count
        self.expert_rows = self.sources * (main + self.share)

    def bases(self):
        expert = np.arange(self.experts_all)
        owner, local = expert // self.local_experts, expert % self.local_experts
        main = ((self.first + local) * self.rows + owner) * self.main
        tail = owner * self.main + local * self.share
        both = np.stack([main, tail]).astype(np.float32)
        return np.pad(both, ((0, 0), (0, 128 - self.experts_all)))


def buckets(length):
    distance = np.arange(length)
    bucket = np.zeros(length, np.int64)
    half = DISTANCE_BUCKETS // 2
    for level in range(1, DISTANCE_BUCKETS):
        if level < half:
            limit = level
        else:
            limit = int(math.ceil(half * (MAX_DIST / half) ** ((level - half) / half)))
        bucket += distance >= limit
    return (np.arange(DISTANCE_BUCKETS)[:, None] == bucket[None, :]).astype(np.float32)


def mm(left, right, contract):
    return lax.dot_general(
        left, right, (((contract[0],), (contract[1],)), ((), ())), preferred_element_type=F32
    )


def iota(shape, axis):
    return lax.broadcasted_iota(jnp.int32, shape, axis)


def norm_factor(values):
    return lax.rsqrt(jnp.mean(values * values, axis=-1, keepdims=True) + EPS)


def gelu_pair(x):
    density = jnp.exp(-0.5 * x * x)
    t = 1.0 / (1.0 + (0.3275911 * math.sqrt(0.5)) * jnp.abs(x))
    poly = 0.5 * 1.061405429
    for coefficient in (-1.453152027, 1.421413741, -0.284496736, 0.254829592):
        poly = poly * t + 0.5 * coefficient
    beyond = poly * t * density
    cdf = jnp.where(x >= 0, 1.0 - beyond, beyond)
    return x * cdf, cdf + x * density * (1.0 / math.sqrt(2.0 * math.pi))


def slot_onehots(aux, slots):
    positions = iota((aux.shape[0], slots), 1).astype(F32)
    return [(aux[:, 2 + c : 3 + c] == positions) for c in range(TOP)]


def vmem_grant(scratch, spare):
    held = 0
    for ref in scratch:
        if getattr(ref, "memory_space", None) == pltpu.VMEM:
            held += math.prod(ref.shape) * jnp.dtype(ref.dtype).itemsize
    return -(-held // MIB) + spare


def fits(*scratches):
    return vmem_grant([ref for scratch in scratches for ref in scratch.values()], 11) <= 62


def vmem_spec():
    return pl.BlockSpec(memory_space=pltpu.VMEM)


def hbm_spec():
    return pl.BlockSpec(memory_space=pltpu.HBM)


def in_hbm(array):
    return pltpu.with_memory_space_constraint(array, pltpu.HBM)


def shape(dims, kind):
    return jax.ShapeDtypeStruct(dims, kind)


def launch(body, near=None, held=None, outs=None, kept=None, state=None, scratch=None, spare=10, cost=None, **params):
    near, held, outs, kept, scratch = (dict(part or {}) for part in (near, held, outs, kept, scratch))
    state = {} if state is None else state
    old = [name for name in kept if name in state]
    names_in, names_out = list(near) + list(held), list(outs) + list(kept)

    def kernel(*refs):
        refs = list(refs)
        given, refs = refs[: len(names_in)], refs[len(names_in) + len(old) :]
        body(SimpleNamespace(**dict(zip(names_in + names_out + list(scratch), given + refs))))

    out_shapes = list(outs.values()) + [pltpu.HBM(dims, kind) for dims, kind in kept.values()]
    plain = [isinstance(out, jax.ShapeDtypeStruct) for out in out_shapes]
    estimate = {}
    if cost is not None:
        estimate["cost_estimate"] = pl.CostEstimate(flops=cost[0], bytes_accessed=cost[1], transcendentals=0)
    results = pl.pallas_call(
        kernel,
        out_shape=out_shapes,
        in_specs=[vmem_spec()] * len(near) + [hbm_spec()] * (len(held) + len(old)),
        out_specs=[vmem_spec() if near_by else hbm_spec() for near_by in plain],
        scratch_shapes=list(scratch.values()),
        input_output_aliases={len(names_in) + i: names_out.index(name) for i, name in enumerate(old)},
        compiler_params=pltpu.CompilerParams(
            vmem_limit_bytes=vmem_grant(scratch.values(), spare) * MIB, **params
        ),
        **estimate,
    )(*near.values(), *map(in_hbm, held.values()), *(in_hbm(state[name]) for name in old))
    results = dict(zip(names_out, results))
    for name in kept:
        state[name] = results.pop(name)
    return results


def of_micro(rows, m):
    if isinstance(m, int):
        return rows[m : m + 1]
    row = rows[0:1]
    for i in range(1, rows.shape[0]):
        row = jnp.where(m == i, rows[i : i + 1], row)
    return row


def as_column(row):
    return jnp.broadcast_to(row, (8, row.shape[1])).T[:, 0:1]


class Copies:
    def __init__(self, sems):
        self.sems, self.count, self.open = sems, 0, []

    def load(self, source, target):
        copy = pltpu.make_async_copy(source, target, self.sems.at[self.count])
        self.count += 1
        copy.start()
        return copy

    def save(self, source, target):
        self.open.append(self.load(source, target))

    def wait(self):
        for copy in self.open:
            copy.wait()


def remote(source, target, send, receive, where):
    return pltpu.make_async_remote_copy(
        src_ref=source, dst_ref=target, send_sem=send, recv_sem=receive, device_id=where, device_id_type=MESH
    )


def forward_micro(geo, tick):
    if tick == 0:
        return 0
    return geo.micro - 1 if tick == geo.micro else tick - lax.axis_index("section")


def backward_micro(geo, step):
    if step == 0:
        return geo.micro - 1
    return 0 if step == geo.micro else geo.micro - step - lax.axis_index("section")


class Across:
    def __init__(self, sender, sems, at=0):
        self.section = lax.axis_index("section")
        self.sender, self.other = sender, {"section": 1 - self.section}
        self.send_sem, self.recv_sem = sems.at[at], sems.at[at + 1]

    def greet(self):
        pl.semaphore_signal(pltpu.get_barrier_semaphore(), inc=1, device_id=self.other, device_id_type=MESH)

    def copy(self, source, target):
        return remote(source, target, self.send_sem, self.recv_sem, self.other)

    def send(self, source, target):
        @pl.when(self.section == self.sender)
        def _():
            self.copy(source, target).start()

    def sent(self, source, target):
        @pl.when(self.section == self.sender)
        def _():
            self.copy(source, target).wait_send()

    def take(self, target):
        @pl.when(self.section != self.sender)
        def _():
            self.copy(target, target).wait_recv()


def prepare(experts_all, at):
    heads, length = at.bias_here.shape[:2]
    width = at.small.shape[0]
    copies = Copies(at.sems)
    copies.load(at.packed.at[:, pl.ds(4 * width, 128)], at.small).wait()
    rows = at.small[...].astype(F32).T
    at.gains_here[0:2, :] = rows[experts_all : experts_all + 2]
    copies.save(at.gains_here, at.gains)
    picked = (at.head_pick[...] * rows[experts_all + 2 : experts_all + 3]).astype(BF16)
    by_distance = mm(picked, at.spread[...], (1, 0))
    for h in range(heads):
        block = by_distance[h : h + 1, :]
        step = 1
        while step < length:
            block = jnp.concatenate([block, pltpu.roll(block, step, 1)], axis=0)
            step *= 2
        at.bias_here[h] = block.astype(BF16)
    copies.save(at.bias_here, at.bias)
    copies.wait()


def diagonal_sums(block):
    length = block.shape[1]
    size = block.shape[0] // 2
    while size >= 1:
        block = block[:size] + pltpu.roll(block[size:], length - size, 1)
        size //= 2
    return block


def only_section(geo, tick):
    return {0: 0, geo.micro: 1}.get(tick)


def where_active(active, body, at):
    if active is None:
        body(at)
    else:
        pl.when(lax.axis_index("section") == active)(partial(body, at))


def dense_forward_part(geo, tick, at, copies, enter, across, loaded, fused=True):
    length, width, heads = geo.length, geo.width, geo.heads
    size = width // heads
    per = 128 // size
    m = forward_micro(geo, tick)
    gains_load = copies.load(at.gains, at.gains_here)
    thirds = [pl.ds(third * width, width) for third in range(3)]
    packed_qkv = [copies.load(at.packed.at[:, third], at.qkv_w.at[:, third]) for third in thirds]
    if tick == 0:
        copies.load(at.inputs.at[m], at.stream).wait()
    else:
        first = lax.axis_index("section") == 0
        own = pltpu.make_async_copy(at.inputs.at[m], at.stream, at.stream_sem)
        if tick == 1:
            enter()
            across.send(at.out.at[0] if fused else at.out_before.at[0], at.stream_in)
        else:
            came = pltpu.make_async_copy(at.received, at.stream, at.stream_sem)

        @pl.when(first)
        def _():
            own.start()
            own.wait()

        if tick == 1:
            across.take(at.stream_in)

            @pl.when(jnp.logical_not(first))
            def _():
                at.stream[...] = at.stream_in[...]
        else:

            @pl.when(jnp.logical_not(first))
            def _():
                came.start()
                came.wait()

    packed_rest = copies.load(at.packed.at[:, pl.ds(3 * width, width + 128)], at.rest_w)
    bias_load = copies.load(at.bias, at.bias_here)
    copies.save(at.stream, at.kept_stream.at[m])
    stream = at.stream[...].astype(F32)
    gains_load.wait()
    at.normed[...] = (stream * norm_factor(stream) * at.gains_here[0:1, :]).astype(BF16)
    copies.save(at.normed, at.kept_normed.at[m])
    for third, load in zip(thirds, packed_qkv):
        load.wait()
        at.qkv[:, third] = mm(at.normed[...], at.qkv_w[:, third], (1, 0)).astype(BF16)
    copies.save(at.qkv, at.kept_qkv.at[m])
    key_at, query_at = iota((length, length), 0), iota((length, length), 1)
    segments = of_micro(at.segments[...], m).astype(F32)
    allowed = (key_at <= query_at) & (as_column(segments) == segments)
    which = iota((length, 128), 1) // size
    head_row = iota((128, length), 0) // size
    scale = 1.0 / math.sqrt(size)
    zero = jnp.zeros((length, 128), BF16)
    bias_load.wait()
    for j in range(width // 128):
        queries = at.qkv[:, 128 * j : 128 * (j + 1)]
        keys = at.qkv[:, width + 128 * j : width + 128 * (j + 1)]
        values = at.qkv[:, 2 * width + 128 * j : 2 * width + 128 * (j + 1)]
        turned_values = values.astype(F32).T
        context = jnp.zeros((128, length), F32)
        for part in range(per):
            h = j * per + part
            own = which == part
            scores = mm(jnp.where(own, keys, zero), queries, (1, 1)) * scale + at.bias_here[h].astype(F32)
            scores = jnp.where(allowed, scores, -1e30)
            exponent = jnp.exp(scores - jnp.max(scores, axis=0, keepdims=True))
            prob = (exponent * (1.0 / jnp.sum(exponent, axis=0, keepdims=True))).astype(BF16)
            at.prob[h] = prob
            own_values = jnp.where(head_row == part, turned_values, 0.0).astype(BF16)
            context = context + mm(own_values, prob, (1, 0))
        at.context[:, 128 * j : 128 * (j + 1)] = context.T.astype(BF16)
    copies.save(at.prob, at.kept_prob.at[m])
    copies.save(at.context, at.kept_context.at[m])
    packed_rest.wait()
    loaded()
    residual = stream + mm(at.context[...], at.rest_w[:, :width], (1, 0))
    at.residual[...] = residual
    copies.save(at.residual, at.kept_residual.at[m])
    moe_in = (residual * norm_factor(residual) * at.gains_here[1:2, :]).astype(BF16)
    at.moe_in[...] = moe_in
    copies.save(at.moe_in, at.kept_moe_in.at[m])
    logits = mm(moe_in, at.rest_w[:, width:], (1, 0))
    expert_at = iota(logits.shape, 1)
    picks = [(as_column(at.routes[0, m, c : c + 1, :].astype(F32)) == expert_at.astype(F32)).astype(F32) for c in range(TOP)]
    chosen = [jnp.sum(pick * logits, axis=1, keepdims=True) for pick in picks]
    top = jnp.maximum(chosen[0], chosen[1])
    powers = [jnp.exp(value - top) for value in chosen]
    total = powers[0] + powers[1]
    shares = [power / total for power in powers]
    order = of_micro(at.order[0, :, 0, :], m).astype(F32)
    before = (order < as_column(order)).astype(BF16)
    counts = [mm(before, pick.astype(BF16), (1, 0)) for pick in picks]
    counts[1] = counts[1] + jnp.sum(picks[0], axis=0, keepdims=True)
    slots = []
    for pick, count in zip(picks, counts):
        rank = jnp.sum(pick * count, axis=1, keepdims=True)
        main = jnp.sum(pick * at.bases[0:1, :], axis=1, keepdims=True)
        tail = jnp.sum(pick * at.bases[1:2, :], axis=1, keepdims=True)
        place = jnp.where(rank < geo.main, main + rank, tail + rank - geo.main)
        slots.append(jnp.where(rank < geo.capacity, place, -1.0))
    lane = iota((length, 128), 1)
    aux = jnp.zeros((length, 128), F32)
    for place, value in enumerate(shares + slots):
        aux = jnp.where(lane == place, value, aux)
    at.aux[...] = aux
    copies.save(at.aux, at.kept_aux.at[m])
    first, second = slot_onehots(aux, geo.slots)
    at.slots[...] = mm((first | second).astype(BF16), moe_in, (0, 0)).astype(BF16).reshape(at.slots.shape)


def dense_forward_body(geo, tick, at):
    across = Across(0, at.across_sems) if tick == 1 else None
    if across:
        across.greet()

    def enter():
        pl.semaphore_wait(pltpu.get_barrier_semaphore(), 1)

    copies = Copies(at.sems)
    dense_forward_part(geo, tick, at, copies, enter, across, lambda: None, fused=False)
    copies.save(at.slots, at.slot_rows)
    copies.wait()
    if across:
        across.sent(at.out_before.at[0], at.stream_in)


def dense_forward_scratch(geo, tick):
    length, width, heads = geo.length, geo.width, geo.heads
    scratch = dict(
        stream=pltpu.VMEM((length, width), BF16),
        qkv_w=pltpu.VMEM((width, 3 * width), BF16),
        rest_w=pltpu.VMEM((width, width + 128), BF16),
        bias_here=pltpu.VMEM((heads, length, length), BF16),
        normed=pltpu.VMEM((length, width), BF16),
        qkv=pltpu.VMEM((length, 3 * width), BF16),
        prob=pltpu.VMEM((heads, length, length), BF16),
        context=pltpu.VMEM((length, width), BF16),
        residual=pltpu.VMEM((length, width), F32),
        moe_in=pltpu.VMEM((length, width), BF16),
        aux=pltpu.VMEM((length, 128), F32),
        slots=pltpu.VMEM((geo.units, geo.rows, geo.main, width), BF16),
        gains_here=pltpu.VMEM((8, width), F32),
        sems=pltpu.SemaphoreType.DMA((20 + width // 128,)),
        stream_sem=pltpu.SemaphoreType.DMA,
        across_sems=pltpu.SemaphoreType.DMA((4,)),
    )
    if tick == 1:
        scratch["stream_in"] = pltpu.VMEM((length, width), BF16)
    return scratch


def dense_forward_refs(geo, tick, given, state, received):
    micro, length, width, heads = geo.micro, geo.length, geo.width, geo.heads
    near = {name: given[name] for name in ("segments", "order", "routes", "bases")}
    held = {name: given[name] for name in ("packed", "bias", "inputs", "gains")}
    if tick > 1:
        held["received"] = received
    kept = dict(
        kept_stream=((micro, length, width), BF16),
        kept_normed=((micro, length, width), BF16),
        kept_qkv=((micro, length, 3 * width), BF16),
        kept_prob=((micro, heads, length, length), BF16),
        kept_context=((micro, length, width), BF16),
        kept_residual=((micro, length, width), F32),
        kept_moe_in=((micro, length, width), BF16),
        kept_aux=((micro, length, 128), F32),
    )
    return near, held, kept


def dense_forward(geo, tick, given, state, received):
    near, held, kept = dense_forward_refs(geo, tick, given, state, received)
    params = {}
    if tick == 1:
        held["out_before"] = state["out"]
        params = dict(collective_id=5 + 2 * geo.micro, has_side_effects=True)
    return launch(
        partial(where_active, only_section(geo, tick), partial(dense_forward_body, geo, tick)),
        near=near,
        held=held,
        outs=dict(slot_rows=pltpu.HBM((geo.units, geo.rows, geo.main, geo.width), BF16)),
        kept=kept,
        state=state,
        scratch=dense_forward_scratch(geo, tick),
        cost=(2_000_000_000, 14_000_000),
        **params,
    )["slot_rows"]


def combine(home, aux, result, picked_ref):
    for c, onehot in enumerate(slot_onehots(aux, home.shape[0])):
        picked = mm(onehot.astype(BF16), home, (1, 0))
        picked_ref[c] = picked.astype(BF16)
        result = result + aux[:, c : c + 1] * picked
    return result


def spread(incoming, aux, slots):
    total = 0.0
    for c, onehot in enumerate(slot_onehots(aux, slots)):
        total = total + mm(onehot.astype(BF16), (aux[:, c : c + 1] * incoming).astype(BF16), (0, 0))
    return total.astype(BF16)


def gate_gradients(incoming, picked_ref):
    lane = iota((incoming.shape[0], 128), 1)
    gates = jnp.zeros(lane.shape, F32)
    for c in range(TOP):
        gate = jnp.sum(picked_ref[c].astype(F32) * incoming, axis=1, keepdims=True)
        gates = jnp.where(lane == c, gate, gates)
    return gates


def expert_picker(geo, e):
    dims = (geo.sources * geo.share, geo.sources * geo.main)
    own, place = iota(dims, 0), iota(dims, 1)
    return (place == own // geo.share * geo.main + e * geo.share + own % geo.share).astype(BF16)


class Exchange:
    def __init__(self, geo, at, x, active=None):
        self.geo, self.x, self.at = geo, x, at
        self.relay = geo.chips // 2 if active is not None and geo.chips > 1 else None
        self.near_rows = geo.cores
        self.ahead = 2 if self.relay else 1
        self.peers = geo.cols - 1
        self.other = {"section": 1 - lax.axis_index("section")}
        self.r, self.c = lax.axis_index("row"), lax.axis_index("col")
        self.z, self.core = self.r // geo.cores, self.r % geo.cores
        self.partner = self.z * geo.cores + (self.core + 1) % geo.cores

    def far(self, direct):
        chips = sorted(range(1, self.geo.chips), key=lambda k: abs(2 * k - self.geo.chips))
        return [k for k in chips if direct or k != self.relay]

    def far_rows(self, direct):
        return self.geo.cores * len(self.far(direct))

    def kinds(self):
        first = self.geo.first if self.relay else 0
        return [(pl.ds(at, n), direct) for at, n, direct in ((0, first, True), (first, self.geo.units - first, False)) if n]

    def chip(self, k):
        return (self.z + k + self.geo.chips) % self.geo.chips

    def row(self, k, d):
        return self.partner if k == 0 else self.chip(k) * self.geo.cores + d

    def col(self, j):
        return (self.c + j + self.geo.cols) % self.geo.cols

    def rows(self, k):
        return pl.ds(self.chip(k) * self.geo.cores, self.geo.cores)

    def others(self, k):
        return range(self.geo.cores - 1) if k == 0 else range(self.geo.cores)

    def greet(self):
        barrier = pltpu.get_barrier_semaphore()
        for k in range(self.geo.chips):
            for d in self.others(k):
                pl.semaphore_signal(barrier, inc=1, device_id={"row": self.row(k, d)}, device_id_type=MESH)
        for j in range(1, self.geo.cols):
            pl.semaphore_signal(barrier, inc=1, device_id={"col": self.col(j)}, device_id_type=MESH)
        if self.relay:
            pl.semaphore_signal(barrier, inc=1, device_id=self.other, device_id_type=MESH)

    def await_greetings(self, more):
        more = more + (1 if self.relay else 0)
        pl.semaphore_wait(pltpu.get_barrier_semaphore(), self.geo.rows + self.geo.cols - 2 + more)

    def came(self, block, sem):
        remote(block, block, self.at.done, sem, self.other).wait_recv()

    def left(self, block, sem):
        remote(block, block, sem, self.at.done, self.other).wait_send()


    def own(self, u):
        return pltpu.make_async_copy(
            self.x.at[u, self.r], self.at.inbox.at[u, self.c, self.r], self.at.own_sem.at[u]
        )

    def kind(self, u):
        if not (self.relay and self.geo.first):
            return 0
        return int(u < self.geo.first) if isinstance(u, int) else (u + self.geo.units - 1) // self.geo.units * -1 + 1

    def send(self, u, k):
        for d in self.others(k):
            remote(
                self.x.at[u, self.row(k, d)], self.at.inbox.at[u, self.c, self.r], self.at.in_send.at[self.kind(u)],
                self.at.in_recv.at[u, k], {"row": self.row(k, d)},
            ).start()

    def send_out(self, u):
        if self.relay:
            remote(
                self.x.at[u, self.rows(self.relay)], self.at.via_x.at[u], self.at.via_send,
                self.at.via_x_recv.at[u], self.other,
            ).start()

    def hand_over(self, u, k):
        block = self.at.inbox.at[u, self.c, self.rows(-k)]
        for j in range(1, self.geo.cols):
            remote(block, block, self.at.pass_send.at[u], self.at.pass_recv.at[u], {"col": self.col(j)}).start()

    def each(self, body):
        lax.fori_loop(0, self.geo.units, lambda u, carry: (body(u), carry)[1], 0)

    def open(self):
        for u in range(min(self.ahead, self.geo.units)):
            direct = u < self.geo.first
            for k in self.far(direct):
                self.send(u, k)
            if not direct:
                self.send_out(u)

        def body(u):
            self.own(u).start()
            self.send(u, 0)

        self.each(body)
        for u in range(min(3, self.geo.units)):
            self.pass_on_own(u)

    def pass_on_own(self, u):
        self.own(u).wait()
        if self.geo.cores > 1:
            self.came(self.at.inbox.at[u, self.c, pl.ds(0, 1)], self.at.in_recv.at[u, 0])
        self.hand_over(u, 0)

    def pass_on(self, u, direct=False):
        @pl.when(u + self.ahead < self.geo.units)
        def _():
            self.send_out(u + self.ahead)

        for k in self.far(direct):
            self.came(self.at.inbox.at[u, self.c, self.rows(-k)], self.at.in_recv.at[u, k])

            @pl.when(u + self.ahead < self.geo.units)
            def _():
                if k in self.far(False):
                    self.send(u + self.ahead, k)

            self.hand_over(u, k)

        @pl.when(u + 3 < self.geo.units)
        def _():
            self.pass_on_own(u + 3)

    def collect(self, u, direct=False):
        if self.peers:
            block = self.at.inbox.at[u, pl.ds(0, self.peers), pl.ds(0, self.near_rows + self.far_rows(direct))]
            self.came(block, self.at.pass_recv.at[u])
            self.left(block, self.at.pass_send.at[u])
        if self.relay and not direct:
            self.came(self.at.inbox.at[u, :, pl.ds(0, self.geo.cores)], self.at.into_recv.at[u])


    def send_parts(self, u, far, direct=False):
        if far and self.relay and not direct:
            for j in range(self.geo.cols):
                remote(
                    self.at.inbox.at[u, self.col(j), self.rows(self.relay)], self.at.via_part.at[u, j],
                    self.at.via_part_send, self.at.via_part_recv.at[u], self.other,
                ).start()
        for k in self.far(direct) if far else (0,):
            for j in range(1, self.geo.cols):
                remote(
                    self.at.inbox.at[u, self.col(j), self.rows(k)], self.at.arrived.at[u, j - 1, self.rows(k)],
                    self.at.out_send.at[self.kind(u)], self.at.out_recv.at[u, k], {"col": self.col(j)},
                ).start()

    def send_home(self, u, far, direct=False):
        for k in self.far(direct) if far else (0,):
            rows = self.rows(k)
            if self.peers:
                self.came(self.at.arrived.at[u, :, rows], self.at.out_recv.at[u, k])
            total = self.at.inbox[u, self.c, rows].astype(F32)
            for j in range(1, self.geo.cols):
                total = total + self.at.arrived[u, j - 1, rows].astype(F32)
            self.at.stage[u, rows] = total.astype(BF16)
            for d in self.others(k):
                remote(
                    self.at.stage.at[u, self.row(k, d)], self.at.home.at[u, self.r], self.at.home_send.at[self.kind(u)],
                    self.at.home_recv.at[self.kind(u)], {"row": self.row(k, d)},
                ).start()
            if k == 0:
                self.at.home[u, self.r] = self.at.stage[u, self.r]

    def finish(self):
        at, cores = self.at, self.geo.cores
        for units, direct in self.kinds():
            sent_rows = self.far_rows(direct) + cores - 1
            if sent_rows:
                block = at.home.at[units, pl.ds(0, sent_rows)]
                self.came(block, at.home_recv.at[int(direct)])
                self.left(block, at.home_send.at[int(direct)])
                self.left(block, at.in_send.at[int(direct)])
            if self.peers:
                block = at.arrived.at[units, :, pl.ds(0, self.near_rows + self.far_rows(direct))]
                self.left(block, at.out_send.at[int(direct)])
            if self.relay and not direct:
                self.came(at.home.at[units, pl.ds(0, cores)], at.home_in_recv)
                self.left(at.via_x.at[units], at.via_send)
                self.left(at.via_part.at[units], at.via_part_send)


    def along(self, u, d, source, target, at):
        where = {"row": self.row(self.relay, d)}
        return remote(
            source.at[u, d], target.at[u, self.core], self.at.core_sems.at[at, u, d],
            self.at.core_sems.at[at + 1, u, self.core], where,
        )

    def along_came(self, u, d, target, at):
        self.came(target.at[u, d], self.at.core_sems.at[at + 1, u, d])

    def across(self, u, j):
        return remote(
            self.at.via_z.at[u], self.at.via_y.at[u, j - 1], self.at.via_sems.at[2, u, j], self.at.via_sems.at[3, u, j],
            {"col": self.col(j)},
        )

    def into(self, u, j):
        source = self.at.via_y.at[u, j - 1] if j else self.at.via_z.at[u]
        target = self.at.inbox.at[u, self.col(-j), self.rows(-self.relay)]
        return remote(source, target, self.at.via_sems.at[0, u, j], self.at.into_recv.at[u], self.other)

    def part_across(self, u, j):
        return remote(
            self.at.via_part.at[u, j], self.at.via_sum.at[u, j - 1], self.at.via_sems.at[4, u, j],
            self.at.via_sems.at[5, u, j], {"col": self.col(j)},
        )

    def home_in(self, u):
        return remote(
            self.at.via_home.at[u], self.at.home.at[u, self.rows(-self.relay)], self.at.via_sems.at[1, u, 0],
            self.at.home_in_recv, self.other,
        )

    def carry(self):
        geo, at = self.geo, self.at
        cores, columns = range(geo.cores), range(1, geo.cols)

        def rows_out(u):
            self.came(at.via_x.at[u], at.via_x_recv.at[u])
            for d in cores:
                self.along(u, d, at.via_x, at.via_z, 0).start()

        def rows_on(u):
            for d in cores:
                self.along_came(u, d, at.via_z, 0)
            self.into(u, 0).start()
            for j in columns:
                self.across(u, j).start()

        def rows_in(u):
            for j in columns:
                self.across(u, j).wait_recv()
                self.into(u, j).start()

        def parts_out(u):
            self.came(at.via_part.at[u], at.via_part_recv.at[u])
            for j in columns:
                self.part_across(u, j).start()

        def parts_on(u):
            total = at.via_part[u, 0].astype(F32)
            for j in columns:
                self.part_across(u, j).wait_recv()
                total = total + at.via_sum[u, j - 1].astype(F32)
            at.via_total[u] = total.astype(BF16)
            for d in cores:
                self.along(u, d, at.via_total, at.via_home, 2).start()

        def parts_in(u):
            for d in cores:
                self.along_came(u, d, at.via_home, 2)
            self.home_in(u).start()

        units = list(range(geo.first, geo.units))
        for steps in ((rows_out, rows_on, rows_in), (parts_out, parts_on, parts_in)):
            for t in range(len(units) + 2):
                for lag, work in enumerate(steps):
                    if 0 <= t - lag < len(units):
                        work(units[t - lag])
        for u in units:
            for d in cores:
                self.along(u, d, at.via_x, at.via_z, 0).wait_send()
                self.along(u, d, at.via_total, at.via_home, 2).wait_send()
            for j in range(geo.cols):
                self.into(u, j).wait_send()
            for j in columns:
                self.across(u, j).wait_send()
                self.part_across(u, j).wait_send()
            self.home_in(u).wait_send()


def run_experts(geo, exchange, rows, total, shared, loads, expert, saves, opened=lambda: None):
    first, count = geo.first, geo.sources * geo.main
    inbox = exchange.at.inbox
    width = inbox.shape[-1]
    exchange.open()
    opened()
    if first:
        exchange.pass_on(0, True)
    exchange.pass_on(first)
    if first:
        exchange.collect(0, True)
        shared[...] = jnp.zeros(shared.shape, F32)

    def step(e, carry):
        u = e + first
        slot = e % 2

        @pl.when(e + 1 < geo.local_experts)
        def _():
            exchange.pass_on(u + 1)

        exchange.collect(u)

        @pl.when(e >= 2)
        def _():
            for copy in saves(e - 2, slot):
                copy.wait()

        rows[slot, :count] = inbox[u].reshape(count, width)
        if first:
            picker = expert_picker(geo, e)
            tail = inbox[0].reshape(count, width)
            rows[slot, count:] = mm(picker, tail, (1, 0)).astype(BF16)
        for copy in loads(e):
            copy.wait()
        expert(e, slot)
        for copy in saves(e, slot):
            copy.start()
        inbox[u] = total[:count].astype(BF16).reshape(inbox.shape[1:])
        exchange.send_parts(u, True)
        if first:
            shared[...] += mm(picker, total[count:].astype(BF16), (0, 0))

        @pl.when(e >= 1)
        def _():
            exchange.send_home(u - 1, True)
            if exchange.relay:
                exchange.send_parts(u - 1, False)

        return carry

    lax.fori_loop(0, geo.local_experts, step, 0)
    if first:
        inbox[0] = shared[...].astype(BF16).reshape(inbox.shape[1:])
        exchange.send_parts(0, True, True)
    near = [u for u in range(geo.units) if not exchange.relay or u < first or u == geo.units - 1]
    half = len(near) // 2
    exchange.send_home(geo.units - 1, True)
    for u in near[half:]:
        exchange.send_parts(u, False)
    if first:
        exchange.send_home(0, True, True)
    for u in near[:half]:
        exchange.send_parts(u, False)
    exchange.each(lambda u: exchange.send_home(u, False))
    for e in range(max(0, geo.local_experts - 2), geo.local_experts):
        for copy in saves(e, e % 2):
            copy.wait()
    exchange.finish()


def share_work(exchange, active, work):
    if not exchange.relay:
        work()
        return
    section = lax.axis_index("section")
    pl.when(section == active)(work)

    @pl.when(section != active)
    def _():
        exchange.await_greetings(0)
        exchange.carry()


def start_loads(geo, loads):
    for e in range(geo.local_experts):
        for copy in loads(e):
            copy.start()


def forward_body(geo, tick, tile, fused, at):
    m = forward_micro(geo, tick)
    take, send = fused and tick == 1, 1 <= tick < geo.micro
    active = only_section(geo, tick)
    exchange = Exchange(geo, at, at.slots if fused else at.slot_rows, active)
    exchange.greet()
    across_in, across_out = Across(0, at.across_sems, 2), Across(0, at.across_sems)
    if take or send:
        across_out.greet()
    w_in, w_out = at.w_in_here, at.w_out_here

    def loads(e):
        return (
            pltpu.make_async_copy(at.w_in.at[e], w_in.at[e], at.load_sem.at[e, 0]),
            pltpu.make_async_copy(at.w_out.at[e], w_out.at[e], at.load_sem.at[e, 1]),
        )

    def saves(e, slot):
        return (
            pltpu.make_async_copy(at.rows.at[slot], at.kept_rows.at[m, e], at.save_sem.at[slot, 0]),
            pltpu.make_async_copy(at.wide.at[slot], at.kept_hidden.at[m, e], at.save_sem.at[slot, 1]),
            pltpu.make_async_copy(at.slope.at[slot], at.kept_slope.at[m, e], at.save_sem.at[slot, 2]),
        )

    def expert(e, slot):
        for f in range(0, geo.hidden, tile):
            value, derivative = gelu_pair(mm(at.rows[slot], w_in[e, :, f : f + tile], (1, 0)))
            value = value.astype(BF16)
            at.wide[slot, :, f : f + tile] = value
            at.slope[slot, :, f : f + tile] = derivative.astype(BF16)
            product = mm(value, w_out[e, f : f + tile, :], (1, 0))
            at.total[...] = product if f == 0 else at.total[...] + product

    def enter():
        exchange.await_greetings(int(take or send))

    def work():
        copies = Copies(at.sems)
        if fused:
            dense_forward_part(geo, tick, at, copies, enter, across_in, lambda: start_loads(geo, loads))
            if not take:
                enter()
        else:
            start_loads(geo, loads)
            aux_load = copies.load(at.kept_aux.at[m], at.aux)
            residual_load = copies.load(at.kept_residual.at[m], at.residual)
            enter()
        run_experts(geo, exchange, at.rows, at.total, at.shared, loads, expert, saves)
        if not fused:
            aux_load.wait()
            residual_load.wait()
        home = at.home[...].reshape(geo.slots, geo.width)
        at.result[...] = combine(home, at.aux[...], at.residual[...], at.picked).astype(BF16)
        if send:
            across_out.send(at.result, at.received_out)
        copies.save(at.result, at.out.at[m])
        copies.save(at.picked, at.kept_picked.at[m])
        copies.wait()
        if take:
            across_in.sent(at.out.at[0], at.stream_in)
        if send:
            across_out.take(at.received_out)
            across_out.sent(at.result, at.received_out)

    share_work(exchange, active, work)


def backward_body(geo, step, tile, fused, at):
    m = backward_micro(geo, step)
    take, send = step == 1, fused and 1 <= step < geo.micro
    active = only_section(geo, geo.micro - step)
    exchange = Exchange(geo, at, at.slot_grad, active)
    exchange.greet()
    first = lax.axis_index("section") == 0
    across, across_out = Across(1, at.across_sems), Across(1, at.across_sems, 2)
    if take or send:
        across.greet()
    w_in, w_out = at.w_in_here, at.w_out_here

    def loads(e):
        return (
            pltpu.make_async_copy(at.w_out.at[e], w_out.at[e], at.load_sem.at[e, 1]),
            pltpu.make_async_copy(at.kept_slope.at[m, e], at.slope.at[e], at.load_sem.at[e, 2]),
            pltpu.make_async_copy(at.w_in.at[e], w_in.at[e], at.load_sem.at[e, 0]),
        )

    def saves(e, slot):
        return (
            pltpu.make_async_copy(at.rows.at[slot], at.kept_seen.at[m, e], at.save_sem.at[slot, 0]),
            pltpu.make_async_copy(at.wide.at[slot], at.kept_pre.at[m, e], at.save_sem.at[slot, 1]),
        )

    def expert(e, slot):
        for f in range(0, geo.hidden, tile):
            grad = mm(at.rows[slot], w_out[e, f : f + tile, :], (1, 1))
            value = (grad * at.slope[e, :, f : f + tile].astype(F32)).astype(BF16)
            at.wide[slot, :, f : f + tile] = value
            product = mm(value, w_in[e, :, f : f + tile], (1, 1))
            at.total[...] = product if f == 0 else at.total[...] + product

    def incoming_load():
        own = pltpu.make_async_copy(at.cotangent.at[m], at.incoming_here, at.incoming_sem)
        if step == 0:
            return [own], [own]
        if step == 1:
            return [], [own]
        return [pltpu.make_async_copy(at.received, at.incoming_here, at.incoming_sem)], [own]

    def of_sections(action):
        early, late = incoming_load()

        @pl.when(first)
        def _():
            for copy in early:
                getattr(copy, action)()

        @pl.when(jnp.logical_not(first))
        def _():
            for copy in late:
                getattr(copy, action)()

    def work():
        copies = Copies(at.sems)
        picked_load = copies.load(at.kept_picked.at[m], at.picked)
        aux_load = copies.load(at.kept_aux.at[m], at.aux)
        of_sections("start")
        start_loads(geo, loads)
        dense_loads = dense_backward_loads(geo, m, at, copies) if fused else None
        exchange.await_greetings(int(take or send))
        if take:
            across.send(at.sent, at.incoming_far)
            across.take(at.incoming_far)

            @pl.when(first)
            def _():
                at.incoming_here[...] = at.incoming_far[...]

        of_sections("wait")
        aux_load.wait()
        slot_grad = spread(at.incoming_here[...].astype(F32), at.aux[...], geo.slots)
        at.slot_grad[...] = slot_grad.reshape(at.slot_grad.shape)

        def opened():
            picked_load.wait()
            at.incoming[...] = at.incoming_here[...]
            at.gates[...] = gate_gradients(at.incoming_here[...].astype(F32), at.picked)

        run_experts(geo, exchange, at.rows, at.total, at.shared, loads, expert, saves, opened)
        first_slots, second_slots = slot_onehots(at.aux[...], geo.slots)
        home = at.home[...].reshape(geo.slots, geo.width)
        at.moe_grad[...] = mm((first_slots | second_slots).astype(BF16), home, (1, 0))
        if fused:
            dense_backward_part(geo, step, at, copies, dense_loads, lambda: None, across_out if send else None)
        if take:
            across.sent(at.sent, at.incoming_far)

    share_work(exchange, active, work)


def tile_of(hidden, limit):
    return limit if hidden % limit == 0 else hidden


def experts_scratch(geo, slope_slots):
    rows, local, width, hidden = geo.expert_rows, geo.local_experts, geo.width, geo.hidden
    steps = max(1, geo.cols - 1)
    one = pltpu.SemaphoreType.DMA
    two = pltpu.SemaphoreType.DMA((2,))
    unit = pltpu.SemaphoreType.DMA((geo.units,))
    return dict(
        inbox=pltpu.VMEM((geo.units, geo.cols, geo.rows, geo.main, width), BF16),
        arrived=pltpu.VMEM((geo.units, steps, geo.rows, geo.main, width), BF16),
        stage=pltpu.VMEM((geo.units, geo.rows, geo.main, width), BF16),
        home=pltpu.VMEM((geo.units, geo.rows, geo.main, width), BF16),
        picked=pltpu.VMEM((TOP, geo.length, width), BF16),
        aux=pltpu.VMEM((geo.length, 128), F32),
        rows=pltpu.VMEM((2, rows, width), BF16),
        wide=pltpu.VMEM((2, rows, hidden), BF16),
        slope=pltpu.VMEM((slope_slots, rows, hidden), BF16),
        w_in_here=pltpu.VMEM((local, width, hidden), BF16),
        w_out_here=pltpu.VMEM((local, hidden, width), BF16),
        total=pltpu.VMEM((rows, width), F32),
        shared=pltpu.VMEM((geo.sources * geo.main if geo.share else 16, width), F32),
        via_x=pltpu.VMEM((geo.units, geo.cores, geo.main, width), BF16),
        via_z=pltpu.VMEM((geo.units, geo.cores, geo.main, width), BF16),
        via_y=pltpu.VMEM((geo.units, steps, geo.cores, geo.main, width), BF16),
        via_part=pltpu.VMEM((geo.units, geo.cols, geo.cores, geo.main, width), BF16),
        via_sum=pltpu.VMEM((geo.units, steps, geo.cores, geo.main, width), BF16),
        via_total=pltpu.VMEM((geo.units, geo.cores, geo.main, width), BF16),
        via_home=pltpu.VMEM((geo.units, geo.cores, geo.main, width), BF16),
        via_sems=pltpu.SemaphoreType.DMA((6, geo.units, geo.cols)),
        core_sems=pltpu.SemaphoreType.DMA((4, geo.units, geo.cores)),
        own_sem=unit, pass_send=unit, pass_recv=unit, into_recv=unit, via_x_recv=unit, via_part_recv=unit,
        in_send=two, out_send=two, home_send=two, home_recv=two, home_in_recv=one, via_send=one, via_part_send=one,
        done=one,
        in_recv=pltpu.SemaphoreType.DMA((geo.units, geo.chips)),
        out_recv=pltpu.SemaphoreType.DMA((geo.units, geo.chips)),
        load_sem=pltpu.SemaphoreType.DMA((local, 3)),
        save_sem=pltpu.SemaphoreType.DMA((2, 3)),
        sems=pltpu.SemaphoreType.DMA((6,)),
        across_sems=pltpu.SemaphoreType.DMA((4,)),
    )


def experts_cost(geo):
    weights = geo.local_experts * geo.hidden * geo.width
    return (4 * geo.expert_rows * weights, 4 * weights)


def forward_scratch(geo):
    scratch = experts_scratch(geo, 2)
    scratch["residual"] = pltpu.VMEM((geo.length, geo.width), F32)
    scratch["result"] = pltpu.VMEM((geo.length, geo.width), BF16)
    return scratch


def forward_tick(geo, tick, given, state, received):
    micro, length, width = geo.micro, geo.length, geo.width
    rows, local, hidden = geo.expert_rows, geo.local_experts, geo.hidden
    dense, scratch = dense_forward_scratch(geo, tick), forward_scratch(geo)
    fused = fits(dense, scratch)
    near, kept = {}, {}
    held = dict(w_in=given["w_in"], w_out=given["w_out"])
    if fused:
        near, dense_held, kept = dense_forward_refs(geo, tick, given, state, received)
        held.update(dense_held)
        scratch.update(dense)
    else:
        held["slot_rows"] = dense_forward(geo, tick, given, state, received)
        held.update(kept_aux=state["kept_aux"], kept_residual=state["kept_residual"])
    kept.update(
        out=((micro, length, width), BF16),
        kept_picked=((micro, TOP, length, width), BF16),
        kept_rows=((micro, local, rows, width), BF16),
        kept_hidden=((micro, local, rows, hidden), BF16),
        kept_slope=((micro, local, rows, hidden), BF16),
    )
    results = launch(
        partial(forward_body, geo, tick, tile_of(hidden, 768), fused),
        near=near,
        held=held,
        outs=dict(received_out=pltpu.HBM((length, width), BF16)) if 1 <= tick < micro else {},
        kept=kept,
        state=state,
        scratch=scratch,
        cost=experts_cost(geo),
        collective_id=3 + tick,
        has_side_effects=True,
    )
    return results.get("received_out")


def backward_step(geo, step, given, state, sent, received):
    micro, length, width = geo.micro, geo.length, geo.width
    rows, local, hidden = geo.expert_rows, geo.local_experts, geo.hidden
    scratch = experts_scratch(geo, local)
    scratch["slot_grad"] = pltpu.VMEM((geo.units, geo.rows, geo.main, width), BF16)
    scratch["incoming_here"] = pltpu.VMEM((length, width), BF16)
    scratch["incoming_sem"] = pltpu.SemaphoreType.DMA
    held = dict(
        cotangent=given["cotangent"], w_in=given["w_in"], w_out=given["w_out"], kept_aux=state["kept_aux"],
        kept_picked=state["kept_picked"], kept_slope=state["kept_slope"],
    )
    if step == 1:
        held["sent"] = sent
        scratch["incoming_far"] = pltpu.VMEM((length, width), BF16)
    elif step:
        held["received"] = received
    between = dict(
        moe_grad=shape((length, width), F32), gates=shape((length, 128), F32), incoming=shape((length, width), BF16)
    )
    dense = dense_backward_scratch(geo)
    near, outs, kept = {}, between, {}
    between_scratch = {name: pltpu.VMEM(one.shape, one.dtype) for name, one in between.items()}
    fused = fits(scratch, dense, between_scratch)
    if fused:
        near, dense_held, outs, kept = dense_backward_refs(geo, step, given, state)
        held.update(dense_held)
        scratch.update(dense)
        scratch.update(between_scratch)
    kept.update(
        kept_seen=((micro, local, rows, width), BF16),
        kept_pre=((micro, local, rows, hidden), BF16),
    )
    results = launch(
        partial(backward_body, geo, step, tile_of(hidden, 768), fused),
        near=near,
        held=held,
        outs=outs,
        kept=kept,
        state=state,
        scratch=scratch,
        cost=experts_cost(geo),
        collective_id=4 + micro + step,
        has_side_effects=True,
    )
    return results if fused else dense_backward(geo, step, results, given, state)


class Shards:
    def __init__(self, geo):
        self.cores, self.chips, self.cols = geo.cores, geo.chips, geo.cols
        r, self.c = lax.axis_index("row"), lax.axis_index("col")
        self.z, self.core = r // self.cores, r % self.cores

    def chip(self, k):
        return (self.z + k + self.chips) % self.chips

    def col(self, j):
        return (self.c + j + self.cols) % self.cols

    def row(self, z, other=0):
        return z * self.cores + (self.core + other) % self.cores

    def greet(self):
        barrier = pltpu.get_barrier_semaphore()
        targets = [{"row": self.row(self.chip(k))} for k in range(1, self.chips)]
        targets += [{"col": self.col(j)} for j in range(1, self.cols)]
        targets += [{"row": self.row(self.z, 1)}] * (self.cores - 1)
        for target in targets:
            pl.semaphore_signal(barrier, inc=1, device_id=target, device_id_type=MESH)
        self.greeted = len(targets)

    def await_greetings(self):
        pl.semaphore_wait(pltpu.get_barrier_semaphore(), self.greeted)


def gather_kernel(geo, pieces, qkv, out, router, gain_one, gain_two, terms, all_ref, small, own_sems, z_send, z_recv,
                  y_send, y_recv, core_send, core_recv):
    at = Shards(geo)
    at.greet()
    share, total = all_ref.shape[2:]
    narrow, wide = out.shape[1], qkv.shape[1]
    mine = all_ref.at[at.row(at.z), at.c]
    copies = Copies(own_sems)
    copies.save(qkv, mine.at[:, pl.ds(0, wide)])
    copies.save(out, mine.at[:, pl.ds(wide, narrow)])
    experts_all, count = router.shape[0], terms.shape[1]

    def unit(dims, shift=0):
        return (iota(dims, 0) + shift == iota(dims, 1)).astype(BF16)

    columns = mm(router[...], unit((experts_all, 128)), (0, 0))
    long_terms = mm(terms[...], unit((count, share)), (1, 0)).astype(BF16)
    for k, row in enumerate((gain_one[...], gain_two[...], long_terms)):
        columns = columns + mm(row, unit((1, 128), experts_all + k), (0, 0))
    small[...] = columns.astype(BF16)
    copies.save(small, mine.at[:, pl.ds(wide + narrow, 128)])
    copies.wait()
    at.await_greetings()
    step = total // pieces

    def block(k, j, h):
        return all_ref.at[at.row(at.chip(-k)), at.col(-j), :, pl.ds(h * step, step)]

    def pass_z(k, h):
        own = block(0, 0, h)
        remote(own, own, z_send, z_recv.at[h, k - 1], {"row": at.row(at.chip(k))}).start()

    def pass_y(k, h):
        for j in range(1, at.cols):
            one = block(k, 0, h)
            remote(one, one, y_send, y_recv.at[h, k, j - 1], {"col": at.col(j)}).start()

    def pass_core(k, j, h):
        if at.cores > 1:
            one = block(k, j, h)
            remote(one, one, core_send, core_recv, {"row": at.row(at.z, 1)}).start()

    def came(one, sem):
        remote(one, one, core_send, sem, {"row": at.row(at.z, 1)}).wait_recv()

    def left(one, sem):
        remote(one, one, sem, core_recv, {"row": at.row(at.z, 1)}).wait_send()

    def take_y(h):
        for k in range(at.chips):
            for j in range(1, at.cols):
                came(block(k, j, h), y_recv.at[h, k, j - 1])
                pass_core(k, j, h)

    ahead, lag = min(3, pieces), 2
    far = sorted(range(1, at.chips), key=lambda k: abs(2 * k - at.chips))
    for h in range(ahead):
        for k in far:
            pass_z(k, h)
    for h in range(min(lag, pieces)):
        pass_y(0, h)
    for h in range(pieces):
        pass_core(0, 0, h)
    for h in range(pieces):
        if h + lag < pieces:
            pass_y(0, h + lag)
        for k in far:
            came(block(k, 0, h), z_recv.at[h, k - 1])
            if h + ahead < pieces:
                pass_z(k, h + ahead)
            pass_y(k, h)
            pass_core(k, 0, h)
        if h >= lag:
            take_y(h - lag)
    for h in range(max(0, pieces - lag), pieces):
        take_y(h)
    if at.cores > 1:
        came(all_ref.at[pl.ds(0, at.chips)], core_recv)
        left(all_ref.at[pl.ds(0, at.chips)], core_send)
    if at.chips > 1:
        left(all_ref.at[pl.ds(0, at.chips - 1), 0], z_send)
    if at.cols > 1:
        left(all_ref.at[pl.ds(0, at.chips), pl.ds(0, at.cols - 1)], y_send)


def gather_shards(geo, qkv, out, router, gain_one, gain_two, terms):
    share, total = qkv.shape[0], qkv.shape[1] + out.shape[1] + 128
    pieces = 5 if total % 640 == 0 else 1
    one = pltpu.SemaphoreType.DMA
    return pl.pallas_call(
        partial(gather_kernel, geo, pieces),
        out_shape=pltpu.HBM((geo.rows, geo.cols, share, total), BF16),
        in_specs=[hbm_spec()] * 2 + [vmem_spec()] * 4,
        out_specs=hbm_spec(),
        scratch_shapes=[
            pltpu.VMEM((share, 128), BF16),
            pltpu.SemaphoreType.DMA((3,)),
            one, pltpu.SemaphoreType.DMA((pieces, max(1, geo.chips - 1))),
            one, pltpu.SemaphoreType.DMA((pieces, geo.chips, max(1, geo.cols - 1))),
            one, one,
        ],
        compiler_params=pltpu.CompilerParams(collective_id=1, has_side_effects=True),
    )(in_hbm(qkv), in_hbm(out), router, gain_one, gain_two, terms)


def reduce_part(shards, refs, groups):
    at = shards
    started = []

    def start(copy):
        copy.start()
        started.append(copy)

    def to_core(g, k):
        return remote(
            refs.part.at[at.row(at.chip(k), 1), :, :, lanes[g]], refs.from_core.at[k, :, :, lanes[g]],
            refs.core_send.at[g, k], refs.core_recv.at[g, k], {"row": at.row(at.z, 1)},
        )

    def to_col(g, k, j):
        return remote(
            refs.pair.at[k, at.col(j), :, lanes[g]], refs.from_col.at[k, j - 1, :, lanes[g]],
            refs.y_send.at[g, k, j - 1], refs.y_recv.at[g, k, j - 1], {"col": at.col(j)},
        )

    def to_chip(g, k):
        return remote(
            refs.column.at[k - 1, :, lanes[g]], refs.from_chip.at[k - 1, :, lanes[g]], refs.z_send.at[g, k - 1],
            refs.z_recv.at[g, k - 1], {"row": at.row(at.chip(k))},
        )

    def sum_cores(g, k):
        total = refs.part[at.row(at.chip(k)), :, :, lanes[g]].astype(F32)
        if at.cores > 1:
            to_core(g, k).wait_recv()
            total = total + refs.from_core[k, :, :, lanes[g]].astype(F32)
        refs.pair[k, :, :, lanes[g]] = total.astype(BF16)
        for j in range(1, at.cols):
            start(to_col(g, k, j))

    def sum_cols(g, k):
        total = refs.pair[k, at.c, :, lanes[g]].astype(F32)
        for j in range(1, at.cols):
            to_col(g, k, j).wait_recv()
            total = total + refs.from_col[k, j - 1, :, lanes[g]].astype(F32)
        if k:
            refs.column[k - 1, :, lanes[g]] = total.astype(BF16)
            start(to_chip(g, k))
        else:
            refs.shard[:, lanes[g]] = total

    lanes, waiting = [], []

    def advance(g, k):
        sum_cores(g, k)
        waiting.append((g, k))
        if len(waiting) > 2:
            sum_cols(*waiting.pop(0))

    far = sorted(range(1, at.chips), key=lambda k: abs(2 * k - at.chips))
    for places in groups:
        lanes.append(places)
        g = len(lanes) - 1
        if at.cores > 1:
            for k in far + [0]:
                start(to_core(g, k))
        if g:
            for k in far:
                advance(g - 1, k)
    for k in far:
        advance(len(lanes) - 1, k)
    for g in range(len(lanes)):
        advance(g, 0)
    while waiting:
        sum_cols(*waiting.pop(0))
    for g in range(len(lanes)):
        for k in far:
            to_chip(g, k).wait_recv()
            refs.shard[:, lanes[g]] += refs.from_chip[k - 1, :, lanes[g]].astype(F32)
    for copy in started:
        copy.wait_send()


def reduce_scratch(geo, share, width):
    chips, steps, far = geo.chips, max(1, geo.cols - 1), max(1, geo.chips - 1)
    z = pltpu.SemaphoreType.DMA((4, far))
    y = pltpu.SemaphoreType.DMA((4, chips, steps))
    core = pltpu.SemaphoreType.DMA((4, chips))
    return dict(
        from_core=pltpu.VMEM((chips, geo.cols, share, width), BF16),
        from_col=pltpu.VMEM((chips, steps, share, width), BF16),
        from_chip=pltpu.VMEM((far, share, width), BF16),
        pair=pltpu.VMEM((chips, geo.cols, share, width), BF16),
        column=pltpu.VMEM((far, share, width), BF16),
        core_send=core, core_recv=core, y_send=y, y_recv=y, z_send=z, z_recv=z,
    )


def expert_weights_kernel(experts_all, rows, pre, hidden, seen, packed, in_grad, out_grad, qkv, out, router, one, two,
                          terms):
    def product(left, right):
        left, right = (ref[:, 0].reshape(-1, ref.shape[-1]) for ref in (left, right))
        return mm(left, right, (0, 0))

    in_grad[0, 0] = product(rows, pre)
    out_grad[0, 0] = product(hidden, seen)

    @pl.when((pl.program_id(0) == 0) & (pl.program_id(1) == 0))
    def _():
        wide, narrow = qkv.shape[2], out.shape[2]
        qkv[0] = packed[:, :wide]
        out[0] = packed[:, wide : wide + narrow]
        small = packed[:, wide + narrow :]
        dims = (experts_all + 8, 128)
        pick = (iota(dims, 0) == iota(dims, 1)).astype(F32)
        lines = lax.dot_general(
            pick, small, (((1,), (1,)), ((), ())), precision=lax.Precision.HIGHEST, preferred_element_type=F32
        )
        router[0] = lines[:experts_all]
        one[...] = lines[experts_all : experts_all + 1]
        two[...] = lines[experts_all + 1 : experts_all + 2]
        terms[...] = lines[experts_all + 2 : experts_all + 3, : terms.shape[1]]


def expert_weights(geo, state, packed, terms):
    micro, local, count, width, hidden = geo.micro, geo.local_experts, geo.expert_rows, geo.width, geo.hidden
    tile = tile_of(hidden, 768)
    narrow = pl.BlockSpec((micro, 1, count, width), lambda e, f: (0, e, 0, 0))
    wide = pl.BlockSpec((micro, 1, count, tile), lambda e, f: (0, e, 0, f))
    flops = 4 * micro * local * count * width * hidden
    share = packed.shape[0]
    small = [(1, share, 3 * width), (1, share, width), (1, geo.experts_all, share), (1, share), (1, share), (1, terms)]

    def whole(dims):
        return pl.BlockSpec(dims, lambda e, f: (0,) * len(dims))

    return pl.pallas_call(
        partial(expert_weights_kernel, geo.experts_all),
        out_shape=[shape((1, local, width, hidden), F32), shape((1, local, hidden, width), F32)]
        + [shape(dims, F32) for dims in small],
        grid=(local, hidden // tile),
        in_specs=[narrow, wide, wide, narrow, whole(packed.shape)],
        out_specs=[
            pl.BlockSpec((1, 1, width, tile), lambda e, f: (0, e, 0, f)),
            pl.BlockSpec((1, 1, tile, width), lambda e, f: (0, e, f, 0)),
        ]
        + [whole(dims) for dims in small],
        compiler_params=pltpu.CompilerParams(vmem_limit_bytes=48 * MIB),
        cost_estimate=pl.CostEstimate(
            flops=flops, bytes_accessed=8 * local * hidden * width, transcendentals=0
        ),
    )(*(in_hbm(state[name]) for name in ("kept_rows", "kept_pre", "kept_hidden", "kept_seen")), packed)


def norm_backward(values, gain, grad):
    factor = norm_factor(values)
    unit = values * factor
    weighted = grad * gain
    inner = jnp.mean(weighted * unit, axis=-1, keepdims=True)
    return factor * (weighted - unit * inner), jnp.sum(grad * unit, axis=0, keepdims=True)


def dense_backward_loads(geo, m, at, copies):
    width = geo.width
    return dict(
        rest=copies.load(at.packed.at[:, pl.ds(3 * width, width + 128)], at.rest_w),
        gains=copies.load(at.gains, at.gains_here),
        residual=copies.load(at.kept_residual.at[m], at.residual),
        qkv=copies.load(at.kept_qkv.at[m], at.qkv),
        prob=copies.load(at.kept_prob.at[m], at.prob),
        stream=copies.load(at.kept_stream.at[m], at.stream),
        qkv_w=copies.load(at.packed.at[:, pl.ds(0, 3 * width)], at.qkv_w),
    )


def dense_backward_part(geo, step, at, copies, loads, enter, across):
    length, width, heads = geo.length, geo.width, geo.heads
    size = width // heads
    per = 128 // size
    m = backward_micro(geo, step)
    send = across is not None
    aux = at.aux[...]
    slope = aux[:, 0:1] * aux[:, 1:2] * (at.gates[:, 0:1] - at.gates[:, 1:2])
    expert_at = iota((length, 128), 1).astype(F32)
    logit_grad = (
        jnp.where(as_column(at.routes[0, m, 0:1, :].astype(F32)) == expert_at, slope, 0.0)
        - jnp.where(as_column(at.routes[0, m, 1:2, :].astype(F32)) == expert_at, slope, 0.0)
    ).astype(BF16)
    at.logit[...] = logit_grad
    copies.save(at.logit, at.kept_logit.at[m])
    loads["rest"].wait()
    moe_grad = at.moe_grad[...] + mm(logit_grad, at.rest_w[:, width:], (1, 1))
    loads["residual"].wait()
    loads["gains"].wait()
    part, gain_two = norm_backward(at.residual[...], at.gains_here[1:2, :], moe_grad)
    residual_grad = at.incoming[...].astype(F32) + part
    at.branch[...] = residual_grad.astype(BF16)
    copies.save(at.branch, at.kept_branch.at[m])
    at.context_grad[...] = mm(at.branch[...], at.rest_w[:, :width], (1, 1)).astype(BF16)
    which = iota((length, 128), 1) // size
    head_row = iota((128, length), 0) // size
    scale = 1.0 / math.sqrt(size)
    zero = jnp.zeros((length, 128), BF16)
    loads["qkv"].wait()
    loads["prob"].wait()
    at.sums[...] = jnp.zeros(at.sums.shape, F32)
    for j in range(width // 128):
        places = [slice(base * width + 128 * j, base * width + 128 * (j + 1)) for base in range(3)]
        queries, keys, values = (at.qkv[:, place] for place in places)
        grad = at.context_grad[:, places[0]]
        turned_keys = keys.astype(F32).T
        totals = [jnp.zeros(dims, F32) for dims in ((128, length), (length, 128), (length, 128))]
        for part_at in range(per):
            h = j * per + part_at
            own = which == part_at
            own_grad = jnp.where(own, grad, zero)
            prob = at.prob[h]
            prob_grad = mm(values, own_grad, (1, 1))
            weighted = prob.astype(F32)
            shift = jnp.sum(weighted * prob_grad, axis=0, keepdims=True)
            score_grad = (weighted * (prob_grad - shift)).astype(BF16)
            at.sums[h : h + 1, :] = diagonal_sums(score_grad.astype(F32))
            own_keys = jnp.where(head_row == part_at, turned_keys, 0.0).astype(BF16)
            totals[0] = totals[0] + mm(own_keys, score_grad, (1, 0))
            totals[1] = totals[1] + mm(score_grad, jnp.where(own, queries, zero), (1, 0))
            totals[2] = totals[2] + mm(prob, own_grad, (1, 0))
        at.qkv_grad[:, places[0]] = (totals[0].T * scale).astype(BF16)
        at.qkv_grad[:, places[1]] = (totals[1] * scale).astype(BF16)
        at.qkv_grad[:, places[2]] = totals[2].astype(BF16)
    copies.save(at.qkv_grad, at.kept_qkv_grad.at[m])
    copies.save(at.sums, at.kept_sums.at[m])
    loads["qkv_w"].wait()
    normed_grad = mm(at.qkv_grad[...], at.qkv_w[...], (1, 1))
    loads["stream"].wait()
    part, gain_one = norm_backward(at.stream[...].astype(F32), at.gains_here[0:1, :], normed_grad)
    at.gain_parts[...] = jnp.zeros(at.gain_parts.shape, F32)
    at.gain_parts[0:1, :] = gain_one
    at.gain_parts[1:2, :] = gain_two
    copies.save(at.gain_parts, at.kept_gains.at[m])
    in_grad = residual_grad + part
    at.in_grad_here[...] = in_grad
    copies.save(at.in_grad_here, at.in_grad.at[m])
    if step < geo.micro:
        at.sent_here[...] = in_grad.astype(BF16)
    if send:
        enter()
        across.send(at.sent_here, at.received_out)
    elif step < geo.micro:
        copies.save(at.sent_here, at.sent_out)
    copies.wait()
    if send:
        across.take(at.received_out)
        across.sent(at.sent_here, at.received_out)


def dense_backward_body(geo, step, at):
    send = 1 <= step < geo.micro
    across = Across(1, at.across_sems) if send else None
    if send:
        across.greet()

    def enter():
        pl.semaphore_wait(pltpu.get_barrier_semaphore(), 1)

    m = backward_micro(geo, step)
    copies = Copies(at.sems)
    aux_load = copies.load(at.kept_aux.at[m], at.aux)
    loads = dense_backward_loads(geo, m, at, copies)
    aux_load.wait()
    dense_backward_part(geo, step, at, copies, loads, enter, across)


def dense_backward_scratch(geo):
    length, width, heads = geo.length, geo.width, geo.heads
    return dict(
        aux=pltpu.VMEM((length, 128), F32),
        rest_w=pltpu.VMEM((width, width + 128), BF16),
        qkv_w=pltpu.VMEM((width, 3 * width), BF16),
        residual=pltpu.VMEM((length, width), F32),
        qkv=pltpu.VMEM((length, 3 * width), BF16),
        prob=pltpu.VMEM((heads, length, length), BF16),
        stream=pltpu.VMEM((length, width), BF16),
        logit=pltpu.VMEM((length, 128), BF16),
        branch=pltpu.VMEM((length, width), BF16),
        context_grad=pltpu.VMEM((length, width), BF16),
        qkv_grad=pltpu.VMEM((length, 3 * width), BF16),
        sums=pltpu.VMEM((geo.tall, length), F32),
        gain_parts=pltpu.VMEM((8, width), F32),
        in_grad_here=pltpu.VMEM((length, width), F32),
        gains_here=pltpu.VMEM((8, width), F32),
        sent_here=pltpu.VMEM((length, width), BF16),
        sems=pltpu.SemaphoreType.DMA((20,)),
        across_sems=pltpu.SemaphoreType.DMA((4,)),
    )


def dense_backward_refs(geo, step, given, state):
    micro, length, width = geo.micro, geo.length, geo.width
    outs = {}
    if 1 <= step < micro:
        outs["received_out"] = pltpu.HBM((length, width), BF16)
    elif step < micro:
        outs["sent_out"] = pltpu.HBM((length, width), BF16)
    names = ("kept_aux", "kept_residual", "kept_qkv", "kept_prob", "kept_stream")
    held = dict({name: state[name] for name in names}, packed=given["packed"], gains=given["gains"])
    kept = dict(
        in_grad=((micro, length, width), F32),
        kept_branch=((micro, length, width), BF16),
        kept_qkv_grad=((micro, length, 3 * width), BF16),
        kept_logit=((micro, length, 128), BF16),
        kept_gains=((micro, 8, width), F32),
        kept_sums=((micro, geo.tall, length), F32),
    )
    return dict(routes=given["routes"]), held, outs, kept


def dense_backward(geo, step, near, given, state):
    more, held, outs, kept = dense_backward_refs(geo, step, given, state)
    params = {}
    if 1 <= step < geo.micro:
        params = dict(collective_id=5 + 2 * geo.micro + step, has_side_effects=True)
    return launch(
        partial(where_active, only_section(geo, geo.micro - step), partial(dense_backward_body, geo, step)),
        near=dict(near, **more),
        held=held,
        outs=outs,
        kept=kept,
        state=state,
        scratch=dense_backward_scratch(geo),
        cost=(3_000_000_000, 14_000_000),
        **params,
    )


DENSE_GRADS = ("normed", "qkv_grad", "context", "branch", "moe_in", "logit")


def dense_weights_groups(geo, at):
    width = geo.width
    copies = Copies(at.sems)
    loads = {}
    for name in DENSE_GRADS + ("gains", "sums"):
        loads[name] = copies.load(getattr(at, "kept_" + name), getattr(at, name))

    def product(left, right):
        left, right = (ref[...].reshape(-1, ref.shape[-1]) for ref in (left, right))
        return mm(left, right, (0, 0))

    def ready(*names):
        for name in names:
            loads[name].wait()

    def put(places, block):
        block = block.astype(BF16)
        if len(at.part.shape) == 4:
            at.part[:, :, :, places] = block.reshape(at.part.shape[:3] + block.shape[1:])
        else:
            at.part[:, places] = block

    ready("normed", "qkv_grad")
    normed = at.normed[...].reshape(-1, width)
    for j in range(0, 3 * width, width):
        grad = at.qkv_grad[:, :, j : j + width].reshape(-1, width)
        put(slice(j, j + width), mm(normed, grad, (0, 0)))
        yield slice(j, j + width)
    ready("context", "branch")
    put(slice(3 * width, 4 * width), product(at.context, at.branch))
    ready("moe_in", "logit", "gains", "sums")
    small = product(at.moe_in, at.logit)
    by_term = lax.dot_general(
        jnp.sum(at.sums[...], axis=0), at.spread[...].astype(F32), (((1,), (1,)), ((), ())),
        precision=lax.Precision.HIGHEST, preferred_element_type=F32,
    )
    bias_row = jnp.sum(by_term[: geo.heads] * at.head_pick[...], axis=0, keepdims=True)
    gain_rows = jnp.sum(at.gains[...], axis=0)
    place = iota((128, width), 0)
    rows = jnp.zeros((128, width), F32)
    for k, row in enumerate((gain_rows[0:1], gain_rows[1:2], bias_row)):
        rows = jnp.where(place == geo.experts_all + k, row, rows)
    put(slice(4 * width, 4 * width + 128), small + rows.T)
    yield slice(3 * width, 4 * width + 128)


def dense_weights_body(geo, at):
    for _ in dense_weights_groups(geo, at):
        pass


def reduce_body(geo, at):
    shards = Shards(geo)
    shards.greet()

    def groups():
        for g, places in enumerate(dense_weights_groups(geo, at)):
            if g == 0:
                shards.await_greetings()
            yield places

    reduce_part(shards, at, groups())


def dense_weights(geo, head_pick, spread_table, state):
    held = {"kept_" + name: state["kept_" + name] for name in DENSE_GRADS + ("gains", "sums")}
    scratch = {name: pltpu.VMEM(held["kept_" + name].shape, BF16) for name in DENSE_GRADS}
    scratch.update(
        sems=pltpu.SemaphoreType.DMA((len(DENSE_GRADS) + 2,)),
        gains=pltpu.VMEM(state["kept_gains"].shape, F32), sums=pltpu.VMEM(state["kept_sums"].shape, F32),
    )
    share, total = geo.width // geo.sources, 4 * geo.width + 128
    parts = (geo.rows, geo.cols, share, total)
    fused = share % 16 == 0
    outs = dict(shard=shape((share, total), F32)) if fused else dict(part=shape((geo.width, total), BF16))
    params = {}
    if fused:
        scratch.update(reduce_scratch(geo, share, total), part=pltpu.VMEM(parts, BF16))
        params = dict(collective_id=2, has_side_effects=True)
    results = launch(
        partial(reduce_body if fused else dense_weights_body, geo),
        near=dict(head_pick=head_pick, spread=spread_table),
        held=held,
        outs=outs,
        scratch=scratch,
        spare=24,
        cost=(3_000_000_000, 10_000_000),
        **params,
    )
    if fused:
        return results["shard"]

    def body(at):
        shards = Shards(geo)
        shards.greet()
        shards.await_greetings()
        reduce_part(shards, at, [slice(0, total)])

    return launch(
        body,
        near=dict(part=results["part"].reshape(parts)),
        outs=dict(shard=shape((share, total), F32)),
        scratch=reduce_scratch(geo, share, total),
        collective_id=2,
        has_side_effects=True,
    )["shard"]


def on_device(
    inputs, cotangent, segments, routes, order, attn_gain, qkv_weight, position_bias, out_weight, moe_gain,
    router_weight, expert_in, expert_out,
):
    micro, length, width = inputs.shape
    local_experts, hidden = expert_in.shape[1], expert_in.shape[3]
    experts_all = router_weight.shape[2]
    row_count, col_count = lax.axis_size("row"), lax.axis_size("col")
    devices = row_count * col_count
    share = width // devices
    terms = position_bias.shape[1]
    heads = terms * devices // DISTANCE_BUCKETS
    geo = Geometry(micro, length, width, heads, experts_all, local_experts, hidden, row_count, col_count)
    packed = gather_shards(
        geo, qkv_weight[0], out_weight[0], router_weight[0].T, attn_gain, moe_gain, position_bias
    ).reshape(width, -1)
    indicator = buckets(length)
    row_at = np.arange(width)
    term_at = np.where(row_at % share < terms, row_at // share * terms + row_at % share, -1)
    head_pick = jnp.asarray((term_at % heads == np.arange(heads)[:, None]) & (term_at >= 0), F32)
    spread_table = jnp.asarray(indicator[np.maximum(term_at, 0) // heads], BF16)
    prepared = launch(
        partial(prepare, experts_all),
        near=dict(head_pick=head_pick, spread=spread_table),
        held=dict(packed=packed),
        outs=dict(gains=pltpu.HBM((8, width), F32), bias=pltpu.HBM((heads, length, length), BF16)),
        scratch=dict(
            small=pltpu.VMEM((width, 128), BF16), gains_here=pltpu.VMEM((8, width), F32),
            bias_here=pltpu.VMEM((heads, length, length), BF16), sems=pltpu.SemaphoreType.DMA((3,)),
        ),
        cost=(50_000_000, 6_000_000),
    )
    given = dict(
        prepared, packed=packed, inputs=inputs, cotangent=cotangent, w_in=expert_in[0], w_out=expert_out[0],
        segments=segments, order=order, routes=jnp.swapaxes(routes, 2, 3),
        bases=jnp.asarray(geo.bases()),
    )
    state = {}
    received = None
    for tick in range(micro + 1):
        received = forward_tick(geo, tick, given, state, received)
    sent = received = None
    for step in range(micro + 1):
        passed = backward_step(geo, step, given, state, sent, received)
        sent, received = passed.get("sent_out"), passed.get("received_out")
    packed = dense_weights(geo, head_pick, spread_table, state)
    expert_in_grad, expert_out_grad, qkv, out, router, gain_one, gain_two, bias = expert_weights(
        geo, state, packed, terms
    )
    return (
        state["out"][None], state["in_grad"][None], gain_one, qkv, bias, out, gain_two,
        jnp.swapaxes(router, 1, 2), expert_in_grad,
        expert_out_grad,
    )


def solution(mesh):
    tokens = ("row", "col")
    return jax.shard_map(
        on_device,
        mesh=mesh,
        in_specs=(
            P(None, tokens, None),
            P(None, tokens, None),
            P(None, tokens),
            P("section", None, tokens, None),
            P("section", None, tokens, None),
            P("section", tokens),
            P("section", tokens, None),
            P("section", tokens),
            P("section", tokens, None),
            P("section", tokens),
            P("section", tokens, None),
            P("section", "row", None, "col"),
            P("section", "row", "col", None),
        ),
        out_specs=(
            P("section", None, tokens, None),
            P("section", None, tokens, None),
            P("section", tokens),
            P("section", tokens, None),
            P("section", tokens),
            P("section", tokens, None),
            P("section", tokens),
            P("section", tokens, None),
            P("section", "row", None, "col"),
            P("section", "row", "col", None),
        ),
        check_vma=False,
    )
```
